32 devices in a mesh: dp: 8 (over y, x, core), enc: 4 (over z).
Axes of the slice: x: 2, y: 2, z: 4, core: 2. Of those that a mesh axis runs over, the one named last changes fastest.
Arguments:
- hidden_in: bfloat16 [4096, 1472], P(('dp', 'enc')), may hold values from -6 to 6
- encoder_out: bfloat16 [8192, 1472], P(('dp', 'enc')), may hold values from -6 to 6
- grad_out: bfloat16 [4096, 1472], P(('dp', 'enc')), may hold values from -6 to 6
- tgt_lengths: int32 [8, 4], P('dp'), may hold values from 1 to 509, as said below
- enc_lengths: int32 [8, 4], P('dp'), may hold values from 1 to 1021, as said below
- rel_bucket: int32 [512], replicated, may hold values from 0 to 31, as said below
- norm1_gain: float32 [1472], replicated, may hold values from 0.5 to 1.5
- self_q: float32 [1472, 384], P(None, ('dp', 'enc')), may hold values from -0.01953125 to 0.01953125
- self_k: float32 [1472, 384], P(None, ('dp', 'enc')), may hold values from -0.15625 to 0.15625
- self_v: float32 [1472, 384], P(None, ('dp', 'enc')), may hold values from -0.15625 to 0.15625
- self_o: float32 [384, 1472], P(('dp', 'enc')), may hold values from -1.75 to 1.75
- rel_table: float32 [32, 6], replicated, may hold values from -4 to 4
- norm2_gain: float32 [1472], replicated, may hold values from 0.5 to 1.5
- cross_q: float32 [1472, 384], P(None, ('dp', 'enc')), may hold values from -0.01953125 to 0.01953125
- cross_k: float32 [1472, 384], P(None, ('dp', 'enc')), may hold values from -0.15625 to 0.15625
- cross_v: float32 [1472, 384], P(None, ('dp', 'enc')), may hold values from -0.15625 to 0.15625
- cross_o: float32 [384, 1472], P(('dp', 'enc')), may hold values from -2.5 to 2.5
- norm3_gain: float32 [1472], replicated, may hold values from 0.5 to 1.5
- ff_gate: float32 [1472, 3584], P(None, ('dp', 'enc')), may hold values from -0.15625 to 0.15625
- ff_up: float32 [1472, 3584], P(None, ('dp', 'enc')), may hold values from -0.15625 to 0.15625
- ff_out: float32 [3584, 1472], P(('dp', 'enc')), may hold values from -0.09375 to 0.09375
Outputs:
- hidden_out: bfloat16 [4096, 1472], P(('dp', 'enc'))
- hidden_grad: float32 [4096, 1472], P(('dp', 'enc'))
- encoder_grad: float32 [8192, 1472], P(('dp', 'enc'))
- norm1_gain_grad: float32 [1472], replicated
- self_q_grad: float32 [1472, 384], P(None, ('dp', 'enc'))
- self_k_grad: float32 [1472, 384], P(None, ('dp', 'enc'))
- self_v_grad: float32 [1472, 384], P(None, ('dp', 'enc'))
- self_o_grad: float32 [384, 1472], P(('dp', 'enc'))
- rel_table_grad: float32 [32, 6], replicated
- norm2_gain_grad: float32 [1472], replicated
- cross_q_grad: float32 [1472, 384], P(None, ('dp', 'enc'))
- cross_k_grad: float32 [1472, 384], P(None, ('dp', 'enc'))
- cross_v_grad: float32 [1472, 384], P(None, ('dp', 'enc'))
- cross_o_grad: float32 [384, 1472], P(('dp', 'enc'))
- norm3_gain_grad: float32 [1472], replicated
- ff_gate_grad: float32 [1472, 3584], P(None, ('dp', 'enc'))
- ff_up_grad: float32 [1472, 3584], P(None, ('dp', 'enc'))
- ff_out_grad: float32 [3584, 1472], P(('dp', 'enc'))
The draws below stay inside these ranges and needn't reach their ends.
Inputs may be any that keep to these rules, and one draw needn't show every extreme that they name: `tgt_lengths`: row g holds the target lengths of group g's 4 items, whose rows follow one another in that order; each row sums to 512. In each row one item, the same as in enc_lengths, is longer than 384; the others are at most 32, rounded down. In one group the other items have length 1. `enc_lengths`: row g holds the encoder lengths of group g's 4 items in the same order; each row sums to 1024. The item that is long in tgt_lengths is longer than 768; the others are at most 64, rounded down. In one group the other items have length 1. `rel_bucket`: entry d is the bucket of a key d rows before its query: 0 at d = 0, never falling as d grows, and 31 for every d of 31 or more.
All inputs are finite; a program needn't handle non-finite values.
Results may differ from the reference program's by a relative error of at most 0.03.
Values may be sent and summed in bfloat16 or wider, within the bound.
A program may use at most 384 MiB of HBM per device.

```python
import jax
import jax.numpy as jnp
from jax import lax

D = 1472
FF = 3584
HEADS = 6
HEAD = 64
BUCKETS = 32
ITEMS = 4
TOK_DEV = 128
ENC_DEV = 256
INNER = 384
TOK_DP = 512
ENC_DP = 1024
GROUPS = 8
TOKENS = 4096
ENC_ROWS = 8192


def long_slot(key):
    return jax.random.randint(key, (GROUPS, 1), 0, ITEMS)


def packed_lengths(key, short_most, group_total, chosen):
    pick_key = jax.random.fold_in(key, 11)
    short_lengths = jax.random.randint(key, (GROUPS, ITEMS), 1, short_most + 1)
    forced_group = jax.random.randint(pick_key, (), 0, GROUPS)
    group_rows = jnp.arange(GROUPS, dtype=jnp.int32)[:, None]
    short_lengths = jnp.where(group_rows == forced_group, 1, short_lengths)
    slots = jnp.arange(ITEMS, dtype=jnp.int32)[None, :]
    is_long = slots == chosen
    others = jnp.sum(jnp.where(is_long, 0, short_lengths), axis=1, keepdims=True)
    return jnp.where(is_long, group_total - others, short_lengths).astype(jnp.int32)


def draw_tgt_lengths(key, part):
    chosen = long_slot(key)
    key = jax.random.fold_in(key, 3)
    return packed_lengths(key, TOK_DEV // ITEMS, TOK_DP, chosen)


def draw_enc_lengths(key, part):
    chosen = long_slot(key)
    key = jax.random.fold_in(key, 5)
    return packed_lengths(key, ENC_DEV // ITEMS, ENC_DP, chosen)


def draw_rel_bucket(key, part):
    key = jax.random.fold_in(key, 7)
    steps_up = jax.random.randint(key, (TOK_DP,), 1, 3)
    steps_up = jnp.where(jnp.arange(TOK_DP) == 0, 0, steps_up)
    return jnp.minimum(jnp.cumsum(steps_up), BUCKETS - 1).astype(jnp.int32)


def levels(rng, extent, cuts, low, high):
    def one(dim, parts):
        heights = jax.random.uniform(jax.random.fold_in(jax.random.fold_in(rng, 6), dim), (parts,), jnp.float32, low / len(cuts), high / len(cuts))
        return jnp.repeat(jnp.exp(heights), extent[dim] // parts).reshape((-1,) + (1,) * (len(extent) - dim - 1))

    level = one(*cuts[0])
    for cut in cuts[1:]:
        level = level * one(*cut)
    return level


def normal_values(own_key, extent, spread, limit, pieces=(), kind=jnp.bfloat16):
    array = spread * jax.random.normal(own_key, extent, jnp.float32)
    if pieces:
        array = array * levels(own_key, extent, pieces, -0.22, 0.18)
    return jnp.clip(array, -limit, limit).astype(kind)


def setup_inputs(seed: int = 0) -> dict:
    key_of = jax.random.split(jax.random.key(seed), 22)
    hidden_in = normal_values(key_of[0], (TOKENS, D), 1.0, 6.0, ((0, 32),))
    encoder_out = normal_values(key_of[1], (ENC_ROWS, D), 1.0, 6.0, ((0, 32),))
    grad_out = normal_values(key_of[2], (TOKENS, D), 1.0, 6.0, ((0, 32),))
    tgt_lengths = draw_tgt_lengths(jax.random.fold_in(key_of[21], 71), 0)
    enc_lengths = draw_enc_lengths(jax.random.fold_in(key_of[21], 71), 0)
    rel_bucket = draw_rel_bucket(jax.random.fold_in(key_of[21], 71), 0)
    norm1_gain = jnp.clip(1.0 + 0.1 * jax.random.normal(key_of[6], (D,), jnp.float32), 0.5, 1.5)
    self_q = normal_values(key_of[7], (D, INNER), (D * HEAD) ** -0.5, 0.01953125, ((1, 32),), jnp.float32)
    self_k = normal_values(key_of[8], (D, INNER), D ** -0.5, 0.15625, ((1, 32),), jnp.float32)
    self_v = normal_values(key_of[9], (D, INNER), D ** -0.5, 0.15625, ((1, 32),), jnp.float32)
    self_o = normal_values(key_of[10], (INNER, D), (INNER // 32) ** -0.5, 1.75, ((0, 32),), jnp.float32)
    rel_table = normal_values(key_of[11], (BUCKETS, HEADS), 1.0, 4.0, (), jnp.float32)
    norm2_gain = jnp.clip(1.0 + 0.1 * jax.random.normal(key_of[12], (D,), jnp.float32), 0.5, 1.5)
    cross_q = normal_values(key_of[13], (D, INNER), (D * HEAD) ** -0.5, 0.01953125, ((1, 32),), jnp.float32)
    cross_k = normal_values(key_of[14], (D, INNER), D ** -0.5, 0.15625, ((1, 32),), jnp.float32)
    cross_v = normal_values(key_of[15], (D, INNER), D ** -0.5, 0.15625, ((1, 32),), jnp.float32)
    cross_o = normal_values(key_of[16], (INNER, D), (INNER // 64) ** -0.5, 2.5, ((0, 32),), jnp.float32)
    norm3_gain = jnp.clip(1.0 + 0.1 * jax.random.normal(key_of[17], (D,), jnp.float32), 0.5, 1.5)
    ff_gate = normal_values(key_of[18], (D, FF), D ** -0.5, 0.15625, ((1, 32),), jnp.float32)
    ff_up = normal_values(key_of[19], (D, FF), D ** -0.5, 0.15625, ((1, 32),), jnp.float32)
    ff_out = normal_values(key_of[20], (FF, D), FF ** -0.5, 0.09375, ((0, 32),), jnp.float32)
    return {"hidden_in": hidden_in, "encoder_out": encoder_out, "grad_out": grad_out, "tgt_lengths": tgt_lengths, "enc_lengths": enc_lengths, "rel_bucket": rel_bucket, "norm1_gain": norm1_gain, "self_q": self_q, "self_k": self_k, "self_v": self_v, "self_o": self_o, "rel_table": rel_table, "norm2_gain": norm2_gain, "cross_q": cross_q, "cross_k": cross_k, "cross_v": cross_v, "cross_o": cross_o, "norm3_gain": norm3_gain, "ff_gate": ff_gate, "ff_up": ff_up, "ff_out": ff_out}


EPSILON = 1e-06
MASKED = -1e+30
HIGHEST = lax.Precision.HIGHEST

@jax.custom_vjp
def low(v):
    return lax.optimization_barrier(v.astype(jnp.bfloat16)).astype(jnp.float32)

@jax.custom_vjp
def low_back(v):
    return v

def low_keep(v):
    return (low(v), None)

def low_pass(kept, grad):
    return (grad,)

def back_keep(v):
    return (v, None)

def back_low(kept, grad):
    return (low(grad),)
low.defvjp(low_keep, low_pass)
low_back.defvjp(back_keep, back_low)

def product(left, right):
    return jnp.dot(left, right, precision=HIGHEST, preferred_element_type=jnp.float32)

def rms_scale(values, gain):
    return values * lax.rsqrt(lax.optimization_barrier(jnp.mean(values * values, axis=-1, keepdims=True)) + EPSILON) * gain

def item_ids(lengths, total_rows):
    ends = jnp.cumsum(lengths)
    places = jnp.arange(total_rows, dtype=jnp.int32)
    return lax.optimization_barrier(jnp.sum((ends[None, :] <= places[:, None]).astype(jnp.int32), axis=1)).astype(jnp.int32)

def masked_softmax_values(scores, allowed, value_heads):
    scores = jnp.where(allowed[None], low_back(scores), MASKED)
    largest = lax.optimization_barrier(jnp.max(scores, axis=2, keepdims=True))
    weights = jnp.exp(scores - largest)
    totals = lax.optimization_barrier(jnp.sum(weights, axis=2))
    numerator = low_back(jnp.einsum('hqk,khe->qhe', low(weights), value_heads, precision=HIGHEST))
    return low(numerator / jnp.transpose(totals)[:, :, None]).reshape(numerator.shape[0], HEADS * HEAD)

def attend(queries, key_rows, value_rows, geometry):
    total_rows = queries.shape[0]
    block_rows = min(512, total_rows)
    key_heads = key_rows.reshape(key_rows.shape[0], HEADS, HEAD)
    value_heads = value_rows.reshape(value_rows.shape[0], HEADS, HEAD)

    def one_block(inputs):
        query_block, first_row = inputs
        scores = jnp.einsum('qhe,khe->hqk', query_block.reshape(block_rows, HEADS, HEAD), key_heads, precision=HIGHEST)
        scores, allowed = geometry(scores, first_row + jnp.arange(block_rows, dtype=jnp.int32))
        return masked_softmax_values(scores, allowed, value_heads)
    starts = jnp.arange(total_rows // block_rows, dtype=jnp.int32) * block_rows
    blocked = queries.reshape(total_rows // block_rows, block_rows, HEADS * HEAD)
    result = lax.map(jax.checkpoint(one_block), (blocked, starts))
    return result.reshape(total_rows, HEADS * HEAD)

def self_geometry(item_of, buckets, rel_bias):
    total_rows = item_of.shape[0]
    places = jnp.arange(total_rows, dtype=jnp.int32)

    def apply_bias(scores, query_rows):
        distance = query_rows[:, None] - places[None, :]
        bucket_index = buckets[jnp.clip(distance, 0, total_rows - 1)]
        position_bias = jnp.transpose(rel_bias[bucket_index], (2, 0, 1))
        allowed = (distance >= 0) & (item_of[query_rows][:, None] == item_of[None, :])
        return (scores + position_bias, allowed)
    return apply_bias

def cross_geometry(query_items, key_items):

    def apply_mask(scores, query_rows):
        return (scores, query_items[query_rows][:, None] == key_items[None, :])
    return apply_mask

def group_layer(hidden, encoded, tgt_len, enc_len, buckets, weights):
    gain_one, w_query, w_key, w_value, w_out, rel_bias, gain_two, c_query, c_key, c_value, c_out, gain_three, w_gate, w_up, w_down = weights
    tgt_items = item_ids(tgt_len, TOK_DP)
    enc_items = item_ids(enc_len, ENC_DP)
    normed = low(rms_scale(hidden, gain_one))
    queries = low(low_back(product(normed, w_query)))
    key_rows = low(low_back(product(normed, w_key)))
    value_rows = low(low_back(product(normed, w_value)))
    attended = attend(queries, key_rows, value_rows, self_geometry(tgt_items, buckets, rel_bias))
    after_self = hidden + low_back(product(attended, w_out))
    normed_two = low(rms_scale(after_self, gain_two))
    cross_queries = low(low_back(product(normed_two, c_query)))
    cross_keys = low(low_back(product(encoded, c_key)))
    cross_values = low(low_back(product(encoded, c_value)))
    attended_two = attend(cross_queries, cross_keys, cross_values, cross_geometry(tgt_items, enc_items))
    after_cross = after_self + low_back(product(attended_two, c_out))
    normed_three = low(rms_scale(after_cross, gain_three))
    gate_pre = low_back(product(normed_three, w_gate))
    up_pre = low_back(product(normed_three, w_up))
    hidden_act = low(jax.nn.gelu(gate_pre, approximate=True) * up_pre)
    return after_cross + low_back(product(hidden_act, w_down))

def reference(hidden_in, encoder_out, grad_out, tgt_lengths, enc_lengths, rel_bucket, norm1_gain, self_q, self_k, self_v, self_o, rel_table, norm2_gain, cross_q, cross_k, cross_v, cross_o, norm3_gain, ff_gate, ff_up, ff_out):
    masters = (norm1_gain, self_q, self_k, self_v, self_o, rel_table, norm2_gain, cross_q, cross_k, cross_v, cross_o, norm3_gain, ff_gate, ff_up, ff_out)

    def forward(hidden, encoded, params):
        weights = (params[0], low(params[1]), low(params[2]), low(params[3]), low(params[4]), params[5], params[6], low(params[7]), low(params[8]), low(params[9]), low(params[10]), params[11], low(params[12]), low(params[13]), low(params[14]))

        def one_group(carry, group):
            layer_out = jax.checkpoint(group_layer)(group[0], group[1], group[2], group[3], rel_bucket, weights)
            return (carry, layer_out)
        groups_in = (hidden.reshape(GROUPS, TOK_DP, D), encoded.reshape(GROUPS, ENC_DP, D), tgt_lengths, enc_lengths)
        unused_carry, stacked = lax.scan(one_group, jnp.int32(0), groups_in)
        return stacked.reshape(TOKENS, D)
    result, pull = jax.vjp(forward, hidden_in.astype(jnp.float32), encoder_out.astype(jnp.float32), masters)
    input_grad, encoder_grad, param_grads = pull(grad_out.astype(jnp.float32))
    return (result.astype(jnp.bfloat16), input_grad, encoder_grad, param_grads[0], param_grads[1], param_grads[2], param_grads[3], param_grads[4], param_grads[5], param_grads[6], param_grads[7], param_grads[8], param_grads[9], param_grads[10], param_grads[11], param_grads[12], param_grads[13], param_grads[14])
```

```python
import functools

import jax
import jax.numpy as jnp
from jax import lax
from jax.experimental import pallas as pl
from jax.experimental.pallas import tpu as pltpu
from jax.sharding import PartitionSpec as P

HEADS = 6
HEAD = 64
BUCKETS = 32
EPSILON = 1e-06
MASKED = -1e30
PAD = 16
MESH = pl.DeviceIdType.MESH
LOW = jnp.bfloat16
F32 = jnp.float32
NN = (((1,), (0,)), ((), ()))
NT = (((1,), (1,)), ((), ()))
TN = (((0,), (0,)), ((), ()))
ANY = pl.BlockSpec(memory_space=pl.ANY)
VM = pl.BlockSpec(memory_space=pltpu.VMEM)


def mm(left, right, dims=NN):
    return lax.dot_general(left, right, dims, preferred_element_type=F32)


def places():
    dp = lax.axis_index("dp")
    enc = lax.axis_index("enc")
    core = lax.rem(dp, 2)
    x = lax.rem(lax.div(dp, 2), 2)
    y = lax.div(dp, 4)
    sib = dp + 1 - 2 * core
    xn = dp + 2 - 4 * x
    yn = dp + 4 - 8 * y
    return dp, enc, sib, xn, yn


def enter(dp, enc, sib, xn, yn):
    barrier = pltpu.get_barrier_semaphore()
    targets = [(sib, enc), (xn, enc), (yn, enc), (xn + yn - dp, enc)]
    targets += [(dp, lax.rem(enc + k, 4)) for k in (1, 2, 3)]
    for target in targets:
        pl.semaphore_signal(barrier, inc=1, device_id=target, device_id_type=MESH)
    pl.semaphore_wait(barrier, len(targets))


class Sems:
    def __init__(self, send, recv):
        self.send, self.recv, self.used = send, recv, 0

    def take(self, count):
        first = self.used
        self.used += count
        return first


def remote(src, dst, send, recv, target):
    return pltpu.make_async_remote_copy(
        src_ref=src, dst_ref=dst, send_sem=send, recv_sem=recv, device_id=target, device_id_type=MESH
    )


class ZGather:
    def __init__(self, at, own, where, sems):
        self.at, self.own, self.sems = at, own, sems
        self.dp, self.enc = where[0], where[1]
        self.base = sems.take(4)

    def _copy(self, src_ref, place, k, target):
        s = self.sems
        return remote(
            src_ref, self.at(place), s.send.at[self.base + k], s.recv.at[self.base + place], (self.dp, target)
        )

    def _direct(self, act):
        enc = self.enc
        for k in (1, 3, 2):
            target = lax.rem(enc + k, 4)
            if k == 2:
                act(self._copy(self.own, enc, k, target))
            else:

                @pl.when(enc != (3 if k == 1 else 0))
                def _():
                    act(self._copy(self.own, enc, k, target))

    def start(self):
        self._direct(lambda c: c.start())

    def _middle(self, act):
        enc = self.enc

        @pl.when((enc == 1) | (enc == 2))
        def _():
            src = 3 * (2 - enc)
            act(self._copy(self.at(src), src, 0, 3 * (enc - 1)), src)

    def forward(self):
        def go(copy, src):
            copy.wait_recv()
            copy.start()

        self._middle(go)

    def wait(self, k):
        enc = self.enc
        place = lax.rem(enc + k, 4)
        copy = self._copy(self.at(place), place, 0, enc)
        if k == 2:

            @pl.when((enc == 0) | (enc == 3))
            def _():
                copy.wait_recv()
        else:
            copy.wait_recv()

    def finish(self):
        self._direct(lambda c: c.wait_send())
        self._middle(lambda c, src: c.wait_send())


class ChipGather:
    def __init__(self, at, own, rows, where, sems):
        self.at, self.own, self.rows, self.sems, self.where = at, own, rows, sems, where
        self.base = sems.take(9)
        self.half = (rows // 2 + PAD - 1) // PAD * PAD

    def _copy(self, i):
        dp, enc, sib, xn, yn = self.where
        rows, half = self.rows, self.half
        diag = xn + yn - dp
        block, lo, n, target = (
            (dp, 0, rows, xn),
            (dp, 0, rows, yn),
            (dp, 0, rows, sib),
            (xn, 0, rows, sib),
            (yn, 0, rows, sib),
            (xn, 0, half, yn),
            (yn, half, rows - half, xn),
            (diag, 0, half, sib),
            (diag, half, rows - half, sib),
        )[i]
        src = self.own if i < 3 else self.at(block, lo, n)
        s = self.sems
        return remote(
            src, self.at(block, lo, n), s.send.at[self.base + i], s.recv.at[self.base + i], (target, enc)
        )

    def step1(self):
        for i in (0, 1, 2):
            self._copy(i).start()

    def step2(self):
        self._copy(0).wait_recv()
        self._copy(5).start()
        self._copy(3).start()
        self._copy(1).wait_recv()
        self._copy(6).start()
        self._copy(4).start()

    def step3(self):
        self._copy(5).wait_recv()
        self._copy(7).start()
        self._copy(6).wait_recv()
        self._copy(8).start()

    def done(self):
        for i in (2, 3, 4, 7, 8):
            self._copy(i).wait_recv()

    def finish(self):
        for i in range(9):
            self._copy(i).wait_send()


def spread_matrix(padded, compact, width):
    row = lax.broadcasted_iota(jnp.int32, (padded, compact), 0)
    col = lax.broadcasted_iota(jnp.int32, (padded, compact), 1)
    scale = (1 << 19) // width + 1
    place = col + (PAD - width) * lax.shift_right_logical(col * scale, 19)
    return jnp.where(row == place, 1.0, 0.0).astype(LOW)


def rms_rows(values, gain):
    inv = lax.rsqrt(jnp.mean(values * values, axis=-1, keepdims=True) + EPSILON)
    return values * inv * gain


def low_lanes(rows):
    return lax.broadcasted_iota(jnp.int32, (rows, 2 * HEAD), 1) < HEAD


def one_head(pair, half):
    keep = low_lanes(pair.shape[0])
    if half:
        keep = jnp.logical_not(keep)
    return jnp.where(keep, pair.astype(F32), 0.0).astype(LOW)


def self_bias(rel_u, rows, cols):
    wide = jnp.broadcast_to(rel_u, (rows, rel_u.shape[1]))
    return pltpu.roll(wide, 0, 1, stride=1, stride_axis=0)[:, :cols]


def item_of(lengths_ref, place):
    end, item = jnp.int32(0), jnp.zeros_like(place)
    for b in range(4):
        end = end + lengths_ref[0, b]
        item = item + jnp.where(end <= place, 1, 0)
    return item


def attention_pair(q_pair, k_pair, v_pair, allowed, biases, keep_probs):
    rows = q_pair.shape[0]
    nums, totals = [], []
    for half in (0, 1):
        scores = mm(one_head(q_pair, half), k_pair, NT)
        if biases is not None:
            scores = scores + biases[half]
        scores = jnp.where(allowed, scores, MASKED)
        weights = jnp.exp(scores - jnp.max(scores, axis=1, keepdims=True))
        totals.append(jnp.sum(weights, axis=1, keepdims=True))
        probs = weights.astype(LOW)
        keep_probs(half, probs)
        nums.append(mm(probs, v_pair))
    low = low_lanes(rows)
    return jnp.where(low, nums[0], nums[1]), jnp.where(low, totals[0], totals[1])


def forward_kernel(
    width,
    tgt_len, enc_len, x_ref, e_ref, dy_ref, watt_ref, wff_ref, gain1, gain2, gain3, rel_u,
    watt_out, wff_out, dy_out, x1_out, x2_out, n3_out, q1_out, kv1_out, q2_out, kv2_out,
    pr1_out, pr2_out, num1_out, num2_out, tot1_out, tot2_out,
    w, pm, send, recv, local,
):
    where = places()
    dp, enc, sib, xn, yn = where
    sems = Sems(send, recv)
    own, wide = x_ref.shape
    own_enc = e_ref.shape[0]
    inner = HEADS * HEAD
    padded = w.shape[1]
    ff_rows = wff_ref.shape[1]
    group = 4 * own

    def rows_at(ref, first, count):
        return ref.at[pl.ds(pl.multiple_of(first, PAD), count), :]

    def mats_at(ref, lo, hi, first, count):
        return ref.at[lo:hi, pl.ds(pl.multiple_of(first, PAD), count), :]

    chunks = ((0, 3), (3, 5), (5, 8))
    zs, chips = [], []
    for lo, hi in chunks:
        zs.append(
            ZGather(
                lambda e, lo=lo, hi=hi: mats_at(w, lo, hi, dp * 4 * PAD + e * PAD, PAD),
                watt_ref.at[lo:hi], where, sems,
            )
        )
        chips.append(
            ChipGather(
                lambda d, a, n, lo=lo, hi=hi: mats_at(w, lo, hi, d * 4 * PAD + a, n),
                mats_at(w, lo, hi, dp * 4 * PAD, 4 * PAD), 4 * PAD, where, sems,
            )
        )
    ff = ChipGather(
        lambda d, a, n: mats_at(wff_out, 0, 3, d * ff_rows + a, n), wff_ref, ff_rows, where, sems
    )
    dyz = ZGather(lambda e: rows_at(dy_out, e * own, own), dy_ref, where, sems)
    kvz = ZGather(
        lambda e: rows_at(kv1_out, e * own, own), rows_at(kv1_out, enc * own, own), where, sems
    )
    kvz2 = ZGather(
        lambda e: rows_at(kv2_out, e * own_enc, own_enc),
        rows_at(kv2_out, enc * own_enc, own_enc), where, sems,
    )

    enter(*where)
    zs[0].start()
    own_dy = pltpu.make_async_copy(dy_ref, rows_at(dy_out, enc * own, own), local.at[0])
    own_ff = pltpu.make_async_copy(wff_ref, mats_at(wff_out, 0, 3, dp * ff_rows, ff_rows), local.at[1])
    own_dy.start()
    own_ff.start()
    w[:, pl.ds(pl.multiple_of(dp * 4 * PAD + enc * PAD, PAD), PAD), :] = watt_ref[...]
    pm[...] = spread_matrix(padded, inner, width)
    x = x_ref[...].astype(F32)
    n1 = rms_rows(x, gain1[...]).astype(LOW)

    def compact(values):
        return mm(values.astype(LOW), pm[...]).astype(LOW)

    def spread(values):
        return mm(values, pm[...], NT).astype(LOW)

    zs[0].forward()
    for k in (1, 2, 3):
        zs[0].wait(k)
    chips[0].step1()
    zs[1].start()
    zs[1].forward()
    for k in (1, 2, 3):
        zs[1].wait(k)
    chips[0].step2()
    chips[1].step1()
    zs[2].start()
    chips[0].step3()
    chips[0].done()

    q1 = compact(mm(n1, w[0], NT))
    own_rows = pl.ds(pl.multiple_of(enc * own, PAD), own)
    kv1_out[own_rows, 0:inner] = compact(mm(n1, w[1], NT))
    kv1_out[own_rows, inner : 2 * inner] = compact(mm(n1, w[2], NT))
    q1_out[...] = q1
    kvz.start()
    zs[2].forward()
    chips[1].step2()
    for k in (1, 2, 3):
        zs[2].wait(k)
    chips[2].step1()
    chips[1].step3()
    chips[1].done()
    kvz.forward()
    own_enc_rows = pl.ds(pl.multiple_of(enc * own_enc, PAD), own_enc)
    kv2_out[own_enc_rows, 0:inner] = compact(mm(e_ref[...], w[3], NT))
    kv2_out[own_enc_rows, inner : 2 * inner] = compact(mm(e_ref[...], w[4], NT))
    kvz2.start()
    chips[2].step2()
    ff.step1()
    for k in (1, 2, 3):
        kvz.wait(k)

    row_place = enc * own + lax.broadcasted_iota(jnp.int32, (own, 1), 0)
    col_place = lax.broadcasted_iota(jnp.int32, (1, group), 1)
    own_items = item_of(tgt_len, row_place)
    allowed = (own_items == item_of(tgt_len, col_place)) & (col_place <= row_place)
    for pair in range(HEADS // 2):
        lanes = slice(pair * 2 * HEAD, (pair + 1) * 2 * HEAD)
        far = slice(inner + pair * 2 * HEAD, inner + (pair + 1) * 2 * HEAD)

        def keep(half, probs, pair=pair):
            pr1_out[2 * pair + half] = probs

        num, total = attention_pair(
            q1[:, lanes], kv1_out[:, lanes], kv1_out[:, far], allowed,
            [self_bias(rel_u[2 * pair + half : 2 * pair + half + 1, :], own, group) for half in (0, 1)],
            keep,
        )
        num1_out[:, lanes] = num
        tot1_out[:, lanes] = total
    kvz2.forward()
    dyz.start()
    chips[2].step3()
    chips[2].done()
    saves = [
        pltpu.make_async_copy(w, watt_out, local.at[2]),
    ]
    for c in saves:
        c.start()
    ff.step2()
    o1 = (num1_out[...] / tot1_out[...]).astype(LOW)
    x1 = x + mm(spread(o1), w[5])
    x1_out[...] = x1
    n2 = rms_rows(x1, gain2[...]).astype(LOW)
    q2 = compact(mm(n2, w[6], NT))
    q2_out[...] = q2
    for k in (1, 2, 3):
        kvz2.wait(k)
    enc_place = lax.broadcasted_iota(jnp.int32, (1, 4 * own_enc), 1)
    allowed2 = own_items == item_of(enc_len, enc_place)
    for pair in range(HEADS // 2):
        lanes = slice(pair * 2 * HEAD, (pair + 1) * 2 * HEAD)
        far = slice(inner + pair * 2 * HEAD, inner + (pair + 1) * 2 * HEAD)

        def keep2(half, probs, pair=pair):
            pr2_out[2 * pair + half] = probs

        num, total = attention_pair(
            q2[:, lanes], kv2_out[:, lanes], kv2_out[:, far], allowed2, None, keep2
        )
        num2_out[:, lanes] = num
        tot2_out[:, lanes] = total
    dyz.forward()
    ff.step3()
    o2 = (num2_out[...] / tot2_out[...]).astype(LOW)
    x2 = x1 + mm(spread(o2), w[7])
    x2_out[...] = x2
    n3_out[...] = rms_rows(x2, gain3[...]).astype(LOW)
    for k in (1, 2, 3):
        dyz.wait(k)
    ff.done()
    for part in zs + chips + [ff, dyz, kvz, kvz2]:
        part.finish()
    own_dy.wait()
    own_ff.wait()
    for c in saves:
        c.wait()


def sds(shape, dtype):
    return jax.ShapeDtypeStruct(shape, dtype)


def call_forward(width, tgt_len, enc_len, x, e, dy, watt, wff, g1, g2, g3, rel_u):
    own, wide = x.shape
    own_enc = e.shape[0]
    inner = HEADS * HEAD
    padded = 32 * PAD
    SM = pl.BlockSpec(memory_space=pltpu.SMEM)
    return pl.pallas_call(
        functools.partial(forward_kernel, width),
        out_shape=(
            sds((8, padded, wide), LOW),
            sds((3, 8 * wff.shape[1], wide), LOW),
            sds((4 * own, wide), LOW),
            sds((own, wide), F32),
            sds((own, wide), F32),
            sds((own, wide), LOW),
            sds((own, inner), LOW),
            sds((4 * own, 2 * inner), LOW),
            sds((own, inner), LOW),
            sds((4 * own_enc, 2 * inner), LOW),
            sds((HEADS, own, 4 * own), LOW),
            sds((HEADS, own, 4 * own_enc), LOW),
            sds((own, inner), F32),
            sds((own, inner), F32),
            sds((own, inner), F32),
            sds((own, inner), F32),
        ),
        in_specs=[SM, SM, VM, VM, ANY, VM, ANY, VM, VM, VM, VM],
        out_specs=(ANY, ANY, ANY) + (VM,) * 13,
        scratch_shapes=[
            pltpu.VMEM((8, padded, wide), LOW),
            pltpu.VMEM((padded, inner), LOW),
            pltpu.SemaphoreType.DMA((60,)),
            pltpu.SemaphoreType.DMA((60,)),
            pltpu.SemaphoreType.DMA((3,)),
        ],
        compiler_params=pltpu.CompilerParams(
            collective_id=1, has_side_effects=True, vmem_limit_bytes=56 * 2**20
        ),
        name="attention_forward",
    )(tgt_len, enc_len, x, e, dy, watt, wff, g1, g2, g3, rel_u)


def pack_weights(self_q, self_k, self_v, self_o, cross_q, cross_k, cross_v, cross_o, ff_gate, ff_up, ff_out):
    cols = jnp.stack(
        [w.T for w in (self_q, self_k, self_v, cross_k, cross_v)] + [self_o, cross_q.T, cross_o]
    ).astype(LOW)
    watt = jnp.pad(cols, ((0, 0), (0, PAD - cols.shape[1]), (0, 0)))
    wff = jnp.stack([ff_gate.T, ff_up.T, ff_out]).astype(LOW)
    return watt, wff


def bias_rows(rel_bucket, rel_table, enc, own, group):
    starts = jnp.sum(
        (rel_bucket[None, :] < jnp.arange(BUCKETS, dtype=jnp.int32)[:, None]).astype(jnp.int32), axis=1
    )
    k = jnp.arange(group + own, dtype=jnp.int32)
    distance = enc * own - jnp.where(k < group, k, k - group - own)
    ends = jnp.concatenate([starts[1:], jnp.full((1,), group, jnp.int32)])
    inside = (distance[None, :] >= starts[:, None]) & (distance[None, :] < ends[:, None])
    return inside, jnp.sum(jnp.where(inside[:, None, :], rel_table[:, :, None], 0.0), axis=0)


class ZScatter:
    def __init__(self, src_at, dst_at, where, sems):
        self.src_at, self.dst_at, self.sems = src_at, dst_at, sems
        self.dp, self.enc = where[0], where[1]
        self.base = sems.take(3)

    def _copy(self, k):
        place = lax.rem(self.enc + k, 4)
        s = self.sems
        return remote(
            self.src_at(place), self.dst_at(3 - k),
            s.send.at[self.base + k - 1], s.recv.at[self.base + 3 - k], (self.dp, place),
        )

    def start(self, k):
        self._copy(k).start()

    def start_all(self):
        for k in (1, 3, 2):
            self.start(k)

    def wait(self):
        for k in (1, 2, 3):
            self._copy(k).wait_recv()

    def finish(self):
        for k in (1, 2, 3):
            self._copy(k).wait_send()


def rms_back(values, gain, grad):
    inv = lax.rsqrt(jnp.mean(values * values, axis=-1, keepdims=True) + EPSILON)
    scaled = grad * gain
    mean = jnp.mean(values * scaled, axis=-1, keepdims=True)
    gain_grad = jnp.sum(grad * values * inv, axis=0, keepdims=True)
    return inv * scaled - values * (inv * inv * inv * mean), gain_grad


GELU_A = 0.7978845608028654
GELU_B = 0.044715


def ff_kernel(
    n3_ref, x2_ref, dy_ref, dyall_ref, wff_ref, gain3,
    dx2_out, part_out, sums_out, gain_out,
    w, n3, dy, act, dgate, dup, part, got, grads, core_got, own_sum, send, recv, local,
):
    where = places()
    dp, enc, sib, xn, yn = where
    core = lax.rem(dp, 2)
    sems = Sems(send, recv)
    own = n3_ref.shape[0]
    ff_rows = grads.shape[3]

    def rows_of(place):
        return pl.ds(pl.multiple_of(place * own, PAD), own)

    gather = ZGather(lambda e: n3.at[rows_of(e), :], n3_ref, where, sems)
    scatter = ZScatter(lambda e: part.at[e], lambda slot: got.at[slot], where, sems)
    loads = [
        pltpu.make_async_copy(wff_ref, w, local.at[0]),
        pltpu.make_async_copy(dyall_ref, dy, local.at[1]),
    ]
    for c in loads:
        c.start()
    enter(*where)
    gather.start()
    n3[rows_of(enc), :] = n3_ref[...]
    for c in loads:
        c.wait()

    def block(place):
        rows = rows_of(place)
        normed = n3[rows, :]
        gate = mm(normed, w[0], NT)
        up = mm(normed, w[1], NT)
        dh = mm(dy[rows, :], w[2], NT)
        square = gate * gate
        t = jnp.tanh(GELU_A * gate * (1.0 + GELU_B * square))
        half = 0.5 * (1.0 + t)
        g = gate * half
        slope = half + 0.5 * gate * (1.0 - t * t) * (GELU_A * (1.0 + 3.0 * GELU_B * square))
        hidden = (g * up).astype(LOW)
        dg = (dh * up * slope).astype(LOW)
        du = (dh * g).astype(LOW)
        act[rows, :] = hidden
        dgate[rows, :] = dg
        dup[rows, :] = du
        part_out[rows, :] = mm(hidden, w[2]).astype(LOW)
        return mm(dg, w[0]) + mm(du, w[1])

    own_sum[...] = block(enc)
    first = jnp.where(enc == 3, 3, 1)
    for step in range(3):
        if step == 1:
            gather.forward()
            gather.wait(2)
            place = lax.rem(enc + 2, 4)
            part[place] = block(place).astype(LOW)
            scatter.start(2)
        else:
            for k in (1, 3):

                @pl.when(first == (k if step == 0 else 4 - k))
                def _(k=k):
                    gather.wait(k)

            place = lax.rem(enc + (first if step == 0 else 4 - first), 4)
            part[place] = block(place).astype(LOW)
            for k in (1, 3):

                @pl.when(first == (k if step == 0 else 4 - k))
                def _(k=k):
                    scatter.start(k)

    swaps = []
    base = sems.take(3)
    for m, (left, right) in ((2, (act, dy)), (0, (dgate, n3)), (1, (dup, n3))):
        whole = mm(left[...], right[...], TN).astype(LOW)
        for j in range(4):
            for c in range(2):
                first_row = (2 * j + c) * ff_rows
                grads[m, j, c] = whole[first_row : first_row + ff_rows]
        swap = remote(
            grads.at[m, :, 1 - core], core_got.at[m], send.at[base + m], recv.at[base + m], (sib, enc)
        )
        swap.start()
        swaps.append((m, swap))
    for m, swap in swaps:
        swap.wait_recv()
        for j in range(4):
            sums_out[m, j] = (grads[m, j, core].astype(F32) + core_got[m, j].astype(F32)).astype(LOW)
    scatter.wait()
    dn3 = own_sum[...] + got[0].astype(F32) + got[1].astype(F32) + got[2].astype(F32)
    dv, gain_grad = rms_back(x2_ref[...], gain3[...], dn3)
    dx2_out[...] = dy_ref[...].astype(F32) + dv
    gain_out[...] = gain_grad
    gather.finish()
    scatter.finish()
    for m, swap in swaps:
        swap.wait_send()


def call_ff(n3, x2, dy, dy_all, wff, g3):
    own, wide = n3.shape
    ff_all = wff.shape[1]
    ff_rows = ff_all // 8
    group = 4 * own
    return pl.pallas_call(
        ff_kernel,
        out_shape=(
            sds((own, wide), F32),
            sds((group, wide), LOW),
            sds((3, 4, ff_rows, wide), LOW),
            sds((1, wide), F32),
        ),
        in_specs=[VM, VM, VM, ANY, ANY, VM],
        out_specs=(VM,) * 4,
        scratch_shapes=[
            pltpu.VMEM((3, ff_all, wide), LOW),
            pltpu.VMEM((group, wide), LOW),
            pltpu.VMEM((group, wide), LOW),
            pltpu.VMEM((group, ff_all), LOW),
            pltpu.VMEM((group, ff_all), LOW),
            pltpu.VMEM((group, ff_all), LOW),
            pltpu.VMEM((4, own, wide), LOW),
            pltpu.VMEM((3, own, wide), LOW),
            pltpu.VMEM((3, 4, 2, ff_rows, wide), LOW),
            pltpu.VMEM((3, 4, ff_rows, wide), LOW),
            pltpu.VMEM((own, wide), F32),
            pltpu.SemaphoreType.DMA((10,)),
            pltpu.SemaphoreType.DMA((10,)),
            pltpu.SemaphoreType.DMA((2,)),
        ],
        compiler_params=pltpu.CompilerParams(
            collective_id=2, has_side_effects=True, vmem_limit_bytes=60 * 2**20
        ),
        name="feed_forward",
    )(n3, x2, dy, dy_all, wff, g3)


class GradReduce:
    def __init__(self, lo, hi, bufs, out, where, sems):
        self.lo, self.hi, self.bufs, self.out, self.where, self.sems = lo, hi, bufs, out, where, sems
        self.base = sems.take(4)
        grads, core_got, chip_got, line, line_got = bufs
        self.line = ZScatter(
            lambda e: line.at[lo:hi, e], lambda slot: line_got.at[slot, lo:hi], where, sems
        )

    def _core(self):
        dp, enc, sib, xn, yn = self.where
        grads, core_got = self.bufs[:2]
        s = self.sems
        return remote(
            grads.at[self.lo : self.hi, :, 1 - lax.rem(dp, 2)], core_got.at[self.lo : self.hi],
            s.send.at[self.base], s.recv.at[self.base], (sib, enc),
        )

    def _chip(self, i):
        dp, enc, sib, xn, yn = self.where
        core_got, chip_got = self.bufs[1:3]
        s = self.sems
        target = (xn, yn, xn + yn - dp)[i]
        return remote(
            core_got.at[self.lo : self.hi, lax.div(target, 2)], chip_got.at[i, self.lo : self.hi],
            s.send.at[self.base + 1 + i], s.recv.at[self.base + 1 + i], (target, enc),
        )

    def step1(self):
        self._core().start()

    def step2(self):
        grads, core_got = self.bufs[:2]
        core = lax.rem(self.where[0], 2)
        self._core().wait_recv()
        for m in range(self.lo, self.hi):
            core_got[m] = (grads[m, :, core].astype(F32) + core_got[m].astype(F32)).astype(LOW)
        for i in (2, 0, 1):
            self._chip(i).start()

    def step3(self):
        core_got, chip_got, line = self.bufs[1:4]
        chip = lax.div(self.where[0], 2)
        for i in range(3):
            self._chip(i).wait_recv()
        for m in range(self.lo, self.hi):
            total = core_got[m, chip].astype(F32)
            for i in range(3):
                total = total + chip_got[i, m].astype(F32)
            total = total.astype(LOW)
            for e in range(4):
                line[m, e] = total[e * PAD : (e + 1) * PAD]
        self.line.start_all()

    def step4(self):
        line, line_got = self.bufs[3:5]
        enc = self.where[1]
        self.line.wait()
        for m in range(self.lo, self.hi):
            total = line[m, enc].astype(F32)
            for slot in range(3):
                total = total + line_got[slot, m].astype(F32)
            self.out[m] = total

    def finish(self):
        self._core().wait_send()
        for i in range(3):
            self._chip(i).wait_send()
        self.line.finish()


def backward_pair(q_pair, k_pair, v_pair, probs_ref, pair, dnum, dtotals):
    rows = q_pair.shape[0]
    parts, scores = [], []
    for half in (0, 1):
        dw = mm(one_head(dnum, half), v_pair, NT)
        ds = (probs_ref[2 * pair + half].astype(F32) * (dw + dtotals[half])).astype(LOW)
        scores.append(ds)
        parts.append(mm(ds, k_pair))
    dq = jnp.where(low_lanes(rows), parts[0], parts[1])
    dk = mm(jnp.concatenate(scores, axis=0), jnp.concatenate([one_head(q_pair, h) for h in (0, 1)], axis=0), TN)
    probs = jnp.concatenate([probs_ref[2 * pair + h] for h in (0, 1)], axis=0)
    dv = mm(probs, jnp.concatenate([one_head(dnum, h) for h in (0, 1)], axis=0), TN)
    return dq, dk, dv, scores


def total_grads(product, total):
    low = low_lanes(product.shape[0])
    out = []
    for half in (0, 1):
        keep = low if half == 0 else jnp.logical_not(low)
        top = jnp.sum(jnp.where(keep, product, 0.0), axis=1, keepdims=True)
        tot = total[:, half * HEAD : half * HEAD + 1]
        out.append(-top / (tot * tot))
    return out


def backward_kernel(
    width,
    x_ref, e_ref, x1_ref, x2_ref, dx2_ref, gain1, gain2, gain3_grad, inside,
    q1, kv1, q2, kv2, pr1, pr2, num1, num2, tot1, tot2, watt_ref, part_ref, sums_ref,
    hidden_out, hidden_grad, encoder_grad, att_out, ff_out, small_out,
    w, pm, grads, core_got, chip_got, line, line_got, ff_got, ff_own, part, part_got,
    kvp1, kvp1_got, kvp2, kvp2_got, dq, vec, vec_got, send, recv, local,
):
    where = places()
    dp, enc, sib, xn, yn = where
    sems = Sems(send, recv)
    own, wide = x_ref.shape
    own_enc = e_ref.shape[0]
    inner = HEADS * HEAD
    padded = w.shape[1]
    chip = lax.div(dp, 2)

    out_z = ZScatter(lambda e: part_ref.at[e], lambda slot: part_got.at[slot], where, sems)
    kv1_z = ZScatter(lambda e: kvp1.at[e], lambda slot: kvp1_got.at[slot], where, sems)
    kv2_z = ZScatter(lambda e: kvp2.at[e], lambda slot: kvp2_got.at[slot], where, sems)
    bufs = (grads, core_got, chip_got, line, line_got)
    batches = [GradReduce(lo, lo + 2, bufs, att_out, where, sems) for lo in (0, 2, 4, 6)]
    ff_base = sems.take(3)
    vec_base = sems.take(3)
    vec_z = ZScatter(lambda e: vec.at[3], lambda slot: vec_got.at[3 + slot], where, sems)

    def ff_copy(i):
        target = (xn, yn, xn + yn - dp)[i]
        return remote(
            sums_ref.at[:, lax.div(target, 2)], ff_got.at[i],
            send.at[ff_base + i], recv.at[ff_base + i], (target, enc),
        )

    def vec_copy(i):
        target = (sib, xn, yn)[i]
        return remote(
            vec.at[i], vec_got.at[i], send.at[vec_base + i], recv.at[vec_base + i], (target, enc)
        )

    def load(slot, m, i):
        return pltpu.make_async_copy(watt_ref.at[m], w.at[slot], local.at[i])

    first_loads = [load(slot, m, slot) for slot, m in enumerate((7, 6, 5, 1, 2))]
    for c in first_loads:
        c.start()
    own_part = pltpu.make_async_copy(part_ref.at[enc], part, local.at[8])
    own_ff = pltpu.make_async_copy(sums_ref.at[:, chip], ff_own, local.at[9])
    own_part.start()
    own_ff.start()
    enter(*where)
    out_z.start_all()
    for i in (2, 0, 1):
        ff_copy(i).start()
    pm[...] = spread_matrix(padded, inner, width)

    def compact(values):
        high = values.astype(LOW)
        rest = (values - high.astype(F32)).astype(LOW)
        return mm(high, pm[...]) + mm(rest, pm[...])

    def spread(values):
        return mm(values, pm[...], NT).astype(LOW)

    def put_grad(m, left, right):
        whole = mm(left, right, TN).astype(LOW)
        for j in range(4):
            for c in range(2):
                grads[m, j, c] = whole[(2 * j + c) * 4 * PAD : (2 * j + c + 1) * 4 * PAD]

    b2 = dx2_ref[...].astype(LOW)
    first_loads[0].wait()
    do2 = compact(mm(b2, w[0], NT))
    put_grad(0, spread((num2[...] / tot2[...]).astype(LOW)), b2)
    dnum2 = (do2 / tot2[...]).astype(LOW)
    prod2 = do2 * num2[...]
    for pair in range(HEADS // 2):
        lanes = slice(pair * 2 * HEAD, (pair + 1) * 2 * HEAD)
        far = slice(inner + pair * 2 * HEAD, inner + (pair + 1) * 2 * HEAD)
        dtot = total_grads(prod2[:, lanes], tot2[:, lanes])
        dq_pair, dk, dv, _ = backward_pair(
            q2[:, lanes], kv2[:, lanes], kv2[:, far], pr2, pair, dnum2[:, lanes], dtot
        )
        dq[:, lanes] = dq_pair.astype(LOW)
        for e in range(4):
            kvp2[e, :, lanes] = dk[e * own_enc : (e + 1) * own_enc].astype(LOW)
            kvp2[e, :, far] = dv[e * own_enc : (e + 1) * own_enc].astype(LOW)
    kv2_z.start_all()
    dq2 = spread(dq[...])
    x1 = x1_ref[...]
    put_grad(1, dq2, rms_rows(x1, gain2[...]).astype(LOW))
    batches[0].step1()
    first_loads[1].wait()
    dv2, gain2_grad = rms_back(x1, gain2[...], mm(dq2, w[1]))
    dx1 = dx2_ref[...] + dv2
    b1 = dx1.astype(LOW)
    first_loads[2].wait()
    do1 = compact(mm(b1, w[2], NT))
    late = [load(2, 0, 5), load(0, 3, 6), load(1, 4, 7)]
    for c in late:
        c.start()
    put_grad(2, spread((num1[...] / tot1[...]).astype(LOW)), b1)
    batches[0].step2()
    dnum1 = (do1 / tot1[...]).astype(LOW)
    prod1 = do1 * num1[...]
    vec[0] = jnp.zeros(vec.shape[1:], F32)
    flip_row = lax.broadcasted_iota(jnp.int32, (own, own), 0)
    flip_col = lax.broadcasted_iota(jnp.int32, (own, own), 1)
    flip = jnp.where(flip_row + flip_col == own - 1, 1.0, 0.0).astype(LOW)
    for pair in range(HEADS // 2):
        lanes = slice(pair * 2 * HEAD, (pair + 1) * 2 * HEAD)
        far = slice(inner + pair * 2 * HEAD, inner + (pair + 1) * 2 * HEAD)
        dtot = total_grads(prod1[:, lanes], tot1[:, lanes])
        dq_pair, dk, dv, scores = backward_pair(
            q1[:, lanes], kv1[:, lanes], kv1[:, far], pr1, pair, dnum1[:, lanes], dtot
        )
        dq[:, lanes] = dq_pair.astype(LOW)
        for e in range(4):
            kvp1[e, :, lanes] = dk[e * own : (e + 1) * own].astype(LOW)
            kvp1[e, :, far] = dv[e * own : (e + 1) * own].astype(LOW)
        for half in (0, 1):
            ds = mm(flip, scores[half])
            long = jnp.concatenate([ds, jnp.zeros((own, own), F32)], axis=1)
            turned = pltpu.roll(long, 0, 1, stride=1, stride_axis=0)
            by_distance = jnp.sum(turned, axis=0, keepdims=True)
            vec[0, 8 + 2 * pair + half : 9 + 2 * pair + half, 0:BUCKETS] = lax.dot_general(
                by_distance, inside[...], NT, precision=lax.Precision.HIGHEST, preferred_element_type=F32
            )
    kv1_z.start_all()
    dq1 = spread(dq[...])
    x = x_ref[...].astype(F32)
    n1 = rms_rows(x, gain1[...]).astype(LOW)
    put_grad(3, dq1, n1)
    batches[1].step1()
    batches[0].step3()
    for c in late:
        c.wait()
    dn1 = mm(dq1, w[2])
    batches[1].step2()

    kv2_z.wait()
    low2 = (
        kvp2[enc].astype(F32) + kvp2_got[0].astype(F32) + kvp2_got[1].astype(F32) + kvp2_got[2].astype(F32)
    ).astype(LOW)
    dk2 = spread(low2[:, :inner])
    dv2 = spread(low2[:, inner:])
    put_grad(4, dk2, e_ref[...])
    put_grad(5, dv2, e_ref[...])
    batches[2].step1()
    encoder_grad[...] = mm(dk2, w[0]) + mm(dv2, w[1])

    kv1_z.wait()
    low1 = (
        kvp1[enc].astype(F32) + kvp1_got[0].astype(F32) + kvp1_got[1].astype(F32) + kvp1_got[2].astype(F32)
    ).astype(LOW)
    dk1 = spread(low1[:, :inner])
    dv1 = spread(low1[:, inner:])
    put_grad(6, dk1, n1)
    put_grad(7, dv1, n1)
    batches[3].step1()
    batches[2].step2()
    first_loads[3].wait()
    first_loads[4].wait()
    dn1 = dn1 + mm(dk1, w[3]) + mm(dv1, w[4])
    dv_x, gain1_grad = rms_back(x, gain1[...], dn1)
    hidden_grad[...] = dx1 + dv_x
    vec[0, 0:1, :] = gain1_grad
    vec[0, 1:2, :] = gain2_grad
    vec[0, 2:3, :] = gain3_grad[...]
    vec_copy(0).start()
    batches[3].step2()
    batches[0].step4()
    for i in (1, 2, 3):
        if i < 4:
            vec_copy(i - 1).wait_recv()
            vec[i] = vec[i - 1] + vec_got[i - 1]
            if i < 3:
                vec_copy(i).start()
            else:
                vec_z.start_all()
        batches[i].step3()
    own_ff.wait()
    for i in range(3):
        ff_copy(i).wait_recv()
    for m in range(3):
        ff_out[m] = (
            ff_own[m].astype(F32) + ff_got[0, m].astype(F32) + ff_got[1, m].astype(F32) + ff_got[2, m].astype(F32)
        )
    out_z.wait()
    own_part.wait()
    hidden_out[...] = (
        x2_ref[...] + (part[...].astype(F32) + part_got[0].astype(F32))
        + (part_got[1].astype(F32) + part_got[2].astype(F32))
    ).astype(LOW)
    for batch in batches[1:]:
        batch.step4()
    vec_z.wait()
    small_out[...] = vec[3] + vec_got[3] + vec_got[4] + vec_got[5]
    for part_done in [out_z, kv1_z, kv2_z, vec_z] + batches:
        part_done.finish()
    for i in range(3):
        ff_copy(i).wait_send()
        vec_copy(i).wait_send()


def call_backward(width, x, e, x1, x2, dx2, g1, g2, gain3_grad, inside, saved, watt, part, sums):
    own, wide = x.shape
    own_enc = e.shape[0]
    inner = HEADS * HEAD
    padded = watt.shape[1]
    ff_rows = sums.shape[2]
    return pl.pallas_call(
        functools.partial(backward_kernel, width),
        out_shape=(
            sds((own, wide), LOW),
            sds((own, wide), F32),
            sds((own_enc, wide), F32),
            sds((8, PAD, wide), F32),
            sds((3, ff_rows, wide), F32),
            sds((16, wide), F32),
        ),
        in_specs=[VM] * 19 + [ANY] * 3,
        out_specs=(VM,) * 6,
        scratch_shapes=[
            pltpu.VMEM((5, padded, wide), LOW),
            pltpu.VMEM((padded, inner), LOW),
            pltpu.VMEM((8, 4, 2, 4 * PAD, wide), LOW),
            pltpu.VMEM((8, 4, 4 * PAD, wide), LOW),
            pltpu.VMEM((3, 8, 4 * PAD, wide), LOW),
            pltpu.VMEM((8, 4, PAD, wide), LOW),
            pltpu.VMEM((3, 8, PAD, wide), LOW),
            pltpu.VMEM((3, 3, ff_rows, wide), LOW),
            pltpu.VMEM((3, ff_rows, wide), LOW),
            pltpu.VMEM((own, wide), LOW),
            pltpu.VMEM((3, own, wide), LOW),
            pltpu.VMEM((4, own, 2 * inner), LOW),
            pltpu.VMEM((3, own, 2 * inner), LOW),
            pltpu.VMEM((4, own_enc, 2 * inner), LOW),
            pltpu.VMEM((3, own_enc, 2 * inner), LOW),
            pltpu.VMEM((own, inner), LOW),
            pltpu.VMEM((4, 16, wide), F32),
            pltpu.VMEM((6, 16, wide), F32),
            pltpu.SemaphoreType.DMA((46,)),
            pltpu.SemaphoreType.DMA((46,)),
            pltpu.SemaphoreType.DMA((10,)),
        ],
        compiler_params=pltpu.CompilerParams(
            collective_id=3, has_side_effects=True, vmem_limit_bytes=62 * 2**20
        ),
        name="attention_backward",
    )(x, e, x1, x2, dx2, g1, g2, gain3_grad, inside, *saved, watt, part.reshape(4, own, wide), sums)


def fast_body(
    hidden_in, encoder_out, grad_out, tgt_lengths, enc_lengths, rel_bucket, norm1_gain,
    self_q, self_k, self_v, self_o, rel_table, norm2_gain,
    cross_q, cross_k, cross_v, cross_o, norm3_gain, ff_gate, ff_up, ff_out,
):
    own = hidden_in.shape[0]
    width = self_q.shape[1]
    watt, wff = pack_weights(
        self_q, self_k, self_v, self_o, cross_q, cross_k, cross_v, cross_o, ff_gate, ff_up, ff_out
    )
    inside, rel_u = bias_rows(rel_bucket, rel_table, lax.axis_index("enc"), own, 4 * own)
    g1, g2, g3 = norm1_gain[None], norm2_gain[None], norm3_gain[None]
    fwd = call_forward(
        width, tgt_lengths, enc_lengths, hidden_in, encoder_out, grad_out, watt, wff, g1, g2, g3, rel_u
    )
    watt_all, wff_all, dy_all, x1, x2, n3 = fwd[:6]
    dx2, part, sums, gain3_grad = call_ff(n3, x2, grad_out, dy_all, wff_all, g3)
    saved = fwd[6:]
    hidden_out, hidden_grad, encoder_grad, att, ff, small = call_backward(
        width, hidden_in, encoder_out, x1, x2, dx2, g1, g2, gain3_grad,
        jnp.roll(inside.astype(F32), own - 1, axis=1), saved, watt_all, part, sums,
    )
    o2, q2, o1, q1, k2, v2, k1, v1 = (att[m, :width] for m in range(8))
    return (
        hidden_out, hidden_grad, encoder_grad, small[0],
        q1.T, k1.T, v1.T, o1, small[8 : 8 + HEADS, :BUCKETS].T,
        small[1], q2.T, k2.T, v2.T, o2, small[2], ff[0].T, ff[1].T, ff[2],
    )


def rms_scale(values, gain):
    return values * lax.rsqrt(jnp.mean(values * values, axis=-1, keepdims=True) + EPSILON) * gain


def gated_gelu(gate_pre, up_pre):
    return jax.nn.gelu(gate_pre, approximate=True) * up_pre


def item_ids(lengths, total_rows):
    ends = jnp.cumsum(lengths)
    places = jnp.arange(total_rows, dtype=jnp.int32)
    return jnp.sum((ends[None, :] <= places[:, None]).astype(jnp.int32), axis=1)


def product(left, right):
    return jnp.dot(left, right, preferred_element_type=jnp.float32)


def product_tn(left, right):
    return lax.dot_general(
        left, right, (((0,), (0,)), ((), ())), preferred_element_type=jnp.float32
    )


def product_nt(left, right):
    return lax.dot_general(
        left, right, (((1,), (1,)), ((), ())), preferred_element_type=jnp.float32
    )


def to_pieces(grad, shard_dim, shards):
    if shard_dim == 0:
        return grad.reshape(shards, -1)
    rows = grad.shape[0]
    return jnp.transpose(grad.reshape(rows, shards, -1), (1, 0, 2)).reshape(shards, -1)


def from_pieces(received, shard_dim, shape, shards):
    summed = jnp.sum(received, axis=0)
    if shard_dim == 0:
        return summed.reshape(shape[0] // shards, shape[1])
    return summed.reshape(shape[0], shape[1] // shards)


def head_pair(matrix, pair_index):
    return lax.dynamic_slice_in_dim(matrix, pair_index * 2 * HEAD, 2 * HEAD, 1).reshape(
        matrix.shape[0], 2, HEAD
    )


def pair_stats(stats, pair_index):
    return lax.dynamic_slice_in_dim(stats, pair_index * 2, 2, 0)


def relative_bias(distance, bias_info, pair_index):
    starts, table = bias_info
    table_pair = lax.dynamic_slice_in_dim(table, pair_index * 2, 2, 1)

    def add_step(bucket, total):
        rise = table_pair[bucket] - table_pair[bucket - 1]
        return total + jnp.where(distance[None] >= starts[bucket], rise[:, None, None], 0.0)

    start_bias = jnp.broadcast_to(table_pair[0][:, None, None], (2,) + distance.shape)
    return lax.fori_loop(1, BUCKETS, add_step, start_bias)


def relative_grads(distance, starts, score_grad):

    def one_step(bucket):
        return jnp.sum(jnp.where(distance[None] >= starts[bucket], score_grad, 0.0), axis=(1, 2))

    steps_sum = lax.map(one_step, jnp.arange(BUCKETS, dtype=jnp.int32))
    return steps_sum - jnp.concatenate([steps_sum[1:], jnp.zeros((1, 2), jnp.float32)], axis=0)


def pair_scores(query_block, key_rows, pair_index, layout):
    allowed, distance, bias_info = layout
    scores = jnp.einsum(
        "qhe,khe->hqk",
        head_pair(query_block, pair_index),
        head_pair(key_rows, pair_index),
        preferred_element_type=jnp.float32,
    )
    if bias_info is not None:
        scores = scores + relative_bias(distance, bias_info, pair_index)
    return jnp.where(allowed[None], scores, MASKED)


def forward_parts(query_block, key_rows, value_rows, layout):
    block_rows = query_block.shape[0]
    width = 2 * HEAD

    def forward_one_pair(pair_index, carry):
        numerator, largest, totals = carry
        scores = pair_scores(query_block, key_rows, pair_index, layout)
        pair_top = jnp.max(scores, axis=2)
        weights = jnp.exp(scores - pair_top[:, :, None])
        partial_sum = jnp.einsum(
            "hqk,khe->qhe",
            weights.astype(jnp.bfloat16),
            head_pair(value_rows, pair_index),
            preferred_element_type=jnp.float32,
        )
        numerator = lax.dynamic_update_slice_in_dim(
            numerator, partial_sum.reshape(block_rows, width), pair_index * width, 1
        )
        largest = lax.dynamic_update_slice_in_dim(largest, pair_top, pair_index * 2, 0)
        totals = lax.dynamic_update_slice_in_dim(
            totals, jnp.sum(weights, axis=2), pair_index * 2, 0
        )
        return (numerator, largest, totals)

    start_state = (
        jnp.zeros((block_rows, HEADS * HEAD), jnp.float32),
        jnp.zeros((HEADS, block_rows), jnp.float32),
        jnp.zeros((HEADS, block_rows), jnp.float32),
    )
    return lax.fori_loop(0, HEADS // 2, forward_one_pair, start_state)


def backward_parts(query_block, key_rows, value_rows, layout, top_rows, num_grad, total_grad):
    allowed, distance, bias_info = layout
    block_rows = query_block.shape[0]
    key_count = key_rows.shape[0]
    width = 2 * HEAD

    def backward_one_pair(pair_index, carry):
        query_grad, key_grad, value_grad, bias_grad = carry
        query_pair = head_pair(query_block, pair_index)
        key_pair = head_pair(key_rows, pair_index)
        value_pair = head_pair(value_rows, pair_index)
        grad_pair = head_pair(num_grad, pair_index)
        scores = pair_scores(query_block, key_rows, pair_index, layout)
        weights = jnp.exp(scores - pair_stats(top_rows, pair_index)[:, :, None])
        weight_grad = jnp.einsum(
            "qhe,khe->hqk", grad_pair, value_pair, preferred_element_type=jnp.float32
        )
        score_grad = (
            weights * (weight_grad + pair_stats(total_grad, pair_index)[:, :, None])
        ).astype(jnp.bfloat16)
        part_query = jnp.einsum(
            "hqk,khe->qhe", score_grad, key_pair, preferred_element_type=jnp.float32
        )
        part_key = jnp.einsum(
            "hqk,qhe->khe", score_grad, query_pair, preferred_element_type=jnp.float32
        )
        part_value = jnp.einsum(
            "hqk,qhe->khe",
            weights.astype(jnp.bfloat16),
            grad_pair,
            preferred_element_type=jnp.float32,
        )
        query_grad = lax.dynamic_update_slice_in_dim(
            query_grad, part_query.reshape(block_rows, width), pair_index * width, 1
        )
        key_grad = lax.dynamic_update_slice_in_dim(
            key_grad, part_key.reshape(key_count, width), pair_index * width, 1
        )
        value_grad = lax.dynamic_update_slice_in_dim(
            value_grad, part_value.reshape(key_count, width), pair_index * width, 1
        )
        if bias_info is not None:
            pair_bias_grad = relative_grads(distance, bias_info[0], score_grad.astype(jnp.float32))
            bias_grad = lax.dynamic_update_slice_in_dim(
                bias_grad, pair_bias_grad, pair_index * 2, 1
            )
        return (query_grad, key_grad, value_grad, bias_grad)

    bias_start = None if bias_info is None else jnp.zeros((BUCKETS, HEADS), jnp.float32)
    start_state = (
        jnp.zeros((block_rows, HEADS * HEAD), jnp.float32),
        jnp.zeros((key_count, HEADS * HEAD), jnp.float32),
        jnp.zeros((key_count, HEADS * HEAD), jnp.float32),
        bias_start,
    )
    return lax.fori_loop(0, HEADS // 2, backward_one_pair, start_state)


def normalize(numerator, totals):
    row_count = numerator.shape[0]
    shaped = numerator.reshape(row_count, HEADS, HEAD) / jnp.transpose(totals)[:, :, None]
    return shaped.reshape(row_count, HEADS * HEAD).astype(jnp.bfloat16)


def output_grads(out_grad, numerator, totals):
    row_count = out_grad.shape[0]
    per_total = jnp.transpose(totals)
    shaped_grad = out_grad.reshape(row_count, HEADS, HEAD)
    num_grad = (
        (shaped_grad / per_total[:, :, None]).reshape(row_count, HEADS * HEAD).astype(jnp.bfloat16)
    )
    total_grad = -jnp.sum(shaped_grad * numerator.reshape(row_count, HEADS, HEAD), axis=2) / (
        per_total * per_total
    )
    return (num_grad, jnp.transpose(total_grad))


def body(
    hidden_in,
    encoder_out,
    grad_out,
    tgt_lengths,
    enc_lengths,
    rel_bucket,
    norm1_gain,
    self_q,
    self_k,
    self_v,
    self_o,
    rel_table,
    norm2_gain,
    cross_q,
    cross_k,
    cross_v,
    cross_o,
    norm3_gain,
    ff_gate,
    ff_up,
    ff_out,
):
    w_query, w_key, w_value, w_out, c_query, c_key, c_value, c_out, w_gate, w_up, w_down = (
        lax.all_gather(self_q.astype(jnp.bfloat16), ("dp", "enc"), axis=1, tiled=True),
        lax.all_gather(self_k.astype(jnp.bfloat16), ("dp", "enc"), axis=1, tiled=True),
        lax.all_gather(self_v.astype(jnp.bfloat16), ("dp", "enc"), axis=1, tiled=True),
        lax.all_gather(self_o.astype(jnp.bfloat16), ("dp", "enc"), axis=0, tiled=True),
        lax.all_gather(cross_q.astype(jnp.bfloat16), ("dp", "enc"), axis=1, tiled=True),
        lax.all_gather(cross_k.astype(jnp.bfloat16), ("dp", "enc"), axis=1, tiled=True),
        lax.all_gather(cross_v.astype(jnp.bfloat16), ("dp", "enc"), axis=1, tiled=True),
        lax.all_gather(cross_o.astype(jnp.bfloat16), ("dp", "enc"), axis=0, tiled=True),
        lax.all_gather(ff_gate.astype(jnp.bfloat16), ("dp", "enc"), axis=1, tiled=True),
        lax.all_gather(ff_up.astype(jnp.bfloat16), ("dp", "enc"), axis=1, tiled=True),
        lax.all_gather(ff_out.astype(jnp.bfloat16), ("dp", "enc"), axis=0, tiled=True),
    )
    enc_count = lax.axis_size("enc")
    enc_place = lax.axis_index("enc")
    own_rows = hidden_in.shape[0]
    group_rows = own_rows * enc_count
    own_enc = encoder_out.shape[0]
    group_enc = own_enc * enc_count
    tgt_items = item_ids(tgt_lengths[0], group_rows)
    enc_items = item_ids(enc_lengths[0], group_enc)
    row_start = enc_place * own_rows
    own_items = lax.dynamic_slice_in_dim(tgt_items, row_start, own_rows)
    own_enc_items = lax.dynamic_slice_in_dim(enc_items, enc_place * own_enc, own_enc)
    bucket_starts = jnp.sum(
        (rel_bucket[None, :] < jnp.arange(BUCKETS, dtype=jnp.int32)[:, None]).astype(jnp.int32),
        axis=1,
    )
    query_place = row_start + jnp.arange(own_rows, dtype=jnp.int32)
    distance = query_place[:, None] - jnp.arange(group_rows, dtype=jnp.int32)[None, :]
    self_layout = (
        (distance >= 0) & (own_items[:, None] == tgt_items[None, :]),
        distance,
        (bucket_starts, rel_table),
    )
    hidden = hidden_in.astype(jnp.float32)
    normed_full, pull_one = jax.vjp(rms_scale, hidden, norm1_gain)
    normed = normed_full.astype(jnp.bfloat16)
    queries = product(normed, w_query).astype(jnp.bfloat16)
    key_own = product(normed, w_key).astype(jnp.bfloat16)
    value_own = product(normed, w_value).astype(jnp.bfloat16)
    key_group, value_group = (
        lax.all_gather(key_own, "enc", axis=0, tiled=True),
        lax.all_gather(value_own, "enc", axis=0, tiled=True),
    )
    self_num, self_top, self_total = forward_parts(queries, key_group, value_group, self_layout)
    attended = normalize(self_num, self_total)
    after_self = hidden + product(attended, w_out)
    normed_two_full, pull_two = jax.vjp(rms_scale, after_self, norm2_gain)
    normed_two = normed_two_full.astype(jnp.bfloat16)
    cross_queries = product(normed_two, c_query).astype(jnp.bfloat16)
    cross_keys = product(encoder_out, c_key).astype(jnp.bfloat16)
    cross_values = product(encoder_out, c_value).astype(jnp.bfloat16)
    query_group = lax.all_gather(cross_queries, "enc", axis=0, tiled=True)
    block_rows = min(512, group_rows)
    block_count = group_rows // block_rows

    def block_layout(first_row):
        query_items = lax.dynamic_slice_in_dim(tgt_items, first_row, block_rows)
        return (query_items[:, None] == own_enc_items[None, :], None, None)

    def block_forward(block_index, carry):
        numerator_all, top_all, total_all = carry
        first_row = block_index * block_rows
        block_num, block_top, block_total = forward_parts(
            lax.dynamic_slice_in_dim(query_group, first_row, block_rows, 0),
            cross_keys,
            cross_values,
            block_layout(first_row),
        )
        numerator_all = lax.dynamic_update_slice_in_dim(numerator_all, block_num, first_row, 0)
        top_all = lax.dynamic_update_slice_in_dim(top_all, block_top, first_row, 1)
        total_all = lax.dynamic_update_slice_in_dim(total_all, block_total, first_row, 1)
        return (numerator_all, top_all, total_all)

    numerator_all, local_tops, total_all = lax.fori_loop(
        0,
        block_count,
        block_forward,
        (
            jnp.zeros((group_rows, HEADS * HEAD), jnp.float32),
            jnp.zeros((HEADS, group_rows), jnp.float32),
            jnp.zeros((HEADS, group_rows), jnp.float32),
        ),
    )
    group_top = lax.pmax(local_tops, "enc")
    rescale = jnp.exp(local_tops - group_top)
    numerator_all = (
        numerator_all.reshape(group_rows, HEADS, HEAD) * jnp.transpose(rescale)[:, :, None]
    ).reshape(group_rows, HEADS * HEAD)
    total_all = total_all * rescale
    cross_num, cross_total = (
        lax.psum_scatter(
            numerator_all.astype(jnp.bfloat16), "enc", scatter_dimension=0, tiled=True
        ).astype(jnp.float32),
        lax.psum_scatter(
            total_all.astype(jnp.bfloat16), "enc", scatter_dimension=1, tiled=True
        ).astype(jnp.float32),
    )
    attended_two = normalize(cross_num, cross_total)
    after_cross = after_self + product(attended_two, c_out)
    normed_three_full, pull_three = jax.vjp(rms_scale, after_cross, norm3_gain)
    normed_three = normed_three_full.astype(jnp.bfloat16)
    gate_pre = product(normed_three, w_gate)
    up_pre = product(normed_three, w_up)
    activated, pull_act = jax.vjp(gated_gelu, gate_pre, up_pre)
    hidden_act = activated.astype(jnp.bfloat16)
    hidden_out = (after_cross + product(hidden_act, w_down)).astype(jnp.bfloat16)
    out_grad = grad_out.astype(jnp.float32)
    down_grad = product_tn(hidden_act, grad_out)
    act_grad = product_nt(grad_out, w_down)
    gate_grad_full, up_grad_full = pull_act(act_grad)
    gate_grad = gate_grad_full.astype(jnp.bfloat16)
    up_grad = up_grad_full.astype(jnp.bfloat16)
    gate_w_grad = product_tn(normed_three, gate_grad)
    up_w_grad = product_tn(normed_three, up_grad)
    normed_three_grad = product_nt(gate_grad, w_gate) + product_nt(up_grad, w_up)
    cross_res_grad, gain_three_grad = pull_three(normed_three_grad)
    after_cross_grad = out_grad + cross_res_grad
    branch_two = after_cross_grad.astype(jnp.bfloat16)
    c_out_grad = product_tn(attended_two, branch_two)
    cross_out_grad = product_nt(branch_two, c_out)
    cross_num_grad, cross_total_grad = output_grads(cross_out_grad, cross_num, cross_total)
    num_grad_group = lax.all_gather(cross_num_grad, "enc", axis=0, tiled=True)
    total_grad_group = lax.all_gather(cross_total_grad, "enc", axis=1, tiled=True)

    def block_backward(block_index, carry):
        query_grad_all, key_grad_sum, value_grad_sum = carry
        first_row = block_index * block_rows
        block_query_grad, block_key_grad, block_value_grad, unused_bias = backward_parts(
            lax.dynamic_slice_in_dim(query_group, first_row, block_rows, 0),
            cross_keys,
            cross_values,
            block_layout(first_row),
            lax.dynamic_slice_in_dim(group_top, first_row, block_rows, 1),
            lax.dynamic_slice_in_dim(num_grad_group, first_row, block_rows, 0),
            lax.dynamic_slice_in_dim(total_grad_group, first_row, block_rows, 1),
        )
        query_grad_all = lax.dynamic_update_slice_in_dim(
            query_grad_all, block_query_grad, first_row, 0
        )
        return (query_grad_all, key_grad_sum + block_key_grad, value_grad_sum + block_value_grad)

    query_grad_all, cross_key_grad, cross_value_grad = lax.fori_loop(
        0,
        block_count,
        block_backward,
        (
            jnp.zeros((group_rows, HEADS * HEAD), jnp.float32),
            jnp.zeros((own_enc, HEADS * HEAD), jnp.float32),
            jnp.zeros((own_enc, HEADS * HEAD), jnp.float32),
        ),
    )
    cross_query_grad = lax.psum_scatter(
        query_grad_all.astype(jnp.bfloat16), "enc", scatter_dimension=0, tiled=True
    )
    cross_key_low = cross_key_grad.astype(jnp.bfloat16)
    cross_value_low = cross_value_grad.astype(jnp.bfloat16)
    c_query_grad = product_tn(normed_two, cross_query_grad)
    c_key_grad = product_tn(encoder_out, cross_key_low)
    c_value_grad = product_tn(encoder_out, cross_value_low)
    encoder_grad = product_nt(cross_key_low, c_key) + product_nt(cross_value_low, c_value)
    self_res_grad, gain_two_grad = pull_two(product_nt(cross_query_grad, c_query))
    after_self_grad = after_cross_grad + self_res_grad
    branch_one = after_self_grad.astype(jnp.bfloat16)
    w_out_grad = product_tn(attended, branch_one)
    self_out_grad = product_nt(branch_one, w_out)
    self_num_grad, self_total_grad = output_grads(self_out_grad, self_num, self_total)
    self_query_grad, key_grad_rows, value_grad_rows, table_grad = backward_parts(
        queries, key_group, value_group, self_layout, self_top, self_num_grad, self_total_grad
    )
    self_key_grad, self_value_grad = (
        lax.psum_scatter(
            key_grad_rows.astype(jnp.bfloat16), "enc", scatter_dimension=0, tiled=True
        ).astype(jnp.float32),
        lax.psum_scatter(
            value_grad_rows.astype(jnp.bfloat16), "enc", scatter_dimension=0, tiled=True
        ).astype(jnp.float32),
    )
    query_low = self_query_grad.astype(jnp.bfloat16)
    key_low = self_key_grad.astype(jnp.bfloat16)
    value_low = self_value_grad.astype(jnp.bfloat16)
    w_query_grad = product_tn(normed, query_low)
    w_key_grad = product_tn(normed, key_low)
    w_value_grad = product_tn(normed, value_low)
    normed_grad = (
        product_nt(query_low, w_query) + product_nt(key_low, w_key) + product_nt(value_low, w_value)
    )
    input_res_grad, gain_one_grad = pull_one(normed_grad)
    hidden_grad = after_self_grad + input_res_grad
    shards = lax.axis_size(("dp", "enc"))
    full_grads = (
        w_query_grad,
        w_key_grad,
        w_value_grad,
        w_out_grad,
        c_query_grad,
        c_key_grad,
        c_value_grad,
        c_out_grad,
        gate_w_grad,
        up_w_grad,
        down_grad,
    )
    shard_dims = (1, 1, 1, 0, 1, 1, 1, 0, 1, 1, 0)
    piece_rows = tuple(
        (to_pieces(grad, place, shards) for grad, place in zip(full_grads, shard_dims))
    )
    received = (
        lax.all_to_all(
            piece_rows[0].astype(jnp.bfloat16),
            ("dp", "enc"),
            split_axis=0,
            concat_axis=0,
            tiled=True,
        ).astype(jnp.float32),
        lax.all_to_all(
            piece_rows[1].astype(jnp.bfloat16),
            ("dp", "enc"),
            split_axis=0,
            concat_axis=0,
            tiled=True,
        ).astype(jnp.float32),
        lax.all_to_all(
            piece_rows[2].astype(jnp.bfloat16),
            ("dp", "enc"),
            split_axis=0,
            concat_axis=0,
            tiled=True,
        ).astype(jnp.float32),
        lax.all_to_all(
            piece_rows[3].astype(jnp.bfloat16),
            ("dp", "enc"),
            split_axis=0,
            concat_axis=0,
            tiled=True,
        ).astype(jnp.float32),
        lax.all_to_all(
            piece_rows[4].astype(jnp.bfloat16),
            ("dp", "enc"),
            split_axis=0,
            concat_axis=0,
            tiled=True,
        ).astype(jnp.float32),
        lax.all_to_all(
            piece_rows[5].astype(jnp.bfloat16),
            ("dp", "enc"),
            split_axis=0,
            concat_axis=0,
            tiled=True,
        ).astype(jnp.float32),
        lax.all_to_all(
            piece_rows[6].astype(jnp.bfloat16),
            ("dp", "enc"),
            split_axis=0,
            concat_axis=0,
            tiled=True,
        ).astype(jnp.float32),
        lax.all_to_all(
            piece_rows[7].astype(jnp.bfloat16),
            ("dp", "enc"),
            split_axis=0,
            concat_axis=0,
            tiled=True,
        ).astype(jnp.float32),
        lax.all_to_all(
            piece_rows[8].astype(jnp.bfloat16),
            ("dp", "enc"),
            split_axis=0,
            concat_axis=0,
            tiled=True,
        ).astype(jnp.float32),
        lax.all_to_all(
            piece_rows[9].astype(jnp.bfloat16),
            ("dp", "enc"),
            split_axis=0,
            concat_axis=0,
            tiled=True,
        ).astype(jnp.float32),
        lax.all_to_all(
            piece_rows[10].astype(jnp.bfloat16),
            ("dp", "enc"),
            split_axis=0,
            concat_axis=0,
            tiled=True,
        ).astype(jnp.float32),
    )
    weight_grads = tuple(
        (
            from_pieces(piece, place, grad.shape, shards)
            for piece, place, grad in zip(received, shard_dims, full_grads)
        )
    )
    small_sums = lax.psum(
        (gain_one_grad, gain_two_grad, gain_three_grad, table_grad), ("dp", "enc")
    )
    return (
        hidden_out,
        hidden_grad,
        encoder_grad,
        small_sums[0],
        weight_grads[0],
        weight_grads[1],
        weight_grads[2],
        weight_grads[3],
        small_sums[3],
        small_sums[1],
        weight_grads[4],
        weight_grads[5],
        weight_grads[6],
        weight_grads[7],
        small_sums[2],
        weight_grads[8],
        weight_grads[9],
        weight_grads[10],
    )


def solution(mesh):
    return jax.shard_map(
        fast_body if dict(mesh.shape) == {"dp": 8, "enc": 4} else body,
        mesh=mesh,
        in_specs=(
            P(("dp", "enc"), None),
            P(("dp", "enc"), None),
            P(("dp", "enc"), None),
            P("dp", None),
            P("dp", None),
            P(),
            P(),
            P(None, ("dp", "enc")),
            P(None, ("dp", "enc")),
            P(None, ("dp", "enc")),
            P(("dp", "enc"), None),
            P(),
            P(),
            P(None, ("dp", "enc")),
            P(None, ("dp", "enc")),
            P(None, ("dp", "enc")),
            P(("dp", "enc"), None),
            P(),
            P(None, ("dp", "enc")),
            P(None, ("dp", "enc")),
            P(("dp", "enc"), None),
        ),
        out_specs=(
            P(("dp", "enc"), None),
            P(("dp", "enc"), None),
            P(("dp", "enc"), None),
            P(),
            P(None, ("dp", "enc")),
            P(None, ("dp", "enc")),
            P(None, ("dp", "enc")),
            P(("dp", "enc"), None),
            P(),
            P(),
            P(None, ("dp", "enc")),
            P(None, ("dp", "enc")),
            P(None, ("dp", "enc")),
            P(("dp", "enc"), None),
            P(),
            P(None, ("dp", "enc")),
            P(None, ("dp", "enc")),
            P(("dp", "enc"), None),
        ),
        check_vma=False,
    )
```

```python
import functools

import jax
import jax.numpy as jnp
from jax import lax
from jax.experimental import pallas as pl
from jax.experimental.pallas import tpu as pltpu
from jax.sharding import PartitionSpec as P

HEADS = 6
HEAD = 64
BUCKETS = 32
EPSILON = 1e-06
MASKED = -1e30
PAD = 16
MESH = pl.DeviceIdType.MESH
LOW = jnp.bfloat16
F32 = jnp.float32
NN = (((1,), (0,)), ((), ()))
NT = (((1,), (1,)), ((), ()))
TN = (((0,), (0,)), ((), ()))
ANY = pl.BlockSpec(memory_space=pl.ANY)
VM = pl.BlockSpec(memory_space=pltpu.VMEM)


def mm(left, right, dims=NN):
    return lax.dot_general(left, right, dims, preferred_element_type=F32)


def places():
    dp = lax.axis_index("dp")
    enc = lax.axis_index("enc")
    core = lax.rem(dp, 2)
    x = lax.rem(lax.div(dp, 2), 2)
    y = lax.div(dp, 4)
    sib = dp + 1 - 2 * core
    xn = dp + 2 - 4 * x
    yn = dp + 4 - 8 * y
    return dp, enc, sib, xn, yn


def enter(dp, enc, sib, xn, yn):
    barrier = pltpu.get_barrier_semaphore()
    targets = [(sib, enc), (xn, enc), (yn, enc), (xn + yn - dp, enc)]
    targets += [(dp, lax.rem(enc + k, 4)) for k in (1, 2, 3)]
    for target in targets:
        pl.semaphore_signal(barrier, inc=1, device_id=target, device_id_type=MESH)
    pl.semaphore_wait(barrier, len(targets))


class Sems:
    def __init__(self, send, recv):
        self.send, self.recv, self.used = send, recv, 0

    def take(self, count):
        first = self.used
        self.used += count
        return first


def remote(src, dst, send, recv, target):
    return pltpu.make_async_remote_copy(
        src_ref=src, dst_ref=dst, send_sem=send, recv_sem=recv, device_id=target, device_id_type=MESH
    )


class ZGather:
    def __init__(self, at, own, where, sems):
        self.at, self.own, self.sems = at, own, sems
        self.dp, self.enc = where[0], where[1]
        self.base = sems.take(6)

    def _copy(self, hop, side):
        s = self.sems
        place = self.enc - side * hop
        src = self.own if hop == 0 else self.at(place)
        return remote(
            src, self.at(place), s.send.at[self.base + hop + (3 if side == 1 else 0)],
            s.recv.at[self.base + place], (self.dp, self.enc + side),
        )

    def _has(self, hop, side):
        enc = self.enc
        return enc - hop >= 0 if side == 1 else enc + hop <= 3

    def _goes(self, side):
        return self.enc < 3 if side == 1 else self.enc > 0

    def start(self):
        for side in (1, -1):

            @pl.when(self._goes(side))
            def _(side=side):
                self._copy(0, side).start()

    def hop(self, hop):
        s = self.sems
        for side in (1, -1):

            @pl.when(self._has(hop, side))
            def _(side=side):
                place = self.enc - side * hop
                remote(
                    self.at(place), self.at(place), s.send.at[self.base], s.recv.at[self.base + place],
                    (self.dp, self.enc),
                ).wait_recv()

            if hop < 3:

                @pl.when(self._has(hop, side) & self._goes(side))
                def _(side=side):
                    self._copy(hop, side).start()

    def finish(self):
        for side in (1, -1):
            for hop in (0, 1, 2):

                @pl.when(self._has(hop, side) & self._goes(side))
                def _(side=side, hop=hop):
                    self._copy(hop, side).wait_send()


class ChipGather:
    def __init__(self, at, own, where, sems):
        self.at, self.own, self.sems, self.where = at, own, sems, where
        self.base = sems.take(9)

    def _copy(self, i):
        dp, enc, sib, xn, yn = self.where
        diag = xn + yn - dp
        block, part, target = (
            (dp, 0, xn),
            (dp, 0, yn),
            (dp, 0, sib),
            (xn, 0, sib),
            (yn, 0, sib),
            (xn, 1, yn),
            (yn, 2, xn),
            (diag, 1, sib),
            (diag, 2, sib),
        )[i]
        src = self.own if i < 3 else self.at(block, part)
        s = self.sems
        return remote(
            src, self.at(block, part), s.send.at[self.base + i], s.recv.at[self.base + i], (target, enc)
        )

    def step1(self):
        for i in (0, 1, 2):
            self._copy(i).start()

    def step2(self):
        self._copy(0).wait_recv()
        self._copy(5).start()
        self._copy(3).start()
        self._copy(1).wait_recv()
        self._copy(6).start()
        self._copy(4).start()

    def step3(self):
        self._copy(5).wait_recv()
        self._copy(7).start()
        self._copy(6).wait_recv()
        self._copy(8).start()

    def done(self):
        for i in (2, 3, 4, 7, 8):
            self._copy(i).wait_recv()

    def finish(self):
        for i in range(9):
            self._copy(i).wait_send()


def over(values, by):
    return lax.shift_right_logical(values * ((1 << 16) // by + 1), 16)


def regroup_matrix(count, width, block):
    shape = (4 * block, count * 4 * width)
    row = lax.broadcasted_iota(jnp.int32, shape, 0)
    col = lax.broadcasted_iota(jnp.int32, shape, 1)
    place = over(row, block)
    inside = row - place * block
    m = over(inside, width)
    take = (m * 4 + place) * width + inside - m * width
    return jnp.where((take == col) & (m < count), 1.0, 0.0).astype(LOW)


def rms_rows(values, gain):
    inv = lax.rsqrt(jnp.mean(values * values, axis=-1, keepdims=True) + EPSILON)
    return values * inv * gain


def low_lanes(rows):
    return lax.broadcasted_iota(jnp.int32, (rows, 2 * HEAD), 1) < HEAD


def one_head(pair, half):
    keep = low_lanes(pair.shape[0])
    if half:
        keep = jnp.logical_not(keep)
    return jnp.where(keep, pair.astype(F32), 0.0).astype(LOW)


def self_bias(rel_u, rows, cols):
    wide = jnp.broadcast_to(rel_u, (rows, rel_u.shape[1]))
    return pltpu.roll(wide, 0, 1, stride=1, stride_axis=0)[:, :cols]


def item_of(lengths_ref, place):
    end, item = jnp.int32(0), jnp.zeros_like(place)
    for b in range(4):
        end = end + lengths_ref[0, b]
        item = item + jnp.where(end <= place, 1, 0)
    return item


def attention_pair(q_pair, k_pair, v_pair, allowed, biases, keep_probs):
    rows = q_pair.shape[0]
    nums, totals = [], []
    for half in (0, 1):
        scores = mm(one_head(q_pair, half), k_pair, NT)
        if biases is not None:
            scores = scores + biases[half]
        scores = jnp.where(allowed, scores, MASKED)
        weights = jnp.exp(scores - jnp.max(scores, axis=1, keepdims=True))
        totals.append(jnp.sum(weights, axis=1, keepdims=True))
        probs = weights.astype(LOW)
        keep_probs(half, probs)
        nums.append(mm(probs, v_pair))
    low = low_lanes(rows)
    return jnp.where(low, nums[0], nums[1]), jnp.where(low, totals[0], totals[1])


def forward_kernel(
    width,
    tgt_len, enc_len, x_ref, e_ref, dy_ref, watt_ref, wff_ref, gains, rel_u,
    watt_out, wff_out, dy_out, x1_out, x2_out, n3_out, q1_out, kv1_out, q2_out, kv2_out,
    pr1_out, pr2_out, num1_out, num2_out, tot1_out, tot2_out,
    w, packed, send, recv, local,
):
    where = places()
    dp, enc, sib, xn, yn = where
    sems = Sems(send, recv)
    own, wide = x_ref.shape
    own_enc = e_ref.shape[0]
    inner = HEADS * HEAD
    line = 4 * width
    ff_rows = wff_ref.shape[1]
    ff_half = (ff_rows // 2 + PAD - 1) // PAD * PAD
    group = 4 * own

    def rows_at(ref, first, count):
        return ref.at[pl.ds(pl.multiple_of(first, PAD), count), :]

    def mats_at(ref, lo, hi, first, count):
        return ref.at[lo:hi, pl.ds(pl.multiple_of(first, PAD), count), :]

    zs = [
        ZGather(lambda e, g=g: packed.at[g, e], watt_ref.at[g], where, sems) for g in (0, 1)
    ]
    chips = []
    for lo, mid, hi in ((0, 2, 3), (3, 4, 5), (5, 6, 8)):
        cuts = ((lo, hi), (lo, mid), (mid, hi))
        chips.append(
            ChipGather(
                lambda d, part, cuts=cuts: mats_at(w, *cuts[part], d * line, line),
                mats_at(w, lo, hi, dp * line, line), where, sems,
            )
        )
    ff_cuts = ((0, ff_rows), (0, ff_half), (ff_half, ff_rows - ff_half))
    ff = ChipGather(
        lambda d, part: mats_at(wff_out, 0, 3, d * ff_rows + ff_cuts[part][0], ff_cuts[part][1]),
        wff_ref, where, sems,
    )
    dyz = ZGather(lambda e: rows_at(dy_out, e * own, own), dy_ref, where, sems)
    kvz = ZGather(
        lambda e: rows_at(kv1_out, e * own, own), rows_at(kv1_out, enc * own, own), where, sems
    )
    kvz2 = ZGather(
        lambda e: rows_at(kv2_out, e * own_enc, own_enc),
        rows_at(kv2_out, enc * own_enc, own_enc), where, sems,
    )

    enter(*where)
    zs[0].start()
    own_dy = pltpu.make_async_copy(dy_ref, rows_at(dy_out, enc * own, own), local.at[0])
    own_ff = pltpu.make_async_copy(wff_ref, mats_at(wff_out, 0, 3, dp * ff_rows, ff_rows), local.at[1])
    own_dy.start()
    own_ff.start()
    for g in (0, 1):
        packed[g, enc] = watt_ref[g]
    x = x_ref[...].astype(F32)
    n1 = rms_rows(x, gains[0:1, :]).astype(LOW)
    regroup = regroup_matrix(4, width, 4 * width)

    def unpack(g):
        rows = mm(regroup, packed[g].reshape(4 * line, wide)).astype(LOW)
        for m in range(4):
            w[4 * g + m, pl.ds(pl.multiple_of(dp * line, PAD), line), :] = rows[m * line : (m + 1) * line]

    for hop in (1, 2, 3):
        zs[0].hop(hop)
    unpack(0)
    chips[0].step1()
    zs[1].start()
    zs[1].hop(1)
    zs[1].hop(2)
    chips[0].step2()
    zs[1].hop(3)
    unpack(1)
    chips[1].step1()
    dyz.start()
    chips[0].step3()
    chips[0].done()

    q1 = mm(n1, w[0], NT).astype(LOW)
    own_rows = pl.ds(pl.multiple_of(enc * own, PAD), own)
    kv1_out[own_rows, 0:inner] = mm(n1, w[1], NT).astype(LOW)
    kv1_out[own_rows, inner : 2 * inner] = mm(n1, w[2], NT).astype(LOW)
    q1_out[...] = q1
    kvz.start()
    chips[1].step2()
    chips[2].step1()
    dyz.hop(1)
    kvz.hop(1)
    chips[1].step3()
    chips[1].done()
    own_enc_rows = pl.ds(pl.multiple_of(enc * own_enc, PAD), own_enc)
    kv2_out[own_enc_rows, 0:inner] = mm(e_ref[...], w[3], NT).astype(LOW)
    kv2_out[own_enc_rows, inner : 2 * inner] = mm(e_ref[...], w[4], NT).astype(LOW)
    kvz.hop(2)
    kvz2.start()
    chips[2].step2()
    ff.step1()
    kvz.hop(3)

    row_place = enc * own + lax.broadcasted_iota(jnp.int32, (own, 1), 0)
    col_place = lax.broadcasted_iota(jnp.int32, (1, group), 1)
    own_items = item_of(tgt_len, row_place)
    allowed = (own_items == item_of(tgt_len, col_place)) & (col_place <= row_place)
    for pair in range(HEADS // 2):
        lanes = slice(pair * 2 * HEAD, (pair + 1) * 2 * HEAD)
        far = slice(inner + pair * 2 * HEAD, inner + (pair + 1) * 2 * HEAD)

        def keep(half, probs, pair=pair):
            pr1_out[2 * pair + half] = probs

        num, total = attention_pair(
            q1[:, lanes], kv1_out[:, lanes], kv1_out[:, far], allowed,
            [self_bias(rel_u[2 * pair + half : 2 * pair + half + 1, :], own, group) for half in (0, 1)],
            keep,
        )
        num1_out[:, lanes] = num
        tot1_out[:, lanes] = total
        if pair == 1:
            kvz2.hop(1)
    chips[2].step3()
    dyz.hop(2)
    chips[2].done()
    saves = [
        pltpu.make_async_copy(w, watt_out, local.at[2]),
    ]
    for c in saves:
        c.start()
    o1 = (num1_out[...] / tot1_out[...]).astype(LOW)
    x1 = x + mm(o1, w[5])
    x1_out[...] = x1
    n2 = rms_rows(x1, gains[1:2, :]).astype(LOW)
    q2 = mm(n2, w[6], NT).astype(LOW)
    q2_out[...] = q2
    kvz2.hop(2)
    ff.step2()
    kvz2.hop(3)
    enc_place = lax.broadcasted_iota(jnp.int32, (1, 4 * own_enc), 1)
    allowed2 = own_items == item_of(enc_len, enc_place)
    for pair in range(HEADS // 2):
        lanes = slice(pair * 2 * HEAD, (pair + 1) * 2 * HEAD)
        far = slice(inner + pair * 2 * HEAD, inner + (pair + 1) * 2 * HEAD)

        def keep2(half, probs, pair=pair):
            pr2_out[2 * pair + half] = probs

        num, total = attention_pair(
            q2[:, lanes], kv2_out[:, lanes], kv2_out[:, far], allowed2, None, keep2
        )
        num2_out[:, lanes] = num
        tot2_out[:, lanes] = total
    ff.step3()
    o2 = (num2_out[...] / tot2_out[...]).astype(LOW)
    x2 = x1 + mm(o2, w[7])
    x2_out[...] = x2
    n3_out[...] = rms_rows(x2, gains[2:3, :]).astype(LOW)
    dyz.hop(3)
    ff.done()
    for part in zs + chips + [ff, dyz, kvz, kvz2]:
        part.finish()
    own_dy.wait()
    own_ff.wait()
    for c in saves:
        c.wait()


def sds(shape, dtype):
    return jax.ShapeDtypeStruct(shape, dtype)


def call_forward(width, tgt_len, enc_len, x, e, dy, watt, wff, gains, rel_u):
    own, wide = x.shape
    own_enc = e.shape[0]
    inner = HEADS * HEAD
    SM = pl.BlockSpec(memory_space=pltpu.SMEM)
    return pl.pallas_call(
        functools.partial(forward_kernel, width),
        out_shape=(
            sds((8, inner, wide), LOW),
            sds((3, 8 * wff.shape[1], wide), LOW),
            sds((4 * own, wide), LOW),
            sds((own, wide), F32),
            sds((own, wide), F32),
            sds((own, wide), LOW),
            sds((own, inner), LOW),
            sds((4 * own, 2 * inner), LOW),
            sds((own, inner), LOW),
            sds((4 * own_enc, 2 * inner), LOW),
            sds((HEADS, own, 4 * own), LOW),
            sds((HEADS, own, 4 * own_enc), LOW),
            sds((own, inner), F32),
            sds((own, inner), F32),
            sds((own, inner), F32),
            sds((own, inner), F32),
        ),
        in_specs=[SM, SM, VM, VM, ANY, VM, ANY, VM, VM],
        out_specs=(ANY, ANY, ANY) + (VM,) * 13,
        scratch_shapes=[
            pltpu.VMEM((8, inner, wide), LOW),
            pltpu.VMEM((2, 4, 4 * width, wide), LOW),
            pltpu.SemaphoreType.DMA((66,)),
            pltpu.SemaphoreType.DMA((66,)),
            pltpu.SemaphoreType.DMA((3,)),
        ],
        compiler_params=pltpu.CompilerParams(
            collective_id=1, has_side_effects=True, vmem_limit_bytes=56 * 2**20
        ),
        name="attention_forward",
    )(tgt_len, enc_len, x, e, dy, watt, wff, gains, rel_u)


def pack_weights(self_q, self_k, self_v, self_o, cross_q, cross_k, cross_v, cross_o, ff_gate, ff_up, ff_out):
    rows = jnp.stack(
        [w.T for w in (self_q, self_k, self_v, cross_k, cross_v)] + [self_o, cross_q.T, cross_o]
    ).astype(LOW)
    wff = jnp.stack([ff_gate.T, ff_up.T, ff_out]).astype(LOW)
    return rows.reshape(2, 4 * rows.shape[1], rows.shape[2]), wff


def bias_rows(rel_bucket, rel_table, enc, own, group):
    starts = jnp.sum(
        (rel_bucket[None, :] < jnp.arange(BUCKETS, dtype=jnp.int32)[:, None]).astype(jnp.int32), axis=1
    )
    k = jnp.arange(group + own, dtype=jnp.int32)
    distance = enc * own - jnp.where(k < group, k, k - group - own)
    ends = jnp.concatenate([starts[1:], jnp.full((1,), group, jnp.int32)])
    inside = (distance[None, :] >= starts[:, None]) & (distance[None, :] < ends[:, None])
    return inside, jnp.sum(jnp.where(inside[:, None, :], rel_table[:, :, None], 0.0), axis=0)


class ZScatter:
    def __init__(self, src_at, dst_at, where, sems, meet=None):
        self.src_at, self.dst_at, self.sems, self.meet = src_at, dst_at, sems, meet
        self.dp, self.enc = where[0], where[1]
        self.base = sems.take(3 if meet is None else 4)
        self.middle = (self.enc == 1) | (self.enc == 2)

    def _copy(self, place, merged=False):
        k = lax.rem(place - self.enc + 4, 4)
        s = self.sems
        return remote(
            self.meet if merged else self.src_at(place), self.dst_at(3 - k),
            s.send.at[self.base + k - 1], s.recv.at[self.base + 3 - k], (self.dp, place),
        )

    def _to_meet(self):
        s = self.sems
        far = 3 - self.enc
        return remote(
            self.src_at(far), self.meet, s.send.at[self.base + 3], s.recv.at[self.base + 3],
            (self.dp, 1 + lax.div(self.enc, 2)),
        )

    def start(self, place):
        self._copy(place).start()

    def start_all(self):
        enc = self.enc
        if self.meet is None:
            for k in (2, 1, 3):
                self.start(lax.rem(enc + k, 4))
            return

        @pl.when(jnp.logical_not(self.middle))
        def _():
            self._to_meet().start()
            self.start(lax.rem(enc + 2, 4))
            self.start(1 + lax.div(enc, 2))

        @pl.when(self.middle)
        def _():
            self.start(enc - 1)
            self.start(enc + 1)

    def merge(self):
        @pl.when(self.middle)
        def _():
            far = lax.rem(self.enc + 2, 4)
            self._to_meet().wait_recv()
            self.meet[...] = (self.meet[...].astype(F32) + self.src_at(far)[...].astype(F32)).astype(LOW)
            self._copy(far, merged=True).start()

    def _each(self, act):
        enc = self.enc
        if self.meet is None:
            for k in (1, 2, 3):
                act(lax.rem(enc + k, 4))
            return
        act(lax.rem(enc + 2, 4))

        @pl.when(enc > 0)
        def _():
            act(enc - 1)

        @pl.when(enc < 3)
        def _():
            act(enc + 1)

    def wait(self):
        def one(place):
            k = lax.rem(self.enc - place + 4, 4)
            s = self.sems
            remote(
                self.dst_at(3 - k), self.dst_at(3 - k), s.send.at[self.base], s.recv.at[self.base + 3 - k],
                (self.dp, self.enc),
            ).wait_recv()

        self._each(one)

    def clear(self):
        if self.meet is not None:

            @pl.when(self.enc == 0)
            def _():
                ref = self.dst_at(2)
                ref[...] = jnp.zeros(ref.shape, ref.dtype)

            @pl.when(self.enc == 3)
            def _():
                ref = self.dst_at(0)
                ref[...] = jnp.zeros(ref.shape, ref.dtype)

    def finish(self):
        self._each(lambda place: self._copy(place).wait_send())
        if self.meet is not None:

            @pl.when(jnp.logical_not(self.middle))
            def _():
                self._to_meet().wait_send()


def rms_back(values, gain, grad):
    inv = lax.rsqrt(jnp.mean(values * values, axis=-1, keepdims=True) + EPSILON)
    scaled = grad * gain
    mean = jnp.mean(values * scaled, axis=-1, keepdims=True)
    gain_grad = jnp.sum(grad * values * inv, axis=0, keepdims=True)
    return inv * scaled - values * (inv * inv * inv * mean), gain_grad


GELU_A = 0.7978845608028654
GELU_B = 0.044715


def ff_kernel(
    n3_ref, x2_ref, dy_ref, dyall_ref, wff_ref, gains,
    dx2_out, part_out, sums_out, gain_out,
    w, n3, dy, act, dgate, dup, part, got, grads, core_got, own_sum, send, recv, local,
):
    where = places()
    dp, enc, sib, xn, yn = where
    core = lax.rem(dp, 2)
    sems = Sems(send, recv)
    own = n3_ref.shape[0]
    ff_rows = grads.shape[3]

    def rows_of(place):
        return pl.ds(pl.multiple_of(place * own, PAD), own)

    gather = ZGather(lambda e: n3.at[rows_of(e), :], n3_ref, where, sems)
    scatter = ZScatter(lambda e: part.at[e], lambda slot: got.at[slot], where, sems)
    loads = [
        pltpu.make_async_copy(wff_ref, w, local.at[0]),
        pltpu.make_async_copy(dyall_ref, dy, local.at[1]),
    ]
    for c in loads:
        c.start()
    enter(*where)
    gather.start()
    n3[rows_of(enc), :] = n3_ref[...]
    for c in loads:
        c.wait()

    def block(place):
        rows = rows_of(place)
        normed = n3[rows, :]
        gate = mm(normed, w[0], NT)
        up = mm(normed, w[1], NT)
        dh = mm(dy[rows, :], w[2], NT)
        square = gate * gate
        t = jnp.tanh(GELU_A * gate * (1.0 + GELU_B * square))
        half = 0.5 * (1.0 + t)
        g = gate * half
        slope = half + 0.5 * gate * (1.0 - t * t) * (GELU_A * (1.0 + 3.0 * GELU_B * square))
        hidden = (g * up).astype(LOW)
        dg = (dh * up * slope).astype(LOW)
        du = (dh * g).astype(LOW)
        act[rows, :] = hidden
        dgate[rows, :] = dg
        dup[rows, :] = du
        part_out[rows, :] = mm(hidden, w[2]).astype(LOW)
        return mm(dg, w[0]) + mm(du, w[1])

    own_sum[...] = block(enc)
    near = 1 + lax.rem(enc, 2)
    last = jnp.where(enc < 2, 3, 0)
    for hop, place in ((1, near), (2, 6 - enc - near - last), (3, last)):
        gather.hop(hop)
        part[place] = block(place).astype(LOW)
        scatter.start(place)

    swaps = []
    base = sems.take(3)
    for m, (left, right) in ((2, (act, dy)), (0, (dgate, n3)), (1, (dup, n3))):
        whole = mm(left[...], right[...], TN).astype(LOW)
        for j in range(4):
            for c in range(2):
                first_row = (2 * j + c) * ff_rows
                grads[m, j, c] = whole[first_row : first_row + ff_rows]
        swap = remote(
            grads.at[m, :, 1 - core], core_got.at[m], send.at[base + m], recv.at[base + m], (sib, enc)
        )
        swap.start()
        swaps.append((m, swap))
    for m, swap in swaps:
        swap.wait_recv()
        for j in range(4):
            sums_out[m, j] = (grads[m, j, core].astype(F32) + core_got[m, j].astype(F32)).astype(LOW)
    scatter.wait()
    dn3 = own_sum[...] + got[0].astype(F32) + got[1].astype(F32) + got[2].astype(F32)
    dv, gain_grad = rms_back(x2_ref[...], gains[2:3, :], dn3)
    dx2_out[...] = dy_ref[...].astype(F32) + dv
    gain_out[...] = gain_grad
    gather.finish()
    scatter.finish()
    for m, swap in swaps:
        swap.wait_send()


def call_ff(n3, x2, dy, dy_all, wff, gains):
    own, wide = n3.shape
    ff_all = wff.shape[1]
    ff_rows = ff_all // 8
    group = 4 * own
    return pl.pallas_call(
        ff_kernel,
        out_shape=(
            sds((own, wide), F32),
            sds((group, wide), LOW),
            sds((3, 4, ff_rows, wide), LOW),
            sds((1, wide), F32),
        ),
        in_specs=[VM, VM, VM, ANY, ANY, VM],
        out_specs=(VM,) * 4,
        scratch_shapes=[
            pltpu.VMEM((3, ff_all, wide), LOW),
            pltpu.VMEM((group, wide), LOW),
            pltpu.VMEM((group, wide), LOW),
            pltpu.VMEM((group, ff_all), LOW),
            pltpu.VMEM((group, ff_all), LOW),
            pltpu.VMEM((group, ff_all), LOW),
            pltpu.VMEM((4, own, wide), LOW),
            pltpu.VMEM((3, own, wide), LOW),
            pltpu.VMEM((3, 4, 2, ff_rows, wide), LOW),
            pltpu.VMEM((3, 4, ff_rows, wide), LOW),
            pltpu.VMEM((own, wide), F32),
            pltpu.SemaphoreType.DMA((12,)),
            pltpu.SemaphoreType.DMA((12,)),
            pltpu.SemaphoreType.DMA((2,)),
        ],
        compiler_params=pltpu.CompilerParams(
            collective_id=2, has_side_effects=True, vmem_limit_bytes=60 * 2**20
        ),
        name="feed_forward",
    )(n3, x2, dy, dy_all, wff, gains)


class GradReduce:
    def __init__(self, lo, hi, bufs, out, where, sems):
        self.lo, self.hi, self.bufs, self.out, self.where, self.sems = lo, hi, bufs, out, where, sems
        self.base = sems.take(4)
        line, line_got, line_meet, self.rows = bufs[3:7]
        at = lo // 2
        self.line = ZScatter(
            lambda e: line.at[at, e], lambda slot: line_got.at[slot, at], where, sems, line_meet.at[at]
        )

    def _core(self):
        dp, enc, sib, xn, yn = self.where
        grads, core_got = self.bufs[:2]
        s = self.sems
        return remote(
            grads.at[self.lo : self.hi, :, 1 - lax.rem(dp, 2)], core_got.at[self.lo : self.hi],
            s.send.at[self.base], s.recv.at[self.base], (sib, enc),
        )

    def _chip(self, i):
        dp, enc, sib, xn, yn = self.where
        core_got, chip_got = self.bufs[1:3]
        s = self.sems
        target = (xn, yn, xn + yn - dp)[i]
        return remote(
            core_got.at[self.lo : self.hi, lax.div(target, 2)], chip_got.at[i, self.lo : self.hi],
            s.send.at[self.base + 1 + i], s.recv.at[self.base + 1 + i], (target, enc),
        )

    def step1(self):
        self._core().start()

    def step2(self):
        grads, core_got = self.bufs[:2]
        core = lax.rem(self.where[0], 2)
        self._core().wait_recv()
        for m in range(self.lo, self.hi):
            core_got[m] = (grads[m, :, core].astype(F32) + core_got[m].astype(F32)).astype(LOW)
        for i in (2, 0, 1):
            self._chip(i).start()

    def step3(self, regroup):
        core_got, chip_got, line = self.bufs[1:4]
        chip = lax.div(self.where[0], 2)
        for i in range(3):
            self._chip(i).wait_recv()
        totals = []
        for m in range(self.lo, self.hi):
            total = core_got[m, chip].astype(F32)
            for i in range(3):
                total = total + chip_got[i, m].astype(F32)
            totals.append(total.astype(LOW))
        rows = mm(regroup, jnp.concatenate(totals, axis=0)).astype(LOW)
        for e in range(4):
            line[self.lo // 2, e] = rows[e * self.rows : (e + 1) * self.rows]
        self.line.start_all()

    def merge(self):
        self.line.merge()

    def step4(self):
        line, line_got = self.bufs[3:5]
        at = self.lo // 2
        self.line.wait()
        total = line[at, self.where[1]].astype(F32)
        for slot in range(3):
            total = total + line_got[slot, at].astype(F32)
        self.out[at] = total

    def finish(self):
        self._core().wait_send()
        for i in range(3):
            self._chip(i).wait_send()
        self.line.finish()


def backward_pair(q_pair, k_pair, v_pair, probs_ref, pair, dnum, dtotals):
    rows = q_pair.shape[0]
    parts, scores = [], []
    for half in (0, 1):
        dw = mm(one_head(dnum, half), v_pair, NT)
        ds = (probs_ref[2 * pair + half].astype(F32) * (dw + dtotals[half])).astype(LOW)
        scores.append(ds)
        parts.append(mm(ds, k_pair))
    dq = jnp.where(low_lanes(rows), parts[0], parts[1])
    dk = mm(jnp.concatenate(scores, axis=0), jnp.concatenate([one_head(q_pair, h) for h in (0, 1)], axis=0), TN)
    probs = jnp.concatenate([probs_ref[2 * pair + h] for h in (0, 1)], axis=0)
    dv = mm(probs, jnp.concatenate([one_head(dnum, h) for h in (0, 1)], axis=0), TN)
    return dq, dk, dv, scores


def total_grads(product, total):
    low = low_lanes(product.shape[0])
    out = []
    for half in (0, 1):
        keep = low if half == 0 else jnp.logical_not(low)
        top = jnp.sum(jnp.where(keep, product, 0.0), axis=1, keepdims=True)
        tot = total[:, half * HEAD : half * HEAD + 1]
        out.append(-top / (tot * tot))
    return out


def backward_kernel(
    width,
    x_ref, e_ref, x1_ref, x2_ref, dx2_ref, gains, gain3_grad, inside,
    q1, kv1, q2, kv2, pr1, pr2, num1, num2, tot1, tot2, part_ref, watt_ref, sums_ref,
    hidden_out, hidden_grad, encoder_grad, att_out, ff_out, small_out,
    w, grads, core_got, chip_got, line, line_got, line_meet, ff_got, ff_own, part_got, part_meet,
    kvp1, kvp1_got, kvp1_meet, kvp2, kvp2_got, kvp2_meet, dq, vec, vec_got, send, recv, local,
):
    where = places()
    dp, enc, sib, xn, yn = where
    sems = Sems(send, recv)
    own, wide = x_ref.shape
    own_enc = e_ref.shape[0]
    inner = HEADS * HEAD
    chip = lax.div(dp, 2)
    block = line.shape[2]

    out_z = ZScatter(lambda e: part_ref.at[e], lambda slot: part_got.at[slot], where, sems, part_meet)
    kv1_z = ZScatter(lambda e: kvp1.at[e], lambda slot: kvp1_got.at[slot], where, sems, kvp1_meet)
    kv2_z = ZScatter(lambda e: kvp2.at[e], lambda slot: kvp2_got.at[slot], where, sems, kvp2_meet)
    bufs = (grads, core_got, chip_got, line, line_got, line_meet, block)
    batches = [GradReduce(lo, lo + 2, bufs, att_out, where, sems) for lo in (0, 2, 4, 6)]
    ff_base = sems.take(3)
    vec_base = sems.take(3)
    vec_z = ZScatter(lambda e: vec.at[3], lambda slot: vec_got.at[3 + slot], where, sems)

    def ff_copy(i):
        target = (xn, yn, xn + yn - dp)[i]
        return remote(
            sums_ref.at[:, lax.div(target, 2)], ff_got.at[i],
            send.at[ff_base + i], recv.at[ff_base + i], (target, enc),
        )

    def vec_copy(i):
        target = (sib, xn, yn)[i]
        return remote(
            vec.at[i], vec_got.at[i], send.at[vec_base + i], recv.at[vec_base + i], (target, enc)
        )

    def load(slot, m, i):
        return pltpu.make_async_copy(watt_ref.at[m], w.at[slot], local.at[i])

    first_loads = [load(slot, m, slot) for slot, m in enumerate((7, 6, 5, 1, 2))]
    for c in first_loads:
        c.start()
    own_ff = pltpu.make_async_copy(sums_ref.at[:, chip], ff_own, local.at[8])
    own_ff.start()
    enter(*where)
    out_z.start_all()
    for i in (2, 0, 1):
        ff_copy(i).start()
    for part in [out_z, kv1_z, kv2_z] + [batch.line for batch in batches]:
        part.clear()
    regroup = regroup_matrix(2, width, block)

    def put_grad(m, left, right):
        whole = mm(left, right, TN).astype(LOW)
        rows = 4 * width
        for j in range(4):
            for c in range(2):
                grads[m, j, c] = whole[(2 * j + c) * rows : (2 * j + c + 1) * rows]

    b2 = dx2_ref[...].astype(LOW)
    first_loads[0].wait()
    do2 = mm(b2, w[0], NT)
    dnum2 = (do2 / tot2[...]).astype(LOW)
    prod2 = do2 * num2[...]
    for pair in range(HEADS // 2):
        lanes = slice(pair * 2 * HEAD, (pair + 1) * 2 * HEAD)
        far = slice(inner + pair * 2 * HEAD, inner + (pair + 1) * 2 * HEAD)
        dtot = total_grads(prod2[:, lanes], tot2[:, lanes])
        dq_pair, dk, dv, _ = backward_pair(
            q2[:, lanes], kv2[:, lanes], kv2[:, far], pr2, pair, dnum2[:, lanes], dtot
        )
        dq[:, lanes] = dq_pair.astype(LOW)
        for e in range(4):
            kvp2[e, :, lanes] = dk[e * own_enc : (e + 1) * own_enc].astype(LOW)
            kvp2[e, :, far] = dv[e * own_enc : (e + 1) * own_enc].astype(LOW)
    kv2_z.start_all()
    out_z.merge()
    dq2 = dq[...]
    put_grad(0, (num2[...] / tot2[...]).astype(LOW), b2)
    x1 = x1_ref[...]
    put_grad(1, dq2, rms_rows(x1, gains[1:2, :]).astype(LOW))
    batches[0].step1()
    first_loads[1].wait()
    dv2, gain2_grad = rms_back(x1, gains[1:2, :], mm(dq2, w[1]))
    dx1 = dx2_ref[...] + dv2
    b1 = dx1.astype(LOW)
    first_loads[2].wait()
    do1 = mm(b1, w[2], NT)
    late = [load(2, 0, 5), load(0, 3, 6), load(1, 4, 7)]
    for c in late:
        c.start()
    dnum1 = (do1 / tot1[...]).astype(LOW)
    prod1 = do1 * num1[...]
    batches[0].step2()
    vec[0] = jnp.zeros(vec.shape[1:], F32)
    flip_row = lax.broadcasted_iota(jnp.int32, (own, own), 0)
    flip_col = lax.broadcasted_iota(jnp.int32, (own, own), 1)
    flip = jnp.where(flip_row + flip_col == own - 1, 1.0, 0.0).astype(LOW)
    all_scores = []
    for pair in range(HEADS // 2):
        lanes = slice(pair * 2 * HEAD, (pair + 1) * 2 * HEAD)
        far = slice(inner + pair * 2 * HEAD, inner + (pair + 1) * 2 * HEAD)
        dtot = total_grads(prod1[:, lanes], tot1[:, lanes])
        dq_pair, dk, dv, scores = backward_pair(
            q1[:, lanes], kv1[:, lanes], kv1[:, far], pr1, pair, dnum1[:, lanes], dtot
        )
        dq[:, lanes] = dq_pair.astype(LOW)
        for e in range(4):
            kvp1[e, :, lanes] = dk[e * own : (e + 1) * own].astype(LOW)
            kvp1[e, :, far] = dv[e * own : (e + 1) * own].astype(LOW)
        all_scores += scores
    kv1_z.start_all()
    kv2_z.merge()
    for h, ds in enumerate(all_scores):
        long = jnp.concatenate([mm(flip, ds), jnp.zeros((own, own), F32)], axis=1)
        turned = pltpu.roll(long, 0, 1, stride=1, stride_axis=0)
        by_distance = jnp.sum(turned, axis=0, keepdims=True)
        vec[0, 8 + h : 9 + h, 0:BUCKETS] = lax.dot_general(
            by_distance, inside[...], NT, precision=lax.Precision.HIGHEST, preferred_element_type=F32
        )
    dq1 = dq[...]
    x = x_ref[...].astype(F32)
    n1 = rms_rows(x, gains[0:1, :]).astype(LOW)
    put_grad(2, (num1[...] / tot1[...]).astype(LOW), b1)
    put_grad(3, dq1, n1)
    batches[1].step1()
    kv1_z.merge()
    batches[0].step3(regroup)
    for c in late:
        c.wait()
    dn1 = mm(dq1, w[2])
    batches[1].step2()

    out_z.wait()
    hidden_out[...] = (
        x2_ref[...] + (part_ref[enc].astype(F32) + part_got[0].astype(F32))
        + (part_got[1].astype(F32) + part_got[2].astype(F32))
    ).astype(LOW)

    kv1_z.wait()
    low1 = (
        kvp1[enc].astype(F32) + kvp1_got[0].astype(F32) + kvp1_got[1].astype(F32) + kvp1_got[2].astype(F32)
    ).astype(LOW)
    dk1 = low1[:, :inner]
    dv1 = low1[:, inner:]
    put_grad(4, dk1, n1)
    put_grad(5, dv1, n1)
    batches[2].step1()
    batches[0].merge()
    first_loads[3].wait()
    first_loads[4].wait()
    dn1 = dn1 + mm(dk1, w[3]) + mm(dv1, w[4])
    dv_x, gain1_grad = rms_back(x, gains[0:1, :], dn1)
    hidden_grad[...] = dx1 + dv_x
    vec[0, 0:1, :] = gain1_grad
    vec[0, 1:2, :] = gain2_grad
    vec[0, 2:3, :] = gain3_grad[...]
    vec_copy(0).start()
    batches[2].step2()

    kv2_z.wait()
    low2 = (
        kvp2[enc].astype(F32) + kvp2_got[0].astype(F32) + kvp2_got[1].astype(F32) + kvp2_got[2].astype(F32)
    ).astype(LOW)
    dk2 = low2[:, :inner]
    dv2 = low2[:, inner:]
    put_grad(6, dk2, e_ref[...])
    put_grad(7, dv2, e_ref[...])
    batches[3].step1()
    batches[1].step3(regroup)
    encoder_grad[...] = mm(dk2, w[0]) + mm(dv2, w[1])
    batches[3].step2()
    batches[1].merge()
    vec_copy(0).wait_recv()
    vec[1] = vec[0] + vec_got[0]
    vec_copy(1).start()
    batches[2].step3(regroup)
    vec_copy(1).wait_recv()
    vec[2] = vec[1] + vec_got[1]
    vec_copy(2).start()
    batches[0].step4()
    batches[2].merge()
    vec_copy(2).wait_recv()
    vec[3] = vec[2] + vec_got[2]
    vec_z.start_all()
    batches[3].step3(regroup)
    own_ff.wait()
    for i in range(3):
        ff_copy(i).wait_recv()
    for m in range(3):
        ff_out[m] = (
            ff_own[m].astype(F32) + ff_got[0, m].astype(F32) + ff_got[1, m].astype(F32) + ff_got[2, m].astype(F32)
        )
    batches[3].merge()
    for batch in batches[1:]:
        batch.step4()
    vec_z.wait()
    small_out[...] = vec[3] + vec_got[3] + vec_got[4] + vec_got[5]
    for done in [out_z, kv1_z, kv2_z, vec_z] + batches:
        done.finish()
    for i in range(3):
        ff_copy(i).wait_send()
        vec_copy(i).wait_send()


def call_backward(width, x, e, x1, x2, dx2, gains, gain3_grad, inside, saved, watt, part, sums):
    own, wide = x.shape
    own_enc = e.shape[0]
    inner = HEADS * HEAD
    rows = 4 * width
    block = (2 * width + PAD - 1) // PAD * PAD
    ff_rows = sums.shape[2]
    return pl.pallas_call(
        functools.partial(backward_kernel, width),
        out_shape=(
            sds((own, wide), LOW),
            sds((own, wide), F32),
            sds((own_enc, wide), F32),
            sds((4, block, wide), F32),
            sds((3, ff_rows, wide), F32),
            sds((16, wide), F32),
        ),
        in_specs=[VM] * 19 + [ANY] * 2,
        out_specs=(VM,) * 6,
        scratch_shapes=[
            pltpu.VMEM((5, inner, wide), LOW),
            pltpu.VMEM((8, 4, 2, rows, wide), LOW),
            pltpu.VMEM((8, 4, rows, wide), LOW),
            pltpu.VMEM((3, 8, rows, wide), LOW),
            pltpu.VMEM((4, 4, block, wide), LOW),
            pltpu.VMEM((3, 4, block, wide), LOW),
            pltpu.VMEM((4, block, wide), LOW),
            pltpu.VMEM((3, 3, ff_rows, wide), LOW),
            pltpu.VMEM((3, ff_rows, wide), LOW),
            pltpu.VMEM((3, own, wide), LOW),
            pltpu.VMEM((own, wide), LOW),
            pltpu.VMEM((4, own, 2 * inner), LOW),
            pltpu.VMEM((3, own, 2 * inner), LOW),
            pltpu.VMEM((own, 2 * inner), LOW),
            pltpu.VMEM((4, own_enc, 2 * inner), LOW),
            pltpu.VMEM((3, own_enc, 2 * inner), LOW),
            pltpu.VMEM((own_enc, 2 * inner), LOW),
            pltpu.VMEM((own, inner), LOW),
            pltpu.VMEM((4, 16, wide), F32),
            pltpu.VMEM((6, 16, wide), F32),
            pltpu.SemaphoreType.DMA((54,)),
            pltpu.SemaphoreType.DMA((54,)),
            pltpu.SemaphoreType.DMA((9,)),
        ],
        compiler_params=pltpu.CompilerParams(
            collective_id=3, has_side_effects=True, vmem_limit_bytes=62 * 2**20
        ),
        name="attention_backward",
    )(x, e, x1, x2, dx2, gains, gain3_grad, inside, *saved, part.reshape(4, own, wide), watt, sums)


def fast_body(
    hidden_in, encoder_out, grad_out, tgt_lengths, enc_lengths, rel_bucket, norm1_gain,
    self_q, self_k, self_v, self_o, rel_table, norm2_gain,
    cross_q, cross_k, cross_v, cross_o, norm3_gain, ff_gate, ff_up, ff_out,
):
    own = hidden_in.shape[0]
    width = self_q.shape[1]
    watt, wff = pack_weights(
        self_q, self_k, self_v, self_o, cross_q, cross_k, cross_v, cross_o, ff_gate, ff_up, ff_out
    )
    inside, rel_u = bias_rows(rel_bucket, rel_table, lax.axis_index("enc"), own, 4 * own)
    gains = jnp.stack([norm1_gain, norm2_gain, norm3_gain])
    fwd = call_forward(
        width, tgt_lengths, enc_lengths, hidden_in, encoder_out, grad_out, watt, wff, gains, rel_u
    )
    watt_all, wff_all, dy_all, x1, x2, n3 = fwd[:6]
    dx2, part, sums, gain3_grad = call_ff(n3, x2, grad_out, dy_all, wff_all, gains)
    saved = fwd[6:]
    hidden_out, hidden_grad, encoder_grad, att, ff, small = call_backward(
        width, hidden_in, encoder_out, x1, x2, dx2, gains, gain3_grad,
        jnp.roll(inside.astype(F32), own - 1, axis=1), saved, watt_all, part, sums,
    )
    o2, q2, o1, q1, k1, v1, k2, v2 = (att[m // 2, m % 2 * width : (m % 2 + 1) * width] for m in range(8))
    return (
        hidden_out, hidden_grad, encoder_grad, small[0],
        q1.T, k1.T, v1.T, o1, small[8 : 8 + HEADS, :BUCKETS].T,
        small[1], q2.T, k2.T, v2.T, o2, small[2], ff[0].T, ff[1].T, ff[2],
    )


def rms_scale(values, gain):
    return values * lax.rsqrt(jnp.mean(values * values, axis=-1, keepdims=True) + EPSILON) * gain


def gated_gelu(gate_pre, up_pre):
    return jax.nn.gelu(gate_pre, approximate=True) * up_pre


def item_ids(lengths, total_rows):
    ends = jnp.cumsum(lengths)
    places = jnp.arange(total_rows, dtype=jnp.int32)
    return jnp.sum((ends[None, :] <= places[:, None]).astype(jnp.int32), axis=1)


def product(left, right):
    return jnp.dot(left, right, preferred_element_type=jnp.float32)


def product_tn(left, right):
    return lax.dot_general(
        left, right, (((0,), (0,)), ((), ())), preferred_element_type=jnp.float32
    )


def product_nt(left, right):
    return lax.dot_general(
        left, right, (((1,), (1,)), ((), ())), preferred_element_type=jnp.float32
    )


def to_pieces(grad, shard_dim, shards):
    if shard_dim == 0:
        return grad.reshape(shards, -1)
    rows = grad.shape[0]
    return jnp.transpose(grad.reshape(rows, shards, -1), (1, 0, 2)).reshape(shards, -1)


def from_pieces(received, shard_dim, shape, shards):
    summed = jnp.sum(received, axis=0)
    if shard_dim == 0:
        return summed.reshape(shape[0] // shards, shape[1])
    return summed.reshape(shape[0], shape[1] // shards)


def head_pair(matrix, pair_index):
    return lax.dynamic_slice_in_dim(matrix, pair_index * 2 * HEAD, 2 * HEAD, 1).reshape(
        matrix.shape[0], 2, HEAD
    )


def pair_stats(stats, pair_index):
    return lax.dynamic_slice_in_dim(stats, pair_index * 2, 2, 0)


def relative_bias(distance, bias_info, pair_index):
    starts, table = bias_info
    table_pair = lax.dynamic_slice_in_dim(table, pair_index * 2, 2, 1)

    def add_step(bucket, total):
        rise = table_pair[bucket] - table_pair[bucket - 1]
        return total + jnp.where(distance[None] >= starts[bucket], rise[:, None, None], 0.0)

    start_bias = jnp.broadcast_to(table_pair[0][:, None, None], (2,) + distance.shape)
    return lax.fori_loop(1, BUCKETS, add_step, start_bias)


def relative_grads(distance, starts, score_grad):

    def one_step(bucket):
        return jnp.sum(jnp.where(distance[None] >= starts[bucket], score_grad, 0.0), axis=(1, 2))

    steps_sum = lax.map(one_step, jnp.arange(BUCKETS, dtype=jnp.int32))
    return steps_sum - jnp.concatenate([steps_sum[1:], jnp.zeros((1, 2), jnp.float32)], axis=0)


def pair_scores(query_block, key_rows, pair_index, layout):
    allowed, distance, bias_info = layout
    scores = jnp.einsum(
        "qhe,khe->hqk",
        head_pair(query_block, pair_index),
        head_pair(key_rows, pair_index),
        preferred_element_type=jnp.float32,
    )
    if bias_info is not None:
        scores = scores + relative_bias(distance, bias_info, pair_index)
    return jnp.where(allowed[None], scores, MASKED)


def forward_parts(query_block, key_rows, value_rows, layout):
    block_rows = query_block.shape[0]
    width = 2 * HEAD

    def forward_one_pair(pair_index, carry):
        numerator, largest, totals = carry
        scores = pair_scores(query_block, key_rows, pair_index, layout)
        pair_top = jnp.max(scores, axis=2)
        weights = jnp.exp(scores - pair_top[:, :, None])
        partial_sum = jnp.einsum(
            "hqk,khe->qhe",
            weights.astype(jnp.bfloat16),
            head_pair(value_rows, pair_index),
            preferred_element_type=jnp.float32,
        )
        numerator = lax.dynamic_update_slice_in_dim(
            numerator, partial_sum.reshape(block_rows, width), pair_index * width, 1
        )
        largest = lax.dynamic_update_slice_in_dim(largest, pair_top, pair_index * 2, 0)
        totals = lax.dynamic_update_slice_in_dim(
            totals, jnp.sum(weights, axis=2), pair_index * 2, 0
        )
        return (numerator, largest, totals)

    start_state = (
        jnp.zeros((block_rows, HEADS * HEAD), jnp.float32),
        jnp.zeros((HEADS, block_rows), jnp.float32),
        jnp.zeros((HEADS, block_rows), jnp.float32),
    )
    return lax.fori_loop(0, HEADS // 2, forward_one_pair, start_state)


def backward_parts(query_block, key_rows, value_rows, layout, top_rows, num_grad, total_grad):
    allowed, distance, bias_info = layout
    block_rows = query_block.shape[0]
    key_count = key_rows.shape[0]
    width = 2 * HEAD

    def backward_one_pair(pair_index, carry):
        query_grad, key_grad, value_grad, bias_grad = carry
        query_pair = head_pair(query_block, pair_index)
        key_pair = head_pair(key_rows, pair_index)
        value_pair = head_pair(value_rows, pair_index)
        grad_pair = head_pair(num_grad, pair_index)
        scores = pair_scores(query_block, key_rows, pair_index, layout)
        weights = jnp.exp(scores - pair_stats(top_rows, pair_index)[:, :, None])
        weight_grad = jnp.einsum(
            "qhe,khe->hqk", grad_pair, value_pair, preferred_element_type=jnp.float32
        )
        score_grad = (
            weights * (weight_grad + pair_stats(total_grad, pair_index)[:, :, None])
        ).astype(jnp.bfloat16)
        part_query = jnp.einsum(
            "hqk,khe->qhe", score_grad, key_pair, preferred_element_type=jnp.float32
        )
        part_key = jnp.einsum(
            "hqk,qhe->khe", score_grad, query_pair, preferred_element_type=jnp.float32
        )
        part_value = jnp.einsum(
            "hqk,qhe->khe",
            weights.astype(jnp.bfloat16),
            grad_pair,
            preferred_element_type=jnp.float32,
        )
        query_grad = lax.dynamic_update_slice_in_dim(
            query_grad, part_query.reshape(block_rows, width), pair_index * width, 1
        )
        key_grad = lax.dynamic_update_slice_in_dim(
            key_grad, part_key.reshape(key_count, width), pair_index * width, 1
        )
        value_grad = lax.dynamic_update_slice_in_dim(
            value_grad, part_value.reshape(key_count, width), pair_index * width, 1
        )
        if bias_info is not None:
            pair_bias_grad = relative_grads(distance, bias_info[0], score_grad.astype(jnp.float32))
            bias_grad = lax.dynamic_update_slice_in_dim(
                bias_grad, pair_bias_grad, pair_index * 2, 1
            )
        return (query_grad, key_grad, value_grad, bias_grad)

    bias_start = None if bias_info is None else jnp.zeros((BUCKETS, HEADS), jnp.float32)
    start_state = (
        jnp.zeros((block_rows, HEADS * HEAD), jnp.float32),
        jnp.zeros((key_count, HEADS * HEAD), jnp.float32),
        jnp.zeros((key_count, HEADS * HEAD), jnp.float32),
        bias_start,
    )
    return lax.fori_loop(0, HEADS // 2, backward_one_pair, start_state)


def normalize(numerator, totals):
    row_count = numerator.shape[0]
    shaped = numerator.reshape(row_count, HEADS, HEAD) / jnp.transpose(totals)[:, :, None]
    return shaped.reshape(row_count, HEADS * HEAD).astype(jnp.bfloat16)


def output_grads(out_grad, numerator, totals):
    row_count = out_grad.shape[0]
    per_total = jnp.transpose(totals)
    shaped_grad = out_grad.reshape(row_count, HEADS, HEAD)
    num_grad = (
        (shaped_grad / per_total[:, :, None]).reshape(row_count, HEADS * HEAD).astype(jnp.bfloat16)
    )
    total_grad = -jnp.sum(shaped_grad * numerator.reshape(row_count, HEADS, HEAD), axis=2) / (
        per_total * per_total
    )
    return (num_grad, jnp.transpose(total_grad))


def body(
    hidden_in,
    encoder_out,
    grad_out,
    tgt_lengths,
    enc_lengths,
    rel_bucket,
    norm1_gain,
    self_q,
    self_k,
    self_v,
    self_o,
    rel_table,
    norm2_gain,
    cross_q,
    cross_k,
    cross_v,
    cross_o,
    norm3_gain,
    ff_gate,
    ff_up,
    ff_out,
):
    w_query, w_key, w_value, w_out, c_query, c_key, c_value, c_out, w_gate, w_up, w_down = (
        lax.all_gather(self_q.astype(jnp.bfloat16), ("dp", "enc"), axis=1, tiled=True),
        lax.all_gather(self_k.astype(jnp.bfloat16), ("dp", "enc"), axis=1, tiled=True),
        lax.all_gather(self_v.astype(jnp.bfloat16), ("dp", "enc"), axis=1, tiled=True),
        lax.all_gather(self_o.astype(jnp.bfloat16), ("dp", "enc"), axis=0, tiled=True),
        lax.all_gather(cross_q.astype(jnp.bfloat16), ("dp", "enc"), axis=1, tiled=True),
        lax.all_gather(cross_k.astype(jnp.bfloat16), ("dp", "enc"), axis=1, tiled=True),
        lax.all_gather(cross_v.astype(jnp.bfloat16), ("dp", "enc"), axis=1, tiled=True),
        lax.all_gather(cross_o.astype(jnp.bfloat16), ("dp", "enc"), axis=0, tiled=True),
        lax.all_gather(ff_gate.astype(jnp.bfloat16), ("dp", "enc"), axis=1, tiled=True),
        lax.all_gather(ff_up.astype(jnp.bfloat16), ("dp", "enc"), axis=1, tiled=True),
        lax.all_gather(ff_out.astype(jnp.bfloat16), ("dp", "enc"), axis=0, tiled=True),
    )
    enc_count = lax.axis_size("enc")
    enc_place = lax.axis_index("enc")
    own_rows = hidden_in.shape[0]
    group_rows = own_rows * enc_count
    own_enc = encoder_out.shape[0]
    group_enc = own_enc * enc_count
    tgt_items = item_ids(tgt_lengths[0], group_rows)
    enc_items = item_ids(enc_lengths[0], group_enc)
    row_start = enc_place * own_rows
    own_items = lax.dynamic_slice_in_dim(tgt_items, row_start, own_rows)
    own_enc_items = lax.dynamic_slice_in_dim(enc_items, enc_place * own_enc, own_enc)
    bucket_starts = jnp.sum(
        (rel_bucket[None, :] < jnp.arange(BUCKETS, dtype=jnp.int32)[:, None]).astype(jnp.int32),
        axis=1,
    )
    query_place = row_start + jnp.arange(own_rows, dtype=jnp.int32)
    distance = query_place[:, None] - jnp.arange(group_rows, dtype=jnp.int32)[None, :]
    self_layout = (
        (distance >= 0) & (own_items[:, None] == tgt_items[None, :]),
        distance,
        (bucket_starts, rel_table),
    )
    hidden = hidden_in.astype(jnp.float32)
    normed_full, pull_one = jax.vjp(rms_scale, hidden, norm1_gain)
    normed = normed_full.astype(jnp.bfloat16)
    queries = product(normed, w_query).astype(jnp.bfloat16)
    key_own = product(normed, w_key).astype(jnp.bfloat16)
    value_own = product(normed, w_value).astype(jnp.bfloat16)
    key_group, value_group = (
        lax.all_gather(key_own, "enc", axis=0, tiled=True),
        lax.all_gather(value_own, "enc", axis=0, tiled=True),
    )
    self_num, self_top, self_total = forward_parts(queries, key_group, value_group, self_layout)
    attended = normalize(self_num, self_total)
    after_self = hidden + product(attended, w_out)
    normed_two_full, pull_two = jax.vjp(rms_scale, after_self, norm2_gain)
    normed_two = normed_two_full.astype(jnp.bfloat16)
    cross_queries = product(normed_two, c_query).astype(jnp.bfloat16)
    cross_keys = product(encoder_out, c_key).astype(jnp.bfloat16)
    cross_values = product(encoder_out, c_value).astype(jnp.bfloat16)
    query_group = lax.all_gather(cross_queries, "enc", axis=0, tiled=True)
    block_rows = min(512, group_rows)
    block_count = group_rows // block_rows

    def block_layout(first_row):
        query_items = lax.dynamic_slice_in_dim(tgt_items, first_row, block_rows)
        return (query_items[:, None] == own_enc_items[None, :], None, None)

    def block_forward(block_index, carry):
        numerator_all, top_all, total_all = carry
        first_row = block_index * block_rows
        block_num, block_top, block_total = forward_parts(
            lax.dynamic_slice_in_dim(query_group, first_row, block_rows, 0),
            cross_keys,
            cross_values,
            block_layout(first_row),
        )
        numerator_all = lax.dynamic_update_slice_in_dim(numerator_all, block_num, first_row, 0)
        top_all = lax.dynamic_update_slice_in_dim(top_all, block_top, first_row, 1)
        total_all = lax.dynamic_update_slice_in_dim(total_all, block_total, first_row, 1)
        return (numerator_all, top_all, total_all)

    numerator_all, local_tops, total_all = lax.fori_loop(
        0,
        block_count,
        block_forward,
        (
            jnp.zeros((group_rows, HEADS * HEAD), jnp.float32),
            jnp.zeros((HEADS, group_rows), jnp.float32),
            jnp.zeros((HEADS, group_rows), jnp.float32),
        ),
    )
    group_top = lax.pmax(local_tops, "enc")
    rescale = jnp.exp(local_tops - group_top)
    numerator_all = (
        numerator_all.reshape(group_rows, HEADS, HEAD) * jnp.transpose(rescale)[:, :, None]
    ).reshape(group_rows, HEADS * HEAD)
    total_all = total_all * rescale
    cross_num, cross_total = (
        lax.psum_scatter(
            numerator_all.astype(jnp.bfloat16), "enc", scatter_dimension=0, tiled=True
        ).astype(jnp.float32),
        lax.psum_scatter(
            total_all.astype(jnp.bfloat16), "enc", scatter_dimension=1, tiled=True
        ).astype(jnp.float32),
    )
    attended_two = normalize(cross_num, cross_total)
    after_cross = after_self + product(attended_two, c_out)
    normed_three_full, pull_three = jax.vjp(rms_scale, after_cross, norm3_gain)
    normed_three = normed_three_full.astype(jnp.bfloat16)
    gate_pre = product(normed_three, w_gate)
    up_pre = product(normed_three, w_up)
    activated, pull_act = jax.vjp(gated_gelu, gate_pre, up_pre)
    hidden_act = activated.astype(jnp.bfloat16)
    hidden_out = (after_cross + product(hidden_act, w_down)).astype(jnp.bfloat16)
    out_grad = grad_out.astype(jnp.float32)
    down_grad = product_tn(hidden_act, grad_out)
    act_grad = product_nt(grad_out, w_down)
    gate_grad_full, up_grad_full = pull_act(act_grad)
    gate_grad = gate_grad_full.astype(jnp.bfloat16)
    up_grad = up_grad_full.astype(jnp.bfloat16)
    gate_w_grad = product_tn(normed_three, gate_grad)
    up_w_grad = product_tn(normed_three, up_grad)
    normed_three_grad = product_nt(gate_grad, w_gate) + product_nt(up_grad, w_up)
    cross_res_grad, gain_three_grad = pull_three(normed_three_grad)
    after_cross_grad = out_grad + cross_res_grad
    branch_two = after_cross_grad.astype(jnp.bfloat16)
    c_out_grad = product_tn(attended_two, branch_two)
    cross_out_grad = product_nt(branch_two, c_out)
    cross_num_grad, cross_total_grad = output_grads(cross_out_grad, cross_num, cross_total)
    num_grad_group = lax.all_gather(cross_num_grad, "enc", axis=0, tiled=True)
    total_grad_group = lax.all_gather(cross_total_grad, "enc", axis=1, tiled=True)

    def block_backward(block_index, carry):
        query_grad_all, key_grad_sum, value_grad_sum = carry
        first_row = block_index * block_rows
        block_query_grad, block_key_grad, block_value_grad, unused_bias = backward_parts(
            lax.dynamic_slice_in_dim(query_group, first_row, block_rows, 0),
            cross_keys,
            cross_values,
            block_layout(first_row),
            lax.dynamic_slice_in_dim(group_top, first_row, block_rows, 1),
            lax.dynamic_slice_in_dim(num_grad_group, first_row, block_rows, 0),
            lax.dynamic_slice_in_dim(total_grad_group, first_row, block_rows, 1),
        )
        query_grad_all = lax.dynamic_update_slice_in_dim(
            query_grad_all, block_query_grad, first_row, 0
        )
        return (query_grad_all, key_grad_sum + block_key_grad, value_grad_sum + block_value_grad)

    query_grad_all, cross_key_grad, cross_value_grad = lax.fori_loop(
        0,
        block_count,
        block_backward,
        (
            jnp.zeros((group_rows, HEADS * HEAD), jnp.float32),
            jnp.zeros((own_enc, HEADS * HEAD), jnp.float32),
            jnp.zeros((own_enc, HEADS * HEAD), jnp.float32),
        ),
    )
    cross_query_grad = lax.psum_scatter(
        query_grad_all.astype(jnp.bfloat16), "enc", scatter_dimension=0, tiled=True
    )
    cross_key_low = cross_key_grad.astype(jnp.bfloat16)
    cross_value_low = cross_value_grad.astype(jnp.bfloat16)
    c_query_grad = product_tn(normed_two, cross_query_grad)
    c_key_grad = product_tn(encoder_out, cross_key_low)
    c_value_grad = product_tn(encoder_out, cross_value_low)
    encoder_grad = product_nt(cross_key_low, c_key) + product_nt(cross_value_low, c_value)
    self_res_grad, gain_two_grad = pull_two(product_nt(cross_query_grad, c_query))
    after_self_grad = after_cross_grad + self_res_grad
    branch_one = after_self_grad.astype(jnp.bfloat16)
    w_out_grad = product_tn(attended, branch_one)
    self_out_grad = product_nt(branch_one, w_out)
    self_num_grad, self_total_grad = output_grads(self_out_grad, self_num, self_total)
    self_query_grad, key_grad_rows, value_grad_rows, table_grad = backward_parts(
        queries, key_group, value_group, self_layout, self_top, self_num_grad, self_total_grad
    )
    self_key_grad, self_value_grad = (
        lax.psum_scatter(
            key_grad_rows.astype(jnp.bfloat16), "enc", scatter_dimension=0, tiled=True
        ).astype(jnp.float32),
        lax.psum_scatter(
            value_grad_rows.astype(jnp.bfloat16), "enc", scatter_dimension=0, tiled=True
        ).astype(jnp.float32),
    )
    query_low = self_query_grad.astype(jnp.bfloat16)
    key_low = self_key_grad.astype(jnp.bfloat16)
    value_low = self_value_grad.astype(jnp.bfloat16)
    w_query_grad = product_tn(normed, query_low)
    w_key_grad = product_tn(normed, key_low)
    w_value_grad = product_tn(normed, value_low)
    normed_grad = (
        product_nt(query_low, w_query) + product_nt(key_low, w_key) + product_nt(value_low, w_value)
    )
    input_res_grad, gain_one_grad = pull_one(normed_grad)
    hidden_grad = after_self_grad + input_res_grad
    shards = lax.axis_size(("dp", "enc"))
    full_grads = (
        w_query_grad,
        w_key_grad,
        w_value_grad,
        w_out_grad,
        c_query_grad,
        c_key_grad,
        c_value_grad,
        c_out_grad,
        gate_w_grad,
        up_w_grad,
        down_grad,
    )
    shard_dims = (1, 1, 1, 0, 1, 1, 1, 0, 1, 1, 0)
    piece_rows = tuple(
        (to_pieces(grad, place, shards) for grad, place in zip(full_grads, shard_dims))
    )
    received = (
        lax.all_to_all(
            piece_rows[0].astype(jnp.bfloat16),
            ("dp", "enc"),
            split_axis=0,
            concat_axis=0,
            tiled=True,
        ).astype(jnp.float32),
        lax.all_to_all(
            piece_rows[1].astype(jnp.bfloat16),
            ("dp", "enc"),
            split_axis=0,
            concat_axis=0,
            tiled=True,
        ).astype(jnp.float32),
        lax.all_to_all(
            piece_rows[2].astype(jnp.bfloat16),
            ("dp", "enc"),
            split_axis=0,
            concat_axis=0,
            tiled=True,
        ).astype(jnp.float32),
        lax.all_to_all(
            piece_rows[3].astype(jnp.bfloat16),
            ("dp", "enc"),
            split_axis=0,
            concat_axis=0,
            tiled=True,
        ).astype(jnp.float32),
        lax.all_to_all(
            piece_rows[4].astype(jnp.bfloat16),
            ("dp", "enc"),
            split_axis=0,
            concat_axis=0,
            tiled=True,
        ).astype(jnp.float32),
        lax.all_to_all(
            piece_rows[5].astype(jnp.bfloat16),
            ("dp", "enc"),
            split_axis=0,
            concat_axis=0,
            tiled=True,
        ).astype(jnp.float32),
        lax.all_to_all(
            piece_rows[6].astype(jnp.bfloat16),
            ("dp", "enc"),
            split_axis=0,
            concat_axis=0,
            tiled=True,
        ).astype(jnp.float32),
        lax.all_to_all(
            piece_rows[7].astype(jnp.bfloat16),
            ("dp", "enc"),
            split_axis=0,
            concat_axis=0,
            tiled=True,
        ).astype(jnp.float32),
        lax.all_to_all(
            piece_rows[8].astype(jnp.bfloat16),
            ("dp", "enc"),
            split_axis=0,
            concat_axis=0,
            tiled=True,
        ).astype(jnp.float32),
        lax.all_to_all(
            piece_rows[9].astype(jnp.bfloat16),
            ("dp", "enc"),
            split_axis=0,
            concat_axis=0,
            tiled=True,
        ).astype(jnp.float32),
        lax.all_to_all(
            piece_rows[10].astype(jnp.bfloat16),
            ("dp", "enc"),
            split_axis=0,
            concat_axis=0,
            tiled=True,
        ).astype(jnp.float32),
    )
    weight_grads = tuple(
        (
            from_pieces(piece, place, grad.shape, shards)
            for piece, place, grad in zip(received, shard_dims, full_grads)
        )
    )
    small_sums = lax.psum(
        (gain_one_grad, gain_two_grad, gain_three_grad, table_grad), ("dp", "enc")
    )
    return (
        hidden_out,
        hidden_grad,
        encoder_grad,
        small_sums[0],
        weight_grads[0],
        weight_grads[1],
        weight_grads[2],
        weight_grads[3],
        small_sums[3],
        small_sums[1],
        weight_grads[4],
        weight_grads[5],
        weight_grads[6],
        weight_grads[7],
        small_sums[2],
        weight_grads[8],
        weight_grads[9],
        weight_grads[10],
    )


def solution(mesh):
    return jax.shard_map(
        fast_body if dict(mesh.shape) == {"dp": 8, "enc": 4} else body,
        mesh=mesh,
        in_specs=(
            P(("dp", "enc"), None),
            P(("dp", "enc"), None),
            P(("dp", "enc"), None),
            P("dp", None),
            P("dp", None),
            P(),
            P(),
            P(None, ("dp", "enc")),
            P(None, ("dp", "enc")),
            P(None, ("dp", "enc")),
            P(("dp", "enc"), None),
            P(),
            P(),
            P(None, ("dp", "enc")),
            P(None, ("dp", "enc")),
            P(None, ("dp", "enc")),
            P(("dp", "enc"), None),
            P(),
            P(None, ("dp", "enc")),
            P(None, ("dp", "enc")),
            P(("dp", "enc"), None),
        ),
        out_specs=(
            P(("dp", "enc"), None),
            P(("dp", "enc"), None),
            P(("dp", "enc"), None),
            P(),
            P(None, ("dp", "enc")),
            P(None, ("dp", "enc")),
            P(None, ("dp", "enc")),
            P(("dp", "enc"), None),
            P(),
            P(),
            P(None, ("dp", "enc")),
            P(None, ("dp", "enc")),
            P(None, ("dp", "enc")),
            P(("dp", "enc"), None),
            P(),
            P(None, ("dp", "enc")),
            P(None, ("dp", "enc")),
            P(("dp", "enc"), None),
        ),
        check_vma=False,
    )
```

```python
import functools

import jax
import jax.numpy as jnp
from jax import lax
from jax.experimental import pallas as pl
from jax.experimental.pallas import tpu as pltpu
from jax.sharding import PartitionSpec as P

HEADS = 6
HEAD = 64
BUCKETS = 32
EPSILON = 1e-06
MASKED = -1e30
PAD = 16
MESH = pl.DeviceIdType.MESH
LOW = jnp.bfloat16
F32 = jnp.float32
NN = (((1,), (0,)), ((), ()))
NT = (((1,), (1,)), ((), ()))
TN = (((0,), (0,)), ((), ()))
ANY = pl.BlockSpec(memory_space=pl.ANY)
VM = pl.BlockSpec(memory_space=pltpu.VMEM)


def mm(left, right, dims=NN):
    return lax.dot_general(left, right, dims, preferred_element_type=F32)


def places():
    dp = lax.axis_index("dp")
    enc = lax.axis_index("enc")
    core = lax.rem(dp, 2)
    x = lax.rem(lax.div(dp, 2), 2)
    y = lax.div(dp, 4)
    sib = dp + 1 - 2 * core
    xn = dp + 2 - 4 * x
    yn = dp + 4 - 8 * y
    return dp, enc, sib, xn, yn


def enter(dp, enc, sib, xn, yn):
    barrier = pltpu.get_barrier_semaphore()
    targets = [(sib, enc), (xn, enc), (yn, enc), (xn + yn - dp, enc)]
    targets += [(dp, lax.rem(enc + k, 4)) for k in (1, 2, 3)]
    for target in targets:
        pl.semaphore_signal(barrier, inc=1, device_id=target, device_id_type=MESH)
    pl.semaphore_wait(barrier, len(targets))


class Sems:
    def __init__(self, send, recv):
        self.send, self.recv, self.used = send, recv, 0

    def take(self, count):
        first = self.used
        self.used += count
        return first


def remote(src, dst, send, recv, target):
    return pltpu.make_async_remote_copy(
        src_ref=src, dst_ref=dst, send_sem=send, recv_sem=recv, device_id=target, device_id_type=MESH
    )


class ZGather:
    def __init__(self, at, own, where, sems):
        self.at, self.own, self.sems = at, own, sems
        self.dp, self.enc = where[0], where[1]
        self.base = sems.take(6)

    def _copy(self, hop, side):
        s = self.sems
        place = self.enc - side * hop
        src = self.own if hop == 0 else self.at(place)
        return remote(
            src, self.at(place), s.send.at[self.base + hop + (3 if side == 1 else 0)],
            s.recv.at[self.base + place], (self.dp, self.enc + side),
        )

    def _has(self, hop, side):
        enc = self.enc
        return enc - hop >= 0 if side == 1 else enc + hop <= 3

    def _goes(self, side):
        return self.enc < 3 if side == 1 else self.enc > 0

    def start(self):
        for side in (1, -1):

            @pl.when(self._goes(side))
            def _(side=side):
                self._copy(0, side).start()

    def hop(self, hop):
        s = self.sems
        for side in (1, -1):

            @pl.when(self._has(hop, side))
            def _(side=side):
                place = self.enc - side * hop
                remote(
                    self.at(place), self.at(place), s.send.at[self.base], s.recv.at[self.base + place],
                    (self.dp, self.enc),
                ).wait_recv()

            if hop < 3:

                @pl.when(self._has(hop, side) & self._goes(side))
                def _(side=side):
                    self._copy(hop, side).start()

    def finish(self):
        for side in (1, -1):
            for hop in (0, 1, 2):

                @pl.when(self._has(hop, side) & self._goes(side))
                def _(side=side, hop=hop):
                    self._copy(hop, side).wait_send()


class ChipGather:
    def __init__(self, at, own, where, sems):
        self.at, self.own, self.sems, self.where = at, own, sems, where
        self.base = sems.take(9)

    def _copy(self, i):
        dp, enc, sib, xn, yn = self.where
        diag = xn + yn - dp
        block, part, target = (
            (dp, 0, xn),
            (dp, 0, yn),
            (dp, 0, sib),
            (xn, 0, sib),
            (yn, 0, sib),
            (xn, 1, yn),
            (yn, 2, xn),
            (diag, 1, sib),
            (diag, 2, sib),
        )[i]
        src = self.own if i < 3 else self.at(block, part)
        s = self.sems
        return remote(
            src, self.at(block, part), s.send.at[self.base + i], s.recv.at[self.base + i], (target, enc)
        )

    def step1(self):
        for i in (0, 1, 2):
            self._copy(i).start()

    def step2(self):
        self._copy(0).wait_recv()
        self._copy(5).start()
        self._copy(3).start()
        self._copy(1).wait_recv()
        self._copy(6).start()
        self._copy(4).start()

    def step3(self):
        self._copy(5).wait_recv()
        self._copy(7).start()
        self._copy(6).wait_recv()
        self._copy(8).start()

    def done(self):
        for i in (2, 3, 4, 7, 8):
            self._copy(i).wait_recv()

    def finish(self):
        for i in range(9):
            self._copy(i).wait_send()


def over(values, by):
    return lax.shift_right_logical(values * ((1 << 16) // by + 1), 16)


def regroup_matrix(count, width, block):
    shape = (4 * block, count * 4 * width)
    row = lax.broadcasted_iota(jnp.int32, shape, 0)
    col = lax.broadcasted_iota(jnp.int32, shape, 1)
    place = over(row, block)
    inside = row - place * block
    m = over(inside, width)
    take = (m * 4 + place) * width + inside - m * width
    return jnp.where((take == col) & (m < count), 1.0, 0.0).astype(LOW)


def rms_rows(values, gain):
    inv = lax.rsqrt(jnp.mean(values * values, axis=-1, keepdims=True) + EPSILON)
    return values * inv * gain


def low_lanes(rows):
    return lax.broadcasted_iota(jnp.int32, (rows, 2 * HEAD), 1) < HEAD


def one_head(pair, half):
    keep = low_lanes(pair.shape[0])
    if half:
        keep = jnp.logical_not(keep)
    return jnp.where(keep, pair.astype(F32), 0.0).astype(LOW)


def self_bias(rel_u, rows, cols):
    wide = jnp.broadcast_to(rel_u, (rows, rel_u.shape[1]))
    return pltpu.roll(wide, 0, 1, stride=1, stride_axis=0)[:, :cols]


def item_of(lengths_ref, place):
    end, item = jnp.int32(0), jnp.zeros_like(place)
    for b in range(4):
        end = end + lengths_ref[0, b]
        item = item + jnp.where(end <= place, 1, 0)
    return item


def attention_pair(q_pair, k_pair, v_pair, allowed, biases, keep_probs):
    rows = q_pair.shape[0]
    nums, totals = [], []
    for half in (0, 1):
        scores = mm(one_head(q_pair, half), k_pair, NT)
        if biases is not None:
            scores = scores + biases[half]
        scores = jnp.where(allowed, scores, MASKED)
        weights = jnp.exp(scores - jnp.max(scores, axis=1, keepdims=True))
        totals.append(jnp.sum(weights, axis=1, keepdims=True))
        probs = weights.astype(LOW)
        keep_probs(half, probs)
        nums.append(mm(probs, v_pair))
    low = low_lanes(rows)
    return jnp.where(low, nums[0], nums[1]), jnp.where(low, totals[0], totals[1])


def forward_kernel(
    width,
    tgt_len, enc_len, x_ref, e_ref, dy_ref, watt_ref, wff_ref, gains, rel_u,
    watt_out, wff_out, dy_out, x1_out, x2_out, n3_out, q1_out, kv1_out, q2_out, kv2_out,
    pr1_out, pr2_out, num1_out, num2_out, tot1_out, tot2_out,
    w, packed, send, recv, local,
):
    where = places()
    dp, enc, sib, xn, yn = where
    sems = Sems(send, recv)
    own, wide = x_ref.shape
    own_enc = e_ref.shape[0]
    inner = HEADS * HEAD
    line = 4 * width
    ff_rows = wff_ref.shape[1]
    ff_half = (ff_rows // 2 + PAD - 1) // PAD * PAD
    group = 4 * own

    def rows_at(ref, first, count):
        return ref.at[pl.ds(pl.multiple_of(first, PAD), count), :]

    def mats_at(ref, lo, hi, first, count):
        return ref.at[lo:hi, pl.ds(pl.multiple_of(first, PAD), count), :]

    zs = [
        ZGather(lambda e, g=g: packed.at[g, e], watt_ref.at[g], where, sems) for g in (0, 1)
    ]
    chips = []
    for lo in (0, 2, 4, 6):
        hi = lo + 2
        cuts = ((lo, hi), (lo, lo + 1), (lo + 1, hi))
        chips.append(
            ChipGather(
                lambda d, part, cuts=cuts: mats_at(w, *cuts[part], d * line, line),
                mats_at(w, lo, hi, dp * line, line), where, sems,
            )
        )
    ff_cuts = ((0, ff_rows), (0, ff_half), (ff_half, ff_rows - ff_half))
    ffs = [
        ChipGather(
            lambda d, part, m=m: mats_at(wff_out, m, m + 1, d * ff_rows + ff_cuts[part][0], ff_cuts[part][1]),
            wff_ref.at[m : m + 1], where, sems,
        )
        for m in range(3)
    ]
    dyz = ZGather(lambda e: rows_at(dy_out, e * own, own), dy_ref, where, sems)
    kvz = ZGather(
        lambda e: rows_at(kv1_out, e * own, own), rows_at(kv1_out, enc * own, own), where, sems
    )
    kvz2 = ZGather(
        lambda e: rows_at(kv2_out, e * own_enc, own_enc),
        rows_at(kv2_out, enc * own_enc, own_enc), where, sems,
    )

    enter(*where)
    zs[0].start()
    own_dy = pltpu.make_async_copy(dy_ref, rows_at(dy_out, enc * own, own), local.at[0])
    own_ff = pltpu.make_async_copy(wff_ref, mats_at(wff_out, 0, 3, dp * ff_rows, ff_rows), local.at[1])
    own_dy.start()
    own_ff.start()
    for g in (0, 1):
        packed[g, enc] = watt_ref[g]
    x = x_ref[...].astype(F32)
    n1 = rms_rows(x, gains[0:1, :]).astype(LOW)
    regroup = regroup_matrix(4, width, 4 * width)

    def unpack(g):
        rows = mm(regroup, packed[g].reshape(4 * line, wide)).astype(LOW)
        for m in range(4):
            w[4 * g + m, pl.ds(pl.multiple_of(dp * line, PAD), line), :] = rows[m * line : (m + 1) * line]

    for hop in (1, 2, 3):
        zs[0].hop(hop)
    unpack(0)
    chips[0].step1()
    chips[1].step1()
    zs[1].start()
    dyz.start()
    zs[1].hop(1)
    chips[0].step2()
    zs[1].hop(2)
    chips[1].step2()
    zs[1].hop(3)
    unpack(1)
    chips[2].step1()
    chips[0].step3()
    chips[0].done()
    own_enc_rows = pl.ds(pl.multiple_of(enc * own_enc, PAD), own_enc)
    kv2_out[own_enc_rows, 0:inner] = mm(e_ref[...], w[0], NT).astype(LOW)
    kv2_out[own_enc_rows, inner : 2 * inner] = mm(e_ref[...], w[1], NT).astype(LOW)
    kvz2.start()
    chips[3].step1()
    chips[1].step3()
    chips[1].done()
    own_rows = pl.ds(pl.multiple_of(enc * own, PAD), own)
    kv1_out[own_rows, 0:inner] = mm(n1, w[2], NT).astype(LOW)
    kv1_out[own_rows, inner : 2 * inner] = mm(n1, w[3], NT).astype(LOW)
    kvz.start()
    dyz.hop(1)
    chips[2].step2()
    ffs[0].step1()
    kvz2.hop(1)
    chips[3].step2()
    ffs[1].step1()
    kvz.hop(1)
    chips[2].step3()
    ffs[0].step2()
    ffs[2].step1()
    kvz2.hop(2)
    kvz.hop(2)
    dyz.hop(2)
    chips[3].step3()
    chips[2].done()
    q1 = mm(n1, w[4], NT).astype(LOW)
    q1_out[...] = q1
    ffs[1].step2()
    kvz.hop(3)

    row_place = enc * own + lax.broadcasted_iota(jnp.int32, (own, 1), 0)
    col_place = lax.broadcasted_iota(jnp.int32, (1, group), 1)
    own_items = item_of(tgt_len, row_place)
    allowed = (own_items == item_of(tgt_len, col_place)) & (col_place <= row_place)
    for pair in range(HEADS // 2):
        lanes = slice(pair * 2 * HEAD, (pair + 1) * 2 * HEAD)
        far = slice(inner + pair * 2 * HEAD, inner + (pair + 1) * 2 * HEAD)

        def keep(half, probs, pair=pair):
            pr1_out[2 * pair + half] = probs

        num, total = attention_pair(
            q1[:, lanes], kv1_out[:, lanes], kv1_out[:, far], allowed,
            [self_bias(rel_u[2 * pair + half : 2 * pair + half + 1, :], own, group) for half in (0, 1)],
            keep,
        )
        num1_out[:, lanes] = num
        tot1_out[:, lanes] = total
    ffs[0].step3()
    chips[3].done()
    saves = [
        pltpu.make_async_copy(w, watt_out, local.at[2]),
    ]
    for c in saves:
        c.start()
    o1 = (num1_out[...] / tot1_out[...]).astype(LOW)
    x1 = x + mm(o1, w[5])
    x1_out[...] = x1
    n2 = rms_rows(x1, gains[1:2, :]).astype(LOW)
    q2 = mm(n2, w[6], NT).astype(LOW)
    q2_out[...] = q2
    ffs[2].step2()
    ffs[1].step3()
    kvz2.hop(3)
    enc_place = lax.broadcasted_iota(jnp.int32, (1, 4 * own_enc), 1)
    allowed2 = own_items == item_of(enc_len, enc_place)
    for pair in range(HEADS // 2):
        lanes = slice(pair * 2 * HEAD, (pair + 1) * 2 * HEAD)
        far = slice(inner + pair * 2 * HEAD, inner + (pair + 1) * 2 * HEAD)

        def keep2(half, probs, pair=pair):
            pr2_out[2 * pair + half] = probs

        num, total = attention_pair(
            q2[:, lanes], kv2_out[:, lanes], kv2_out[:, far], allowed2, None, keep2
        )
        num2_out[:, lanes] = num
        tot2_out[:, lanes] = total
    ffs[2].step3()
    o2 = (num2_out[...] / tot2_out[...]).astype(LOW)
    x2 = x1 + mm(o2, w[7])
    x2_out[...] = x2
    n3_out[...] = rms_rows(x2, gains[2:3, :]).astype(LOW)
    dyz.hop(3)
    for part in ffs:
        part.done()
    for part in zs + chips + ffs + [dyz, kvz, kvz2]:
        part.finish()
    own_dy.wait()
    own_ff.wait()
    for c in saves:
        c.wait()


def sds(shape, dtype):
    return jax.ShapeDtypeStruct(shape, dtype)


def call_forward(width, tgt_len, enc_len, x, e, dy, watt, wff, gains, rel_u):
    own, wide = x.shape
    own_enc = e.shape[0]
    inner = HEADS * HEAD
    SM = pl.BlockSpec(memory_space=pltpu.SMEM)
    return pl.pallas_call(
        functools.partial(forward_kernel, width),
        out_shape=(
            sds((8, inner, wide), LOW),
            sds((3, 8 * wff.shape[1], wide), LOW),
            sds((4 * own, wide), LOW),
            sds((own, wide), F32),
            sds((own, wide), F32),
            sds((own, wide), LOW),
            sds((own, inner), LOW),
            sds((4 * own, 2 * inner), LOW),
            sds((own, inner), LOW),
            sds((4 * own_enc, 2 * inner), LOW),
            sds((HEADS, own, 4 * own), LOW),
            sds((HEADS, own, 4 * own_enc), LOW),
            sds((own, inner), F32),
            sds((own, inner), F32),
            sds((own, inner), F32),
            sds((own, inner), F32),
        ),
        in_specs=[SM, SM] + [VM] * 7,
        out_specs=(ANY, ANY, ANY) + (VM,) * 13,
        scratch_shapes=[
            pltpu.VMEM((8, inner, wide), LOW),
            pltpu.VMEM((2, 4, 4 * width, wide), LOW),
            pltpu.SemaphoreType.DMA((96,)),
            pltpu.SemaphoreType.DMA((96,)),
            pltpu.SemaphoreType.DMA((3,)),
        ],
        compiler_params=pltpu.CompilerParams(
            collective_id=1, has_side_effects=True, vmem_limit_bytes=56 * 2**20
        ),
        name="attention_forward",
    )(tgt_len, enc_len, x, e, dy, watt, wff, gains, rel_u)


def pack_weights(self_q, self_k, self_v, self_o, cross_q, cross_k, cross_v, cross_o, ff_gate, ff_up, ff_out):
    rows = jnp.stack(
        [w.T for w in (cross_k, cross_v, self_k, self_v, self_q)] + [self_o, cross_q.T, cross_o]
    ).astype(LOW)
    wff = jnp.stack([ff_gate.T, ff_up.T, ff_out]).astype(LOW)
    return rows.reshape(2, 4 * rows.shape[1], rows.shape[2]), wff


def bias_rows(rel_bucket, rel_table, enc, own, group):
    starts = jnp.sum(
        (rel_bucket[None, :] < jnp.arange(BUCKETS, dtype=jnp.int32)[:, None]).astype(jnp.int32), axis=1
    )
    k = jnp.arange(group + own, dtype=jnp.int32)
    distance = enc * own - jnp.where(k < group, k, k - group - own)
    ends = jnp.concatenate([starts[1:], jnp.full((1,), group, jnp.int32)])
    inside = (distance[None, :] >= starts[:, None]) & (distance[None, :] < ends[:, None])
    return inside, jnp.sum(jnp.where(inside[:, None, :], rel_table[:, :, None], 0.0), axis=0)


class ZScatter:
    def __init__(self, src_at, dst_at, where, sems, meet=None):
        self.src_at, self.dst_at, self.sems, self.meet = src_at, dst_at, sems, meet
        self.dp, self.enc = where[0], where[1]
        self.base = sems.take(3 if meet is None else 4)
        self.middle = (self.enc == 1) | (self.enc == 2)

    def _copy(self, place, merged=False):
        k = lax.rem(place - self.enc + 4, 4)
        s = self.sems
        return remote(
            self.meet if merged else self.src_at(place), self.dst_at(3 - k),
            s.send.at[self.base + k - 1], s.recv.at[self.base + 3 - k], (self.dp, place),
        )

    def _to_meet(self):
        s = self.sems
        far = 3 - self.enc
        return remote(
            self.src_at(far), self.meet, s.send.at[self.base + 3], s.recv.at[self.base + 3],
            (self.dp, 1 + lax.div(self.enc, 2)),
        )

    def start(self, place):
        self._copy(place).start()

    def start_all(self):
        enc = self.enc
        if self.meet is None:
            for k in (2, 1, 3):
                self.start(lax.rem(enc + k, 4))
            return

        @pl.when(jnp.logical_not(self.middle))
        def _():
            self._to_meet().start()
            self.start(lax.rem(enc + 2, 4))
            self.start(1 + lax.div(enc, 2))

        @pl.when(self.middle)
        def _():
            self.start(enc - 1)
            self.start(enc + 1)

    def merge(self):
        @pl.when(self.middle)
        def _():
            far = lax.rem(self.enc + 2, 4)
            self._to_meet().wait_recv()
            self.meet[...] = (self.meet[...].astype(F32) + self.src_at(far)[...].astype(F32)).astype(LOW)
            self._copy(far, merged=True).start()

    def _each(self, act):
        enc = self.enc
        if self.meet is None:
            for k in (1, 2, 3):
                act(lax.rem(enc + k, 4))
            return
        act(lax.rem(enc + 2, 4))

        @pl.when(enc > 0)
        def _():
            act(enc - 1)

        @pl.when(enc < 3)
        def _():
            act(enc + 1)

    def wait(self):
        def one(place):
            k = lax.rem(self.enc - place + 4, 4)
            s = self.sems
            remote(
                self.dst_at(3 - k), self.dst_at(3 - k), s.send.at[self.base], s.recv.at[self.base + 3 - k],
                (self.dp, self.enc),
            ).wait_recv()

        self._each(one)

    def clear(self):
        if self.meet is not None:

            @pl.when(self.enc == 0)
            def _():
                ref = self.dst_at(2)
                ref[...] = jnp.zeros(ref.shape, ref.dtype)

            @pl.when(self.enc == 3)
            def _():
                ref = self.dst_at(0)
                ref[...] = jnp.zeros(ref.shape, ref.dtype)

    def finish(self):
        self._each(lambda place: self._copy(place).wait_send())
        if self.meet is not None:

            @pl.when(jnp.logical_not(self.middle))
            def _():
                self._to_meet().wait_send()


def rms_back(values, gain, grad):
    inv = lax.rsqrt(jnp.mean(values * values, axis=-1, keepdims=True) + EPSILON)
    scaled = grad * gain
    mean = jnp.mean(values * scaled, axis=-1, keepdims=True)
    gain_grad = jnp.sum(grad * values * inv, axis=0, keepdims=True)
    return inv * scaled - values * (inv * inv * inv * mean), gain_grad


GELU_A = 0.7978845608028654
GELU_B = 0.044715


def ff_kernel(
    n3_ref, x2_ref, dy_ref, dyall_ref, wff_ref, gains,
    dx2_out, part_out, sums_out, gain_out,
    w, n3, dy, back, act, dgate, dup, part, got, grads, core_got, own_sum, send, recv, local,
):
    where = places()
    dp, enc, sib, xn, yn = where
    core = lax.rem(dp, 2)
    sems = Sems(send, recv)
    own = n3_ref.shape[0]
    ff_rows = grads.shape[3]

    def rows_of(place):
        return pl.ds(pl.multiple_of(place * own, PAD), own)

    gather = ZGather(lambda e: n3.at[rows_of(e), :], n3_ref, where, sems)
    scatter = ZScatter(lambda e: part.at[e], lambda slot: got.at[slot], where, sems)
    loads = [
        pltpu.make_async_copy(wff_ref, w, local.at[0]),
        pltpu.make_async_copy(dyall_ref, dy, local.at[1]),
    ]
    for c in loads:
        c.start()
    enter(*where)
    gather.start()
    n3[rows_of(enc), :] = n3_ref[...]
    for c in loads:
        c.wait()

    back[...] = mm(dy[...], w[2], NT)

    def block(place):
        rows = rows_of(place)
        normed = n3[rows, :]
        gate = mm(normed, w[0], NT)
        up = mm(normed, w[1], NT)
        dh = back[rows, :]
        square = gate * gate
        t = jnp.tanh(GELU_A * gate * (1.0 + GELU_B * square))
        half = 0.5 * (1.0 + t)
        g = gate * half
        slope = half + 0.5 * gate * (1.0 - t * t) * (GELU_A * (1.0 + 3.0 * GELU_B * square))
        hidden = (g * up).astype(LOW)
        dg = (dh * up * slope).astype(LOW)
        du = (dh * g).astype(LOW)
        act[rows, :] = hidden
        dgate[rows, :] = dg
        dup[rows, :] = du
        return mm(dg, w[0]) + mm(du, w[1])

    own_sum[...] = block(enc)
    near = 1 + lax.rem(enc, 2)
    last = jnp.where(enc < 2, 3, 0)
    for hop, place in ((1, near), (2, 6 - enc - near - last), (3, last)):
        gather.hop(hop)
        part[place] = block(place).astype(LOW)
        scatter.start(place)

    part_out[...] = mm(act[...], w[2]).astype(LOW)
    swaps = []
    base = sems.take(3)
    for m, (left, right) in ((2, (act, dy)), (0, (dgate, n3)), (1, (dup, n3))):
        whole = mm(left[...], right[...], TN).astype(LOW)
        for j in range(4):
            for c in range(2):
                first_row = (2 * j + c) * ff_rows
                grads[m, j, c] = whole[first_row : first_row + ff_rows]
        swap = remote(
            grads.at[m, :, 1 - core], core_got.at[m], send.at[base + m], recv.at[base + m], (sib, enc)
        )
        swap.start()
        swaps.append((m, swap))
    for m, swap in swaps:
        swap.wait_recv()
        for j in range(4):
            sums_out[m, j] = (grads[m, j, core].astype(F32) + core_got[m, j].astype(F32)).astype(LOW)
    scatter.wait()
    dn3 = own_sum[...] + got[0].astype(F32) + got[1].astype(F32) + got[2].astype(F32)
    dv, gain_grad = rms_back(x2_ref[...], gains[2:3, :], dn3)
    dx2_out[...] = dy_ref[...].astype(F32) + dv
    gain_out[...] = gain_grad
    gather.finish()
    scatter.finish()
    for m, swap in swaps:
        swap.wait_send()


def call_ff(n3, x2, dy, dy_all, wff, gains):
    own, wide = n3.shape
    ff_all = wff.shape[1]
    ff_rows = ff_all // 8
    group = 4 * own
    return pl.pallas_call(
        ff_kernel,
        out_shape=(
            sds((own, wide), F32),
            sds((group, wide), LOW),
            sds((3, 4, ff_rows, wide), LOW),
            sds((1, wide), F32),
        ),
        in_specs=[VM, VM, VM, ANY, ANY, VM],
        out_specs=(VM,) * 4,
        scratch_shapes=[
            pltpu.VMEM((3, ff_all, wide), LOW),
            pltpu.VMEM((group, wide), LOW),
            pltpu.VMEM((group, wide), LOW),
            pltpu.VMEM((group, ff_all), F32),
            pltpu.VMEM((group, ff_all), LOW),
            pltpu.VMEM((group, ff_all), LOW),
            pltpu.VMEM((group, ff_all), LOW),
            pltpu.VMEM((4, own, wide), LOW),
            pltpu.VMEM((3, own, wide), LOW),
            pltpu.VMEM((3, 4, 2, ff_rows, wide), LOW),
            pltpu.VMEM((3, 4, ff_rows, wide), LOW),
            pltpu.VMEM((own, wide), F32),
            pltpu.SemaphoreType.DMA((12,)),
            pltpu.SemaphoreType.DMA((12,)),
            pltpu.SemaphoreType.DMA((2,)),
        ],
        compiler_params=pltpu.CompilerParams(
            collective_id=2, has_side_effects=True, vmem_limit_bytes=60 * 2**20
        ),
        name="feed_forward",
    )(n3, x2, dy, dy_all, wff, gains)


class ChipReduce:
    def __init__(self, src, got, last, cuts, own, where, sems):
        self.src, self.got, self.last, self.cuts, self.own = src, got, last, cuts, own
        self.sems, self.where = sems, where
        self.x = lax.rem(lax.div(where[0], 2), 2)
        self.y = lax.div(where[0], 4)
        self.base = sems.take(2 * len(cuts))

    def _copy(self, i, second):
        dp, enc, sib, xn, yn = self.where
        m, lo, hi, by_x = self.cuts[i]
        s, at = self.sems, self.base + 2 * i + (1 if second else 0)
        if second:
            src = self.got.at[m, 1 - self.y if by_x else 1 - self.x, lo:hi]
            dst = self.last.at[m, lo:hi]
        else:
            src = self.src.at[m, :, 1 - self.x, lo:hi] if by_x else self.src.at[m, 1 - self.y, :, lo:hi]
            dst = self.got.at[m, :, lo:hi]
        target = xn if by_x != second else yn
        return remote(src, dst, s.send.at[at], s.recv.at[at], (target, enc))

    def start(self):
        for i in range(len(self.cuts)):
            self._copy(i, False).start()

    def turn(self):
        for i, (m, lo, hi, by_x) in enumerate(self.cuts):
            self._copy(i, False).wait_recv()
            for k in range(2):
                self.got[m, k, lo:hi] = (
                    self.own(m, k, lo, hi, by_x).astype(F32) + self.got[m, k, lo:hi].astype(F32)
                ).astype(LOW)
            self._copy(i, True).start()

    def totals(self):
        out = []
        for i, (m, lo, hi, by_x) in enumerate(self.cuts):
            self._copy(i, True).wait_recv()
            mine = self.got[m, self.y if by_x else self.x, lo:hi]
            out.append(mine.astype(F32) + self.last[m, lo:hi].astype(F32))
        return out

    def finish(self):
        for i in range(len(self.cuts)):
            self._copy(i, False).wait_send()
            self._copy(i, True).wait_send()


class CoreReduce:
    def __init__(self, lo, grads, core_got, chip_got, chip_last, where, sems):
        self.lo, self.grads, self.core_got, self.where, self.sems = lo, grads, core_got, where, sems
        self.base = sems.take(1)
        rows = grads.shape[4]
        x = lax.rem(lax.div(where[0], 2), 2)
        y = lax.div(where[0], 4)

        def own(m, k, first, last, by_x):
            return core_got[m, k, x] if by_x else core_got[m, y, k]

        self.chips = ChipReduce(
            core_got, chip_got, chip_last, ((lo, 0, rows, True), (lo + 1, 0, rows, False)), own, where, sems
        )

    def _core(self):
        dp, enc, sib, xn, yn = self.where
        s, lo = self.sems, self.lo
        return remote(
            self.grads.at[lo : lo + 2, :, :, 1 - lax.rem(dp, 2)], self.core_got.at[lo : lo + 2],
            s.send.at[self.base], s.recv.at[self.base], (sib, enc),
        )

    def start(self):
        self._core().start()

    def next(self):
        core = lax.rem(self.where[0], 2)
        self._core().wait_recv()
        for m in (self.lo, self.lo + 1):
            self.core_got[m] = (self.grads[m, :, :, core].astype(F32) + self.core_got[m].astype(F32)).astype(LOW)
        self.chips.start()

    def finish(self):
        self._core().wait_send()
        self.chips.finish()


class LineReduce:
    def __init__(self, parts, width, line, got, meet, out, where, sems):
        self.parts, self.line, self.got, self.out, self.where = parts, line, got, out, where
        self.rows = line.shape[1]
        self.regroup = regroup_matrix(2 * len(parts), width, self.rows)
        self.z = ZScatter(lambda e: line.at[e], lambda slot: got.at[slot], where, sems, meet)

    def start(self):
        totals = [t.astype(LOW) for part in self.parts for t in part.chips.totals()]
        rows = mm(self.regroup, jnp.concatenate(totals, axis=0)).astype(LOW)
        for e in range(4):
            self.line[e] = rows[e * self.rows : (e + 1) * self.rows]
        self.z.start_all()

    def merge(self):
        self.z.merge()

    def done(self):
        self.z.wait()
        total = self.line[self.where[1]].astype(F32)
        for slot in range(3):
            total = total + self.got[slot].astype(F32)
        self.out[...] = total


def backward_pair(q_pair, k_pair, v_pair, probs_ref, pair, dnum, dtotals):
    rows = q_pair.shape[0]
    parts, scores = [], []
    for half in (0, 1):
        dw = mm(one_head(dnum, half), v_pair, NT)
        ds = (probs_ref[2 * pair + half].astype(F32) * (dw + dtotals[half])).astype(LOW)
        scores.append(ds)
        parts.append(mm(ds, k_pair))
    dq = jnp.where(low_lanes(rows), parts[0], parts[1])
    dk = mm(jnp.concatenate(scores, axis=0), jnp.concatenate([one_head(q_pair, h) for h in (0, 1)], axis=0), TN)
    probs = jnp.concatenate([probs_ref[2 * pair + h] for h in (0, 1)], axis=0)
    dv = mm(probs, jnp.concatenate([one_head(dnum, h) for h in (0, 1)], axis=0), TN)
    return dq, dk, dv, scores


def total_grads(product, total):
    low = low_lanes(product.shape[0])
    out = []
    for half in (0, 1):
        keep = low if half == 0 else jnp.logical_not(low)
        top = jnp.sum(jnp.where(keep, product, 0.0), axis=1, keepdims=True)
        tot = total[:, half * HEAD : half * HEAD + 1]
        out.append(-top / (tot * tot))
    return out


def backward_kernel(
    width,
    x_ref, e_ref, x1_ref, x2_ref, dx2_ref, gains, gain3_grad, inside,
    q1, kv1, q2, kv2, pr1, pr2, num1, num2, tot1, tot2, part_ref, watt_ref, sums_ref,
    hidden_out, hidden_grad, encoder_grad, four_out, two_out, ff_out, small_out,
    w, grads, core_got, chip_got, chip_last, line4, line4_got, line4_meet, line2, line2_got, line2_meet,
    ff_own, ff_got, ff_last, part_got, part_meet,
    kvp1, kvp1_got, kvp1_meet, kvp2, kvp2_got, kvp2_meet, dq, vec, vec_got, send, recv, local,
):
    where = places()
    dp, enc, sib, xn, yn = where
    sems = Sems(send, recv)
    own, wide = x_ref.shape
    own_enc = e_ref.shape[0]
    inner = HEADS * HEAD
    chip_x = lax.rem(lax.div(dp, 2), 2)
    chip_y = lax.div(dp, 4)
    ff_rows = ff_last.shape[1]
    ff_half = (ff_rows // 2 + PAD - 1) // PAD * PAD
    part_rows = own // 4

    out_z = [
        ZScatter(
            lambda e, a=a, b=b: part_ref.at[e, a:b], lambda slot, a=a, b=b: part_got.at[slot, a:b],
            where, sems, part_meet.at[a:b],
        )
        for a, b in ((0, part_rows), (part_rows, own))
    ]
    kv1_z = ZScatter(lambda e: kvp1.at[e], lambda slot: kvp1_got.at[slot], where, sems, kvp1_meet)
    kv2_z = ZScatter(lambda e: kvp2.at[e], lambda slot: kvp2_got.at[slot], where, sems, kvp2_meet)
    batches = [CoreReduce(lo, grads, core_got, chip_got, chip_last, where, sems) for lo in (0, 2, 4, 6)]
    lines = [LineReduce(batches[:2], width, line4, line4_got, line4_meet, four_out, where, sems)]
    lines += [
        LineReduce(
            batches[2 + i : 3 + i], width, line2.at[i], line2_got.at[i], line2_meet.at[i], two_out.at[i], where, sems
        )
        for i in (0, 1)
    ]
    ff_cuts = ((0, 0, ff_rows, True), (1, 0, ff_rows, False), (2, 0, ff_half, True), (2, ff_half, ff_rows, False))
    ff = ChipReduce(
        sums_ref, ff_got, ff_last, ff_cuts, lambda m, k, lo, hi, by_x: ff_own[m, k, lo:hi], where, sems
    )
    vec_base = sems.take(3)
    vec_z = ZScatter(lambda e: vec.at[3], lambda slot: vec_got.at[3 + slot], where, sems)

    def vec_copy(i):
        target = (sib, xn, yn)[i]
        return remote(
            vec.at[i], vec_got.at[i], send.at[vec_base + i], recv.at[vec_base + i], (target, enc)
        )

    def load(slot, m, i):
        return pltpu.make_async_copy(watt_ref.at[m], w.at[slot], local.at[i])

    first_loads = [load(slot, m, slot) for slot, m in enumerate((7, 6, 5, 2, 3))]
    for c in first_loads:
        c.start()
    own_ff = [
        pltpu.make_async_copy(
            sums_ref.at[m, :, chip_x, lo:hi] if by_x else sums_ref.at[m, chip_y, :, lo:hi],
            ff_own.at[m, :, lo:hi], local.at[8 + i],
        )
        for i, (m, lo, hi, by_x) in enumerate(ff_cuts)
    ]
    for c in own_ff:
        c.start()
    enter(*where)
    out_z[0].start_all()
    ff.start()
    for part in out_z + [kv1_z, kv2_z] + [line.z for line in lines]:
        part.clear()

    def put_grad(m, left, right):
        whole = mm(left, right, TN).astype(LOW)
        rows = 4 * width
        for y in range(2):
            for x in range(2):
                for c in range(2):
                    at = (4 * y + 2 * x + c) * rows
                    grads[m, y, x, c] = whole[at : at + rows]

    b2 = dx2_ref[...].astype(LOW)
    first_loads[0].wait()
    do2 = mm(b2, w[0], NT)
    dnum2 = (do2 / tot2[...]).astype(LOW)
    prod2 = do2 * num2[...]
    for pair in range(HEADS // 2):
        lanes = slice(pair * 2 * HEAD, (pair + 1) * 2 * HEAD)
        far = slice(inner + pair * 2 * HEAD, inner + (pair + 1) * 2 * HEAD)
        dtot = total_grads(prod2[:, lanes], tot2[:, lanes])
        dq_pair, dk, dv, _ = backward_pair(
            q2[:, lanes], kv2[:, lanes], kv2[:, far], pr2, pair, dnum2[:, lanes], dtot
        )
        dq[:, lanes] = dq_pair.astype(LOW)
        for e in range(4):
            kvp2[e, :, lanes] = dk[e * own_enc : (e + 1) * own_enc].astype(LOW)
            kvp2[e, :, far] = dv[e * own_enc : (e + 1) * own_enc].astype(LOW)
    kv2_z.start_all()
    dq2 = dq[...]
    put_grad(0, (num2[...] / tot2[...]).astype(LOW), b2)
    x1 = x1_ref[...]
    put_grad(1, dq2, rms_rows(x1, gains[1:2, :]).astype(LOW))
    batches[0].start()
    out_z[0].merge()
    first_loads[1].wait()
    dv2, gain2_grad = rms_back(x1, gains[1:2, :], mm(dq2, w[1]))
    dx1 = dx2_ref[...] + dv2
    b1 = dx1.astype(LOW)
    first_loads[2].wait()
    do1 = mm(b1, w[2], NT)
    late = [load(2, 4, 5), load(0, 0, 6), load(1, 1, 7)]
    for c in late:
        c.start()
    dnum1 = (do1 / tot1[...]).astype(LOW)
    prod1 = do1 * num1[...]
    batches[0].next()
    all_scores = []
    for pair in range(HEADS // 2):
        lanes = slice(pair * 2 * HEAD, (pair + 1) * 2 * HEAD)
        far = slice(inner + pair * 2 * HEAD, inner + (pair + 1) * 2 * HEAD)
        dtot = total_grads(prod1[:, lanes], tot1[:, lanes])
        dq_pair, dk, dv, scores = backward_pair(
            q1[:, lanes], kv1[:, lanes], kv1[:, far], pr1, pair, dnum1[:, lanes], dtot
        )
        dq[:, lanes] = dq_pair.astype(LOW)
        for e in range(4):
            kvp1[e, :, lanes] = dk[e * own : (e + 1) * own].astype(LOW)
            kvp1[e, :, far] = dv[e * own : (e + 1) * own].astype(LOW)
        all_scores += scores
    kv1_z.start_all()
    out_z[1].start_all()
    dq1 = dq[...]
    x = x_ref[...].astype(F32)
    n1 = rms_rows(x, gains[0:1, :]).astype(LOW)
    put_grad(2, (num1[...] / tot1[...]).astype(LOW), b1)
    put_grad(3, dq1, n1)
    batches[1].start()
    kv2_z.merge()
    batches[1].next()
    for c in own_ff:
        c.wait()
    ff.turn()
    vec[0] = jnp.zeros(vec.shape[1:], F32)
    flip_row = lax.broadcasted_iota(jnp.int32, (own, own), 0)
    flip_col = lax.broadcasted_iota(jnp.int32, (own, own), 1)
    flip = jnp.where(flip_row + flip_col == own - 1, 1.0, 0.0).astype(LOW)
    for h, ds in enumerate(all_scores):
        long = jnp.concatenate([mm(flip, ds), jnp.zeros((own, own), F32)], axis=1)
        turned = pltpu.roll(long, 0, 1, stride=1, stride_axis=0)
        by_distance = jnp.sum(turned, axis=0, keepdims=True)
        vec[0, 8 + h : 9 + h, 0:BUCKETS] = lax.dot_general(
            by_distance, inside[...], NT, precision=lax.Precision.HIGHEST, preferred_element_type=F32
        )
    batches[0].chips.turn()
    for c in late:
        c.wait()
    dn1 = mm(dq1, w[2])
    batches[1].chips.turn()

    kv2_z.wait()
    low2 = (
        kvp2[enc].astype(F32) + kvp2_got[0].astype(F32) + kvp2_got[1].astype(F32) + kvp2_got[2].astype(F32)
    ).astype(LOW)
    dk2 = low2[:, :inner]
    dv2 = low2[:, inner:]
    put_grad(4, dk2, e_ref[...])
    put_grad(5, dv2, e_ref[...])
    batches[2].start()
    kv1_z.merge()
    lines[0].start()
    batches[2].next()
    encoder_grad[...] = mm(dk2, w[0]) + mm(dv2, w[1])

    kv1_z.wait()
    low1 = (
        kvp1[enc].astype(F32) + kvp1_got[0].astype(F32) + kvp1_got[1].astype(F32) + kvp1_got[2].astype(F32)
    ).astype(LOW)
    dk1 = low1[:, :inner]
    dv1 = low1[:, inner:]
    put_grad(6, dk1, n1)
    put_grad(7, dv1, n1)
    batches[3].start()
    batches[2].chips.turn()
    first_loads[3].wait()
    first_loads[4].wait()
    dn1 = dn1 + mm(dk1, w[3]) + mm(dv1, w[4])
    dv_x, gain1_grad = rms_back(x, gains[0:1, :], dn1)
    hidden_grad[...] = dx1 + dv_x
    out_z[1].merge()
    vec[0, 0:1, :] = gain1_grad
    vec[0, 1:2, :] = gain2_grad
    vec[0, 2:3, :] = gain3_grad[...]
    vec_copy(0).start()
    batches[3].next()
    lines[0].merge()
    vec_copy(0).wait_recv()
    vec[1] = vec[0] + vec_got[0]
    vec_copy(1).start()
    lines[1].start()
    batches[3].chips.turn()
    vec_copy(1).wait_recv()
    vec[2] = vec[1] + vec_got[1]
    vec_copy(2).start()
    vec_copy(2).wait_recv()
    vec[3] = vec[2] + vec_got[2]
    vec_z.start_all()
    lines[2].start()
    lines[1].merge()
    for (m, lo, hi, by_x), total in zip(ff_cuts, ff.totals()):
        ff_out[m, lo:hi] = total
    lines[2].merge()
    lines[0].done()
    for z, rows in zip(out_z, (slice(0, part_rows), slice(part_rows, own))):
        z.wait()
        hidden_out[rows] = (
            x2_ref[rows] + (part_ref[enc, rows].astype(F32) + part_got[0, rows].astype(F32))
            + (part_got[1, rows].astype(F32) + part_got[2, rows].astype(F32))
        ).astype(LOW)
    lines[1].done()
    lines[2].done()
    vec_z.wait()
    small_out[...] = vec[3] + vec_got[3] + vec_got[4] + vec_got[5]
    for done in out_z + [kv1_z, kv2_z, vec_z, ff] + batches + [line.z for line in lines]:
        done.finish()
    for i in range(3):
        vec_copy(i).wait_send()


def call_backward(width, x, e, x1, x2, dx2, gains, gain3_grad, inside, saved, watt, part, sums):
    own, wide = x.shape
    own_enc = e.shape[0]
    inner = HEADS * HEAD
    rows = 4 * width
    block = (2 * width + PAD - 1) // PAD * PAD
    ff_rows = sums.shape[2]
    return pl.pallas_call(
        functools.partial(backward_kernel, width),
        out_shape=(
            sds((own, wide), LOW),
            sds((own, wide), F32),
            sds((own_enc, wide), F32),
            sds((4 * width, wide), F32),
            sds((2, block, wide), F32),
            sds((3, ff_rows, wide), F32),
            sds((16, wide), F32),
        ),
        in_specs=[VM] * 19 + [ANY] * 2,
        out_specs=(VM,) * 7,
        scratch_shapes=[
            pltpu.VMEM((5, inner, wide), LOW),
            pltpu.VMEM((8, 2, 2, 2, rows, wide), LOW),
            pltpu.VMEM((8, 2, 2, rows, wide), LOW),
            pltpu.VMEM((8, 2, rows, wide), LOW),
            pltpu.VMEM((8, rows, wide), LOW),
            pltpu.VMEM((4, 4 * width, wide), LOW),
            pltpu.VMEM((3, 4 * width, wide), LOW),
            pltpu.VMEM((4 * width, wide), LOW),
            pltpu.VMEM((2, 4, block, wide), LOW),
            pltpu.VMEM((2, 3, block, wide), LOW),
            pltpu.VMEM((2, block, wide), LOW),
            pltpu.VMEM((3, 2, ff_rows, wide), LOW),
            pltpu.VMEM((3, 2, ff_rows, wide), LOW),
            pltpu.VMEM((3, ff_rows, wide), LOW),
            pltpu.VMEM((3, own, wide), LOW),
            pltpu.VMEM((own, wide), LOW),
            pltpu.VMEM((4, own, 2 * inner), LOW),
            pltpu.VMEM((3, own, 2 * inner), LOW),
            pltpu.VMEM((own, 2 * inner), LOW),
            pltpu.VMEM((4, own_enc, 2 * inner), LOW),
            pltpu.VMEM((3, own_enc, 2 * inner), LOW),
            pltpu.VMEM((own_enc, 2 * inner), LOW),
            pltpu.VMEM((own, inner), LOW),
            pltpu.VMEM((4, 16, wide), F32),
            pltpu.VMEM((6, 16, wide), F32),
            pltpu.SemaphoreType.DMA((64,)),
            pltpu.SemaphoreType.DMA((64,)),
            pltpu.SemaphoreType.DMA((12,)),
        ],
        compiler_params=pltpu.CompilerParams(
            collective_id=3, has_side_effects=True, vmem_limit_bytes=62 * 2**20
        ),
        name="attention_backward",
    )(
        x, e, x1, x2, dx2, gains, gain3_grad, inside, *saved, part.reshape(4, own, wide), watt,
        sums.reshape(3, 2, 2, ff_rows, wide),
    )


def fast_body(
    hidden_in, encoder_out, grad_out, tgt_lengths, enc_lengths, rel_bucket, norm1_gain,
    self_q, self_k, self_v, self_o, rel_table, norm2_gain,
    cross_q, cross_k, cross_v, cross_o, norm3_gain, ff_gate, ff_up, ff_out,
):
    own = hidden_in.shape[0]
    width = self_q.shape[1]
    watt, wff = pack_weights(
        self_q, self_k, self_v, self_o, cross_q, cross_k, cross_v, cross_o, ff_gate, ff_up, ff_out
    )
    inside, rel_u = bias_rows(rel_bucket, rel_table, lax.axis_index("enc"), own, 4 * own)
    gains = jnp.stack([norm1_gain, norm2_gain, norm3_gain])
    fwd = call_forward(
        width, tgt_lengths, enc_lengths, hidden_in, encoder_out, grad_out, watt, wff, gains, rel_u
    )
    watt_all, wff_all, dy_all, x1, x2, n3 = fwd[:6]
    dx2, part, sums, gain3_grad = call_ff(n3, x2, grad_out, dy_all, wff_all, gains)
    saved = fwd[6:]
    hidden_out, hidden_grad, encoder_grad, four, two, ff, small = call_backward(
        width, hidden_in, encoder_out, x1, x2, dx2, gains, gain3_grad,
        jnp.roll(inside.astype(F32), own - 1, axis=1), saved, watt_all, part, sums,
    )
    o2, q2, o1, q1 = (four[m * width : (m + 1) * width] for m in range(4))
    (k2, v2), (k1, v1) = ((t[:width], t[width : 2 * width]) for t in two)
    return (
        hidden_out, hidden_grad, encoder_grad, small[0],
        q1.T, k1.T, v1.T, o1, small[8 : 8 + HEADS, :BUCKETS].T,
        small[1], q2.T, k2.T, v2.T, o2, small[2], ff[0].T, ff[1].T, ff[2],
    )


def rms_scale(values, gain):
    return values * lax.rsqrt(jnp.mean(values * values, axis=-1, keepdims=True) + EPSILON) * gain


def gated_gelu(gate_pre, up_pre):
    return jax.nn.gelu(gate_pre, approximate=True) * up_pre


def item_ids(lengths, total_rows):
    ends = jnp.cumsum(lengths)
    places = jnp.arange(total_rows, dtype=jnp.int32)
    return jnp.sum((ends[None, :] <= places[:, None]).astype(jnp.int32), axis=1)


def product(left, right):
    return jnp.dot(left, right, preferred_element_type=jnp.float32)


def product_tn(left, right):
    return lax.dot_general(
        left, right, (((0,), (0,)), ((), ())), preferred_element_type=jnp.float32
    )


def product_nt(left, right):
    return lax.dot_general(
        left, right, (((1,), (1,)), ((), ())), preferred_element_type=jnp.float32
    )


def to_pieces(grad, shard_dim, shards):
    if shard_dim == 0:
        return grad.reshape(shards, -1)
    rows = grad.shape[0]
    return jnp.transpose(grad.reshape(rows, shards, -1), (1, 0, 2)).reshape(shards, -1)


def from_pieces(received, shard_dim, shape, shards):
    summed = jnp.sum(received, axis=0)
    if shard_dim == 0:
        return summed.reshape(shape[0] // shards, shape[1])
    return summed.reshape(shape[0], shape[1] // shards)


def head_pair(matrix, pair_index):
    return lax.dynamic_slice_in_dim(matrix, pair_index * 2 * HEAD, 2 * HEAD, 1).reshape(
        matrix.shape[0], 2, HEAD
    )


def pair_stats(stats, pair_index):
    return lax.dynamic_slice_in_dim(stats, pair_index * 2, 2, 0)


def relative_bias(distance, bias_info, pair_index):
    starts, table = bias_info
    table_pair = lax.dynamic_slice_in_dim(table, pair_index * 2, 2, 1)

    def add_step(bucket, total):
        rise = table_pair[bucket] - table_pair[bucket - 1]
        return total + jnp.where(distance[None] >= starts[bucket], rise[:, None, None], 0.0)

    start_bias = jnp.broadcast_to(table_pair[0][:, None, None], (2,) + distance.shape)
    return lax.fori_loop(1, BUCKETS, add_step, start_bias)


def relative_grads(distance, starts, score_grad):

    def one_step(bucket):
        return jnp.sum(jnp.where(distance[None] >= starts[bucket], score_grad, 0.0), axis=(1, 2))

    steps_sum = lax.map(one_step, jnp.arange(BUCKETS, dtype=jnp.int32))
    return steps_sum - jnp.concatenate([steps_sum[1:], jnp.zeros((1, 2), jnp.float32)], axis=0)


def pair_scores(query_block, key_rows, pair_index, layout):
    allowed, distance, bias_info = layout
    scores = jnp.einsum(
        "qhe,khe->hqk",
        head_pair(query_block, pair_index),
        head_pair(key_rows, pair_index),
        preferred_element_type=jnp.float32,
    )
    if bias_info is not None:
        scores = scores + relative_bias(distance, bias_info, pair_index)
    return jnp.where(allowed[None], scores, MASKED)


def forward_parts(query_block, key_rows, value_rows, layout):
    block_rows = query_block.shape[0]
    width = 2 * HEAD

    def forward_one_pair(pair_index, carry):
        numerator, largest, totals = carry
        scores = pair_scores(query_block, key_rows, pair_index, layout)
        pair_top = jnp.max(scores, axis=2)
        weights = jnp.exp(scores - pair_top[:, :, None])
        partial_sum = jnp.einsum(
            "hqk,khe->qhe",
            weights.astype(jnp.bfloat16),
            head_pair(value_rows, pair_index),
            preferred_element_type=jnp.float32,
        )
        numerator = lax.dynamic_update_slice_in_dim(
            numerator, partial_sum.reshape(block_rows, width), pair_index * width, 1
        )
        largest = lax.dynamic_update_slice_in_dim(largest, pair_top, pair_index * 2, 0)
        totals = lax.dynamic_update_slice_in_dim(
            totals, jnp.sum(weights, axis=2), pair_index * 2, 0
        )
        return (numerator, largest, totals)

    start_state = (
        jnp.zeros((block_rows, HEADS * HEAD), jnp.float32),
        jnp.zeros((HEADS, block_rows), jnp.float32),
        jnp.zeros((HEADS, block_rows), jnp.float32),
    )
    return lax.fori_loop(0, HEADS // 2, forward_one_pair, start_state)


def backward_parts(query_block, key_rows, value_rows, layout, top_rows, num_grad, total_grad):
    allowed, distance, bias_info = layout
    block_rows = query_block.shape[0]
    key_count = key_rows.shape[0]
    width = 2 * HEAD

    def backward_one_pair(pair_index, carry):
        query_grad, key_grad, value_grad, bias_grad = carry
        query_pair = head_pair(query_block, pair_index)
        key_pair = head_pair(key_rows, pair_index)
        value_pair = head_pair(value_rows, pair_index)
        grad_pair = head_pair(num_grad, pair_index)
        scores = pair_scores(query_block, key_rows, pair_index, layout)
        weights = jnp.exp(scores - pair_stats(top_rows, pair_index)[:, :, None])
        weight_grad = jnp.einsum(
            "qhe,khe->hqk", grad_pair, value_pair, preferred_element_type=jnp.float32
        )
        score_grad = (
            weights * (weight_grad + pair_stats(total_grad, pair_index)[:, :, None])
        ).astype(jnp.bfloat16)
        part_query = jnp.einsum(
            "hqk,khe->qhe", score_grad, key_pair, preferred_element_type=jnp.float32
        )
        part_key = jnp.einsum(
            "hqk,qhe->khe", score_grad, query_pair, preferred_element_type=jnp.float32
        )
        part_value = jnp.einsum(
            "hqk,qhe->khe",
            weights.astype(jnp.bfloat16),
            grad_pair,
            preferred_element_type=jnp.float32,
        )
        query_grad = lax.dynamic_update_slice_in_dim(
            query_grad, part_query.reshape(block_rows, width), pair_index * width, 1
        )
        key_grad = lax.dynamic_update_slice_in_dim(
            key_grad, part_key.reshape(key_count, width), pair_index * width, 1
        )
        value_grad = lax.dynamic_update_slice_in_dim(
            value_grad, part_value.reshape(key_count, width), pair_index * width, 1
        )
        if bias_info is not None:
            pair_bias_grad = relative_grads(distance, bias_info[0], score_grad.astype(jnp.float32))
            bias_grad = lax.dynamic_update_slice_in_dim(
                bias_grad, pair_bias_grad, pair_index * 2, 1
            )
        return (query_grad, key_grad, value_grad, bias_grad)

    bias_start = None if bias_info is None else jnp.zeros((BUCKETS, HEADS), jnp.float32)
    start_state = (
        jnp.zeros((block_rows, HEADS * HEAD), jnp.float32),
        jnp.zeros((key_count, HEADS * HEAD), jnp.float32),
        jnp.zeros((key_count, HEADS * HEAD), jnp.float32),
        bias_start,
    )
    return lax.fori_loop(0, HEADS // 2, backward_one_pair, start_state)


def normalize(numerator, totals):
    row_count = numerator.shape[0]
    shaped = numerator.reshape(row_count, HEADS, HEAD) / jnp.transpose(totals)[:, :, None]
    return shaped.reshape(row_count, HEADS * HEAD).astype(jnp.bfloat16)


def output_grads(out_grad, numerator, totals):
    row_count = out_grad.shape[0]
    per_total = jnp.transpose(totals)
    shaped_grad = out_grad.reshape(row_count, HEADS, HEAD)
    num_grad = (
        (shaped_grad / per_total[:, :, None]).reshape(row_count, HEADS * HEAD).astype(jnp.bfloat16)
    )
    total_grad = -jnp.sum(shaped_grad * numerator.reshape(row_count, HEADS, HEAD), axis=2) / (
        per_total * per_total
    )
    return (num_grad, jnp.transpose(total_grad))


def body(
    hidden_in,
    encoder_out,
    grad_out,
    tgt_lengths,
    enc_lengths,
    rel_bucket,
    norm1_gain,
    self_q,
    self_k,
    self_v,
    self_o,
    rel_table,
    norm2_gain,
    cross_q,
    cross_k,
    cross_v,
    cross_o,
    norm3_gain,
    ff_gate,
    ff_up,
    ff_out,
):
    w_query, w_key, w_value, w_out, c_query, c_key, c_value, c_out, w_gate, w_up, w_down = (
        lax.all_gather(self_q.astype(jnp.bfloat16), ("dp", "enc"), axis=1, tiled=True),
        lax.all_gather(self_k.astype(jnp.bfloat16), ("dp", "enc"), axis=1, tiled=True),
        lax.all_gather(self_v.astype(jnp.bfloat16), ("dp", "enc"), axis=1, tiled=True),
        lax.all_gather(self_o.astype(jnp.bfloat16), ("dp", "enc"), axis=0, tiled=True),
        lax.all_gather(cross_q.astype(jnp.bfloat16), ("dp", "enc"), axis=1, tiled=True),
        lax.all_gather(cross_k.astype(jnp.bfloat16), ("dp", "enc"), axis=1, tiled=True),
        lax.all_gather(cross_v.astype(jnp.bfloat16), ("dp", "enc"), axis=1, tiled=True),
        lax.all_gather(cross_o.astype(jnp.bfloat16), ("dp", "enc"), axis=0, tiled=True),
        lax.all_gather(ff_gate.astype(jnp.bfloat16), ("dp", "enc"), axis=1, tiled=True),
        lax.all_gather(ff_up.astype(jnp.bfloat16), ("dp", "enc"), axis=1, tiled=True),
        lax.all_gather(ff_out.astype(jnp.bfloat16), ("dp", "enc"), axis=0, tiled=True),
    )
    enc_count = lax.axis_size("enc")
    enc_place = lax.axis_index("enc")
    own_rows = hidden_in.shape[0]
    group_rows = own_rows * enc_count
    own_enc = encoder_out.shape[0]
    group_enc = own_enc * enc_count
    tgt_items = item_ids(tgt_lengths[0], group_rows)
    enc_items = item_ids(enc_lengths[0], group_enc)
    row_start = enc_place * own_rows
    own_items = lax.dynamic_slice_in_dim(tgt_items, row_start, own_rows)
    own_enc_items = lax.dynamic_slice_in_dim(enc_items, enc_place * own_enc, own_enc)
    bucket_starts = jnp.sum(
        (rel_bucket[None, :] < jnp.arange(BUCKETS, dtype=jnp.int32)[:, None]).astype(jnp.int32),
        axis=1,
    )
    query_place = row_start + jnp.arange(own_rows, dtype=jnp.int32)
    distance = query_place[:, None] - jnp.arange(group_rows, dtype=jnp.int32)[None, :]
    self_layout = (
        (distance >= 0) & (own_items[:, None] == tgt_items[None, :]),
        distance,
        (bucket_starts, rel_table),
    )
    hidden = hidden_in.astype(jnp.float32)
    normed_full, pull_one = jax.vjp(rms_scale, hidden, norm1_gain)
    normed = normed_full.astype(jnp.bfloat16)
    queries = product(normed, w_query).astype(jnp.bfloat16)
    key_own = product(normed, w_key).astype(jnp.bfloat16)
    value_own = product(normed, w_value).astype(jnp.bfloat16)
    key_group, value_group = (
        lax.all_gather(key_own, "enc", axis=0, tiled=True),
        lax.all_gather(value_own, "enc", axis=0, tiled=True),
    )
    self_num, self_top, self_total = forward_parts(queries, key_group, value_group, self_layout)
    attended = normalize(self_num, self_total)
    after_self = hidden + product(attended, w_out)
    normed_two_full, pull_two = jax.vjp(rms_scale, after_self, norm2_gain)
    normed_two = normed_two_full.astype(jnp.bfloat16)
    cross_queries = product(normed_two, c_query).astype(jnp.bfloat16)
    cross_keys = product(encoder_out, c_key).astype(jnp.bfloat16)
    cross_values = product(encoder_out, c_value).astype(jnp.bfloat16)
    query_group = lax.all_gather(cross_queries, "enc", axis=0, tiled=True)
    block_rows = min(512, group_rows)
    block_count = group_rows // block_rows

    def block_layout(first_row):
        query_items = lax.dynamic_slice_in_dim(tgt_items, first_row, block_rows)
        return (query_items[:, None] == own_enc_items[None, :], None, None)

    def block_forward(block_index, carry):
        numerator_all, top_all, total_all = carry
        first_row = block_index * block_rows
        block_num, block_top, block_total = forward_parts(
            lax.dynamic_slice_in_dim(query_group, first_row, block_rows, 0),
            cross_keys,
            cross_values,
            block_layout(first_row),
        )
        numerator_all = lax.dynamic_update_slice_in_dim(numerator_all, block_num, first_row, 0)
        top_all = lax.dynamic_update_slice_in_dim(top_all, block_top, first_row, 1)
        total_all = lax.dynamic_update_slice_in_dim(total_all, block_total, first_row, 1)
        return (numerator_all, top_all, total_all)

    numerator_all, local_tops, total_all = lax.fori_loop(
        0,
        block_count,
        block_forward,
        (
            jnp.zeros((group_rows, HEADS * HEAD), jnp.float32),
            jnp.zeros((HEADS, group_rows), jnp.float32),
            jnp.zeros((HEADS, group_rows), jnp.float32),
        ),
    )
    group_top = lax.pmax(local_tops, "enc")
    rescale = jnp.exp(local_tops - group_top)
    numerator_all = (
        numerator_all.reshape(group_rows, HEADS, HEAD) * jnp.transpose(rescale)[:, :, None]
    ).reshape(group_rows, HEADS * HEAD)
    total_all = total_all * rescale
    cross_num, cross_total = (
        lax.psum_scatter(
            numerator_all.astype(jnp.bfloat16), "enc", scatter_dimension=0, tiled=True
        ).astype(jnp.float32),
        lax.psum_scatter(
            total_all.astype(jnp.bfloat16), "enc", scatter_dimension=1, tiled=True
        ).astype(jnp.float32),
    )
    attended_two = normalize(cross_num, cross_total)
    after_cross = after_self + product(attended_two, c_out)
    normed_three_full, pull_three = jax.vjp(rms_scale, after_cross, norm3_gain)
    normed_three = normed_three_full.astype(jnp.bfloat16)
    gate_pre = product(normed_three, w_gate)
    up_pre = product(normed_three, w_up)
    activated, pull_act = jax.vjp(gated_gelu, gate_pre, up_pre)
    hidden_act = activated.astype(jnp.bfloat16)
    hidden_out = (after_cross + product(hidden_act, w_down)).astype(jnp.bfloat16)
    out_grad = grad_out.astype(jnp.float32)
    down_grad = product_tn(hidden_act, grad_out)
    act_grad = product_nt(grad_out, w_down)
    gate_grad_full, up_grad_full = pull_act(act_grad)
    gate_grad = gate_grad_full.astype(jnp.bfloat16)
    up_grad = up_grad_full.astype(jnp.bfloat16)
    gate_w_grad = product_tn(normed_three, gate_grad)
    up_w_grad = product_tn(normed_three, up_grad)
    normed_three_grad = product_nt(gate_grad, w_gate) + product_nt(up_grad, w_up)
    cross_res_grad, gain_three_grad = pull_three(normed_three_grad)
    after_cross_grad = out_grad + cross_res_grad
    branch_two = after_cross_grad.astype(jnp.bfloat16)
    c_out_grad = product_tn(attended_two, branch_two)
    cross_out_grad = product_nt(branch_two, c_out)
    cross_num_grad, cross_total_grad = output_grads(cross_out_grad, cross_num, cross_total)
    num_grad_group = lax.all_gather(cross_num_grad, "enc", axis=0, tiled=True)
    total_grad_group = lax.all_gather(cross_total_grad, "enc", axis=1, tiled=True)

    def block_backward(block_index, carry):
        query_grad_all, key_grad_sum, value_grad_sum = carry
        first_row = block_index * block_rows
        block_query_grad, block_key_grad, block_value_grad, unused_bias = backward_parts(
            lax.dynamic_slice_in_dim(query_group, first_row, block_rows, 0),
            cross_keys,
            cross_values,
            block_layout(first_row),
            lax.dynamic_slice_in_dim(group_top, first_row, block_rows, 1),
            lax.dynamic_slice_in_dim(num_grad_group, first_row, block_rows, 0),
            lax.dynamic_slice_in_dim(total_grad_group, first_row, block_rows, 1),
        )
        query_grad_all = lax.dynamic_update_slice_in_dim(
            query_grad_all, block_query_grad, first_row, 0
        )
        return (query_grad_all, key_grad_sum + block_key_grad, value_grad_sum + block_value_grad)

    query_grad_all, cross_key_grad, cross_value_grad = lax.fori_loop(
        0,
        block_count,
        block_backward,
        (
            jnp.zeros((group_rows, HEADS * HEAD), jnp.float32),
            jnp.zeros((own_enc, HEADS * HEAD), jnp.float32),
            jnp.zeros((own_enc, HEADS * HEAD), jnp.float32),
        ),
    )
    cross_query_grad = lax.psum_scatter(
        query_grad_all.astype(jnp.bfloat16), "enc", scatter_dimension=0, tiled=True
    )
    cross_key_low = cross_key_grad.astype(jnp.bfloat16)
    cross_value_low = cross_value_grad.astype(jnp.bfloat16)
    c_query_grad = product_tn(normed_two, cross_query_grad)
    c_key_grad = product_tn(encoder_out, cross_key_low)
    c_value_grad = product_tn(encoder_out, cross_value_low)
    encoder_grad = product_nt(cross_key_low, c_key) + product_nt(cross_value_low, c_value)
    self_res_grad, gain_two_grad = pull_two(product_nt(cross_query_grad, c_query))
    after_self_grad = after_cross_grad + self_res_grad
    branch_one = after_self_grad.astype(jnp.bfloat16)
    w_out_grad = product_tn(attended, branch_one)
    self_out_grad = product_nt(branch_one, w_out)
    self_num_grad, self_total_grad = output_grads(self_out_grad, self_num, self_total)
    self_query_grad, key_grad_rows, value_grad_rows, table_grad = backward_parts(
        queries, key_group, value_group, self_layout, self_top, self_num_grad, self_total_grad
    )
    self_key_grad, self_value_grad = (
        lax.psum_scatter(
            key_grad_rows.astype(jnp.bfloat16), "enc", scatter_dimension=0, tiled=True
        ).astype(jnp.float32),
        lax.psum_scatter(
            value_grad_rows.astype(jnp.bfloat16), "enc", scatter_dimension=0, tiled=True
        ).astype(jnp.float32),
    )
    query_low = self_query_grad.astype(jnp.bfloat16)
    key_low = self_key_grad.astype(jnp.bfloat16)
    value_low = self_value_grad.astype(jnp.bfloat16)
    w_query_grad = product_tn(normed, query_low)
    w_key_grad = product_tn(normed, key_low)
    w_value_grad = product_tn(normed, value_low)
    normed_grad = (
        product_nt(query_low, w_query) + product_nt(key_low, w_key) + product_nt(value_low, w_value)
    )
    input_res_grad, gain_one_grad = pull_one(normed_grad)
    hidden_grad = after_self_grad + input_res_grad
    shards = lax.axis_size(("dp", "enc"))
    full_grads = (
        w_query_grad,
        w_key_grad,
        w_value_grad,
        w_out_grad,
        c_query_grad,
        c_key_grad,
        c_value_grad,
        c_out_grad,
        gate_w_grad,
        up_w_grad,
        down_grad,
    )
    shard_dims = (1, 1, 1, 0, 1, 1, 1, 0, 1, 1, 0)
    piece_rows = tuple(
        (to_pieces(grad, place, shards) for grad, place in zip(full_grads, shard_dims))
    )
    received = (
        lax.all_to_all(
            piece_rows[0].astype(jnp.bfloat16),
            ("dp", "enc"),
            split_axis=0,
            concat_axis=0,
            tiled=True,
        ).astype(jnp.float32),
        lax.all_to_all(
            piece_rows[1].astype(jnp.bfloat16),
            ("dp", "enc"),
            split_axis=0,
            concat_axis=0,
            tiled=True,
        ).astype(jnp.float32),
        lax.all_to_all(
            piece_rows[2].astype(jnp.bfloat16),
            ("dp", "enc"),
            split_axis=0,
            concat_axis=0,
            tiled=True,
        ).astype(jnp.float32),
        lax.all_to_all(
            piece_rows[3].astype(jnp.bfloat16),
            ("dp", "enc"),
            split_axis=0,
            concat_axis=0,
            tiled=True,
        ).astype(jnp.float32),
        lax.all_to_all(
            piece_rows[4].astype(jnp.bfloat16),
            ("dp", "enc"),
            split_axis=0,
            concat_axis=0,
            tiled=True,
        ).astype(jnp.float32),
        lax.all_to_all(
            piece_rows[5].astype(jnp.bfloat16),
            ("dp", "enc"),
            split_axis=0,
            concat_axis=0,
            tiled=True,
        ).astype(jnp.float32),
        lax.all_to_all(
            piece_rows[6].astype(jnp.bfloat16),
            ("dp", "enc"),
            split_axis=0,
            concat_axis=0,
            tiled=True,
        ).astype(jnp.float32),
        lax.all_to_all(
            piece_rows[7].astype(jnp.bfloat16),
            ("dp", "enc"),
            split_axis=0,
            concat_axis=0,
            tiled=True,
        ).astype(jnp.float32),
        lax.all_to_all(
            piece_rows[8].astype(jnp.bfloat16),
            ("dp", "enc"),
            split_axis=0,
            concat_axis=0,
            tiled=True,
        ).astype(jnp.float32),
        lax.all_to_all(
            piece_rows[9].astype(jnp.bfloat16),
            ("dp", "enc"),
            split_axis=0,
            concat_axis=0,
            tiled=True,
        ).astype(jnp.float32),
        lax.all_to_all(
            piece_rows[10].astype(jnp.bfloat16),
            ("dp", "enc"),
            split_axis=0,
            concat_axis=0,
            tiled=True,
        ).astype(jnp.float32),
    )
    weight_grads = tuple(
        (
            from_pieces(piece, place, grad.shape, shards)
            for piece, place, grad in zip(received, shard_dims, full_grads)
        )
    )
    small_sums = lax.psum(
        (gain_one_grad, gain_two_grad, gain_three_grad, table_grad), ("dp", "enc")
    )
    return (
        hidden_out,
        hidden_grad,
        encoder_grad,
        small_sums[0],
        weight_grads[0],
        weight_grads[1],
        weight_grads[2],
        weight_grads[3],
        small_sums[3],
        small_sums[1],
        weight_grads[4],
        weight_grads[5],
        weight_grads[6],
        weight_grads[7],
        small_sums[2],
        weight_grads[8],
        weight_grads[9],
        weight_grads[10],
    )


def solution(mesh):
    return jax.shard_map(
        fast_body if dict(mesh.shape) == {"dp": 8, "enc": 4} else body,
        mesh=mesh,
        in_specs=(
            P(("dp", "enc"), None),
            P(("dp", "enc"), None),
            P(("dp", "enc"), None),
            P("dp", None),
            P("dp", None),
            P(),
            P(),
            P(None, ("dp", "enc")),
            P(None, ("dp", "enc")),
            P(None, ("dp", "enc")),
            P(("dp", "enc"), None),
            P(),
            P(),
            P(None, ("dp", "enc")),
            P(None, ("dp", "enc")),
            P(None, ("dp", "enc")),
            P(("dp", "enc"), None),
            P(),
            P(None, ("dp", "enc")),
            P(None, ("dp", "enc")),
            P(("dp", "enc"), None),
        ),
        out_specs=(
            P(("dp", "enc"), None),
            P(("dp", "enc"), None),
            P(("dp", "enc"), None),
            P(),
            P(None, ("dp", "enc")),
            P(None, ("dp", "enc")),
            P(None, ("dp", "enc")),
            P(("dp", "enc"), None),
            P(),
            P(),
            P(None, ("dp", "enc")),
            P(None, ("dp", "enc")),
            P(None, ("dp", "enc")),
            P(("dp", "enc"), None),
            P(),
            P(None, ("dp", "enc")),
            P(None, ("dp", "enc")),
            P(("dp", "enc"), None),
        ),
        check_vma=False,
    )
```

```python
import functools

import jax
import jax.numpy as jnp
from jax import lax
from jax.experimental import pallas as pl
from jax.experimental.pallas import tpu as pltpu
from jax.sharding import PartitionSpec as P

HEADS = 6
HEAD = 64
BUCKETS = 32
EPSILON = 1e-06
MASKED = -1e30
PAD = 16
MESH = pl.DeviceIdType.MESH
LOW = jnp.bfloat16
F32 = jnp.float32
NN = (((1,), (0,)), ((), ()))
NT = (((1,), (1,)), ((), ()))
TN = (((0,), (0,)), ((), ()))
ANY = pl.BlockSpec(memory_space=pl.ANY)
VM = pl.BlockSpec(memory_space=pltpu.VMEM)


def mm(left, right, dims=NN):
    return lax.dot_general(left, right, dims, preferred_element_type=F32)


def places():
    dp = lax.axis_index("dp")
    enc = lax.axis_index("enc")
    core = lax.rem(dp, 2)
    x = lax.rem(lax.div(dp, 2), 2)
    y = lax.div(dp, 4)
    sib = dp + 1 - 2 * core
    xn = dp + 2 - 4 * x
    yn = dp + 4 - 8 * y
    return dp, enc, sib, xn, yn


def enter(dp, enc, sib, xn, yn):
    barrier = pltpu.get_barrier_semaphore()
    targets = [(sib, enc), (xn, enc), (yn, enc), (xn + yn - dp, enc)]
    targets += [(dp, lax.rem(enc + k, 4)) for k in (1, 2, 3)]
    for target in targets:
        pl.semaphore_signal(barrier, inc=1, device_id=target, device_id_type=MESH)
    pl.semaphore_wait(barrier, len(targets))


class Sems:
    def __init__(self, send, recv):
        self.send, self.recv, self.used = send, recv, 0

    def take(self, count):
        first = self.used
        self.used += count
        return first


def remote(src, dst, send, recv, target):
    return pltpu.make_async_remote_copy(
        src_ref=src, dst_ref=dst, send_sem=send, recv_sem=recv, device_id=target, device_id_type=MESH
    )


class ZGather:
    def __init__(self, at, own, where, sems):
        self.at, self.own, self.sems = at, own, sems
        self.dp, self.enc = where[0], where[1]
        self.base = sems.take(6)

    def _copy(self, hop, side):
        s = self.sems
        place = self.enc - side * hop
        src = self.own if hop == 0 else self.at(place)
        return remote(
            src, self.at(place), s.send.at[self.base + hop + (3 if side == 1 else 0)],
            s.recv.at[self.base + place], (self.dp, self.enc + side),
        )

    def _has(self, hop, side):
        enc = self.enc
        return enc - hop >= 0 if side == 1 else enc + hop <= 3

    def _goes(self, side):
        return self.enc < 3 if side == 1 else self.enc > 0

    def start(self):
        for side in (1, -1):

            @pl.when(self._goes(side))
            def _(side=side):
                self._copy(0, side).start()

    def hop(self, hop):
        s = self.sems
        for side in (1, -1):

            @pl.when(self._has(hop, side))
            def _(side=side):
                place = self.enc - side * hop
                remote(
                    self.at(place), self.at(place), s.send.at[self.base], s.recv.at[self.base + place],
                    (self.dp, self.enc),
                ).wait_recv()

            if hop < 3:

                @pl.when(self._has(hop, side) & self._goes(side))
                def _(side=side):
                    self._copy(hop, side).start()

    def finish(self):
        for side in (1, -1):
            for hop in (0, 1, 2):

                @pl.when(self._has(hop, side) & self._goes(side))
                def _(side=side, hop=hop):
                    self._copy(hop, side).wait_send()


class ChipGather:
    def __init__(self, at, own, where, sems):
        self.at, self.own, self.sems, self.where = at, own, sems, where
        self.base = sems.take(9)

    def _copy(self, i):
        dp, enc, sib, xn, yn = self.where
        diag = xn + yn - dp
        block, part, target = (
            (dp, 0, xn),
            (dp, 0, yn),
            (dp, 0, sib),
            (xn, 0, sib),
            (yn, 0, sib),
            (xn, 1, yn),
            (yn, 2, xn),
            (diag, 1, sib),
            (diag, 2, sib),
        )[i]
        src = self.own if i < 3 else self.at(block, part)
        s = self.sems
        return remote(
            src, self.at(block, part), s.send.at[self.base + i], s.recv.at[self.base + i], (target, enc)
        )

    def step1(self):
        for i in (0, 1, 2):
            self._copy(i).start()

    def step2(self):
        self._copy(0).wait_recv()
        self._copy(5).start()
        self._copy(3).start()
        self._copy(1).wait_recv()
        self._copy(6).start()
        self._copy(4).start()

    def step3(self):
        self._copy(5).wait_recv()
        self._copy(7).start()
        self._copy(6).wait_recv()
        self._copy(8).start()

    def done(self):
        for i in (2, 3, 4, 7, 8):
            self._copy(i).wait_recv()

    def finish(self):
        for i in range(9):
            self._copy(i).wait_send()


def over(values, by):
    return lax.shift_right_logical(values * ((1 << 16) // by + 1), 16)


def regroup_matrix(count, width, block):
    shape = (4 * block, count * 4 * width)
    row = lax.broadcasted_iota(jnp.int32, shape, 0)
    col = lax.broadcasted_iota(jnp.int32, shape, 1)
    place = over(row, block)
    inside = row - place * block
    m = over(inside, width)
    take = (m * 4 + place) * width + inside - m * width
    return jnp.where((take == col) & (m < count), 1.0, 0.0).astype(LOW)


def rms_rows(values, gain):
    inv = lax.rsqrt(jnp.mean(values * values, axis=-1, keepdims=True) + EPSILON)
    return values * inv * gain


def low_lanes(rows):
    return lax.broadcasted_iota(jnp.int32, (rows, 2 * HEAD), 1) < HEAD


def one_head(pair, half):
    keep = low_lanes(pair.shape[0])
    if half:
        keep = jnp.logical_not(keep)
    return jnp.where(keep, pair.astype(F32), 0.0).astype(LOW)


def self_bias(rel_u, rows, cols):
    wide = jnp.broadcast_to(rel_u, (rows, rel_u.shape[1]))
    return pltpu.roll(wide, 0, 1, stride=1, stride_axis=0)[:, :cols]


def item_of(lengths_ref, place):
    end, item = jnp.int32(0), jnp.zeros_like(place)
    for b in range(4):
        end = end + lengths_ref[0, b]
        item = item + jnp.where(end <= place, 1, 0)
    return item


def attention_pair(q_pair, k_pair, v_pair, allowed, biases, keep_probs):
    rows = q_pair.shape[0]
    nums, totals = [], []
    for half in (0, 1):
        scores = mm(one_head(q_pair, half), k_pair, NT)
        if biases is not None:
            scores = scores + biases[half]
        scores = jnp.where(allowed, scores, MASKED)
        weights = jnp.exp(scores - jnp.max(scores, axis=1, keepdims=True))
        totals.append(jnp.sum(weights, axis=1, keepdims=True))
        probs = weights.astype(LOW)
        keep_probs(half, probs)
        nums.append(mm(probs, v_pair))
    low = low_lanes(rows)
    return jnp.where(low, nums[0], nums[1]), jnp.where(low, totals[0], totals[1])


def forward_kernel(
    width,
    tgt_len, enc_len, x_ref, e_ref, dy_ref, m0, m1, m2, m3, m4, m5, m6, m7, gate_ref, up_ref, down_ref, gain1, gain2, gain3, buckets, table,
    watt_out, wff_out, dy_out, x_out, e_out, x1_out, kv1_out, kv2_out, pr1_out, pr2_out,
    x2_out, n3_out, q1_out, q2_out, num1_out, num2_out, tot1_out, tot2_out,
    w, packed, own_att, ff_own, x_rows, e_rows, dy_rows, x1_rows, kv1, kv2, pr1, pr2, send, recv, local,
):
    where = places()
    dp, enc, sib, xn, yn = where
    sems = Sems(send, recv)
    own, wide = x_rows.shape
    own_enc = e_rows.shape[0]
    inner = HEADS * HEAD
    line = 4 * width
    ff_rows = ff_own.shape[1]
    ff_half = (ff_rows // 2 + PAD - 1) // PAD * PAD
    group = 4 * own

    def rows_at(ref, first, count):
        return ref.at[pl.ds(pl.multiple_of(first, PAD), count), :]

    def mats_at(ref, lo, hi, first, count):
        return ref.at[lo:hi, pl.ds(pl.multiple_of(first, PAD), count), :]

    zs = [
        ZGather(lambda e, g=g: packed.at[g, e], own_att.at[g], where, sems) for g in (0, 1)
    ]
    chips = []
    for lo in (0, 2, 4, 6):
        hi = lo + 2
        cuts = ((lo, hi), (lo, lo + 1), (lo + 1, hi))
        chips.append(
            ChipGather(
                lambda d, part, cuts=cuts: mats_at(w, *cuts[part], d * line, line),
                mats_at(w, lo, hi, dp * line, line), where, sems,
            )
        )
    ff_cuts = ((0, ff_rows), (0, ff_half), (ff_half, ff_rows - ff_half))
    ffs = [
        ChipGather(
            lambda d, part, m=m: mats_at(wff_out, m, m + 1, d * ff_rows + ff_cuts[part][0], ff_cuts[part][1]),
            ff_own.at[m : m + 1], where, sems,
        )
        for m in range(3)
    ]
    dyz = ZGather(lambda e: rows_at(dy_out, e * own, own), dy_rows, where, sems)
    kvz = ZGather(lambda e: rows_at(kv1, e * own, own), rows_at(kv1, enc * own, own), where, sems)
    kvz2 = ZGather(
        lambda e: rows_at(kv2, e * own_enc, own_enc), rows_at(kv2, enc * own_enc, own_enc), where, sems
    )

    def save(i, src, dst):
        return pltpu.make_async_copy(src, dst, local.at[i])

    saves = [
        save(0, dy_rows, rows_at(dy_out, enc * own, own)),
        save(1, ff_own, mats_at(wff_out, 0, 3, dp * ff_rows, ff_rows)),
        save(2, w, watt_out),
        save(3, x_rows, x_out),
        save(4, e_rows, e_out),
        save(5, x1_rows, x1_out),
        save(6, kv1, kv1_out),
        save(7, kv2, kv2_out),
        save(8, pr1, pr1_out),
        save(9, pr2, pr2_out),
    ]

    for g, refs in enumerate(((m0, m1, m2, m3), (m4, m5, m6, m7))):
        rows = jnp.concatenate([ref[...] for ref in refs], axis=0).astype(LOW)
        own_att[g] = rows
        packed[g, enc] = rows
    enter(*where)
    zs[0].start()
    regroup = regroup_matrix(4, width, 4 * width)

    def unpack(g):
        rows = mm(regroup, packed[g].reshape(4 * line, wide)).astype(LOW)
        for m in range(4):
            w[4 * g + m, pl.ds(pl.multiple_of(dp * line, PAD), line), :] = rows[m * line : (m + 1) * line]

    x = jnp.transpose(x_ref[...].astype(F32))
    x_rows[...] = x.astype(LOW)
    n1 = rms_rows(x, gain1[...][None, :]).astype(LOW)
    dy_rows[...] = jnp.transpose(dy_ref[...].astype(F32)).astype(LOW)
    e_rows[...] = jnp.transpose(e_ref[...].astype(F32)).astype(LOW)
    for m, ref in enumerate((gate_ref, up_ref, down_ref)):
        ff_own[m] = ref[...].astype(LOW)
    for i in (0, 1, 3, 4):
        saves[i].start()
    rel_u = rel_rows(buckets, table, enc * own, own, group)
    for hop in (1, 2, 3):
        zs[0].hop(hop)
    unpack(0)
    chips[0].step1()
    chips[1].step1()
    zs[1].start()
    dyz.start()
    zs[1].hop(1)
    chips[0].step2()
    zs[1].hop(2)
    chips[1].step2()
    zs[1].hop(3)
    unpack(1)
    chips[2].step1()
    chips[0].step3()
    chips[0].done()
    own_enc_rows = pl.ds(pl.multiple_of(enc * own_enc, PAD), own_enc)
    kv2[own_enc_rows, 0:inner] = mm(e_rows[...], w[0], NT).astype(LOW)
    kv2[own_enc_rows, inner : 2 * inner] = mm(e_rows[...], w[1], NT).astype(LOW)
    kvz2.start()
    chips[3].step1()
    chips[1].step3()
    chips[1].done()
    own_rows = pl.ds(pl.multiple_of(enc * own, PAD), own)
    kv1[own_rows, 0:inner] = mm(n1, w[2], NT).astype(LOW)
    kv1[own_rows, inner : 2 * inner] = mm(n1, w[3], NT).astype(LOW)
    kvz.start()
    dyz.hop(1)
    chips[2].step2()
    ffs[0].step1()
    kvz2.hop(1)
    chips[3].step2()
    ffs[1].step1()
    kvz.hop(1)
    chips[2].step3()
    ffs[0].step2()
    ffs[2].step1()
    kvz2.hop(2)
    kvz.hop(2)
    dyz.hop(2)
    chips[3].step3()
    chips[2].done()
    q1 = mm(n1, w[4], NT).astype(LOW)
    q1_out[...] = q1
    ffs[1].step2()
    kvz.hop(3)

    row_place = enc * own + lax.broadcasted_iota(jnp.int32, (own, 1), 0)
    col_place = lax.broadcasted_iota(jnp.int32, (1, group), 1)
    own_items = item_of(tgt_len, row_place)
    allowed = (own_items == item_of(tgt_len, col_place)) & (col_place <= row_place)
    for pair in range(HEADS // 2):
        lanes = slice(pair * 2 * HEAD, (pair + 1) * 2 * HEAD)
        far = slice(inner + pair * 2 * HEAD, inner + (pair + 1) * 2 * HEAD)

        def keep(half, probs, pair=pair):
            pr1[2 * pair + half] = probs

        num, total = attention_pair(
            q1[:, lanes], kv1[:, lanes], kv1[:, far], allowed,
            [self_bias(rel_u[2 * pair + half : 2 * pair + half + 1, :], own, group) for half in (0, 1)],
            keep,
        )
        num1_out[:, lanes] = num
        tot1_out[:, lanes] = total
    ffs[0].step3()
    chips[3].done()
    for i in (2, 6, 8):
        saves[i].start()
    o1 = (num1_out[...] / tot1_out[...]).astype(LOW)
    x1 = x + mm(o1, w[5])
    x1_rows[...] = x1
    saves[5].start()
    n2 = rms_rows(x1, gain2[...][None, :]).astype(LOW)
    q2 = mm(n2, w[6], NT).astype(LOW)
    q2_out[...] = q2
    ffs[2].step2()
    ffs[1].step3()
    kvz2.hop(3)
    saves[7].start()
    enc_place = lax.broadcasted_iota(jnp.int32, (1, 4 * own_enc), 1)
    allowed2 = own_items == item_of(enc_len, enc_place)
    for pair in range(HEADS // 2):
        lanes = slice(pair * 2 * HEAD, (pair + 1) * 2 * HEAD)
        far = slice(inner + pair * 2 * HEAD, inner + (pair + 1) * 2 * HEAD)

        def keep2(half, probs, pair=pair):
            pr2[2 * pair + half] = probs

        num, total = attention_pair(
            q2[:, lanes], kv2[:, lanes], kv2[:, far], allowed2, None, keep2
        )
        num2_out[:, lanes] = num
        tot2_out[:, lanes] = total
    ffs[2].step3()
    saves[9].start()
    o2 = (num2_out[...] / tot2_out[...]).astype(LOW)
    x2 = x1 + mm(o2, w[7])
    x2_out[...] = x2
    n3_out[...] = rms_rows(x2, gain3[...][None, :]).astype(LOW)
    dyz.hop(3)
    for part in ffs:
        part.done()
    for part in zs + chips + ffs + [dyz, kvz, kvz2]:
        part.finish()
    for c in saves:
        c.wait()


def sds(shape, dtype):
    return jax.ShapeDtypeStruct(shape, dtype)


def rel_rows(buckets, table, first, own, group):
    inside = bucket_rows(buckets, first, own, group, 0)
    return lax.dot_general(
        table[...], inside, NN, precision=lax.Precision.HIGHEST, preferred_element_type=F32
    )


def bucket_rows(buckets, first, own, group, turn):
    row = buckets[...][None, :]
    bucket = lax.broadcasted_iota(jnp.int32, (BUCKETS, row.shape[1]), 0)
    starts = jnp.sum(jnp.where(row < bucket, 1.0, 0.0), axis=1, keepdims=True)
    ends = jnp.sum(jnp.where(row <= bucket, 1.0, 0.0), axis=1, keepdims=True)
    k = lax.broadcasted_iota(jnp.int32, (1, group + own), 1)
    k = k - turn if turn else jnp.where(k < group, k, k - group - own)
    distance = (first - k).astype(F32)
    return jnp.where((distance >= starts) & (distance < ends), 1.0, 0.0)


def call_forward(width, tgt_len, enc_len, x, e, dy, mats, ffs, gains, buckets, table):
    wide, own = x.shape
    own_enc = e.shape[1]
    inner = HEADS * HEAD
    ff_rows = ffs[0].shape[0]
    SM = pl.BlockSpec(memory_space=pltpu.SMEM)
    saved = (
        sds((8, inner, wide), LOW),
        sds((3, 8 * ff_rows, wide), LOW),
        sds((4 * own, wide), LOW),
        sds((own, wide), LOW),
        sds((own_enc, wide), LOW),
        sds((own, wide), F32),
        sds((4 * own, 2 * inner), LOW),
        sds((4 * own_enc, 2 * inner), LOW),
        sds((HEADS, own, 4 * own), LOW),
        sds((HEADS, own, 4 * own_enc), LOW),
    )
    return pl.pallas_call(
        functools.partial(forward_kernel, width),
        out_shape=saved + (
            sds((own, wide), F32),
            sds((own, wide), LOW),
            sds((own, inner), LOW),
            sds((own, inner), LOW),
            sds((own, inner), F32),
            sds((own, inner), F32),
            sds((own, inner), F32),
            sds((own, inner), F32),
        ),
        in_specs=[SM, SM] + [VM] * 19,
        out_specs=(ANY,) * 10 + (VM,) * 8,
        scratch_shapes=[
            pltpu.VMEM((8, inner, wide), LOW),
            pltpu.VMEM((2, 4, 4 * width, wide), LOW),
            pltpu.VMEM((2, 4 * width, wide), LOW),
            pltpu.VMEM((3, ff_rows, wide), LOW),
            pltpu.VMEM((own, wide), LOW),
            pltpu.VMEM((own_enc, wide), LOW),
            pltpu.VMEM((own, wide), LOW),
            pltpu.VMEM((own, wide), F32),
            pltpu.VMEM((4 * own, 2 * inner), LOW),
            pltpu.VMEM((4 * own_enc, 2 * inner), LOW),
            pltpu.VMEM((HEADS, own, 4 * own), LOW),
            pltpu.VMEM((HEADS, own, 4 * own_enc), LOW),
            pltpu.SemaphoreType.DMA((96,)),
            pltpu.SemaphoreType.DMA((96,)),
            pltpu.SemaphoreType.DMA((10,)),
        ],
        compiler_params=pltpu.CompilerParams(
            collective_id=1, has_side_effects=True, vmem_limit_bytes=56 * 2**20
        ),
        name="attention_forward",
    )(tgt_len, enc_len, x, e, dy, *mats, *ffs, *gains, buckets, table)


class ZScatter:
    def __init__(self, src_at, dst_at, where, sems, meet=None):
        self.src_at, self.dst_at, self.sems, self.meet = src_at, dst_at, sems, meet
        self.dp, self.enc = where[0], where[1]
        self.base = sems.take(3 if meet is None else 4)
        self.middle = (self.enc == 1) | (self.enc == 2)

    def _copy(self, place, merged=False):
        k = lax.rem(place - self.enc + 4, 4)
        s = self.sems
        return remote(
            self.meet if merged else self.src_at(place), self.dst_at(3 - k),
            s.send.at[self.base + k - 1], s.recv.at[self.base + 3 - k], (self.dp, place),
        )

    def _to_meet(self):
        s = self.sems
        far = 3 - self.enc
        return remote(
            self.src_at(far), self.meet, s.send.at[self.base + 3], s.recv.at[self.base + 3],
            (self.dp, 1 + lax.div(self.enc, 2)),
        )

    def start(self, place):
        self._copy(place).start()

    def start_all(self):
        enc = self.enc
        if self.meet is None:
            for k in (2, 1, 3):
                self.start(lax.rem(enc + k, 4))
            return

        @pl.when(jnp.logical_not(self.middle))
        def _():
            self._to_meet().start()
            self.start(lax.rem(enc + 2, 4))
            self.start(1 + lax.div(enc, 2))

        @pl.when(self.middle)
        def _():
            self.start(enc - 1)
            self.start(enc + 1)

    def merge(self):
        @pl.when(self.middle)
        def _():
            far = lax.rem(self.enc + 2, 4)
            self._to_meet().wait_recv()
            self.meet[...] = (self.meet[...].astype(F32) + self.src_at(far)[...].astype(F32)).astype(LOW)
            self._copy(far, merged=True).start()

    def _each(self, act):
        enc = self.enc
        if self.meet is None:
            for k in (1, 2, 3):
                act(lax.rem(enc + k, 4))
            return
        act(lax.rem(enc + 2, 4))

        @pl.when(enc > 0)
        def _():
            act(enc - 1)

        @pl.when(enc < 3)
        def _():
            act(enc + 1)

    def wait(self):
        def one(place):
            k = lax.rem(self.enc - place + 4, 4)
            s = self.sems
            remote(
                self.dst_at(3 - k), self.dst_at(3 - k), s.send.at[self.base], s.recv.at[self.base + 3 - k],
                (self.dp, self.enc),
            ).wait_recv()

        self._each(one)

    def clear(self):
        if self.meet is not None:

            @pl.when(self.enc == 0)
            def _():
                ref = self.dst_at(2)
                ref[...] = jnp.zeros(ref.shape, ref.dtype)

            @pl.when(self.enc == 3)
            def _():
                ref = self.dst_at(0)
                ref[...] = jnp.zeros(ref.shape, ref.dtype)

    def finish(self):
        self._each(lambda place: self._copy(place).wait_send())
        if self.meet is not None:

            @pl.when(jnp.logical_not(self.middle))
            def _():
                self._to_meet().wait_send()


def rms_back(values, gain, grad):
    inv = lax.rsqrt(jnp.mean(values * values, axis=-1, keepdims=True) + EPSILON)
    scaled = grad * gain
    mean = jnp.mean(values * scaled, axis=-1, keepdims=True)
    gain_grad = jnp.sum(grad * values * inv, axis=0, keepdims=True)
    return inv * scaled - values * (inv * inv * inv * mean), gain_grad


GELU_A = 0.7978845608028654
GELU_B = 0.044715


def ff_kernel(
    n3_ref, x2_ref, dyall_ref, wff_ref, gain3,
    dx2_out, gain_out, part_out, sums_out,
    w, n3, dy, back, act, dgate, dup, part, got, grads, core_got, own_sum, out_part, send, recv, local,
):
    where = places()
    dp, enc, sib, xn, yn = where
    core = lax.rem(dp, 2)
    sems = Sems(send, recv)
    own = n3_ref.shape[0]
    ff_rows = grads.shape[3]

    def rows_of(place):
        return pl.ds(pl.multiple_of(place * own, PAD), own)

    gather = ZGather(lambda e: n3.at[rows_of(e), :], n3_ref, where, sems)
    scatter = ZScatter(lambda e: part.at[e], lambda slot: got.at[slot], where, sems)
    loads = [
        pltpu.make_async_copy(wff_ref, w, local.at[0]),
        pltpu.make_async_copy(dyall_ref, dy, local.at[1]),
    ]
    for c in loads:
        c.start()
    enter(*where)
    gather.start()
    n3[rows_of(enc), :] = n3_ref[...]
    for c in loads:
        c.wait()

    back[...] = mm(dy[...], w[2], NT)

    def block(place):
        rows = rows_of(place)
        normed = n3[rows, :]
        gate = mm(normed, w[0], NT)
        up = mm(normed, w[1], NT)
        dh = back[rows, :]
        square = gate * gate
        t = jnp.tanh(GELU_A * gate * (1.0 + GELU_B * square))
        half = 0.5 * (1.0 + t)
        g = gate * half
        slope = half + 0.5 * gate * (1.0 - t * t) * (GELU_A * (1.0 + 3.0 * GELU_B * square))
        hidden = (g * up).astype(LOW)
        dg = (dh * up * slope).astype(LOW)
        du = (dh * g).astype(LOW)
        act[rows, :] = hidden
        dgate[rows, :] = dg
        dup[rows, :] = du
        return mm(dg, w[0]) + mm(du, w[1])

    own_sum[...] = block(enc)
    near = 1 + lax.rem(enc, 2)
    last = jnp.where(enc < 2, 3, 0)
    for hop, place in ((1, near), (2, 6 - enc - near - last), (3, last)):
        gather.hop(hop)
        part[place] = block(place).astype(LOW)
        scatter.start(place)

    out_part[...] = mm(act[...], w[2]).astype(LOW)
    saves = [
        pltpu.make_async_copy(out_part, part_out, local.at[0]),
        pltpu.make_async_copy(core_got, sums_out, local.at[1]),
    ]
    saves[0].start()
    swaps = []
    base = sems.take(3)
    for m, (left, right) in ((2, (act, dy)), (0, (dgate, n3)), (1, (dup, n3))):
        whole = mm(left[...], right[...], TN).astype(LOW)
        for j in range(4):
            for c in range(2):
                first_row = (2 * j + c) * ff_rows
                grads[m, j, c] = whole[first_row : first_row + ff_rows]
        swap = remote(
            grads.at[m, :, 1 - core], core_got.at[m], send.at[base + m], recv.at[base + m], (sib, enc)
        )
        swap.start()
        swaps.append((m, swap))
    for m, swap in swaps:
        swap.wait_recv()
        for j in range(4):
            core_got[m, j] = (grads[m, j, core].astype(F32) + core_got[m, j].astype(F32)).astype(LOW)
    saves[1].start()
    scatter.wait()
    dn3 = own_sum[...] + got[0].astype(F32) + got[1].astype(F32) + got[2].astype(F32)
    dv, gain_grad = rms_back(x2_ref[...], gain3[...][None, :], dn3)
    dx2_out[...] = dy[rows_of(enc), :].astype(F32) + dv
    gain_out[...] = gain_grad
    gather.finish()
    scatter.finish()
    for m, swap in swaps:
        swap.wait_send()
    for c in saves:
        c.wait()


def call_ff(n3, x2, dy_all, wff, gain3):
    own, wide = n3.shape
    ff_all = wff.shape[1]
    ff_rows = ff_all // 8
    group = 4 * own
    return pl.pallas_call(
        ff_kernel,
        out_shape=(
            sds((own, wide), F32),
            sds((1, wide), F32),
            sds((group, wide), LOW),
            sds((3, 4, ff_rows, wide), LOW),
        ),
        in_specs=[VM, VM, ANY, ANY, VM],
        out_specs=(VM, VM, ANY, ANY),
        scratch_shapes=[
            pltpu.VMEM((3, ff_all, wide), LOW),
            pltpu.VMEM((group, wide), LOW),
            pltpu.VMEM((group, wide), LOW),
            pltpu.VMEM((group, ff_all), F32),
            pltpu.VMEM((group, ff_all), LOW),
            pltpu.VMEM((group, ff_all), LOW),
            pltpu.VMEM((group, ff_all), LOW),
            pltpu.VMEM((4, own, wide), LOW),
            pltpu.VMEM((3, own, wide), LOW),
            pltpu.VMEM((3, 4, 2, ff_rows, wide), LOW),
            pltpu.VMEM((3, 4, ff_rows, wide), LOW),
            pltpu.VMEM((own, wide), F32),
            pltpu.VMEM((group, wide), LOW),
            pltpu.SemaphoreType.DMA((12,)),
            pltpu.SemaphoreType.DMA((12,)),
            pltpu.SemaphoreType.DMA((2,)),
        ],
        compiler_params=pltpu.CompilerParams(
            collective_id=2, has_side_effects=True, vmem_limit_bytes=60 * 2**20
        ),
        name="feed_forward",
    )(n3, x2, dy_all, wff, gain3)


class ChipReduce:
    def __init__(self, src, got, last, cuts, own, where, sems):
        self.src, self.got, self.last, self.cuts, self.own = src, got, last, cuts, own
        self.sems, self.where = sems, where
        self.x = lax.rem(lax.div(where[0], 2), 2)
        self.y = lax.div(where[0], 4)
        self.base = sems.take(2 * len(cuts))

    def _copy(self, i, second):
        dp, enc, sib, xn, yn = self.where
        m, lo, hi, by_x = self.cuts[i]
        s, at = self.sems, self.base + 2 * i + (1 if second else 0)
        if second:
            src = self.got.at[m, 1 - self.y if by_x else 1 - self.x, lo:hi]
            dst = self.last.at[m, lo:hi]
        else:
            src = self.src.at[m, :, 1 - self.x, lo:hi] if by_x else self.src.at[m, 1 - self.y, :, lo:hi]
            dst = self.got.at[m, :, lo:hi]
        target = xn if by_x != second else yn
        return remote(src, dst, s.send.at[at], s.recv.at[at], (target, enc))

    def start(self):
        for i in range(len(self.cuts)):
            self._copy(i, False).start()

    def turn(self):
        for i, (m, lo, hi, by_x) in enumerate(self.cuts):
            self._copy(i, False).wait_recv()
            for k in range(2):
                self.got[m, k, lo:hi] = (
                    self.own(m, k, lo, hi, by_x).astype(F32) + self.got[m, k, lo:hi].astype(F32)
                ).astype(LOW)
            self._copy(i, True).start()

    def totals(self):
        out = []
        for i, (m, lo, hi, by_x) in enumerate(self.cuts):
            self._copy(i, True).wait_recv()
            mine = self.got[m, self.y if by_x else self.x, lo:hi]
            out.append(mine.astype(F32) + self.last[m, lo:hi].astype(F32))
        return out

    def finish(self):
        for i in range(len(self.cuts)):
            self._copy(i, False).wait_send()
            self._copy(i, True).wait_send()


class CoreReduce:
    def __init__(self, lo, grads, core_got, chip_got, chip_last, where, sems):
        self.lo, self.grads, self.core_got, self.where, self.sems = lo, grads, core_got, where, sems
        self.base = sems.take(1)
        rows = grads.shape[4]
        x = lax.rem(lax.div(where[0], 2), 2)
        y = lax.div(where[0], 4)

        def own(m, k, first, last, by_x):
            return core_got[m, k, x] if by_x else core_got[m, y, k]

        self.chips = ChipReduce(
            core_got, chip_got, chip_last, ((lo, 0, rows, True), (lo + 1, 0, rows, False)), own, where, sems
        )

    def _core(self):
        dp, enc, sib, xn, yn = self.where
        s, lo = self.sems, self.lo
        return remote(
            self.grads.at[lo : lo + 2, :, :, 1 - lax.rem(dp, 2)], self.core_got.at[lo : lo + 2],
            s.send.at[self.base], s.recv.at[self.base], (sib, enc),
        )

    def start(self):
        self._core().start()

    def next(self):
        core = lax.rem(self.where[0], 2)
        self._core().wait_recv()
        for m in (self.lo, self.lo + 1):
            self.core_got[m] = (self.grads[m, :, :, core].astype(F32) + self.core_got[m].astype(F32)).astype(LOW)
        self.chips.start()

    def finish(self):
        self._core().wait_send()
        self.chips.finish()


class LineReduce:
    def __init__(self, parts, width, line, got, meet, out, where, sems):
        self.parts, self.line, self.got, self.out, self.where = parts, line, got, out, where
        self.rows = line.shape[1]
        self.regroup = regroup_matrix(2 * len(parts), width, self.rows)
        self.z = ZScatter(lambda e: line.at[e], lambda slot: got.at[slot], where, sems, meet)

    def start(self):
        totals = [t.astype(LOW) for part in self.parts for t in part.chips.totals()]
        rows = mm(self.regroup, jnp.concatenate(totals, axis=0)).astype(LOW)
        for e in range(4):
            self.line[e] = rows[e * self.rows : (e + 1) * self.rows]
        self.z.start_all()

    def merge(self):
        self.z.merge()

    def done(self):
        self.z.wait()
        total = self.line[self.where[1]].astype(F32)
        for slot in range(3):
            total = total + self.got[slot].astype(F32)
        self.out[...] = total


def backward_pair(q_pair, k_pair, v_pair, probs_ref, pair, dnum, dtotals):
    rows = q_pair.shape[0]
    parts, scores = [], []
    for half in (0, 1):
        dw = mm(one_head(dnum, half), v_pair, NT)
        ds = (probs_ref[2 * pair + half].astype(F32) * (dw + dtotals[half])).astype(LOW)
        scores.append(ds)
        parts.append(mm(ds, k_pair))
    dq = jnp.where(low_lanes(rows), parts[0], parts[1])
    dk = mm(jnp.concatenate(scores, axis=0), jnp.concatenate([one_head(q_pair, h) for h in (0, 1)], axis=0), TN)
    probs = jnp.concatenate([probs_ref[2 * pair + h] for h in (0, 1)], axis=0)
    dv = mm(probs, jnp.concatenate([one_head(dnum, h) for h in (0, 1)], axis=0), TN)
    return dq, dk, dv, scores


def total_grads(product, total):
    low = low_lanes(product.shape[0])
    out = []
    for half in (0, 1):
        keep = low if half == 0 else jnp.logical_not(low)
        top = jnp.sum(jnp.where(keep, product, 0.0), axis=1, keepdims=True)
        tot = total[:, half * HEAD : half * HEAD + 1]
        out.append(-top / (tot * tot))
    return out


def backward_kernel(
    width,
    dx2_ref, gain1, gain2, gain3_grad, buckets, q1, q2, num1, num2, tot1, tot2, kv2, pr2,
    watt_ref, sums_ref, part_hbm, x_hbm, e_hbm, x1_hbm, x2_hbm, kv1_hbm, pr1_hbm,
    four_out, two_out, small_out, hidden_out, hidden_grad, encoder_grad, ff_out,
    w, grads, core_got, chip_got, chip_last, line4, line4_got, line4_meet, line2, line2_got, line2_meet,
    ff_own, ff_got, ff_last, part_got, part_meet,
    kvp1, kvp1_got, kvp1_meet, kvp2, kvp2_got, kvp2_meet, dq, vec, vec_got,
    part_ref, x_ref, e_ref, x1_ref, x2_ref, kv1, pr1, out_t, grad_t, enc_t, ff_sum, send, recv, local,
):
    where = places()
    dp, enc, sib, xn, yn = where
    sems = Sems(send, recv)
    own, wide = x_ref.shape
    own_enc = e_ref.shape[0]
    inner = HEADS * HEAD
    chip_x = lax.rem(lax.div(dp, 2), 2)
    chip_y = lax.div(dp, 4)
    ff_rows = ff_last.shape[1]
    ff_half = (ff_rows // 2 + PAD - 1) // PAD * PAD
    part_rows = own // 4

    out_z = [
        ZScatter(
            lambda e, a=a, b=b: part_ref.at[e, a:b], lambda slot, a=a, b=b: part_got.at[slot, a:b],
            where, sems, part_meet.at[a:b],
        )
        for a, b in ((0, part_rows), (part_rows, own))
    ]
    kv1_z = ZScatter(lambda e: kvp1.at[e], lambda slot: kvp1_got.at[slot], where, sems, kvp1_meet)
    kv2_z = ZScatter(lambda e: kvp2.at[e], lambda slot: kvp2_got.at[slot], where, sems, kvp2_meet)
    batches = [CoreReduce(lo, grads, core_got, chip_got, chip_last, where, sems) for lo in (0, 2, 4, 6)]
    lines = [LineReduce(batches[:2], width, line4, line4_got, line4_meet, four_out, where, sems)]
    lines += [
        LineReduce(
            batches[2 + i : 3 + i], width, line2.at[i], line2_got.at[i], line2_meet.at[i], two_out.at[i], where, sems
        )
        for i in (0, 1)
    ]
    ff_cuts = ((0, 0, ff_rows, True), (1, 0, ff_rows, False), (2, 0, ff_half, True), (2, ff_half, ff_rows, False))
    ff = ChipReduce(
        sums_ref, ff_got, ff_last, ff_cuts, lambda m, k, lo, hi, by_x: ff_own[m, k, lo:hi], where, sems
    )
    vec_base = sems.take(3)
    vec_z = ZScatter(lambda e: vec.at[3], lambda slot: vec_got.at[3 + slot], where, sems)

    def vec_copy(i):
        target = (sib, xn, yn)[i]
        return remote(
            vec.at[i], vec_got.at[i], send.at[vec_base + i], recv.at[vec_base + i], (target, enc)
        )

    def load(slot, m, i):
        return pltpu.make_async_copy(watt_ref.at[m], w.at[slot], local.at[i])

    pulls = [
        pltpu.make_async_copy(src, dst, local.at[12 + i])
        for i, (src, dst) in enumerate(
            (
                (part_hbm, part_ref), (x1_hbm, x1_ref), (kv1_hbm, kv1), (pr1_hbm, pr1), (x_hbm, x_ref),
                (e_hbm, e_ref), (x2_hbm, x2_ref),
            )
        )
    ]
    pushes = [
        pltpu.make_async_copy(src, dst, local.at[19 + i])
        for i, (src, dst) in enumerate(
            ((grad_t, hidden_grad), (enc_t, encoder_grad), (ff_sum, ff_out), (out_t, hidden_out))
        )
    ]
    first_loads = [load(slot, m, slot) for slot, m in enumerate((7, 6, 5, 2, 3))]
    for c in first_loads[:1] + pulls + first_loads[1:]:
        c.start()
    own_ff = [
        pltpu.make_async_copy(
            sums_ref.at[m, :, chip_x, lo:hi] if by_x else sums_ref.at[m, chip_y, :, lo:hi],
            ff_own.at[m, :, lo:hi], local.at[8 + i],
        )
        for i, (m, lo, hi, by_x) in enumerate(ff_cuts)
    ]
    for c in own_ff:
        c.start()
    enter(*where)
    pulls[0].wait()
    out_z[0].start_all()
    ff.start()
    for part in out_z + [kv1_z, kv2_z] + [line.z for line in lines]:
        part.clear()

    def put_grad(m, left, right):
        whole = mm(left, right, TN).astype(LOW)
        rows = 4 * width
        for y in range(2):
            for x in range(2):
                for c in range(2):
                    at = (4 * y + 2 * x + c) * rows
                    grads[m, y, x, c] = whole[at : at + rows]

    b2 = dx2_ref[...].astype(LOW)
    first_loads[0].wait()
    do2 = mm(b2, w[0], NT)
    dnum2 = (do2 / tot2[...]).astype(LOW)
    prod2 = do2 * num2[...]
    for pair in range(HEADS // 2):
        lanes = slice(pair * 2 * HEAD, (pair + 1) * 2 * HEAD)
        far = slice(inner + pair * 2 * HEAD, inner + (pair + 1) * 2 * HEAD)
        dtot = total_grads(prod2[:, lanes], tot2[:, lanes])
        dq_pair, dk, dv, _ = backward_pair(
            q2[:, lanes], kv2[:, lanes], kv2[:, far], pr2, pair, dnum2[:, lanes], dtot
        )
        dq[:, lanes] = dq_pair.astype(LOW)
        for e in range(4):
            kvp2[e, :, lanes] = dk[e * own_enc : (e + 1) * own_enc].astype(LOW)
            kvp2[e, :, far] = dv[e * own_enc : (e + 1) * own_enc].astype(LOW)
    kv2_z.start_all()
    dq2 = dq[...]
    put_grad(0, (num2[...] / tot2[...]).astype(LOW), b2)
    pulls[1].wait()
    x1 = x1_ref[...]
    put_grad(1, dq2, rms_rows(x1, gain2[...][None, :]).astype(LOW))
    batches[0].start()
    out_z[0].merge()
    first_loads[1].wait()
    dv2, gain2_grad = rms_back(x1, gain2[...][None, :], mm(dq2, w[1]))
    dx1 = dx2_ref[...] + dv2
    b1 = dx1.astype(LOW)
    first_loads[2].wait()
    do1 = mm(b1, w[2], NT)
    late = [load(2, 4, 5), load(0, 0, 6), load(1, 1, 7)]
    for c in late:
        c.start()
    dnum1 = (do1 / tot1[...]).astype(LOW)
    prod1 = do1 * num1[...]
    batches[0].next()
    pulls[2].wait()
    pulls[3].wait()
    all_scores = []
    for pair in range(HEADS // 2):
        lanes = slice(pair * 2 * HEAD, (pair + 1) * 2 * HEAD)
        far = slice(inner + pair * 2 * HEAD, inner + (pair + 1) * 2 * HEAD)
        dtot = total_grads(prod1[:, lanes], tot1[:, lanes])
        dq_pair, dk, dv, scores = backward_pair(
            q1[:, lanes], kv1[:, lanes], kv1[:, far], pr1, pair, dnum1[:, lanes], dtot
        )
        dq[:, lanes] = dq_pair.astype(LOW)
        for e in range(4):
            kvp1[e, :, lanes] = dk[e * own : (e + 1) * own].astype(LOW)
            kvp1[e, :, far] = dv[e * own : (e + 1) * own].astype(LOW)
        all_scores += scores
    kv1_z.start_all()
    out_z[1].start_all()
    dq1 = dq[...]
    pulls[4].wait()
    x = x_ref[...].astype(F32)
    n1 = rms_rows(x, gain1[...][None, :]).astype(LOW)
    put_grad(2, (num1[...] / tot1[...]).astype(LOW), b1)
    put_grad(3, dq1, n1)
    batches[1].start()
    kv2_z.merge()
    batches[1].next()
    for c in own_ff:
        c.wait()
    ff.turn()
    vec[0] = jnp.zeros(vec.shape[1:], F32)
    inside = bucket_rows(buckets, enc * own, own, 4 * own, own - 1)
    flip_row = lax.broadcasted_iota(jnp.int32, (own, own), 0)
    flip_col = lax.broadcasted_iota(jnp.int32, (own, own), 1)
    flip = jnp.where(flip_row + flip_col == own - 1, 1.0, 0.0).astype(LOW)
    for h, ds in enumerate(all_scores):
        long = jnp.concatenate([mm(flip, ds), jnp.zeros((own, own), F32)], axis=1)
        turned = pltpu.roll(long, 0, 1, stride=1, stride_axis=0)
        by_distance = jnp.sum(turned, axis=0, keepdims=True)
        vec[0, 8 + h : 9 + h, 0:BUCKETS] = lax.dot_general(
            by_distance, inside, NT, precision=lax.Precision.HIGHEST, preferred_element_type=F32
        )
    batches[0].chips.turn()
    for c in late:
        c.wait()
    dn1 = mm(dq1, w[2])
    batches[1].chips.turn()

    kv2_z.wait()
    low2 = (
        kvp2[enc].astype(F32) + kvp2_got[0].astype(F32) + kvp2_got[1].astype(F32) + kvp2_got[2].astype(F32)
    ).astype(LOW)
    dk2 = low2[:, :inner]
    dv2 = low2[:, inner:]
    pulls[5].wait()
    put_grad(4, dk2, e_ref[...])
    put_grad(5, dv2, e_ref[...])
    batches[2].start()
    kv1_z.merge()
    lines[0].start()
    batches[2].next()
    enc_t[...] = jnp.transpose(mm(dk2, w[0]) + mm(dv2, w[1]))
    pushes[1].start()

    kv1_z.wait()
    low1 = (
        kvp1[enc].astype(F32) + kvp1_got[0].astype(F32) + kvp1_got[1].astype(F32) + kvp1_got[2].astype(F32)
    ).astype(LOW)
    dk1 = low1[:, :inner]
    dv1 = low1[:, inner:]
    put_grad(6, dk1, n1)
    put_grad(7, dv1, n1)
    batches[3].start()
    batches[2].chips.turn()
    first_loads[3].wait()
    first_loads[4].wait()
    dn1 = dn1 + mm(dk1, w[3]) + mm(dv1, w[4])
    dv_x, gain1_grad = rms_back(x, gain1[...][None, :], dn1)
    grad_t[...] = jnp.transpose(dx1 + dv_x)
    pushes[0].start()
    out_z[1].merge()
    vec[0, 0:1, :] = gain1_grad
    vec[0, 1:2, :] = gain2_grad
    vec[0, 2:3, :] = gain3_grad[...]
    vec_copy(0).start()
    batches[3].next()
    lines[0].merge()
    vec_copy(0).wait_recv()
    vec[1] = vec[0] + vec_got[0]
    vec_copy(1).start()
    lines[1].start()
    batches[3].chips.turn()
    vec_copy(1).wait_recv()
    vec[2] = vec[1] + vec_got[1]
    vec_copy(2).start()
    vec_copy(2).wait_recv()
    vec[3] = vec[2] + vec_got[2]
    vec_z.start_all()
    lines[2].start()
    lines[1].merge()
    for (m, lo, hi, by_x), total in zip(ff_cuts, ff.totals()):
        ff_sum[m, lo:hi] = total
    pushes[2].start()
    lines[2].merge()
    lines[0].done()
    for z in out_z:
        z.wait()
    pulls[6].wait()
    out_t[...] = jnp.transpose(
        x2_ref[...] + (part_ref[enc].astype(F32) + part_got[0].astype(F32))
        + (part_got[1].astype(F32) + part_got[2].astype(F32))
    ).astype(LOW)
    pushes[3].start()
    lines[1].done()
    lines[2].done()
    vec_z.wait()
    small_out[...] = vec[3] + vec_got[3] + vec_got[4] + vec_got[5]
    for done in out_z + [kv1_z, kv2_z, vec_z, ff] + batches + [line.z for line in lines]:
        done.finish()
    for i in range(3):
        vec_copy(i).wait_send()
    for c in pushes:
        c.wait()


def call_backward(width, dx2, gain1, gain2, gain3_grad, buckets, small, watt, sums, part, x, e, x1, x2, kv1, pr1):
    own, wide = x.shape
    own_enc = e.shape[0]
    inner = HEADS * HEAD
    rows = 4 * width
    block = (2 * width + PAD - 1) // PAD * PAD
    ff_rows = sums.shape[2]
    return pl.pallas_call(
        functools.partial(backward_kernel, width),
        out_shape=(
            sds((4 * width, wide), F32),
            sds((2, block, wide), F32),
            sds((16, wide), F32),
            sds((wide, own), LOW),
            sds((wide, own), F32),
            sds((wide, own_enc), F32),
            sds((3, ff_rows, wide), F32),
        ),
        in_specs=[VM] * 13 + [ANY] * 9,
        out_specs=(VM,) * 3 + (ANY,) * 4,
        scratch_shapes=[
            pltpu.VMEM((5, inner, wide), LOW),
            pltpu.VMEM((8, 2, 2, 2, rows, wide), LOW),
            pltpu.VMEM((8, 2, 2, rows, wide), LOW),
            pltpu.VMEM((8, 2, rows, wide), LOW),
            pltpu.VMEM((8, rows, wide), LOW),
            pltpu.VMEM((4, 4 * width, wide), LOW),
            pltpu.VMEM((3, 4 * width, wide), LOW),
            pltpu.VMEM((4 * width, wide), LOW),
            pltpu.VMEM((2, 4, block, wide), LOW),
            pltpu.VMEM((2, 3, block, wide), LOW),
            pltpu.VMEM((2, block, wide), LOW),
            pltpu.VMEM((3, 2, ff_rows, wide), LOW),
            pltpu.VMEM((3, 2, ff_rows, wide), LOW),
            pltpu.VMEM((3, ff_rows, wide), LOW),
            pltpu.VMEM((3, own, wide), LOW),
            pltpu.VMEM((own, wide), LOW),
            pltpu.VMEM((4, own, 2 * inner), LOW),
            pltpu.VMEM((3, own, 2 * inner), LOW),
            pltpu.VMEM((own, 2 * inner), LOW),
            pltpu.VMEM((4, own_enc, 2 * inner), LOW),
            pltpu.VMEM((3, own_enc, 2 * inner), LOW),
            pltpu.VMEM((own_enc, 2 * inner), LOW),
            pltpu.VMEM((own, inner), LOW),
            pltpu.VMEM((4, 16, wide), F32),
            pltpu.VMEM((6, 16, wide), F32),
            pltpu.VMEM((4, own, wide), LOW),
            pltpu.VMEM((own, wide), LOW),
            pltpu.VMEM((own_enc, wide), LOW),
            pltpu.VMEM((own, wide), F32),
            pltpu.VMEM((own, wide), F32),
            pltpu.VMEM(kv1.shape, LOW),
            pltpu.VMEM(pr1.shape, LOW),
            pltpu.VMEM((wide, own), LOW),
            pltpu.VMEM((wide, own), F32),
            pltpu.VMEM((wide, own_enc), F32),
            pltpu.VMEM((3, ff_rows, wide), F32),
            pltpu.SemaphoreType.DMA((64,)),
            pltpu.SemaphoreType.DMA((64,)),
            pltpu.SemaphoreType.DMA((23,)),
        ],
        compiler_params=pltpu.CompilerParams(
            collective_id=3, has_side_effects=True, vmem_limit_bytes=62 * 2**20
        ),
        name="attention_backward",
    )(
        dx2, gain1, gain2, gain3_grad, buckets, *small, watt, sums.reshape(3, 2, 2, ff_rows, wide),
        part.reshape(4, own, wide), x, e, x1, x2, kv1, pr1,
    )


def fast_body(
    hidden_in, encoder_out, grad_out, tgt_lengths, enc_lengths, rel_bucket, norm1_gain,
    self_q, self_k, self_v, self_o, rel_table, norm2_gain,
    cross_q, cross_k, cross_v, cross_o, norm3_gain, ff_gate, ff_up, ff_out,
):
    width = self_q.shape[1]
    mats = (cross_k.T, cross_v.T, self_k.T, self_v.T, self_q.T, self_o, cross_q.T, cross_o)
    (
        watt_all, wff_all, dy_all, x, e, x1, kv1, kv2, pr1, pr2,
        x2, n3, q1, q2, num1, num2, tot1, tot2,
    ) = call_forward(
        width, tgt_lengths, enc_lengths, hidden_in.T, encoder_out.T, grad_out.T, mats,
        (ff_gate.T, ff_up.T, ff_out), (norm1_gain, norm2_gain, norm3_gain), rel_bucket, rel_table.T,
    )
    dx2, gain3_grad, part, sums = call_ff(n3, x2, dy_all, wff_all, norm3_gain)
    four, two, small, hidden_out, hidden_grad, encoder_grad, ff = call_backward(
        width, dx2, norm1_gain, norm2_gain, gain3_grad, rel_bucket,
        (q1, q2, num1, num2, tot1, tot2, kv2, pr2), watt_all, sums, part, x, e, x1, x2, kv1, pr1,
    )
    o2, q2, o1, q1 = (four[m * width : (m + 1) * width] for m in range(4))
    (k2, v2), (k1, v1) = ((t[:width], t[width : 2 * width]) for t in two)
    return (
        hidden_out.T, hidden_grad.T, encoder_grad.T, small[0],
        q1.T, k1.T, v1.T, o1, small[8 : 8 + HEADS, :BUCKETS].T,
        small[1], q2.T, k2.T, v2.T, o2, small[2], ff[0].T, ff[1].T, ff[2],
    )


def rms_scale(values, gain):
    return values * lax.rsqrt(jnp.mean(values * values, axis=-1, keepdims=True) + EPSILON) * gain


def gated_gelu(gate_pre, up_pre):
    return jax.nn.gelu(gate_pre, approximate=True) * up_pre


def item_ids(lengths, total_rows):
    ends = jnp.cumsum(lengths)
    places = jnp.arange(total_rows, dtype=jnp.int32)
    return jnp.sum((ends[None, :] <= places[:, None]).astype(jnp.int32), axis=1)


def product(left, right):
    return jnp.dot(left, right, preferred_element_type=jnp.float32)


def product_tn(left, right):
    return lax.dot_general(
        left, right, (((0,), (0,)), ((), ())), preferred_element_type=jnp.float32
    )


def product_nt(left, right):
    return lax.dot_general(
        left, right, (((1,), (1,)), ((), ())), preferred_element_type=jnp.float32
    )


def to_pieces(grad, shard_dim, shards):
    if shard_dim == 0:
        return grad.reshape(shards, -1)
    rows = grad.shape[0]
    return jnp.transpose(grad.reshape(rows, shards, -1), (1, 0, 2)).reshape(shards, -1)


def from_pieces(received, shard_dim, shape, shards):
    summed = jnp.sum(received, axis=0)
    if shard_dim == 0:
        return summed.reshape(shape[0] // shards, shape[1])
    return summed.reshape(shape[0], shape[1] // shards)


def head_pair(matrix, pair_index):
    return lax.dynamic_slice_in_dim(matrix, pair_index * 2 * HEAD, 2 * HEAD, 1).reshape(
        matrix.shape[0], 2, HEAD
    )


def pair_stats(stats, pair_index):
    return lax.dynamic_slice_in_dim(stats, pair_index * 2, 2, 0)


def relative_bias(distance, bias_info, pair_index):
    starts, table = bias_info
    table_pair = lax.dynamic_slice_in_dim(table, pair_index * 2, 2, 1)

    def add_step(bucket, total):
        rise = table_pair[bucket] - table_pair[bucket - 1]
        return total + jnp.where(distance[None] >= starts[bucket], rise[:, None, None], 0.0)

    start_bias = jnp.broadcast_to(table_pair[0][:, None, None], (2,) + distance.shape)
    return lax.fori_loop(1, BUCKETS, add_step, start_bias)


def relative_grads(distance, starts, score_grad):

    def one_step(bucket):
        return jnp.sum(jnp.where(distance[None] >= starts[bucket], score_grad, 0.0), axis=(1, 2))

    steps_sum = lax.map(one_step, jnp.arange(BUCKETS, dtype=jnp.int32))
    return steps_sum - jnp.concatenate([steps_sum[1:], jnp.zeros((1, 2), jnp.float32)], axis=0)


def pair_scores(query_block, key_rows, pair_index, layout):
    allowed, distance, bias_info = layout
    scores = jnp.einsum(
        "qhe,khe->hqk",
        head_pair(query_block, pair_index),
        head_pair(key_rows, pair_index),
        preferred_element_type=jnp.float32,
    )
    if bias_info is not None:
        scores = scores + relative_bias(distance, bias_info, pair_index)
    return jnp.where(allowed[None], scores, MASKED)


def forward_parts(query_block, key_rows, value_rows, layout):
    block_rows = query_block.shape[0]
    width = 2 * HEAD

    def forward_one_pair(pair_index, carry):
        numerator, largest, totals = carry
        scores = pair_scores(query_block, key_rows, pair_index, layout)
        pair_top = jnp.max(scores, axis=2)
        weights = jnp.exp(scores - pair_top[:, :, None])
        partial_sum = jnp.einsum(
            "hqk,khe->qhe",
            weights.astype(jnp.bfloat16),
            head_pair(value_rows, pair_index),
            preferred_element_type=jnp.float32,
        )
        numerator = lax.dynamic_update_slice_in_dim(
            numerator, partial_sum.reshape(block_rows, width), pair_index * width, 1
        )
        largest = lax.dynamic_update_slice_in_dim(largest, pair_top, pair_index * 2, 0)
        totals = lax.dynamic_update_slice_in_dim(
            totals, jnp.sum(weights, axis=2), pair_index * 2, 0
        )
        return (numerator, largest, totals)

    start_state = (
        jnp.zeros((block_rows, HEADS * HEAD), jnp.float32),
        jnp.zeros((HEADS, block_rows), jnp.float32),
        jnp.zeros((HEADS, block_rows), jnp.float32),
    )
    return lax.fori_loop(0, HEADS // 2, forward_one_pair, start_state)


def backward_parts(query_block, key_rows, value_rows, layout, top_rows, num_grad, total_grad):
    allowed, distance, bias_info = layout
    block_rows = query_block.shape[0]
    key_count = key_rows.shape[0]
    width = 2 * HEAD

    def backward_one_pair(pair_index, carry):
        query_grad, key_grad, value_grad, bias_grad = carry
        query_pair = head_pair(query_block, pair_index)
        key_pair = head_pair(key_rows, pair_index)
        value_pair = head_pair(value_rows, pair_index)
        grad_pair = head_pair(num_grad, pair_index)
        scores = pair_scores(query_block, key_rows, pair_index, layout)
        weights = jnp.exp(scores - pair_stats(top_rows, pair_index)[:, :, None])
        weight_grad = jnp.einsum(
            "qhe,khe->hqk", grad_pair, value_pair, preferred_element_type=jnp.float32
        )
        score_grad = (
            weights * (weight_grad + pair_stats(total_grad, pair_index)[:, :, None])
        ).astype(jnp.bfloat16)
        part_query = jnp.einsum(
            "hqk,khe->qhe", score_grad, key_pair, preferred_element_type=jnp.float32
        )
        part_key = jnp.einsum(
            "hqk,qhe->khe", score_grad, query_pair, preferred_element_type=jnp.float32
        )
        part_value = jnp.einsum(
            "hqk,qhe->khe",
            weights.astype(jnp.bfloat16),
            grad_pair,
            preferred_element_type=jnp.float32,
        )
        query_grad = lax.dynamic_update_slice_in_dim(
            query_grad, part_query.reshape(block_rows, width), pair_index * width, 1
        )
        key_grad = lax.dynamic_update_slice_in_dim(
            key_grad, part_key.reshape(key_count, width), pair_index * width, 1
        )
        value_grad = lax.dynamic_update_slice_in_dim(
            value_grad, part_value.reshape(key_count, width), pair_index * width, 1
        )
        if bias_info is not None:
            pair_bias_grad = relative_grads(distance, bias_info[0], score_grad.astype(jnp.float32))
            bias_grad = lax.dynamic_update_slice_in_dim(
                bias_grad, pair_bias_grad, pair_index * 2, 1
            )
        return (query_grad, key_grad, value_grad, bias_grad)

    bias_start = None if bias_info is None else jnp.zeros((BUCKETS, HEADS), jnp.float32)
    start_state = (
        jnp.zeros((block_rows, HEADS * HEAD), jnp.float32),
        jnp.zeros((key_count, HEADS * HEAD), jnp.float32),
        jnp.zeros((key_count, HEADS * HEAD), jnp.float32),
        bias_start,
    )
    return lax.fori_loop(0, HEADS // 2, backward_one_pair, start_state)


def normalize(numerator, totals):
    row_count = numerator.shape[0]
    shaped = numerator.reshape(row_count, HEADS, HEAD) / jnp.transpose(totals)[:, :, None]
    return shaped.reshape(row_count, HEADS * HEAD).astype(jnp.bfloat16)


def output_grads(out_grad, numerator, totals):
    row_count = out_grad.shape[0]
    per_total = jnp.transpose(totals)
    shaped_grad = out_grad.reshape(row_count, HEADS, HEAD)
    num_grad = (
        (shaped_grad / per_total[:, :, None]).reshape(row_count, HEADS * HEAD).astype(jnp.bfloat16)
    )
    total_grad = -jnp.sum(shaped_grad * numerator.reshape(row_count, HEADS, HEAD), axis=2) / (
        per_total * per_total
    )
    return (num_grad, jnp.transpose(total_grad))


def body(
    hidden_in,
    encoder_out,
    grad_out,
    tgt_lengths,
    enc_lengths,
    rel_bucket,
    norm1_gain,
    self_q,
    self_k,
    self_v,
    self_o,
    rel_table,
    norm2_gain,
    cross_q,
    cross_k,
    cross_v,
    cross_o,
    norm3_gain,
    ff_gate,
    ff_up,
    ff_out,
):
    w_query, w_key, w_value, w_out, c_query, c_key, c_value, c_out, w_gate, w_up, w_down = (
        lax.all_gather(self_q.astype(jnp.bfloat16), ("dp", "enc"), axis=1, tiled=True),
        lax.all_gather(self_k.astype(jnp.bfloat16), ("dp", "enc"), axis=1, tiled=True),
        lax.all_gather(self_v.astype(jnp.bfloat16), ("dp", "enc"), axis=1, tiled=True),
        lax.all_gather(self_o.astype(jnp.bfloat16), ("dp", "enc"), axis=0, tiled=True),
        lax.all_gather(cross_q.astype(jnp.bfloat16), ("dp", "enc"), axis=1, tiled=True),
        lax.all_gather(cross_k.astype(jnp.bfloat16), ("dp", "enc"), axis=1, tiled=True),
        lax.all_gather(cross_v.astype(jnp.bfloat16), ("dp", "enc"), axis=1, tiled=True),
        lax.all_gather(cross_o.astype(jnp.bfloat16), ("dp", "enc"), axis=0, tiled=True),
        lax.all_gather(ff_gate.astype(jnp.bfloat16), ("dp", "enc"), axis=1, tiled=True),
        lax.all_gather(ff_up.astype(jnp.bfloat16), ("dp", "enc"), axis=1, tiled=True),
        lax.all_gather(ff_out.astype(jnp.bfloat16), ("dp", "enc"), axis=0, tiled=True),
    )
    enc_count = lax.axis_size("enc")
    enc_place = lax.axis_index("enc")
    own_rows = hidden_in.shape[0]
    group_rows = own_rows * enc_count
    own_enc = encoder_out.shape[0]
    group_enc = own_enc * enc_count
    tgt_items = item_ids(tgt_lengths[0], group_rows)
    enc_items = item_ids(enc_lengths[0], group_enc)
    row_start = enc_place * own_rows
    own_items = lax.dynamic_slice_in_dim(tgt_items, row_start, own_rows)
    own_enc_items = lax.dynamic_slice_in_dim(enc_items, enc_place * own_enc, own_enc)
    bucket_starts = jnp.sum(
        (rel_bucket[None, :] < jnp.arange(BUCKETS, dtype=jnp.int32)[:, None]).astype(jnp.int32),
        axis=1,
    )
    query_place = row_start + jnp.arange(own_rows, dtype=jnp.int32)
    distance = query_place[:, None] - jnp.arange(group_rows, dtype=jnp.int32)[None, :]
    self_layout = (
        (distance >= 0) & (own_items[:, None] == tgt_items[None, :]),
        distance,
        (bucket_starts, rel_table),
    )
    hidden = hidden_in.astype(jnp.float32)
    normed_full, pull_one = jax.vjp(rms_scale, hidden, norm1_gain)
    normed = normed_full.astype(jnp.bfloat16)
    queries = product(normed, w_query).astype(jnp.bfloat16)
    key_own = product(normed, w_key).astype(jnp.bfloat16)
    value_own = product(normed, w_value).astype(jnp.bfloat16)
    key_group, value_group = (
        lax.all_gather(key_own, "enc", axis=0, tiled=True),
        lax.all_gather(value_own, "enc", axis=0, tiled=True),
    )
    self_num, self_top, self_total = forward_parts(queries, key_group, value_group, self_layout)
    attended = normalize(self_num, self_total)
    after_self = hidden + product(attended, w_out)
    normed_two_full, pull_two = jax.vjp(rms_scale, after_self, norm2_gain)
    normed_two = normed_two_full.astype(jnp.bfloat16)
    cross_queries = product(normed_two, c_query).astype(jnp.bfloat16)
    cross_keys = product(encoder_out, c_key).astype(jnp.bfloat16)
    cross_values = product(encoder_out, c_value).astype(jnp.bfloat16)
    query_group = lax.all_gather(cross_queries, "enc", axis=0, tiled=True)
    block_rows = min(512, group_rows)
    block_count = group_rows // block_rows

    def block_layout(first_row):
        query_items = lax.dynamic_slice_in_dim(tgt_items, first_row, block_rows)
        return (query_items[:, None] == own_enc_items[None, :], None, None)

    def block_forward(block_index, carry):
        numerator_all, top_all, total_all = carry
        first_row = block_index * block_rows
        block_num, block_top, block_total = forward_parts(
            lax.dynamic_slice_in_dim(query_group, first_row, block_rows, 0),
            cross_keys,
            cross_values,
            block_layout(first_row),
        )
        numerator_all = lax.dynamic_update_slice_in_dim(numerator_all, block_num, first_row, 0)
        top_all = lax.dynamic_update_slice_in_dim(top_all, block_top, first_row, 1)
        total_all = lax.dynamic_update_slice_in_dim(total_all, block_total, first_row, 1)
        return (numerator_all, top_all, total_all)

    numerator_all, local_tops, total_all = lax.fori_loop(
        0,
        block_count,
        block_forward,
        (
            jnp.zeros((group_rows, HEADS * HEAD), jnp.float32),
            jnp.zeros((HEADS, group_rows), jnp.float32),
            jnp.zeros((HEADS, group_rows), jnp.float32),
        ),
    )
    group_top = lax.pmax(local_tops, "enc")
    rescale = jnp.exp(local_tops - group_top)
    numerator_all = (
        numerator_all.reshape(group_rows, HEADS, HEAD) * jnp.transpose(rescale)[:, :, None]
    ).reshape(group_rows, HEADS * HEAD)
    total_all = total_all * rescale
    cross_num, cross_total = (
        lax.psum_scatter(
            numerator_all.astype(jnp.bfloat16), "enc", scatter_dimension=0, tiled=True
        ).astype(jnp.float32),
        lax.psum_scatter(
            total_all.astype(jnp.bfloat16), "enc", scatter_dimension=1, tiled=True
        ).astype(jnp.float32),
    )
    attended_two = normalize(cross_num, cross_total)
    after_cross = after_self + product(attended_two, c_out)
    normed_three_full, pull_three = jax.vjp(rms_scale, after_cross, norm3_gain)
    normed_three = normed_three_full.astype(jnp.bfloat16)
    gate_pre = product(normed_three, w_gate)
    up_pre = product(normed_three, w_up)
    activated, pull_act = jax.vjp(gated_gelu, gate_pre, up_pre)
    hidden_act = activated.astype(jnp.bfloat16)
    hidden_out = (after_cross + product(hidden_act, w_down)).astype(jnp.bfloat16)
    out_grad = grad_out.astype(jnp.float32)
    down_grad = product_tn(hidden_act, grad_out)
    act_grad = product_nt(grad_out, w_down)
    gate_grad_full, up_grad_full = pull_act(act_grad)
    gate_grad = gate_grad_full.astype(jnp.bfloat16)
    up_grad = up_grad_full.astype(jnp.bfloat16)
    gate_w_grad = product_tn(normed_three, gate_grad)
    up_w_grad = product_tn(normed_three, up_grad)
    normed_three_grad = product_nt(gate_grad, w_gate) + product_nt(up_grad, w_up)
    cross_res_grad, gain_three_grad = pull_three(normed_three_grad)
    after_cross_grad = out_grad + cross_res_grad
    branch_two = after_cross_grad.astype(jnp.bfloat16)
    c_out_grad = product_tn(attended_two, branch_two)
    cross_out_grad = product_nt(branch_two, c_out)
    cross_num_grad, cross_total_grad = output_grads(cross_out_grad, cross_num, cross_total)
    num_grad_group = lax.all_gather(cross_num_grad, "enc", axis=0, tiled=True)
    total_grad_group = lax.all_gather(cross_total_grad, "enc", axis=1, tiled=True)

    def block_backward(block_index, carry):
        query_grad_all, key_grad_sum, value_grad_sum = carry
        first_row = block_index * block_rows
        block_query_grad, block_key_grad, block_value_grad, unused_bias = backward_parts(
            lax.dynamic_slice_in_dim(query_group, first_row, block_rows, 0),
            cross_keys,
            cross_values,
            block_layout(first_row),
            lax.dynamic_slice_in_dim(group_top, first_row, block_rows, 1),
            lax.dynamic_slice_in_dim(num_grad_group, first_row, block_rows, 0),
            lax.dynamic_slice_in_dim(total_grad_group, first_row, block_rows, 1),
        )
        query_grad_all = lax.dynamic_update_slice_in_dim(
            query_grad_all, block_query_grad, first_row, 0
        )
        return (query_grad_all, key_grad_sum + block_key_grad, value_grad_sum + block_value_grad)

    query_grad_all, cross_key_grad, cross_value_grad = lax.fori_loop(
        0,
        block_count,
        block_backward,
        (
            jnp.zeros((group_rows, HEADS * HEAD), jnp.float32),
            jnp.zeros((own_enc, HEADS * HEAD), jnp.float32),
            jnp.zeros((own_enc, HEADS * HEAD), jnp.float32),
        ),
    )
    cross_query_grad = lax.psum_scatter(
        query_grad_all.astype(jnp.bfloat16), "enc", scatter_dimension=0, tiled=True
    )
    cross_key_low = cross_key_grad.astype(jnp.bfloat16)
    cross_value_low = cross_value_grad.astype(jnp.bfloat16)
    c_query_grad = product_tn(normed_two, cross_query_grad)
    c_key_grad = product_tn(encoder_out, cross_key_low)
    c_value_grad = product_tn(encoder_out, cross_value_low)
    encoder_grad = product_nt(cross_key_low, c_key) + product_nt(cross_value_low, c_value)
    self_res_grad, gain_two_grad = pull_two(product_nt(cross_query_grad, c_query))
    after_self_grad = after_cross_grad + self_res_grad
    branch_one = after_self_grad.astype(jnp.bfloat16)
    w_out_grad = product_tn(attended, branch_one)
    self_out_grad = product_nt(branch_one, w_out)
    self_num_grad, self_total_grad = output_grads(self_out_grad, self_num, self_total)
    self_query_grad, key_grad_rows, value_grad_rows, table_grad = backward_parts(
        queries, key_group, value_group, self_layout, self_top, self_num_grad, self_total_grad
    )
    self_key_grad, self_value_grad = (
        lax.psum_scatter(
            key_grad_rows.astype(jnp.bfloat16), "enc", scatter_dimension=0, tiled=True
        ).astype(jnp.float32),
        lax.psum_scatter(
            value_grad_rows.astype(jnp.bfloat16), "enc", scatter_dimension=0, tiled=True
        ).astype(jnp.float32),
    )
    query_low = self_query_grad.astype(jnp.bfloat16)
    key_low = self_key_grad.astype(jnp.bfloat16)
    value_low = self_value_grad.astype(jnp.bfloat16)
    w_query_grad = product_tn(normed, query_low)
    w_key_grad = product_tn(normed, key_low)
    w_value_grad = product_tn(normed, value_low)
    normed_grad = (
        product_nt(query_low, w_query) + product_nt(key_low, w_key) + product_nt(value_low, w_value)
    )
    input_res_grad, gain_one_grad = pull_one(normed_grad)
    hidden_grad = after_self_grad + input_res_grad
    shards = lax.axis_size(("dp", "enc"))
    full_grads = (
        w_query_grad,
        w_key_grad,
        w_value_grad,
        w_out_grad,
        c_query_grad,
        c_key_grad,
        c_value_grad,
        c_out_grad,
        gate_w_grad,
        up_w_grad,
        down_grad,
    )
    shard_dims = (1, 1, 1, 0, 1, 1, 1, 0, 1, 1, 0)
    piece_rows = tuple(
        (to_pieces(grad, place, shards) for grad, place in zip(full_grads, shard_dims))
    )
    received = (
        lax.all_to_all(
            piece_rows[0].astype(jnp.bfloat16),
            ("dp", "enc"),
            split_axis=0,
            concat_axis=0,
            tiled=True,
        ).astype(jnp.float32),
        lax.all_to_all(
            piece_rows[1].astype(jnp.bfloat16),
            ("dp", "enc"),
            split_axis=0,
            concat_axis=0,
            tiled=True,
        ).astype(jnp.float32),
        lax.all_to_all(
            piece_rows[2].astype(jnp.bfloat16),
            ("dp", "enc"),
            split_axis=0,
            concat_axis=0,
            tiled=True,
        ).astype(jnp.float32),
        lax.all_to_all(
            piece_rows[3].astype(jnp.bfloat16),
            ("dp", "enc"),
            split_axis=0,
            concat_axis=0,
            tiled=True,
        ).astype(jnp.float32),
        lax.all_to_all(
            piece_rows[4].astype(jnp.bfloat16),
            ("dp", "enc"),
            split_axis=0,
            concat_axis=0,
            tiled=True,
        ).astype(jnp.float32),
        lax.all_to_all(
            piece_rows[5].astype(jnp.bfloat16),
            ("dp", "enc"),
            split_axis=0,
            concat_axis=0,
            tiled=True,
        ).astype(jnp.float32),
        lax.all_to_all(
            piece_rows[6].astype(jnp.bfloat16),
            ("dp", "enc"),
            split_axis=0,
            concat_axis=0,
            tiled=True,
        ).astype(jnp.float32),
        lax.all_to_all(
            piece_rows[7].astype(jnp.bfloat16),
            ("dp", "enc"),
            split_axis=0,
            concat_axis=0,
            tiled=True,
        ).astype(jnp.float32),
        lax.all_to_all(
            piece_rows[8].astype(jnp.bfloat16),
            ("dp", "enc"),
            split_axis=0,
            concat_axis=0,
            tiled=True,
        ).astype(jnp.float32),
        lax.all_to_all(
            piece_rows[9].astype(jnp.bfloat16),
            ("dp", "enc"),
            split_axis=0,
            concat_axis=0,
            tiled=True,
        ).astype(jnp.float32),
        lax.all_to_all(
            piece_rows[10].astype(jnp.bfloat16),
            ("dp", "enc"),
            split_axis=0,
            concat_axis=0,
            tiled=True,
        ).astype(jnp.float32),
    )
    weight_grads = tuple(
        (
            from_pieces(piece, place, grad.shape, shards)
            for piece, place, grad in zip(received, shard_dims, full_grads)
        )
    )
    small_sums = lax.psum(
        (gain_one_grad, gain_two_grad, gain_three_grad, table_grad), ("dp", "enc")
    )
    return (
        hidden_out,
        hidden_grad,
        encoder_grad,
        small_sums[0],
        weight_grads[0],
        weight_grads[1],
        weight_grads[2],
        weight_grads[3],
        small_sums[3],
        small_sums[1],
        weight_grads[4],
        weight_grads[5],
        weight_grads[6],
        weight_grads[7],
        small_sums[2],
        weight_grads[8],
        weight_grads[9],
        weight_grads[10],
    )


def solution(mesh):
    return jax.shard_map(
        fast_body if dict(mesh.shape) == {"dp": 8, "enc": 4} else body,
        mesh=mesh,
        in_specs=(
            P(("dp", "enc"), None),
            P(("dp", "enc"), None),
            P(("dp", "enc"), None),
            P("dp", None),
            P("dp", None),
            P(),
            P(),
            P(None, ("dp", "enc")),
            P(None, ("dp", "enc")),
            P(None, ("dp", "enc")),
            P(("dp", "enc"), None),
            P(),
            P(),
            P(None, ("dp", "enc")),
            P(None, ("dp", "enc")),
            P(None, ("dp", "enc")),
            P(("dp", "enc"), None),
            P(),
            P(None, ("dp", "enc")),
            P(None, ("dp", "enc")),
            P(("dp", "enc"), None),
        ),
        out_specs=(
            P(("dp", "enc"), None),
            P(("dp", "enc"), None),
            P(("dp", "enc"), None),
            P(),
            P(None, ("dp", "enc")),
            P(None, ("dp", "enc")),
            P(None, ("dp", "enc")),
            P(("dp", "enc"), None),
            P(),
            P(),
            P(None, ("dp", "enc")),
            P(None, ("dp", "enc")),
            P(None, ("dp", "enc")),
            P(("dp", "enc"), None),
            P(),
            P(None, ("dp", "enc")),
            P(None, ("dp", "enc")),
            P(("dp", "enc"), None),
        ),
        check_vma=False,
    )
```

```python
import functools

import jax
import jax.numpy as jnp
from jax import lax
from jax.experimental import pallas as pl
from jax.experimental.pallas import tpu as pltpu
from jax.sharding import PartitionSpec as P

HEADS = 6
HEAD = 64
BUCKETS = 32
EPSILON = 1e-06
MASKED = -1e30
PAD = 16
MESH = pl.DeviceIdType.MESH
LOW = jnp.bfloat16
F32 = jnp.float32
NN = (((1,), (0,)), ((), ()))
NT = (((1,), (1,)), ((), ()))
TN = (((0,), (0,)), ((), ()))
ANY = pl.BlockSpec(memory_space=pl.ANY)
VM = pl.BlockSpec(memory_space=pltpu.VMEM)


def mm(left, right, dims=NN):
    return lax.dot_general(left, right, dims, preferred_element_type=F32)


def places():
    dp = lax.axis_index("dp")
    enc = lax.axis_index("enc")
    core = lax.rem(dp, 2)
    x = lax.rem(lax.div(dp, 2), 2)
    y = lax.div(dp, 4)
    sib = dp + 1 - 2 * core
    xn = dp + 2 - 4 * x
    yn = dp + 4 - 8 * y
    return dp, enc, sib, xn, yn


def enter(dp, enc, sib, xn, yn):
    barrier = pltpu.get_barrier_semaphore()
    targets = [(sib, enc), (xn, enc), (yn, enc), (xn + yn - dp, enc)]
    targets += [(dp, lax.rem(enc + k, 4)) for k in (1, 2, 3)]
    for target in targets:
        pl.semaphore_signal(barrier, inc=1, device_id=target, device_id_type=MESH)
    pl.semaphore_wait(barrier, len(targets))


class Sems:
    def __init__(self, send, recv):
        self.send, self.recv, self.used = send, recv, 0

    def take(self, count):
        first = self.used
        self.used += count
        return first


def remote(src, dst, send, recv, target):
    return pltpu.make_async_remote_copy(
        src_ref=src, dst_ref=dst, send_sem=send, recv_sem=recv, device_id=target, device_id_type=MESH
    )


class ZGather:
    def __init__(self, at, own, where, sems):
        self.at, self.own, self.sems = at, own, sems
        self.dp, self.enc = where[0], where[1]
        self.base = sems.take(6)

    def _copy(self, hop, side):
        s = self.sems
        place = self.enc - side * hop
        src = self.own if hop == 0 else self.at(place)
        return remote(
            src, self.at(place), s.send.at[self.base + hop + (3 if side == 1 else 0)],
            s.recv.at[self.base + place], (self.dp, self.enc + side),
        )

    def _has(self, hop, side):
        enc = self.enc
        return enc - hop >= 0 if side == 1 else enc + hop <= 3

    def _goes(self, side):
        return self.enc < 3 if side == 1 else self.enc > 0

    def start(self):
        for side in (1, -1):

            @pl.when(self._goes(side))
            def _(side=side):
                self._copy(0, side).start()

    def hop(self, hop):
        s = self.sems
        for side in (1, -1):

            @pl.when(self._has(hop, side))
            def _(side=side):
                place = self.enc - side * hop
                remote(
                    self.at(place), self.at(place), s.send.at[self.base], s.recv.at[self.base + place],
                    (self.dp, self.enc),
                ).wait_recv()

            if hop < 3:

                @pl.when(self._has(hop, side) & self._goes(side))
                def _(side=side):
                    self._copy(hop, side).start()

    def finish(self):
        for side in (1, -1):
            for hop in (0, 1, 2):

                @pl.when(self._has(hop, side) & self._goes(side))
                def _(side=side, hop=hop):
                    self._copy(hop, side).wait_send()


class ChipGather:
    def __init__(self, at, own, where, sems):
        self.at, self.own, self.sems, self.where = at, own, sems, where
        self.base = sems.take(9)

    def _copy(self, i):
        dp, enc, sib, xn, yn = self.where
        diag = xn + yn - dp
        block, part, target = (
            (dp, 0, xn),
            (dp, 0, yn),
            (dp, 0, sib),
            (xn, 0, sib),
            (yn, 0, sib),
            (xn, 1, yn),
            (yn, 2, xn),
            (diag, 1, sib),
            (diag, 2, sib),
        )[i]
        src = self.own if i < 3 else self.at(block, part)
        s = self.sems
        return remote(
            src, self.at(block, part), s.send.at[self.base + i], s.recv.at[self.base + i], (target, enc)
        )

    def step1(self):
        for i in (0, 1, 2):
            self._copy(i).start()

    def step2(self):
        self._copy(0).wait_recv()
        self._copy(5).start()
        self._copy(3).start()
        self._copy(1).wait_recv()
        self._copy(6).start()
        self._copy(4).start()

    def step3(self):
        self._copy(5).wait_recv()
        self._copy(7).start()
        self._copy(6).wait_recv()
        self._copy(8).start()

    def done(self):
        for i in (2, 3, 4, 7, 8):
            self._copy(i).wait_recv()

    def finish(self):
        for i in range(9):
            self._copy(i).wait_send()


def over(values, by):
    return lax.shift_right_logical(values * ((1 << 16) // by + 1), 16)


def regroup_matrix(count, width, block):
    shape = (4 * block, count * 4 * width)
    row = lax.broadcasted_iota(jnp.int32, shape, 0)
    col = lax.broadcasted_iota(jnp.int32, shape, 1)
    place = over(row, block)
    inside = row - place * block
    m = over(inside, width)
    take = (m * 4 + place) * width + inside - m * width
    return jnp.where((take == col) & (m < count), 1.0, 0.0).astype(LOW)


def rms_rows(values, gain):
    inv = lax.rsqrt(jnp.mean(values * values, axis=-1, keepdims=True) + EPSILON)
    return values * inv * gain


def low_lanes(rows):
    return lax.broadcasted_iota(jnp.int32, (rows, 2 * HEAD), 1) < HEAD


def one_head(pair, half):
    keep = low_lanes(pair.shape[0])
    if half:
        keep = jnp.logical_not(keep)
    return jnp.where(keep, pair.astype(F32), 0.0).astype(LOW)


def self_bias(rel_u, rows, cols):
    wide = jnp.broadcast_to(rel_u, (rows, rel_u.shape[1]))
    return pltpu.roll(wide, 0, 1, stride=1, stride_axis=0)[:, :cols]


def item_of(lengths_ref, place):
    end, item = jnp.int32(0), jnp.zeros_like(place)
    for b in range(4):
        end = end + lengths_ref[0, b]
        item = item + jnp.where(end <= place, 1, 0)
    return item


def attention_pair(q_pair, k_pair, v_pair, allowed, biases, keep_probs):
    rows = q_pair.shape[0]
    nums, totals = [], []
    for half in (0, 1):
        scores = mm(one_head(q_pair, half), k_pair, NT)
        if biases is not None:
            scores = scores + biases[half]
        scores = jnp.where(allowed, scores, MASKED)
        weights = jnp.exp(scores - jnp.max(scores, axis=1, keepdims=True))
        totals.append(jnp.sum(weights, axis=1, keepdims=True))
        probs = weights.astype(LOW)
        keep_probs(half, probs)
        nums.append(mm(probs, v_pair))
    low = low_lanes(rows)
    return jnp.where(low, nums[0], nums[1]), jnp.where(low, totals[0], totals[1])


def forward_kernel(
    width,
    tgt_len, enc_len, x_ref, e_ref, dy_ref, m0, m1, m2, m3, m4, m5, m6, m7, gate_ref, up_ref, down_ref, gain1, gain2, gain3, buckets, table,
    watt_out, wff_out, dy_out, x_out, e_out, x1_out, kv1_out, kv2_out, pr1_out, pr2_out,
    x2_out, n3_out, q1_out, q2_out, num1_out, num2_out, tot1_out, tot2_out,
    w, packed, own_att, ff_own, x_rows, e_rows, dy_rows, x1_rows, kv1, kv2, pr1, pr2, send, recv, local,
):
    where = places()
    dp, enc, sib, xn, yn = where
    sems = Sems(send, recv)
    own, wide = x_rows.shape
    own_enc = e_rows.shape[0]
    inner = HEADS * HEAD
    line = 4 * width
    ff_rows = ff_own.shape[1]
    ff_half = (ff_rows // 2 + PAD - 1) // PAD * PAD
    group = 4 * own

    def rows_at(ref, first, count):
        return ref.at[pl.ds(pl.multiple_of(first, PAD), count), :]

    def mats_at(ref, lo, hi, first, count):
        return ref.at[lo:hi, pl.ds(pl.multiple_of(first, PAD), count), :]

    zs = [
        ZGather(lambda e, g=g: packed.at[g, e], own_att.at[g], where, sems) for g in (0, 1)
    ]
    chips = []
    for lo in (0, 2, 4, 6):
        hi = lo + 2
        cuts = ((lo, hi), (lo, lo + 1), (lo + 1, hi))
        chips.append(
            ChipGather(
                lambda d, part, cuts=cuts: mats_at(w, *cuts[part], d * line, line),
                mats_at(w, lo, hi, dp * line, line), where, sems,
            )
        )
    ff_cuts = ((0, ff_rows), (0, ff_half), (ff_half, ff_rows - ff_half))
    ffs = [
        ChipGather(
            lambda d, part, m=m: mats_at(wff_out, m, m + 1, d * ff_rows + ff_cuts[part][0], ff_cuts[part][1]),
            ff_own.at[m : m + 1], where, sems,
        )
        for m in range(3)
    ]
    dyz = ZGather(lambda e: rows_at(dy_out, e * own, own), dy_rows, where, sems)
    kvz = ZGather(lambda e: rows_at(kv1, e * own, own), rows_at(kv1, enc * own, own), where, sems)
    kvz2 = ZGather(
        lambda e: rows_at(kv2, e * own_enc, own_enc), rows_at(kv2, enc * own_enc, own_enc), where, sems
    )

    def save(i, src, dst):
        return pltpu.make_async_copy(src, dst, local.at[i])

    saves = [
        save(0, dy_rows, rows_at(dy_out, enc * own, own)),
        save(1, ff_own, mats_at(wff_out, 0, 3, dp * ff_rows, ff_rows)),
        save(2, w, watt_out),
        save(3, x_rows, x_out),
        save(4, e_rows, e_out),
        save(5, x1_rows, x1_out),
        save(6, kv1, kv1_out),
        save(7, kv2, kv2_out),
        save(8, pr1, pr1_out),
        save(9, pr2, pr2_out),
    ]

    for g, refs in enumerate(((m0, m1, m2, m3), (m4, m5, m6, m7))):
        rows = jnp.concatenate([ref[...] for ref in refs], axis=0).astype(LOW)
        own_att[g] = rows
        packed[g, enc] = rows
    for m, ref in enumerate((gate_ref, up_ref, down_ref)):
        ff_own[m] = ref[...].astype(LOW)
    enter(*where)
    zs[0].start()
    ffs[0].step1()
    regroup = regroup_matrix(4, width, 4 * width)

    def unpack(g):
        rows = mm(regroup, packed[g].reshape(4 * line, wide)).astype(LOW)
        for m in range(4):
            w[4 * g + m, pl.ds(pl.multiple_of(dp * line, PAD), line), :] = rows[m * line : (m + 1) * line]

    x = jnp.transpose(x_ref[...].astype(F32))
    x_rows[...] = x.astype(LOW)
    n1 = rms_rows(x, gain1[...][None, :]).astype(LOW)
    dy_rows[...] = jnp.transpose(dy_ref[...].astype(F32)).astype(LOW)
    e_rows[...] = jnp.transpose(e_ref[...].astype(F32)).astype(LOW)
    for i in (0, 1, 3, 4):
        saves[i].start()
    rel_u = rel_rows(buckets, table, enc * own, own, group)
    zs[0].hop(1)
    zs[0].hop(2)
    zs[1].start()
    zs[0].hop(3)
    unpack(0)
    chips[0].step1()
    chips[1].step1()
    zs[1].hop(1)
    zs[1].hop(2)
    dyz.start()
    chips[0].step2()
    zs[1].hop(3)
    unpack(1)
    chips[1].step2()
    chips[2].step1()
    ffs[0].step2()
    chips[0].step3()
    dyz.hop(1)
    chips[0].done()
    own_enc_rows = pl.ds(pl.multiple_of(enc * own_enc, PAD), own_enc)
    kv2[own_enc_rows, 0:inner] = mm(e_rows[...], w[0], NT).astype(LOW)
    kv2[own_enc_rows, inner : 2 * inner] = mm(e_rows[...], w[1], NT).astype(LOW)
    kvz2.start()
    chips[3].step1()
    chips[1].step3()
    chips[1].done()
    own_rows = pl.ds(pl.multiple_of(enc * own, PAD), own)
    kv1[own_rows, 0:inner] = mm(n1, w[2], NT).astype(LOW)
    kv1[own_rows, inner : 2 * inner] = mm(n1, w[3], NT).astype(LOW)
    kvz.start()
    chips[2].step2()
    ffs[1].step1()
    kvz2.hop(1)
    chips[3].step2()
    kvz.hop(1)
    chips[2].step3()
    ffs[0].step3()
    ffs[1].step2()
    ffs[2].step1()
    kvz2.hop(2)
    kvz.hop(2)
    chips[3].step3()
    chips[2].done()
    q1 = mm(n1, w[4], NT).astype(LOW)
    q1_out[...] = q1
    kvz.hop(3)

    row_place = enc * own + lax.broadcasted_iota(jnp.int32, (own, 1), 0)
    col_place = lax.broadcasted_iota(jnp.int32, (1, group), 1)
    own_items = item_of(tgt_len, row_place)
    allowed = (own_items == item_of(tgt_len, col_place)) & (col_place <= row_place)
    for pair in range(HEADS // 2):
        lanes = slice(pair * 2 * HEAD, (pair + 1) * 2 * HEAD)
        far = slice(inner + pair * 2 * HEAD, inner + (pair + 1) * 2 * HEAD)

        def keep(half, probs, pair=pair):
            pr1[2 * pair + half] = probs

        num, total = attention_pair(
            q1[:, lanes], kv1[:, lanes], kv1[:, far], allowed,
            [self_bias(rel_u[2 * pair + half : 2 * pair + half + 1, :], own, group) for half in (0, 1)],
            keep,
        )
        num1_out[:, lanes] = num
        tot1_out[:, lanes] = total
    ffs[1].step3()
    ffs[2].step2()
    chips[3].done()
    for i in (2, 6, 8):
        saves[i].start()
    o1 = (num1_out[...] / tot1_out[...]).astype(LOW)
    x1 = x + mm(o1, w[5])
    x1_rows[...] = x1
    saves[5].start()
    n2 = rms_rows(x1, gain2[...][None, :]).astype(LOW)
    q2 = mm(n2, w[6], NT).astype(LOW)
    q2_out[...] = q2
    dyz.hop(2)
    kvz2.hop(3)
    saves[7].start()
    enc_place = lax.broadcasted_iota(jnp.int32, (1, 4 * own_enc), 1)
    allowed2 = own_items == item_of(enc_len, enc_place)
    for pair in range(HEADS // 2):
        lanes = slice(pair * 2 * HEAD, (pair + 1) * 2 * HEAD)
        far = slice(inner + pair * 2 * HEAD, inner + (pair + 1) * 2 * HEAD)

        def keep2(half, probs, pair=pair):
            pr2[2 * pair + half] = probs

        num, total = attention_pair(
            q2[:, lanes], kv2[:, lanes], kv2[:, far], allowed2, None, keep2
        )
        num2_out[:, lanes] = num
        tot2_out[:, lanes] = total
    ffs[2].step3()
    saves[9].start()
    o2 = (num2_out[...] / tot2_out[...]).astype(LOW)
    x2 = x1 + mm(o2, w[7])
    x2_out[...] = x2
    n3_out[...] = rms_rows(x2, gain3[...][None, :]).astype(LOW)
    dyz.hop(3)
    for part in ffs:
        part.done()
    for part in zs + chips + ffs + [dyz, kvz, kvz2]:
        part.finish()
    for c in saves:
        c.wait()


def sds(shape, dtype):
    return jax.ShapeDtypeStruct(shape, dtype)


def rel_rows(buckets, table, first, own, group):
    inside = bucket_rows(buckets, first, own, group, 0)
    return lax.dot_general(
        table[...], inside, NN, precision=lax.Precision.HIGHEST, preferred_element_type=F32
    )


def bucket_rows(buckets, first, own, group, turn):
    row = buckets[...][None, :]
    bucket = lax.broadcasted_iota(jnp.int32, (BUCKETS, row.shape[1]), 0)
    starts = jnp.sum(jnp.where(row < bucket, 1.0, 0.0), axis=1, keepdims=True)
    ends = jnp.sum(jnp.where(row <= bucket, 1.0, 0.0), axis=1, keepdims=True)
    k = lax.broadcasted_iota(jnp.int32, (1, group + own), 1)
    k = k - turn if turn else jnp.where(k < group, k, k - group - own)
    distance = (first - k).astype(F32)
    return jnp.where((distance >= starts) & (distance < ends), 1.0, 0.0)


def call_forward(width, tgt_len, enc_len, x, e, dy, mats, ffs, gains, buckets, table):
    wide, own = x.shape
    own_enc = e.shape[1]
    inner = HEADS * HEAD
    ff_rows = ffs[0].shape[0]
    SM = pl.BlockSpec(memory_space=pltpu.SMEM)
    saved = (
        sds((8, inner, wide), LOW),
        sds((3, 8 * ff_rows, wide), LOW),
        sds((4 * own, wide), LOW),
        sds((own, wide), LOW),
        sds((own_enc, wide), LOW),
        sds((own, wide), F32),
        sds((4 * own, 2 * inner), LOW),
        sds((4 * own_enc, 2 * inner), LOW),
        sds((HEADS, own, 4 * own), LOW),
        sds((HEADS, own, 4 * own_enc), LOW),
    )
    return pl.pallas_call(
        functools.partial(forward_kernel, width),
        out_shape=saved + (
            sds((own, wide), F32),
            sds((own, wide), LOW),
            sds((own, inner), LOW),
            sds((own, inner), LOW),
            sds((own, inner), F32),
            sds((own, inner), F32),
            sds((own, inner), F32),
            sds((own, inner), F32),
        ),
        in_specs=[SM, SM] + [VM] * 19,
        out_specs=(ANY,) * 10 + (VM,) * 8,
        scratch_shapes=[
            pltpu.VMEM((8, inner, wide), LOW),
            pltpu.VMEM((2, 4, 4 * width, wide), LOW),
            pltpu.VMEM((2, 4 * width, wide), LOW),
            pltpu.VMEM((3, ff_rows, wide), LOW),
            pltpu.VMEM((own, wide), LOW),
            pltpu.VMEM((own_enc, wide), LOW),
            pltpu.VMEM((own, wide), LOW),
            pltpu.VMEM((own, wide), F32),
            pltpu.VMEM((4 * own, 2 * inner), LOW),
            pltpu.VMEM((4 * own_enc, 2 * inner), LOW),
            pltpu.VMEM((HEADS, own, 4 * own), LOW),
            pltpu.VMEM((HEADS, own, 4 * own_enc), LOW),
            pltpu.SemaphoreType.DMA((96,)),
            pltpu.SemaphoreType.DMA((96,)),
            pltpu.SemaphoreType.DMA((10,)),
        ],
        compiler_params=pltpu.CompilerParams(
            collective_id=1, has_side_effects=True, vmem_limit_bytes=56 * 2**20
        ),
        name="attention_forward",
    )(tgt_len, enc_len, x, e, dy, *mats, *ffs, *gains, buckets, table)


class LineMeet:
    def __init__(self, src, got, meet, where, sems):
        self.src, self.got, self.meet, self.sems = src, got, meet, sems
        self.dp, self.enc = where[0], where[1]
        self.base = sems.take(4)
        self.middle = (self.enc == 1) | (self.enc == 2)
        self.far = jnp.where(self.middle, 3 * (2 - self.enc), 3 - self.enc)
        self.near = jnp.where(self.middle, 3 * (self.enc - 1), 1 + lax.div(self.enc, 2))
        self.other = jnp.where(self.middle, 3 - self.enc, 2 - lax.div(self.enc, 2))

    def _copy(self, src, dst, i, j, target):
        s = self.sems
        return remote(src, dst, s.send.at[self.base + i], s.recv.at[self.base + j], (self.dp, target))

    def _sends(self):
        src, got, meet = self.src, self.got, self.meet
        end = (
            (src.at[self.near], got.at[0], 0, 0, self.near),
            (src.at[self.other], meet.at[0], 1, 2, self.near),
            (src.at[self.far], got.at[0], 2, 0, self.far),
        )
        mid = (
            (src.at[self.far], meet.at[1], 0, 3, self.other),
            (meet.at[0], got.at[1], 1, 1, self.other),
            (meet.at[1], got.at[1], 2, 1, self.near),
        )
        return end, mid

    def ready(self, step):
        end, mid = self._sends()

        @pl.when(jnp.logical_not(self.middle))
        def _():
            self._copy(*end[step]).start()

        if step == 2:

            @pl.when(self.middle)
            def _():
                self._copy(*mid[0]).start()

    def order(self):
        return (
            jnp.where(self.middle, self.other, self.near), jnp.where(self.middle, self.near, self.other), self.far
        )

    def merge(self):
        end, mid = self._sends()

        @pl.when(self.middle)
        def _():
            for i, place in ((0, self.other), (1, self.near)):
                self._copy(self.meet.at[i], self.meet.at[i], 0, 2 + i, self.enc).wait_recv()
                self.meet[i] = (self.meet[i].astype(F32) + self.src[place].astype(F32)).astype(LOW)
                self._copy(*mid[1 + i]).start()

    def wait(self):
        for i in (0, 1):
            self._copy(self.got.at[i], self.got.at[i], 0, i, self.enc).wait_recv()

    def finish(self):
        end, mid = self._sends()

        @pl.when(jnp.logical_not(self.middle))
        def _():
            for args in end:
                self._copy(*args).wait_send()

        @pl.when(self.middle)
        def _():
            for args in mid:
                self._copy(*args).wait_send()


class ZScatter:
    def __init__(self, src_at, dst_at, where, sems, meet=None):
        self.src_at, self.dst_at, self.sems, self.meet = src_at, dst_at, sems, meet
        self.dp, self.enc = where[0], where[1]
        self.base = sems.take(3 if meet is None else 4)
        self.middle = (self.enc == 1) | (self.enc == 2)

    def _copy(self, place, merged=False):
        k = lax.rem(place - self.enc + 4, 4)
        s = self.sems
        return remote(
            self.meet if merged else self.src_at(place), self.dst_at(3 - k),
            s.send.at[self.base + k - 1], s.recv.at[self.base + 3 - k], (self.dp, place),
        )

    def _to_meet(self):
        s = self.sems
        far = 3 - self.enc
        return remote(
            self.src_at(far), self.meet, s.send.at[self.base + 3], s.recv.at[self.base + 3],
            (self.dp, 1 + lax.div(self.enc, 2)),
        )

    def start(self, place):
        self._copy(place).start()

    def start_all(self):
        enc = self.enc
        if self.meet is None:
            for k in (2, 1, 3):
                self.start(lax.rem(enc + k, 4))
            return

        @pl.when(jnp.logical_not(self.middle))
        def _():
            self._to_meet().start()
            self.start(lax.rem(enc + 2, 4))
            self.start(1 + lax.div(enc, 2))

        @pl.when(self.middle)
        def _():
            self.start(enc - 1)
            self.start(enc + 1)

    def merge(self):
        @pl.when(self.middle)
        def _():
            far = lax.rem(self.enc + 2, 4)
            self._to_meet().wait_recv()
            self.meet[...] = (self.meet[...].astype(F32) + self.src_at(far)[...].astype(F32)).astype(LOW)
            self._copy(far, merged=True).start()

    def _each(self, act):
        enc = self.enc
        if self.meet is None:
            for k in (1, 2, 3):
                act(lax.rem(enc + k, 4))
            return
        act(lax.rem(enc + 2, 4))

        @pl.when(enc > 0)
        def _():
            act(enc - 1)

        @pl.when(enc < 3)
        def _():
            act(enc + 1)

    def wait(self):
        def one(place):
            k = lax.rem(self.enc - place + 4, 4)
            s = self.sems
            remote(
                self.dst_at(3 - k), self.dst_at(3 - k), s.send.at[self.base], s.recv.at[self.base + 3 - k],
                (self.dp, self.enc),
            ).wait_recv()

        self._each(one)

    def clear(self):
        if self.meet is not None:

            @pl.when(self.enc == 0)
            def _():
                ref = self.dst_at(2)
                ref[...] = jnp.zeros(ref.shape, ref.dtype)

            @pl.when(self.enc == 3)
            def _():
                ref = self.dst_at(0)
                ref[...] = jnp.zeros(ref.shape, ref.dtype)

    def finish(self):
        self._each(lambda place: self._copy(place).wait_send())
        if self.meet is not None:

            @pl.when(jnp.logical_not(self.middle))
            def _():
                self._to_meet().wait_send()


class ChipReduce:
    def __init__(self, src, got, last, cuts, own, where, sems):
        self.src, self.got, self.last, self.cuts, self.own = src, got, last, cuts, own
        self.sems, self.where = sems, where
        self.x = lax.rem(lax.div(where[0], 2), 2)
        self.y = lax.div(where[0], 4)
        self.base = sems.take(2 * len(cuts))

    def _copy(self, i, second):
        dp, enc, sib, xn, yn = self.where
        m, lo, hi, by_x = self.cuts[i]
        s, at = self.sems, self.base + 2 * i + (1 if second else 0)
        if second:
            src = self.got.at[m, 1 - self.y if by_x else 1 - self.x, lo:hi]
            dst = self.last.at[m, lo:hi]
        else:
            src = self.src.at[m, :, 1 - self.x, lo:hi] if by_x else self.src.at[m, 1 - self.y, :, lo:hi]
            dst = self.got.at[m, :, lo:hi]
        target = xn if by_x != second else yn
        return remote(src, dst, s.send.at[at], s.recv.at[at], (target, enc))

    def start(self):
        for i in range(len(self.cuts)):
            self._copy(i, False).start()

    def turn(self):
        for i, (m, lo, hi, by_x) in enumerate(self.cuts):
            self._copy(i, False).wait_recv()
            for k in range(2):
                self.got[m, k, lo:hi] = (
                    self.own(m, k, lo, hi, by_x).astype(F32) + self.got[m, k, lo:hi].astype(F32)
                ).astype(LOW)
            self._copy(i, True).start()

    def totals(self):
        out = []
        for i, (m, lo, hi, by_x) in enumerate(self.cuts):
            self._copy(i, True).wait_recv()
            mine = self.got[m, self.y if by_x else self.x, lo:hi]
            out.append(mine.astype(F32) + self.last[m, lo:hi].astype(F32))
        return out

    def finish(self):
        for i in range(len(self.cuts)):
            self._copy(i, False).wait_send()
            self._copy(i, True).wait_send()


def rms_back(values, gain, grad):
    inv = lax.rsqrt(jnp.mean(values * values, axis=-1, keepdims=True) + EPSILON)
    scaled = grad * gain
    mean = jnp.mean(values * scaled, axis=-1, keepdims=True)
    gain_grad = jnp.sum(grad * values * inv, axis=0, keepdims=True)
    return inv * scaled - values * (inv * inv * inv * mean), gain_grad


GELU_A = 0.7978845608028654
GELU_B = 0.044715


def ff_kernel(
    n3_ref, x2_hbm, dyall_ref, wff_ref, gain3,
    dx2_out, gain_out, down_out, part_out, sums_out,
    w, n3, dy, back, act, dgate, dup, part, got, meet, grads, core_got, own_sum, out_part, chip_got, chip_last, x2_ref, send, recv, local,
):
    where = places()
    dp, enc, sib, xn, yn = where
    core = lax.rem(dp, 2)
    sems = Sems(send, recv)
    own = n3_ref.shape[0]
    ff_rows = grads.shape[4]
    ff_half = (ff_rows // 2 + PAD - 1) // PAD * PAD
    chip_x = lax.rem(lax.div(dp, 2), 2)
    chip_y = lax.div(dp, 4)

    def rows_of(place):
        return pl.ds(pl.multiple_of(place * own, PAD), own)

    gather = ZGather(lambda e: n3.at[rows_of(e), :], n3_ref, where, sems)
    scatter = LineMeet(part, got, meet, where, sems)
    loads = [
        pltpu.make_async_copy(wff_ref, w, local.at[0]),
        pltpu.make_async_copy(dyall_ref, dy, local.at[1]),
    ]
    pull = pltpu.make_async_copy(x2_hbm, x2_ref, local.at[2])
    for c in loads + [pull]:
        c.start()
    enter(*where)
    gather.start()
    n3[rows_of(enc), :] = n3_ref[...]
    for c in loads:
        c.wait()

    back[...] = mm(dy[...], w[2], NT)

    def block(place):
        rows = rows_of(place)
        normed = n3[rows, :]
        gate = mm(normed, w[0], NT)
        up = mm(normed, w[1], NT)
        dh = back[rows, :]
        square = gate * gate
        t = jnp.tanh(GELU_A * gate * (1.0 + GELU_B * square))
        half = 0.5 * (1.0 + t)
        g = gate * half
        slope = half + 0.5 * gate * (1.0 - t * t) * (GELU_A * (1.0 + 3.0 * GELU_B * square))
        hidden = (g * up).astype(LOW)
        dg = (dh * up * slope).astype(LOW)
        du = (dh * g).astype(LOW)
        act[rows, :] = hidden
        dgate[rows, :] = dg
        dup[rows, :] = du
        return mm(dg, w[0]) + mm(du, w[1])

    own_sum[...] = block(enc)
    for step, place in enumerate(scatter.order()):
        gather.hop(step + 1)
        part[place] = block(place).astype(LOW)
        scatter.ready(step)

    base = sems.take(3)

    def swap(m):
        return remote(
            grads.at[m, :, :, 1 - core], core_got.at[m], send.at[base + m], recv.at[base + m], (sib, enc)
        )

    def put_grad(m, left, right):
        whole = mm(left[...], right[...], TN).astype(LOW)
        for y in range(2):
            for x in range(2):
                for c in range(2):
                    at = (4 * y + 2 * x + c) * ff_rows
                    grads[m, y, x, c] = whole[at : at + ff_rows]
        swap(m).start()

    def sum_cores(m):
        swap(m).wait_recv()
        for y in range(2):
            core_got[m, y] = (grads[m, y, :, core].astype(F32) + core_got[m, y].astype(F32)).astype(LOW)

    down = ChipReduce(
        core_got, chip_got, chip_last, ((2, 0, ff_half, True), (2, ff_half, ff_rows, False)),
        lambda m, k, lo, hi, by_x: core_got[m, k, chip_x, lo:hi] if by_x else core_got[m, chip_y, k, lo:hi],
        where, sems,
    )
    saves = [
        pltpu.make_async_copy(out_part, part_out, local.at[0]),
        pltpu.make_async_copy(core_got.at[0:2], sums_out, local.at[1]),
    ]
    put_grad(2, act, dy)
    out_part[...] = mm(act[...], w[2]).astype(LOW)
    saves[0].start()
    sum_cores(2)
    down.start()
    put_grad(0, dgate, n3)
    put_grad(1, dup, n3)
    scatter.merge()
    sum_cores(0)
    sum_cores(1)
    saves[1].start()
    down.turn()
    scatter.wait()
    dn3 = own_sum[...] + got[0].astype(F32) + got[1].astype(F32)
    pull.wait()
    dv, gain_grad = rms_back(x2_ref[...], gain3[...][None, :], dn3)
    dx2_out[...] = dy[rows_of(enc), :].astype(F32) + dv
    gain_out[...] = gain_grad
    for (m, lo, hi, by_x), total in zip(down.cuts, down.totals()):
        down_out[lo:hi] = total
    down.finish()
    gather.finish()
    scatter.finish()
    for m in range(3):
        swap(m).wait_send()
    for c in saves:
        c.wait()


def call_ff(n3, x2, dy_all, wff, gain3):
    own, wide = n3.shape
    ff_all = wff.shape[1]
    ff_rows = ff_all // 8
    group = 4 * own
    return pl.pallas_call(
        ff_kernel,
        out_shape=(
            sds((own, wide), F32),
            sds((1, wide), F32),
            sds((ff_rows, wide), F32),
            sds((group, wide), LOW),
            sds((2, 2, 2, ff_rows, wide), LOW),
        ),
        in_specs=[VM, ANY, ANY, ANY, VM],
        out_specs=(VM, VM, VM, ANY, ANY),
        scratch_shapes=[
            pltpu.VMEM((3, ff_all, wide), LOW),
            pltpu.VMEM((group, wide), LOW),
            pltpu.VMEM((group, wide), LOW),
            pltpu.VMEM((group, ff_all), F32),
            pltpu.VMEM((group, ff_all), LOW),
            pltpu.VMEM((group, ff_all), LOW),
            pltpu.VMEM((group, ff_all), LOW),
            pltpu.VMEM((4, own, wide), LOW),
            pltpu.VMEM((2, own, wide), LOW),
            pltpu.VMEM((2, own, wide), LOW),
            pltpu.VMEM((3, 2, 2, 2, ff_rows, wide), LOW),
            pltpu.VMEM((3, 2, 2, ff_rows, wide), LOW),
            pltpu.VMEM((own, wide), F32),
            pltpu.VMEM((group, wide), LOW),
            pltpu.VMEM((3, 2, ff_rows, wide), LOW),
            pltpu.VMEM((3, ff_rows, wide), LOW),
            pltpu.VMEM((own, wide), F32),
            pltpu.SemaphoreType.DMA((17,)),
            pltpu.SemaphoreType.DMA((17,)),
            pltpu.SemaphoreType.DMA((3,)),
        ],
        compiler_params=pltpu.CompilerParams(
            collective_id=2, has_side_effects=True, vmem_limit_bytes=60 * 2**20
        ),
        name="feed_forward",
    )(n3, x2, dy_all, wff, gain3)


class CoreReduce:
    def __init__(self, lo, grads, core_got, chip_got, chip_last, where, sems):
        self.lo, self.grads, self.core_got, self.where, self.sems = lo, grads, core_got, where, sems
        self.base = sems.take(1)
        rows = grads.shape[4]
        x = lax.rem(lax.div(where[0], 2), 2)
        y = lax.div(where[0], 4)

        def own(m, k, first, last, by_x):
            return core_got[m, k, x] if by_x else core_got[m, y, k]

        self.chips = ChipReduce(
            core_got, chip_got, chip_last, ((lo, 0, rows, True), (lo + 1, 0, rows, False)), own, where, sems
        )

    def _core(self):
        dp, enc, sib, xn, yn = self.where
        s, lo = self.sems, self.lo
        return remote(
            self.grads.at[lo : lo + 2, :, :, 1 - lax.rem(dp, 2)], self.core_got.at[lo : lo + 2],
            s.send.at[self.base], s.recv.at[self.base], (sib, enc),
        )

    def start(self):
        self._core().start()

    def next(self):
        core = lax.rem(self.where[0], 2)
        self._core().wait_recv()
        for m in (self.lo, self.lo + 1):
            self.core_got[m] = (self.grads[m, :, :, core].astype(F32) + self.core_got[m].astype(F32)).astype(LOW)
        self.chips.start()

    def finish(self):
        self._core().wait_send()
        self.chips.finish()


class LineReduce:
    def __init__(self, parts, width, line, got, meet, out, where, sems):
        self.parts, self.line, self.got, self.out, self.where = parts, line, got, out, where
        self.rows = line.shape[1]
        self.regroup = regroup_matrix(2 * len(parts), width, self.rows)
        self.z = ZScatter(lambda e: line.at[e], lambda slot: got.at[slot], where, sems, meet)

    def start(self):
        totals = [t.astype(LOW) for part in self.parts for t in part.chips.totals()]
        rows = mm(self.regroup, jnp.concatenate(totals, axis=0)).astype(LOW)
        for e in range(4):
            self.line[e] = rows[e * self.rows : (e + 1) * self.rows]
        self.z.start_all()

    def merge(self):
        self.z.merge()

    def done(self):
        self.z.wait()
        total = self.line[self.where[1]].astype(F32)
        for slot in range(3):
            total = total + self.got[slot].astype(F32)
        self.out[...] = total


def backward_pair(q_pair, k_pair, v_pair, probs_ref, pair, dnum, dtotals):
    rows = q_pair.shape[0]
    parts, scores = [], []
    for half in (0, 1):
        dw = mm(one_head(dnum, half), v_pair, NT)
        ds = (probs_ref[2 * pair + half].astype(F32) * (dw + dtotals[half])).astype(LOW)
        scores.append(ds)
        parts.append(mm(ds, k_pair))
    dq = jnp.where(low_lanes(rows), parts[0], parts[1])
    dk = mm(jnp.concatenate(scores, axis=0), jnp.concatenate([one_head(q_pair, h) for h in (0, 1)], axis=0), TN)
    probs = jnp.concatenate([probs_ref[2 * pair + h] for h in (0, 1)], axis=0)
    dv = mm(probs, jnp.concatenate([one_head(dnum, h) for h in (0, 1)], axis=0), TN)
    return dq, dk, dv, scores


def total_grads(product, total):
    low = low_lanes(product.shape[0])
    out = []
    for half in (0, 1):
        keep = low if half == 0 else jnp.logical_not(low)
        top = jnp.sum(jnp.where(keep, product, 0.0), axis=1, keepdims=True)
        tot = total[:, half * HEAD : half * HEAD + 1]
        out.append(-top / (tot * tot))
    return out


def backward_kernel(
    width,
    gain1, gain2, gain3_grad, buckets, q1, q2, num2, tot2,
    watt_ref, sums_ref, part_hbm, dx2_hbm, kv2_hbm, pr2_hbm, num1_hbm, tot1_hbm, x_hbm, e_hbm, x1_hbm, x2_hbm, kv1_hbm, pr1_hbm,
    att_out, small_out, hidden_out, hidden_grad, encoder_grad, gate_out, up_out,
    w, grads, core_got, chip_got, chip_last, line, line_got, line_meet,
    ff_own, ff_got, ff_last, part_got, part_meet,
    kvp1, kvp1_got, kvp1_meet, kvp2, kvp2_got, kvp2_meet, dq, vec, vec_got,
    part_ref, dx2_ref, kv2, pr2, num1, tot1, x_ref, e_ref, x1_ref, x2_ref, kv1, pr1, out_t, grad_t, enc_t, ff_sum, send, recv, local,
):
    where = places()
    dp, enc, sib, xn, yn = where
    sems = Sems(send, recv)
    own, wide = x_ref.shape
    own_enc = e_ref.shape[0]
    inner = HEADS * HEAD
    chip_x = lax.rem(lax.div(dp, 2), 2)
    chip_y = lax.div(dp, 4)
    ff_rows = ff_last.shape[1]
    part_rows = own * 3 // 8

    out_z = [
        ZScatter(
            lambda e, a=a, b=b: part_ref.at[e, a:b], lambda slot, a=a, b=b: part_got.at[slot, a:b],
            where, sems, part_meet.at[a:b],
        )
        for a, b in ((0, part_rows), (part_rows, own))
    ]
    kv1_z = ZScatter(lambda e: kvp1.at[e], lambda slot: kvp1_got.at[slot], where, sems, kvp1_meet)
    kv2_z = ZScatter(lambda e: kvp2.at[e], lambda slot: kvp2_got.at[slot], where, sems, kvp2_meet)
    batches = [CoreReduce(lo, grads, core_got, chip_got, chip_last, where, sems) for lo in (0, 2, 4, 6)]
    lines = [
        LineReduce(batches[2 * i : 2 * i + 2], width, line.at[i], line_got.at[i], line_meet.at[i], att_out.at[i], where, sems)
        for i in (0, 1)
    ]
    ff_cuts = ((0, 0, ff_rows, True), (1, 0, ff_rows, False))
    ff = ChipReduce(
        sums_ref, ff_got, ff_last, ff_cuts, lambda m, k, lo, hi, by_x: ff_own[m, k, lo:hi], where, sems
    )
    vec_base = sems.take(3)
    vec_z = ZScatter(lambda e: vec.at[3], lambda slot: vec_got.at[3 + slot], where, sems)

    def vec_copy(i):
        target = (sib, xn, yn)[i]
        return remote(
            vec.at[i], vec_got.at[i], send.at[vec_base + i], recv.at[vec_base + i], (target, enc)
        )

    def load(slot, m, i):
        return pltpu.make_async_copy(watt_ref.at[m], w.at[slot], local.at[i])

    pulls = [
        pltpu.make_async_copy(src, dst, local.at[12 + i])
        for i, (src, dst) in enumerate(
            (
                (part_hbm, part_ref), (x1_hbm, x1_ref), (kv1_hbm, kv1), (pr1_hbm, pr1), (x_hbm, x_ref),
                (e_hbm, e_ref), (x2_hbm, x2_ref), (dx2_hbm, dx2_ref), (kv2_hbm, kv2), (pr2_hbm, pr2),
                (num1_hbm, num1), (tot1_hbm, tot1),
            )
        )
    ]
    pushes = [
        pltpu.make_async_copy(src, dst, local.at[24 + i])
        for i, (src, dst) in enumerate(
            ((grad_t, hidden_grad), (enc_t, encoder_grad), (ff_sum.at[0], gate_out), (out_t, hidden_out), (ff_sum.at[1], up_out))
        )
    ]
    first_loads = [load(slot, m, slot) for slot, m in enumerate((7, 6, 5, 2, 3))]
    for c in [pulls[7], first_loads[0], pulls[0]] + pulls[8:10] + first_loads[1:3] + pulls[1:7] + pulls[10:] + first_loads[3:]:
        c.start()
    own_ff = [
        pltpu.make_async_copy(
            sums_ref.at[m, :, chip_x, lo:hi] if by_x else sums_ref.at[m, chip_y, :, lo:hi],
            ff_own.at[m, :, lo:hi], local.at[8 + i],
        )
        for i, (m, lo, hi, by_x) in enumerate(ff_cuts)
    ]
    for c in own_ff:
        c.start()
    enter(*where)
    pulls[0].wait()
    out_z[0].start_all()
    ff.start()
    for part in out_z + [kv1_z, kv2_z] + [line.z for line in lines]:
        part.clear()

    def put_grad(m, left, right):
        whole = mm(left, right, TN).astype(LOW)
        rows = 4 * width
        for y in range(2):
            for x in range(2):
                for c in range(2):
                    at = (4 * y + 2 * x + c) * rows
                    grads[m, y, x, c] = whole[at : at + rows]

    pulls[7].wait()
    b2 = dx2_ref[...].astype(LOW)
    first_loads[0].wait()
    do2 = mm(b2, w[0], NT)
    dnum2 = (do2 / tot2[...]).astype(LOW)
    prod2 = do2 * num2[...]
    pulls[8].wait()
    pulls[9].wait()
    for pair in range(HEADS // 2):
        lanes = slice(pair * 2 * HEAD, (pair + 1) * 2 * HEAD)
        far = slice(inner + pair * 2 * HEAD, inner + (pair + 1) * 2 * HEAD)
        dtot = total_grads(prod2[:, lanes], tot2[:, lanes])
        dq_pair, dk, dv, _ = backward_pair(
            q2[:, lanes], kv2[:, lanes], kv2[:, far], pr2, pair, dnum2[:, lanes], dtot
        )
        dq[:, lanes] = dq_pair.astype(LOW)
        for e in range(4):
            kvp2[e, :, lanes] = dk[e * own_enc : (e + 1) * own_enc].astype(LOW)
            kvp2[e, :, far] = dv[e * own_enc : (e + 1) * own_enc].astype(LOW)
    kv2_z.start_all()
    dq2 = dq[...]
    put_grad(0, (num2[...] / tot2[...]).astype(LOW), b2)
    pulls[1].wait()
    x1 = x1_ref[...]
    put_grad(1, dq2, rms_rows(x1, gain2[...][None, :]).astype(LOW))
    batches[0].start()
    out_z[0].merge()
    first_loads[1].wait()
    dv2, gain2_grad = rms_back(x1, gain2[...][None, :], mm(dq2, w[1]))
    dx1 = dx2_ref[...] + dv2
    b1 = dx1.astype(LOW)
    first_loads[2].wait()
    do1 = mm(b1, w[2], NT)
    late = [load(2, 4, 5), load(0, 0, 6), load(1, 1, 7)]
    for c in late:
        c.start()
    pulls[10].wait()
    pulls[11].wait()
    dnum1 = (do1 / tot1[...]).astype(LOW)
    prod1 = do1 * num1[...]
    batches[0].next()
    pulls[2].wait()
    pulls[3].wait()
    all_scores = []
    for pair in range(HEADS // 2):
        lanes = slice(pair * 2 * HEAD, (pair + 1) * 2 * HEAD)
        far = slice(inner + pair * 2 * HEAD, inner + (pair + 1) * 2 * HEAD)
        dtot = total_grads(prod1[:, lanes], tot1[:, lanes])
        dq_pair, dk, dv, scores = backward_pair(
            q1[:, lanes], kv1[:, lanes], kv1[:, far], pr1, pair, dnum1[:, lanes], dtot
        )
        dq[:, lanes] = dq_pair.astype(LOW)
        for e in range(4):
            kvp1[e, :, lanes] = dk[e * own : (e + 1) * own].astype(LOW)
            kvp1[e, :, far] = dv[e * own : (e + 1) * own].astype(LOW)
        all_scores += scores
    kv1_z.start_all()
    out_z[1].start_all()
    dq1 = dq[...]
    pulls[4].wait()
    x = x_ref[...].astype(F32)
    n1 = rms_rows(x, gain1[...][None, :]).astype(LOW)
    put_grad(2, (num1[...] / tot1[...]).astype(LOW), b1)
    put_grad(3, dq1, n1)
    batches[1].start()
    kv2_z.merge()
    batches[1].next()
    for c in own_ff:
        c.wait()
    ff.turn()
    vec[0] = jnp.zeros(vec.shape[1:], F32)
    inside = bucket_rows(buckets, enc * own, own, 4 * own, own - 1)
    flip_row = lax.broadcasted_iota(jnp.int32, (own, own), 0)
    flip_col = lax.broadcasted_iota(jnp.int32, (own, own), 1)
    flip = jnp.where(flip_row + flip_col == own - 1, 1.0, 0.0).astype(LOW)
    for h, ds in enumerate(all_scores):
        long = jnp.concatenate([mm(flip, ds), jnp.zeros((own, own), F32)], axis=1)
        turned = pltpu.roll(long, 0, 1, stride=1, stride_axis=0)
        by_distance = jnp.sum(turned, axis=0, keepdims=True)
        vec[0, 8 + h : 9 + h, 0:BUCKETS] = lax.dot_general(
            by_distance, inside, NT, precision=lax.Precision.HIGHEST, preferred_element_type=F32
        )
    batches[0].chips.turn()
    for c in late:
        c.wait()
    dn1 = mm(dq1, w[2])
    batches[1].chips.turn()

    kv2_z.wait()
    low2 = (
        kvp2[enc].astype(F32) + kvp2_got[0].astype(F32) + kvp2_got[1].astype(F32) + kvp2_got[2].astype(F32)
    ).astype(LOW)
    dk2 = low2[:, :inner]
    dv2 = low2[:, inner:]
    pulls[5].wait()
    put_grad(4, dk2, e_ref[...])
    put_grad(5, dv2, e_ref[...])
    batches[2].start()
    kv1_z.merge()
    lines[0].start()
    batches[2].next()
    enc_t[...] = jnp.transpose(mm(dk2, w[0]) + mm(dv2, w[1]))
    pushes[1].start()

    kv1_z.wait()
    low1 = (
        kvp1[enc].astype(F32) + kvp1_got[0].astype(F32) + kvp1_got[1].astype(F32) + kvp1_got[2].astype(F32)
    ).astype(LOW)
    dk1 = low1[:, :inner]
    dv1 = low1[:, inner:]
    put_grad(6, dk1, n1)
    put_grad(7, dv1, n1)
    batches[3].start()
    batches[2].chips.turn()
    batches[3].next()
    first_loads[3].wait()
    first_loads[4].wait()
    dn1 = dn1 + mm(dk1, w[3]) + mm(dv1, w[4])
    dv_x, gain1_grad = rms_back(x, gain1[...][None, :], dn1)
    vec[0, 0:1, :] = gain1_grad
    vec[0, 1:2, :] = gain2_grad
    vec[0, 2:3, :] = gain3_grad[...]
    vec_copy(0).start()
    out_z[1].merge()
    batches[3].chips.turn()
    vec_copy(0).wait_recv()
    vec[1] = vec[0] + vec_got[0]
    vec_copy(1).start()
    grad_t[...] = jnp.transpose(dx1 + dv_x)
    pushes[0].start()
    lines[1].start()
    lines[0].merge()
    vec_copy(1).wait_recv()
    vec[2] = vec[1] + vec_got[1]
    vec_copy(2).start()
    vec_copy(2).wait_recv()
    vec[3] = vec[2] + vec_got[2]
    vec_z.start_all()
    for (m, lo, hi, by_x), total in zip(ff_cuts, ff.totals()):
        ff_sum[m, lo:hi] = total
    pushes[2].start()
    pushes[4].start()
    lines[1].merge()
    lines[0].done()
    for z in out_z:
        z.wait()
    pulls[6].wait()
    out_t[...] = jnp.transpose(
        x2_ref[...] + (part_ref[enc].astype(F32) + part_got[0].astype(F32))
        + (part_got[1].astype(F32) + part_got[2].astype(F32))
    ).astype(LOW)
    pushes[3].start()
    lines[1].done()
    vec_z.wait()
    small_out[...] = vec[3] + vec_got[3] + vec_got[4] + vec_got[5]
    for done in out_z + [kv1_z, kv2_z, vec_z, ff] + batches + [line.z for line in lines]:
        done.finish()
    for i in range(3):
        vec_copy(i).wait_send()
    for c in pushes:
        c.wait()


def call_backward(width, gain1, gain2, gain3_grad, buckets, small, watt, sums, part, dx2, kv2, pr2, num1, tot1, x, e, x1, x2, kv1, pr1):
    own, wide = x.shape
    own_enc = e.shape[0]
    inner = HEADS * HEAD
    rows = 4 * width
    ff_rows = sums.shape[3]
    return pl.pallas_call(
        functools.partial(backward_kernel, width),
        out_shape=(
            sds((2, 4 * width, wide), F32),
            sds((16, wide), F32),
            sds((wide, own), LOW),
            sds((wide, own), F32),
            sds((wide, own_enc), F32),
            sds((ff_rows, wide), F32),
            sds((ff_rows, wide), F32),
        ),
        in_specs=[VM] * 8 + [ANY] * 14,
        out_specs=(VM,) * 2 + (ANY,) * 5,
        scratch_shapes=[
            pltpu.VMEM((5, inner, wide), LOW),
            pltpu.VMEM((8, 2, 2, 2, rows, wide), LOW),
            pltpu.VMEM((8, 2, 2, rows, wide), LOW),
            pltpu.VMEM((8, 2, rows, wide), LOW),
            pltpu.VMEM((8, rows, wide), LOW),
            pltpu.VMEM((2, 4, 4 * width, wide), LOW),
            pltpu.VMEM((2, 3, 4 * width, wide), LOW),
            pltpu.VMEM((2, 4 * width, wide), LOW),
            pltpu.VMEM((2, 2, ff_rows, wide), LOW),
            pltpu.VMEM((2, 2, ff_rows, wide), LOW),
            pltpu.VMEM((2, ff_rows, wide), LOW),
            pltpu.VMEM((3, own, wide), LOW),
            pltpu.VMEM((own, wide), LOW),
            pltpu.VMEM((4, own, 2 * inner), LOW),
            pltpu.VMEM((3, own, 2 * inner), LOW),
            pltpu.VMEM((own, 2 * inner), LOW),
            pltpu.VMEM((4, own_enc, 2 * inner), LOW),
            pltpu.VMEM((3, own_enc, 2 * inner), LOW),
            pltpu.VMEM((own_enc, 2 * inner), LOW),
            pltpu.VMEM((own, inner), LOW),
            pltpu.VMEM((4, 16, wide), F32),
            pltpu.VMEM((6, 16, wide), F32),
            pltpu.VMEM((4, own, wide), LOW),
            pltpu.VMEM((own, wide), F32),
            pltpu.VMEM(kv2.shape, LOW),
            pltpu.VMEM(pr2.shape, LOW),
            pltpu.VMEM((own, inner), F32),
            pltpu.VMEM((own, inner), F32),
            pltpu.VMEM((own, wide), LOW),
            pltpu.VMEM((own_enc, wide), LOW),
            pltpu.VMEM((own, wide), F32),
            pltpu.VMEM((own, wide), F32),
            pltpu.VMEM(kv1.shape, LOW),
            pltpu.VMEM(pr1.shape, LOW),
            pltpu.VMEM((wide, own), LOW),
            pltpu.VMEM((wide, own), F32),
            pltpu.VMEM((wide, own_enc), F32),
            pltpu.VMEM((2, ff_rows, wide), F32),
            pltpu.SemaphoreType.DMA((64,)),
            pltpu.SemaphoreType.DMA((64,)),
            pltpu.SemaphoreType.DMA((29,)),
        ],
        compiler_params=pltpu.CompilerParams(
            collective_id=3, has_side_effects=True, vmem_limit_bytes=62 * 2**20
        ),
        name="attention_backward",
    )(
        gain1, gain2, gain3_grad, buckets, *small, watt, sums,
        part.reshape(4, own, wide), dx2, kv2, pr2, num1, tot1, x, e, x1, x2, kv1, pr1,
    )


def outputs_kernel(width, *refs):
    big, (att, small) = refs[:6], refs[6:8]
    outs, rows, gains, table = refs[8:14], refs[14:22], refs[22:25], refs[25]
    held, (att_v, small_v), sem = refs[26:32], refs[32:34], refs[34]
    pulls = [pltpu.make_async_copy(a, b, sem.at[i]) for i, (a, b) in enumerate(zip((att, small) + big, (att_v, small_v) + held))]
    pushes = [pltpu.make_async_copy(a, b, sem.at[8 + i]) for i, (a, b) in enumerate(zip(held, outs))]
    for c in pulls:
        c.start()
    pulls[0].wait()
    pulls[1].wait()
    for i, ref in enumerate(rows):
        m = i % 4
        ref[...] = att_v[i // 4, m * width : (m + 1) * width]
    for i, ref in enumerate(gains):
        ref[...] = small_v[i]
    table[...] = small_v[8 : 8 + HEADS, 0:BUCKETS]
    for pull, push in zip(pulls[2:], pushes):
        pull.wait()
        push.start()
    for push in pushes:
        push.wait()


def call_outputs(width, big, att, small):
    wide = att.shape[2]
    return pl.pallas_call(
        functools.partial(outputs_kernel, width),
        out_shape=tuple(sds(a.shape, a.dtype) for a in big)
        + (sds((width, wide), F32),) * 8
        + (sds((wide,), F32),) * 3
        + (sds((HEADS, BUCKETS), F32),),
        in_specs=[ANY] * 8,
        out_specs=(ANY,) * 6 + (VM,) * 12,
        scratch_shapes=[pltpu.VMEM(a.shape, a.dtype) for a in tuple(big) + (att, small)]
        + [pltpu.SemaphoreType.DMA((14,))],
        compiler_params=pltpu.CompilerParams(vmem_limit_bytes=62 * 2**20),
        name="results",
    )(*big, att, small)


def fast_body(
    hidden_in, encoder_out, grad_out, tgt_lengths, enc_lengths, rel_bucket, norm1_gain,
    self_q, self_k, self_v, self_o, rel_table, norm2_gain,
    cross_q, cross_k, cross_v, cross_o, norm3_gain, ff_gate, ff_up, ff_out,
):
    width = self_q.shape[1]
    mats = (cross_k.T, cross_v.T, self_k.T, self_v.T, self_q.T, self_o, cross_q.T, cross_o)
    (
        watt_all, wff_all, dy_all, x, e, x1, kv1, kv2, pr1, pr2,
        x2, n3, q1, q2, num1, num2, tot1, tot2,
    ) = call_forward(
        width, tgt_lengths, enc_lengths, hidden_in.T, encoder_out.T, grad_out.T, mats,
        (ff_gate.T, ff_up.T, ff_out), (norm1_gain, norm2_gain, norm3_gain), rel_bucket, rel_table.T,
    )
    dx2, gain3_grad, down, part, sums = call_ff(n3, x2, dy_all, wff_all, norm3_gain)
    att, small, hidden_out, hidden_grad, encoder_grad, gate, up = call_backward(
        width, norm1_gain, norm2_gain, gain3_grad, rel_bucket, (q1, q2, num2, tot2),
        watt_all, sums, part, dx2, kv2, pr2, num1, tot1, x, e, x1, x2, kv1, pr1,
    )
    (
        hidden_out, hidden_grad, encoder_grad, gate, up, down,
        o2, q2, o1, q1, k2, v2, k1, v1, g1, g2, g3, table,
    ) = call_outputs(width, (hidden_out, hidden_grad, encoder_grad, gate, up, down), att, small)
    return (
        hidden_out.T, hidden_grad.T, encoder_grad.T, g1, q1.T, k1.T, v1.T, o1, table.T,
        g2, q2.T, k2.T, v2.T, o2, g3, gate.T, up.T, down,
    )


def rms_scale(values, gain):
    return values * lax.rsqrt(jnp.mean(values * values, axis=-1, keepdims=True) + EPSILON) * gain


def gated_gelu(gate_pre, up_pre):
    return jax.nn.gelu(gate_pre, approximate=True) * up_pre


def item_ids(lengths, total_rows):
    ends = jnp.cumsum(lengths)
    places = jnp.arange(total_rows, dtype=jnp.int32)
    return jnp.sum((ends[None, :] <= places[:, None]).astype(jnp.int32), axis=1)


def product(left, right):
    return jnp.dot(left, right, preferred_element_type=jnp.float32)


def product_tn(left, right):
    return lax.dot_general(
        left, right, (((0,), (0,)), ((), ())), preferred_element_type=jnp.float32
    )


def product_nt(left, right):
    return lax.dot_general(
        left, right, (((1,), (1,)), ((), ())), preferred_element_type=jnp.float32
    )


def to_pieces(grad, shard_dim, shards):
    if shard_dim == 0:
        return grad.reshape(shards, -1)
    rows = grad.shape[0]
    return jnp.transpose(grad.reshape(rows, shards, -1), (1, 0, 2)).reshape(shards, -1)


def from_pieces(received, shard_dim, shape, shards):
    summed = jnp.sum(received, axis=0)
    if shard_dim == 0:
        return summed.reshape(shape[0] // shards, shape[1])
    return summed.reshape(shape[0], shape[1] // shards)


def head_pair(matrix, pair_index):
    return lax.dynamic_slice_in_dim(matrix, pair_index * 2 * HEAD, 2 * HEAD, 1).reshape(
        matrix.shape[0], 2, HEAD
    )


def pair_stats(stats, pair_index):
    return lax.dynamic_slice_in_dim(stats, pair_index * 2, 2, 0)


def relative_bias(distance, bias_info, pair_index):
    starts, table = bias_info
    table_pair = lax.dynamic_slice_in_dim(table, pair_index * 2, 2, 1)

    def add_step(bucket, total):
        rise = table_pair[bucket] - table_pair[bucket - 1]
        return total + jnp.where(distance[None] >= starts[bucket], rise[:, None, None], 0.0)

    start_bias = jnp.broadcast_to(table_pair[0][:, None, None], (2,) + distance.shape)
    return lax.fori_loop(1, BUCKETS, add_step, start_bias)


def relative_grads(distance, starts, score_grad):

    def one_step(bucket):
        return jnp.sum(jnp.where(distance[None] >= starts[bucket], score_grad, 0.0), axis=(1, 2))

    steps_sum = lax.map(one_step, jnp.arange(BUCKETS, dtype=jnp.int32))
    return steps_sum - jnp.concatenate([steps_sum[1:], jnp.zeros((1, 2), jnp.float32)], axis=0)


def pair_scores(query_block, key_rows, pair_index, layout):
    allowed, distance, bias_info = layout
    scores = jnp.einsum(
        "qhe,khe->hqk",
        head_pair(query_block, pair_index),
        head_pair(key_rows, pair_index),
        preferred_element_type=jnp.float32,
    )
    if bias_info is not None:
        scores = scores + relative_bias(distance, bias_info, pair_index)
    return jnp.where(allowed[None], scores, MASKED)


def forward_parts(query_block, key_rows, value_rows, layout):
    block_rows = query_block.shape[0]
    width = 2 * HEAD

    def forward_one_pair(pair_index, carry):
        numerator, largest, totals = carry
        scores = pair_scores(query_block, key_rows, pair_index, layout)
        pair_top = jnp.max(scores, axis=2)
        weights = jnp.exp(scores - pair_top[:, :, None])
        partial_sum = jnp.einsum(
            "hqk,khe->qhe",
            weights.astype(jnp.bfloat16),
            head_pair(value_rows, pair_index),
            preferred_element_type=jnp.float32,
        )
        numerator = lax.dynamic_update_slice_in_dim(
            numerator, partial_sum.reshape(block_rows, width), pair_index * width, 1
        )
        largest = lax.dynamic_update_slice_in_dim(largest, pair_top, pair_index * 2, 0)
        totals = lax.dynamic_update_slice_in_dim(
            totals, jnp.sum(weights, axis=2), pair_index * 2, 0
        )
        return (numerator, largest, totals)

    start_state = (
        jnp.zeros((block_rows, HEADS * HEAD), jnp.float32),
        jnp.zeros((HEADS, block_rows), jnp.float32),
        jnp.zeros((HEADS, block_rows), jnp.float32),
    )
    return lax.fori_loop(0, HEADS // 2, forward_one_pair, start_state)


def backward_parts(query_block, key_rows, value_rows, layout, top_rows, num_grad, total_grad):
    allowed, distance, bias_info = layout
    block_rows = query_block.shape[0]
    key_count = key_rows.shape[0]
    width = 2 * HEAD

    def backward_one_pair(pair_index, carry):
        query_grad, key_grad, value_grad, bias_grad = carry
        query_pair = head_pair(query_block, pair_index)
        key_pair = head_pair(key_rows, pair_index)
        value_pair = head_pair(value_rows, pair_index)
        grad_pair = head_pair(num_grad, pair_index)
        scores = pair_scores(query_block, key_rows, pair_index, layout)
        weights = jnp.exp(scores - pair_stats(top_rows, pair_index)[:, :, None])
        weight_grad = jnp.einsum(
            "qhe,khe->hqk", grad_pair, value_pair, preferred_element_type=jnp.float32
        )
        score_grad = (
            weights * (weight_grad + pair_stats(total_grad, pair_index)[:, :, None])
        ).astype(jnp.bfloat16)
        part_query = jnp.einsum(
            "hqk,khe->qhe", score_grad, key_pair, preferred_element_type=jnp.float32
        )
        part_key = jnp.einsum(
            "hqk,qhe->khe", score_grad, query_pair, preferred_element_type=jnp.float32
        )
        part_value = jnp.einsum(
            "hqk,qhe->khe",
            weights.astype(jnp.bfloat16),
            grad_pair,
            preferred_element_type=jnp.float32,
        )
        query_grad = lax.dynamic_update_slice_in_dim(
            query_grad, part_query.reshape(block_rows, width), pair_index * width, 1
        )
        key_grad = lax.dynamic_update_slice_in_dim(
            key_grad, part_key.reshape(key_count, width), pair_index * width, 1
        )
        value_grad = lax.dynamic_update_slice_in_dim(
            value_grad, part_value.reshape(key_count, width), pair_index * width, 1
        )
        if bias_info is not None:
            pair_bias_grad = relative_grads(distance, bias_info[0], score_grad.astype(jnp.float32))
            bias_grad = lax.dynamic_update_slice_in_dim(
                bias_grad, pair_bias_grad, pair_index * 2, 1
            )
        return (query_grad, key_grad, value_grad, bias_grad)

    bias_start = None if bias_info is None else jnp.zeros((BUCKETS, HEADS), jnp.float32)
    start_state = (
        jnp.zeros((block_rows, HEADS * HEAD), jnp.float32),
        jnp.zeros((key_count, HEADS * HEAD), jnp.float32),
        jnp.zeros((key_count, HEADS * HEAD), jnp.float32),
        bias_start,
    )
    return lax.fori_loop(0, HEADS // 2, backward_one_pair, start_state)


def normalize(numerator, totals):
    row_count = numerator.shape[0]
    shaped = numerator.reshape(row_count, HEADS, HEAD) / jnp.transpose(totals)[:, :, None]
    return shaped.reshape(row_count, HEADS * HEAD).astype(jnp.bfloat16)


def output_grads(out_grad, numerator, totals):
    row_count = out_grad.shape[0]
    per_total = jnp.transpose(totals)
    shaped_grad = out_grad.reshape(row_count, HEADS, HEAD)
    num_grad = (
        (shaped_grad / per_total[:, :, None]).reshape(row_count, HEADS * HEAD).astype(jnp.bfloat16)
    )
    total_grad = -jnp.sum(shaped_grad * numerator.reshape(row_count, HEADS, HEAD), axis=2) / (
        per_total * per_total
    )
    return (num_grad, jnp.transpose(total_grad))


def body(
    hidden_in,
    encoder_out,
    grad_out,
    tgt_lengths,
    enc_lengths,
    rel_bucket,
    norm1_gain,
    self_q,
    self_k,
    self_v,
    self_o,
    rel_table,
    norm2_gain,
    cross_q,
    cross_k,
    cross_v,
    cross_o,
    norm3_gain,
    ff_gate,
    ff_up,
    ff_out,
):
    w_query, w_key, w_value, w_out, c_query, c_key, c_value, c_out, w_gate, w_up, w_down = (
        lax.all_gather(self_q.astype(jnp.bfloat16), ("dp", "enc"), axis=1, tiled=True),
        lax.all_gather(self_k.astype(jnp.bfloat16), ("dp", "enc"), axis=1, tiled=True),
        lax.all_gather(self_v.astype(jnp.bfloat16), ("dp", "enc"), axis=1, tiled=True),
        lax.all_gather(self_o.astype(jnp.bfloat16), ("dp", "enc"), axis=0, tiled=True),
        lax.all_gather(cross_q.astype(jnp.bfloat16), ("dp", "enc"), axis=1, tiled=True),
        lax.all_gather(cross_k.astype(jnp.bfloat16), ("dp", "enc"), axis=1, tiled=True),
        lax.all_gather(cross_v.astype(jnp.bfloat16), ("dp", "enc"), axis=1, tiled=True),
        lax.all_gather(cross_o.astype(jnp.bfloat16), ("dp", "enc"), axis=0, tiled=True),
        lax.all_gather(ff_gate.astype(jnp.bfloat16), ("dp", "enc"), axis=1, tiled=True),
        lax.all_gather(ff_up.astype(jnp.bfloat16), ("dp", "enc"), axis=1, tiled=True),
        lax.all_gather(ff_out.astype(jnp.bfloat16), ("dp", "enc"), axis=0, tiled=True),
    )
    enc_count = lax.axis_size("enc")
    enc_place = lax.axis_index("enc")
    own_rows = hidden_in.shape[0]
    group_rows = own_rows * enc_count
    own_enc = encoder_out.shape[0]
    group_enc = own_enc * enc_count
    tgt_items = item_ids(tgt_lengths[0], group_rows)
    enc_items = item_ids(enc_lengths[0], group_enc)
    row_start = enc_place * own_rows
    own_items = lax.dynamic_slice_in_dim(tgt_items, row_start, own_rows)
    own_enc_items = lax.dynamic_slice_in_dim(enc_items, enc_place * own_enc, own_enc)
    bucket_starts = jnp.sum(
        (rel_bucket[None, :] < jnp.arange(BUCKETS, dtype=jnp.int32)[:, None]).astype(jnp.int32),
        axis=1,
    )
    query_place = row_start + jnp.arange(own_rows, dtype=jnp.int32)
    distance = query_place[:, None] - jnp.arange(group_rows, dtype=jnp.int32)[None, :]
    self_layout = (
        (distance >= 0) & (own_items[:, None] == tgt_items[None, :]),
        distance,
        (bucket_starts, rel_table),
    )
    hidden = hidden_in.astype(jnp.float32)
    normed_full, pull_one = jax.vjp(rms_scale, hidden, norm1_gain)
    normed = normed_full.astype(jnp.bfloat16)
    queries = product(normed, w_query).astype(jnp.bfloat16)
    key_own = product(normed, w_key).astype(jnp.bfloat16)
    value_own = product(normed, w_value).astype(jnp.bfloat16)
    key_group, value_group = (
        lax.all_gather(key_own, "enc", axis=0, tiled=True),
        lax.all_gather(value_own, "enc", axis=0, tiled=True),
    )
    self_num, self_top, self_total = forward_parts(queries, key_group, value_group, self_layout)
    attended = normalize(self_num, self_total)
    after_self = hidden + product(attended, w_out)
    normed_two_full, pull_two = jax.vjp(rms_scale, after_self, norm2_gain)
    normed_two = normed_two_full.astype(jnp.bfloat16)
    cross_queries = product(normed_two, c_query).astype(jnp.bfloat16)
    cross_keys = product(encoder_out, c_key).astype(jnp.bfloat16)
    cross_values = product(encoder_out, c_value).astype(jnp.bfloat16)
    query_group = lax.all_gather(cross_queries, "enc", axis=0, tiled=True)
    block_rows = min(512, group_rows)
    block_count = group_rows // block_rows

    def block_layout(first_row):
        query_items = lax.dynamic_slice_in_dim(tgt_items, first_row, block_rows)
        return (query_items[:, None] == own_enc_items[None, :], None, None)

    def block_forward(block_index, carry):
        numerator_all, top_all, total_all = carry
        first_row = block_index * block_rows
        block_num, block_top, block_total = forward_parts(
            lax.dynamic_slice_in_dim(query_group, first_row, block_rows, 0),
            cross_keys,
            cross_values,
            block_layout(first_row),
        )
        numerator_all = lax.dynamic_update_slice_in_dim(numerator_all, block_num, first_row, 0)
        top_all = lax.dynamic_update_slice_in_dim(top_all, block_top, first_row, 1)
        total_all = lax.dynamic_update_slice_in_dim(total_all, block_total, first_row, 1)
        return (numerator_all, top_all, total_all)

    numerator_all, local_tops, total_all = lax.fori_loop(
        0,
        block_count,
        block_forward,
        (
            jnp.zeros((group_rows, HEADS * HEAD), jnp.float32),
            jnp.zeros((HEADS, group_rows), jnp.float32),
            jnp.zeros((HEADS, group_rows), jnp.float32),
        ),
    )
    group_top = lax.pmax(local_tops, "enc")
    rescale = jnp.exp(local_tops - group_top)
    numerator_all = (
        numerator_all.reshape(group_rows, HEADS, HEAD) * jnp.transpose(rescale)[:, :, None]
    ).reshape(group_rows, HEADS * HEAD)
    total_all = total_all * rescale
    cross_num, cross_total = (
        lax.psum_scatter(
            numerator_all.astype(jnp.bfloat16), "enc", scatter_dimension=0, tiled=True
        ).astype(jnp.float32),
        lax.psum_scatter(
            total_all.astype(jnp.bfloat16), "enc", scatter_dimension=1, tiled=True
        ).astype(jnp.float32),
    )
    attended_two = normalize(cross_num, cross_total)
    after_cross = after_self + product(attended_two, c_out)
    normed_three_full, pull_three = jax.vjp(rms_scale, after_cross, norm3_gain)
    normed_three = normed_three_full.astype(jnp.bfloat16)
    gate_pre = product(normed_three, w_gate)
    up_pre = product(normed_three, w_up)
    activated, pull_act = jax.vjp(gated_gelu, gate_pre, up_pre)
    hidden_act = activated.astype(jnp.bfloat16)
    hidden_out = (after_cross + product(hidden_act, w_down)).astype(jnp.bfloat16)
    out_grad = grad_out.astype(jnp.float32)
    down_grad = product_tn(hidden_act, grad_out)
    act_grad = product_nt(grad_out, w_down)
    gate_grad_full, up_grad_full = pull_act(act_grad)
    gate_grad = gate_grad_full.astype(jnp.bfloat16)
    up_grad = up_grad_full.astype(jnp.bfloat16)
    gate_w_grad = product_tn(normed_three, gate_grad)
    up_w_grad = product_tn(normed_three, up_grad)
    normed_three_grad = product_nt(gate_grad, w_gate) + product_nt(up_grad, w_up)
    cross_res_grad, gain_three_grad = pull_three(normed_three_grad)
    after_cross_grad = out_grad + cross_res_grad
    branch_two = after_cross_grad.astype(jnp.bfloat16)
    c_out_grad = product_tn(attended_two, branch_two)
    cross_out_grad = product_nt(branch_two, c_out)
    cross_num_grad, cross_total_grad = output_grads(cross_out_grad, cross_num, cross_total)
    num_grad_group = lax.all_gather(cross_num_grad, "enc", axis=0, tiled=True)
    total_grad_group = lax.all_gather(cross_total_grad, "enc", axis=1, tiled=True)

    def block_backward(block_index, carry):
        query_grad_all, key_grad_sum, value_grad_sum = carry
        first_row = block_index * block_rows
        block_query_grad, block_key_grad, block_value_grad, unused_bias = backward_parts(
            lax.dynamic_slice_in_dim(query_group, first_row, block_rows, 0),
            cross_keys,
            cross_values,
            block_layout(first_row),
            lax.dynamic_slice_in_dim(group_top, first_row, block_rows, 1),
            lax.dynamic_slice_in_dim(num_grad_group, first_row, block_rows, 0),
            lax.dynamic_slice_in_dim(total_grad_group, first_row, block_rows, 1),
        )
        query_grad_all = lax.dynamic_update_slice_in_dim(
            query_grad_all, block_query_grad, first_row, 0
        )
        return (query_grad_all, key_grad_sum + block_key_grad, value_grad_sum + block_value_grad)

    query_grad_all, cross_key_grad, cross_value_grad = lax.fori_loop(
        0,
        block_count,
        block_backward,
        (
            jnp.zeros((group_rows, HEADS * HEAD), jnp.float32),
            jnp.zeros((own_enc, HEADS * HEAD), jnp.float32),
            jnp.zeros((own_enc, HEADS * HEAD), jnp.float32),
        ),
    )
    cross_query_grad = lax.psum_scatter(
        query_grad_all.astype(jnp.bfloat16), "enc", scatter_dimension=0, tiled=True
    )
    cross_key_low = cross_key_grad.astype(jnp.bfloat16)
    cross_value_low = cross_value_grad.astype(jnp.bfloat16)
    c_query_grad = product_tn(normed_two, cross_query_grad)
    c_key_grad = product_tn(encoder_out, cross_key_low)
    c_value_grad = product_tn(encoder_out, cross_value_low)
    encoder_grad = product_nt(cross_key_low, c_key) + product_nt(cross_value_low, c_value)
    self_res_grad, gain_two_grad = pull_two(product_nt(cross_query_grad, c_query))
    after_self_grad = after_cross_grad + self_res_grad
    branch_one = after_self_grad.astype(jnp.bfloat16)
    w_out_grad = product_tn(attended, branch_one)
    self_out_grad = product_nt(branch_one, w_out)
    self_num_grad, self_total_grad = output_grads(self_out_grad, self_num, self_total)
    self_query_grad, key_grad_rows, value_grad_rows, table_grad = backward_parts(
        queries, key_group, value_group, self_layout, self_top, self_num_grad, self_total_grad
    )
    self_key_grad, self_value_grad = (
        lax.psum_scatter(
            key_grad_rows.astype(jnp.bfloat16), "enc", scatter_dimension=0, tiled=True
        ).astype(jnp.float32),
        lax.psum_scatter(
            value_grad_rows.astype(jnp.bfloat16), "enc", scatter_dimension=0, tiled=True
        ).astype(jnp.float32),
    )
    query_low = self_query_grad.astype(jnp.bfloat16)
    key_low = self_key_grad.astype(jnp.bfloat16)
    value_low = self_value_grad.astype(jnp.bfloat16)
    w_query_grad = product_tn(normed, query_low)
    w_key_grad = product_tn(normed, key_low)
    w_value_grad = product_tn(normed, value_low)
    normed_grad = (
        product_nt(query_low, w_query) + product_nt(key_low, w_key) + product_nt(value_low, w_value)
    )
    input_res_grad, gain_one_grad = pull_one(normed_grad)
    hidden_grad = after_self_grad + input_res_grad
    shards = lax.axis_size(("dp", "enc"))
    full_grads = (
        w_query_grad,
        w_key_grad,
        w_value_grad,
        w_out_grad,
        c_query_grad,
        c_key_grad,
        c_value_grad,
        c_out_grad,
        gate_w_grad,
        up_w_grad,
        down_grad,
    )
    shard_dims = (1, 1, 1, 0, 1, 1, 1, 0, 1, 1, 0)
    piece_rows = tuple(
        (to_pieces(grad, place, shards) for grad, place in zip(full_grads, shard_dims))
    )
    received = (
        lax.all_to_all(
            piece_rows[0].astype(jnp.bfloat16),
            ("dp", "enc"),
            split_axis=0,
            concat_axis=0,
            tiled=True,
        ).astype(jnp.float32),
        lax.all_to_all(
            piece_rows[1].astype(jnp.bfloat16),
            ("dp", "enc"),
            split_axis=0,
            concat_axis=0,
            tiled=True,
        ).astype(jnp.float32),
        lax.all_to_all(
            piece_rows[2].astype(jnp.bfloat16),
            ("dp", "enc"),
            split_axis=0,
            concat_axis=0,
            tiled=True,
        ).astype(jnp.float32),
        lax.all_to_all(
            piece_rows[3].astype(jnp.bfloat16),
            ("dp", "enc"),
            split_axis=0,
            concat_axis=0,
            tiled=True,
        ).astype(jnp.float32),
        lax.all_to_all(
            piece_rows[4].astype(jnp.bfloat16),
            ("dp", "enc"),
            split_axis=0,
            concat_axis=0,
            tiled=True,
        ).astype(jnp.float32),
        lax.all_to_all(
            piece_rows[5].astype(jnp.bfloat16),
            ("dp", "enc"),
            split_axis=0,
            concat_axis=0,
            tiled=True,
        ).astype(jnp.float32),
        lax.all_to_all(
            piece_rows[6].astype(jnp.bfloat16),
            ("dp", "enc"),
            split_axis=0,
            concat_axis=0,
            tiled=True,
        ).astype(jnp.float32),
        lax.all_to_all(
            piece_rows[7].astype(jnp.bfloat16),
            ("dp", "enc"),
            split_axis=0,
            concat_axis=0,
            tiled=True,
        ).astype(jnp.float32),
        lax.all_to_all(
            piece_rows[8].astype(jnp.bfloat16),
            ("dp", "enc"),
            split_axis=0,
            concat_axis=0,
            tiled=True,
        ).astype(jnp.float32),
        lax.all_to_all(
            piece_rows[9].astype(jnp.bfloat16),
            ("dp", "enc"),
            split_axis=0,
            concat_axis=0,
            tiled=True,
        ).astype(jnp.float32),
        lax.all_to_all(
            piece_rows[10].astype(jnp.bfloat16),
            ("dp", "enc"),
            split_axis=0,
            concat_axis=0,
            tiled=True,
        ).astype(jnp.float32),
    )
    weight_grads = tuple(
        (
            from_pieces(piece, place, grad.shape, shards)
            for piece, place, grad in zip(received, shard_dims, full_grads)
        )
    )
    small_sums = lax.psum(
        (gain_one_grad, gain_two_grad, gain_three_grad, table_grad), ("dp", "enc")
    )
    return (
        hidden_out,
        hidden_grad,
        encoder_grad,
        small_sums[0],
        weight_grads[0],
        weight_grads[1],
        weight_grads[2],
        weight_grads[3],
        small_sums[3],
        small_sums[1],
        weight_grads[4],
        weight_grads[5],
        weight_grads[6],
        weight_grads[7],
        small_sums[2],
        weight_grads[8],
        weight_grads[9],
        weight_grads[10],
    )


def solution(mesh):
    return jax.shard_map(
        fast_body if dict(mesh.shape) == {"dp": 8, "enc": 4} else body,
        mesh=mesh,
        in_specs=(
            P(("dp", "enc"), None),
            P(("dp", "enc"), None),
            P(("dp", "enc"), None),
            P("dp", None),
            P("dp", None),
            P(),
            P(),
            P(None, ("dp", "enc")),
            P(None, ("dp", "enc")),
            P(None, ("dp", "enc")),
            P(("dp", "enc"), None),
            P(),
            P(),
            P(None, ("dp", "enc")),
            P(None, ("dp", "enc")),
            P(None, ("dp", "enc")),
            P(("dp", "enc"), None),
            P(),
            P(None, ("dp", "enc")),
            P(None, ("dp", "enc")),
            P(("dp", "enc"), None),
        ),
        out_specs=(
            P(("dp", "enc"), None),
            P(("dp", "enc"), None),
            P(("dp", "enc"), None),
            P(),
            P(None, ("dp", "enc")),
            P(None, ("dp", "enc")),
            P(None, ("dp", "enc")),
            P(("dp", "enc"), None),
            P(),
            P(),
            P(None, ("dp", "enc")),
            P(None, ("dp", "enc")),
            P(None, ("dp", "enc")),
            P(("dp", "enc"), None),
            P(),
            P(None, ("dp", "enc")),
            P(None, ("dp", "enc")),
            P(("dp", "enc"), None),
        ),
        check_vma=False,
    )
```

```python
import functools

import jax
import jax.numpy as jnp
from jax import lax
from jax.experimental import pallas as pl
from jax.experimental.pallas import tpu as pltpu
from jax.sharding import PartitionSpec as P

HEADS = 6
HEAD = 64
BUCKETS = 32
EPSILON = 1e-06
MASKED = -1e30
PAD = 16
MESH = pl.DeviceIdType.MESH
LOW = jnp.bfloat16
F32 = jnp.float32
NN = (((1,), (0,)), ((), ()))
NT = (((1,), (1,)), ((), ()))
TN = (((0,), (0,)), ((), ()))
ANY = pl.BlockSpec(memory_space=pl.ANY)
VM = pl.BlockSpec(memory_space=pltpu.VMEM)


def mm(left, right, dims=NN):
    return lax.dot_general(left, right, dims, preferred_element_type=F32)


def places():
    dp = lax.axis_index("dp")
    enc = lax.axis_index("enc")
    core = lax.rem(dp, 2)
    x = lax.rem(lax.div(dp, 2), 2)
    y = lax.div(dp, 4)
    sib = dp + 1 - 2 * core
    xn = dp + 2 - 4 * x
    yn = dp + 4 - 8 * y
    return dp, enc, sib, xn, yn


def enter(dp, enc, sib, xn, yn):
    barrier = pltpu.get_barrier_semaphore()
    targets = [(sib, enc), (xn, enc), (yn, enc), (xn + yn - dp, enc)]
    targets += [(dp, lax.rem(enc + k, 4)) for k in (1, 2, 3)]
    for target in targets:
        pl.semaphore_signal(barrier, inc=1, device_id=target, device_id_type=MESH)
    pl.semaphore_wait(barrier, len(targets))


class Sems:
    def __init__(self, send, recv):
        self.send, self.recv, self.used = send, recv, 0

    def take(self, count):
        first = self.used
        self.used += count
        return first


def remote(src, dst, send, recv, target):
    return pltpu.make_async_remote_copy(
        src_ref=src, dst_ref=dst, send_sem=send, recv_sem=recv, device_id=target, device_id_type=MESH
    )


class ZGather:
    def __init__(self, at, own, where, sems):
        self.at, self.own, self.sems = at, own, sems
        self.dp, self.enc = where[0], where[1]
        self.base = sems.take(6)

    def _copy(self, hop, side):
        s = self.sems
        place = self.enc - side * hop
        src = self.own if hop == 0 else self.at(place)
        return remote(
            src, self.at(place), s.send.at[self.base + hop + (3 if side == 1 else 0)],
            s.recv.at[self.base + place], (self.dp, self.enc + side),
        )

    def _has(self, hop, side):
        enc = self.enc
        return enc - hop >= 0 if side == 1 else enc + hop <= 3

    def _goes(self, side):
        return self.enc < 3 if side == 1 else self.enc > 0

    def start(self):
        for side in (1, -1):

            @pl.when(self._goes(side))
            def _(side=side):
                self._copy(0, side).start()

    def hop(self, hop):
        s = self.sems
        for side in (1, -1):

            @pl.when(self._has(hop, side))
            def _(side=side):
                place = self.enc - side * hop
                remote(
                    self.at(place), self.at(place), s.send.at[self.base], s.recv.at[self.base + place],
                    (self.dp, self.enc),
                ).wait_recv()

            if hop < 3:

                @pl.when(self._has(hop, side) & self._goes(side))
                def _(side=side):
                    self._copy(hop, side).start()

    def finish(self):
        for side in (1, -1):
            for hop in (0, 1, 2):

                @pl.when(self._has(hop, side) & self._goes(side))
                def _(side=side, hop=hop):
                    self._copy(hop, side).wait_send()


class ChipGather:
    def __init__(self, at, own, where, sems):
        self.at, self.own, self.sems, self.where = at, own, sems, where
        self.base = sems.take(9)

    def _copy(self, i):
        dp, enc, sib, xn, yn = self.where
        diag = xn + yn - dp
        block, part, target = (
            (dp, 0, xn),
            (dp, 0, yn),
            (dp, 0, sib),
            (xn, 0, sib),
            (yn, 0, sib),
            (xn, 1, yn),
            (yn, 2, xn),
            (diag, 1, sib),
            (diag, 2, sib),
        )[i]
        src = self.own if i < 3 else self.at(block, part)
        s = self.sems
        return remote(
            src, self.at(block, part), s.send.at[self.base + i], s.recv.at[self.base + i], (target, enc)
        )

    def step1(self):
        for i in (0, 1, 2):
            self._copy(i).start()

    def step2(self):
        self._copy(0).wait_recv()
        self._copy(5).start()
        self._copy(3).start()
        self._copy(1).wait_recv()
        self._copy(6).start()
        self._copy(4).start()

    def step3(self):
        self._copy(5).wait_recv()
        self._copy(7).start()
        self._copy(6).wait_recv()
        self._copy(8).start()

    def done(self):
        for i in (2, 3, 4, 7, 8):
            self._copy(i).wait_recv()

    def finish(self):
        for i in range(9):
            self._copy(i).wait_send()


def over(values, by):
    return lax.shift_right_logical(values * ((1 << 16) // by + 1), 16)


def regroup_matrix(count, width, block):
    shape = (4 * block, count * 4 * width)
    row = lax.broadcasted_iota(jnp.int32, shape, 0)
    col = lax.broadcasted_iota(jnp.int32, shape, 1)
    place = over(row, block)
    inside = row - place * block
    m = over(inside, width)
    take = (m * 4 + place) * width + inside - m * width
    return jnp.where((take == col) & (m < count), 1.0, 0.0).astype(LOW)


def rms_rows(values, gain):
    inv = lax.rsqrt(jnp.mean(values * values, axis=-1, keepdims=True) + EPSILON)
    return values * inv * gain


def low_lanes(rows):
    return lax.broadcasted_iota(jnp.int32, (rows, 2 * HEAD), 1) < HEAD


def one_head(pair, half):
    keep = low_lanes(pair.shape[0])
    if half:
        keep = jnp.logical_not(keep)
    return jnp.where(keep, pair.astype(F32), 0.0).astype(LOW)


def self_bias(rel_u, rows, cols):
    wide = jnp.broadcast_to(rel_u, (rows, rel_u.shape[1]))
    return pltpu.roll(wide, 0, 1, stride=1, stride_axis=0)[:, :cols]


def item_of(lengths_ref, place):
    end, item = jnp.int32(0), jnp.zeros_like(place)
    for b in range(4):
        end = end + lengths_ref[0, b]
        item = item + jnp.where(end <= place, 1, 0)
    return item


def attention_pair(q_pair, k_pair, v_pair, allowed, biases, keep_probs):
    rows = q_pair.shape[0]
    nums, totals = [], []
    for half in (0, 1):
        scores = mm(one_head(q_pair, half), k_pair, NT)
        if biases is not None:
            scores = scores + biases[half]
        scores = jnp.where(allowed, scores, MASKED)
        weights = jnp.exp(scores - jnp.max(scores, axis=1, keepdims=True))
        totals.append(jnp.sum(weights, axis=1, keepdims=True))
        probs = weights.astype(LOW)
        keep_probs(half, probs)
        nums.append(mm(probs, v_pair))
    low = low_lanes(rows)
    return jnp.where(low, nums[0], nums[1]), jnp.where(low, totals[0], totals[1])


def forward_kernel(
    width,
    tgt_len, enc_len, x_ref, e_ref, dy_ref, m0, m1, m2, m3, m4, m5, m6, m7, gate_ref, up_ref, down_ref, gain1, gain2, gain3, buckets, table,
    watt_out, wff_out, dy_out, x_out, e_out, x1_out, kv1_out, kv2_out, pr1_out, pr2_out,
    x2_out, n3_out, q1_out, q2_out, num1_out, num2_out, tot1_out, tot2_out,
    w, packed, own_att, ff_own, x_rows, e_rows, dy_rows, x1_rows, kv1, kv2, pr1, pr2, send, recv, local,
):
    where = places()
    dp, enc, sib, xn, yn = where
    sems = Sems(send, recv)
    own, wide = x_rows.shape
    own_enc = e_rows.shape[0]
    inner = HEADS * HEAD
    line = 4 * width
    ff_rows = ff_own.shape[1]
    ff_half = (ff_rows // 2 + PAD - 1) // PAD * PAD
    group = 4 * own

    def rows_at(ref, first, count):
        return ref.at[pl.ds(pl.multiple_of(first, PAD), count), :]

    def mats_at(ref, lo, hi, first, count):
        return ref.at[lo:hi, pl.ds(pl.multiple_of(first, PAD), count), :]

    zs = [
        ZGather(lambda e, g=g: packed.at[g, e], own_att.at[g], where, sems) for g in (0, 1)
    ]
    chips = []
    for lo in (0, 2, 4, 6):
        hi = lo + 2
        cuts = ((lo, hi), (lo, lo + 1), (lo + 1, hi))
        chips.append(
            ChipGather(
                lambda d, part, cuts=cuts: mats_at(w, *cuts[part], d * line, line),
                mats_at(w, lo, hi, dp * line, line), where, sems,
            )
        )
    ff_cuts = ((0, ff_rows), (0, ff_half), (ff_half, ff_rows - ff_half))
    ffs = [
        ChipGather(
            lambda d, part, m=m: mats_at(wff_out, m, m + 1, d * ff_rows + ff_cuts[part][0], ff_cuts[part][1]),
            ff_own.at[m : m + 1], where, sems,
        )
        for m in range(3)
    ]
    dyz = ZGather(lambda e: rows_at(dy_out, e * own, own), dy_rows, where, sems)
    kvz = ZGather(lambda e: rows_at(kv1, e * own, own), rows_at(kv1, enc * own, own), where, sems)
    kvz2 = ZGather(
        lambda e: rows_at(kv2, e * own_enc, own_enc), rows_at(kv2, enc * own_enc, own_enc), where, sems
    )

    def save(i, src, dst):
        return pltpu.make_async_copy(src, dst, local.at[i])

    saves = [
        save(0, dy_rows, rows_at(dy_out, enc * own, own)),
        save(1, ff_own, mats_at(wff_out, 0, 3, dp * ff_rows, ff_rows)),
        save(2, w, watt_out),
        save(3, x_rows, x_out),
        save(4, e_rows, e_out),
        save(5, x1_rows, x1_out),
        save(6, kv1, kv1_out),
        save(7, kv2, kv2_out),
        save(8, pr1, pr1_out),
        save(9, pr2, pr2_out),
    ]

    for g, refs in enumerate(((m0, m1, m2, m3), (m4, m5, m6, m7))):
        rows = jnp.concatenate([ref[...] for ref in refs], axis=0).astype(LOW)
        own_att[g] = rows
        packed[g, enc] = rows
    for m, ref in enumerate((gate_ref, up_ref, down_ref)):
        ff_own[m] = ref[...].astype(LOW)
    enter(*where)
    zs[0].start()
    zs[1].start()
    ffs[0].step1()
    regroup = regroup_matrix(4, width, 4 * width)

    def unpack(g):
        rows = mm(regroup, packed[g].reshape(4 * line, wide)).astype(LOW)
        for m in range(4):
            w[4 * g + m, pl.ds(pl.multiple_of(dp * line, PAD), line), :] = rows[m * line : (m + 1) * line]

    x = jnp.transpose(x_ref[...].astype(F32))
    x_rows[...] = x.astype(LOW)
    n1 = rms_rows(x, gain1[...][None, :]).astype(LOW)
    dy_rows[...] = jnp.transpose(dy_ref[...].astype(F32)).astype(LOW)
    e_rows[...] = jnp.transpose(e_ref[...].astype(F32)).astype(LOW)
    for i in (0, 1, 3, 4):
        saves[i].start()
    rel_u = rel_rows(buckets, table, enc * own, own, group)
    zs[0].hop(1)
    zs[0].hop(2)
    zs[1].hop(1)
    zs[0].hop(3)
    unpack(0)
    chips[0].step1()
    chips[1].step1()
    zs[1].hop(2)
    dyz.start()
    zs[1].hop(3)
    chips[0].step2()
    unpack(1)
    chips[1].step2()
    chips[2].step1()
    ffs[0].step2()
    chips[0].step3()
    dyz.hop(1)
    chips[0].done()
    own_enc_rows = pl.ds(pl.multiple_of(enc * own_enc, PAD), own_enc)
    kv2[own_enc_rows, 0:inner] = mm(e_rows[...], w[0], NT).astype(LOW)
    kv2[own_enc_rows, inner : 2 * inner] = mm(e_rows[...], w[1], NT).astype(LOW)
    kvz2.start()
    chips[3].step1()
    chips[1].step3()
    chips[1].done()
    own_rows = pl.ds(pl.multiple_of(enc * own, PAD), own)
    kv1[own_rows, 0:inner] = mm(n1, w[2], NT).astype(LOW)
    kv1[own_rows, inner : 2 * inner] = mm(n1, w[3], NT).astype(LOW)
    kvz.start()
    chips[2].step2()
    kvz2.hop(1)
    chips[3].step2()
    ffs[1].step1()
    ffs[2].step1()
    kvz.hop(1)
    chips[2].step3()
    ffs[0].step3()
    chips[2].done()
    q1 = mm(n1, w[4], NT).astype(LOW)
    q1_out[...] = q1
    kvz2.hop(2)
    kvz.hop(2)
    dyz.hop(2)
    chips[3].step3()
    ffs[1].step2()
    kvz.hop(3)

    row_place = enc * own + lax.broadcasted_iota(jnp.int32, (own, 1), 0)
    col_place = lax.broadcasted_iota(jnp.int32, (1, group), 1)
    own_items = item_of(tgt_len, row_place)
    allowed = (own_items == item_of(tgt_len, col_place)) & (col_place <= row_place)
    for pair in range(HEADS // 2):
        lanes = slice(pair * 2 * HEAD, (pair + 1) * 2 * HEAD)
        far = slice(inner + pair * 2 * HEAD, inner + (pair + 1) * 2 * HEAD)

        def keep(half, probs, pair=pair):
            pr1[2 * pair + half] = probs

        num, total = attention_pair(
            q1[:, lanes], kv1[:, lanes], kv1[:, far], allowed,
            [self_bias(rel_u[2 * pair + half : 2 * pair + half + 1, :], own, group) for half in (0, 1)],
            keep,
        )
        num1_out[:, lanes] = num
        tot1_out[:, lanes] = total
    ffs[1].step3()
    ffs[2].step2()
    chips[3].done()
    for i in (2, 6, 8):
        saves[i].start()
    o1 = (num1_out[...] / tot1_out[...]).astype(LOW)
    x1 = x + mm(o1, w[5])
    x1_rows[...] = x1
    saves[5].start()
    n2 = rms_rows(x1, gain2[...][None, :]).astype(LOW)
    q2 = mm(n2, w[6], NT).astype(LOW)
    q2_out[...] = q2
    kvz2.hop(3)
    saves[7].start()
    enc_place = lax.broadcasted_iota(jnp.int32, (1, 4 * own_enc), 1)
    allowed2 = own_items == item_of(enc_len, enc_place)
    for pair in range(HEADS // 2):
        lanes = slice(pair * 2 * HEAD, (pair + 1) * 2 * HEAD)
        far = slice(inner + pair * 2 * HEAD, inner + (pair + 1) * 2 * HEAD)

        def keep2(half, probs, pair=pair):
            pr2[2 * pair + half] = probs

        num, total = attention_pair(
            q2[:, lanes], kv2[:, lanes], kv2[:, far], allowed2, None, keep2
        )
        num2_out[:, lanes] = num
        tot2_out[:, lanes] = total
    ffs[2].step3()
    saves[9].start()
    o2 = (num2_out[...] / tot2_out[...]).astype(LOW)
    x2 = x1 + mm(o2, w[7])
    x2_out[...] = x2
    n3_out[...] = rms_rows(x2, gain3[...][None, :]).astype(LOW)
    dyz.hop(3)
    for part in ffs:
        part.done()
    for part in zs + chips + ffs + [dyz, kvz, kvz2]:
        part.finish()
    for c in saves:
        c.wait()


def sds(shape, dtype):
    return jax.ShapeDtypeStruct(shape, dtype)


def rel_rows(buckets, table, first, own, group):
    inside = bucket_rows(buckets, first, own, group, 0)
    return lax.dot_general(
        table[...], inside, NN, precision=lax.Precision.HIGHEST, preferred_element_type=F32
    )


def bucket_rows(buckets, first, own, group, turn):
    row = buckets[...][None, :]
    bucket = lax.broadcasted_iota(jnp.int32, (BUCKETS, row.shape[1]), 0)
    starts = jnp.sum(jnp.where(row < bucket, 1.0, 0.0), axis=1, keepdims=True)
    ends = jnp.sum(jnp.where(row <= bucket, 1.0, 0.0), axis=1, keepdims=True)
    k = lax.broadcasted_iota(jnp.int32, (1, group + own), 1)
    k = k - turn if turn else jnp.where(k < group, k, k - group - own)
    distance = (first - k).astype(F32)
    return jnp.where((distance >= starts) & (distance < ends), 1.0, 0.0)


def call_forward(width, tgt_len, enc_len, x, e, dy, mats, ffs, gains, buckets, table):
    wide, own = x.shape
    own_enc = e.shape[1]
    inner = HEADS * HEAD
    ff_rows = ffs[0].shape[0]
    SM = pl.BlockSpec(memory_space=pltpu.SMEM)
    saved = (
        sds((8, inner, wide), LOW),
        sds((3, 8 * ff_rows, wide), LOW),
        sds((4 * own, wide), LOW),
        sds((own, wide), LOW),
        sds((own_enc, wide), LOW),
        sds((own, wide), F32),
        sds((4 * own, 2 * inner), LOW),
        sds((4 * own_enc, 2 * inner), LOW),
        sds((HEADS, own, 4 * own), LOW),
        sds((HEADS, own, 4 * own_enc), LOW),
    )
    return pl.pallas_call(
        functools.partial(forward_kernel, width),
        out_shape=saved + (
            sds((own, wide), F32),
            sds((own, wide), LOW),
            sds((own, inner), LOW),
            sds((own, inner), LOW),
            sds((own, inner), F32),
            sds((own, inner), F32),
            sds((own, inner), F32),
            sds((own, inner), F32),
        ),
        in_specs=[SM, SM] + [VM] * 19,
        out_specs=(ANY,) * 10 + (VM,) * 8,
        scratch_shapes=[
            pltpu.VMEM((8, inner, wide), LOW),
            pltpu.VMEM((2, 4, 4 * width, wide), LOW),
            pltpu.VMEM((2, 4 * width, wide), LOW),
            pltpu.VMEM((3, ff_rows, wide), LOW),
            pltpu.VMEM((own, wide), LOW),
            pltpu.VMEM((own_enc, wide), LOW),
            pltpu.VMEM((own, wide), LOW),
            pltpu.VMEM((own, wide), F32),
            pltpu.VMEM((4 * own, 2 * inner), LOW),
            pltpu.VMEM((4 * own_enc, 2 * inner), LOW),
            pltpu.VMEM((HEADS, own, 4 * own), LOW),
            pltpu.VMEM((HEADS, own, 4 * own_enc), LOW),
            pltpu.SemaphoreType.DMA((96,)),
            pltpu.SemaphoreType.DMA((96,)),
            pltpu.SemaphoreType.DMA((10,)),
        ],
        compiler_params=pltpu.CompilerParams(
            collective_id=1, has_side_effects=True, vmem_limit_bytes=56 * 2**20
        ),
        name="attention_forward",
    )(tgt_len, enc_len, x, e, dy, *mats, *ffs, *gains, buckets, table)


class LineMeet:
    def __init__(self, src, got, meet, where, sems):
        self.src, self.got, self.meet, self.sems = src, got, meet, sems
        self.dp, self.enc = where[0], where[1]
        self.base = sems.take(4)
        self.middle = (self.enc == 1) | (self.enc == 2)
        self.far = jnp.where(self.middle, 3 * (2 - self.enc), 3 - self.enc)
        self.near = jnp.where(self.middle, 3 * (self.enc - 1), 1 + lax.div(self.enc, 2))
        self.other = jnp.where(self.middle, 3 - self.enc, 2 - lax.div(self.enc, 2))

    def _copy(self, src, dst, i, j, target):
        s = self.sems
        return remote(src, dst, s.send.at[self.base + i], s.recv.at[self.base + j], (self.dp, target))

    def _sends(self):
        src, got, meet = self.src, self.got, self.meet
        end = (
            (src.at[self.near], got.at[0], 0, 0, self.near),
            (src.at[self.other], meet.at[0], 1, 2, self.near),
            (src.at[self.far], got.at[0], 2, 0, self.far),
        )
        mid = (
            (src.at[self.far], meet.at[1], 0, 3, self.other),
            (meet.at[0], got.at[1], 1, 1, self.other),
            (meet.at[1], got.at[1], 2, 1, self.near),
        )
        return end, mid

    def ready(self, step):
        end, mid = self._sends()

        @pl.when(jnp.logical_not(self.middle))
        def _():
            self._copy(*end[step]).start()

        if step == 2:

            @pl.when(self.middle)
            def _():
                self._copy(*mid[0]).start()

    def order(self):
        return (
            jnp.where(self.middle, self.other, self.near), jnp.where(self.middle, self.near, self.other), self.far
        )

    def merge(self):
        end, mid = self._sends()

        @pl.when(self.middle)
        def _():
            for i, place in ((0, self.other), (1, self.near)):
                self._copy(self.meet.at[i], self.meet.at[i], 0, 2 + i, self.enc).wait_recv()
                self.meet[i] = (self.meet[i].astype(F32) + self.src[place].astype(F32)).astype(LOW)
                self._copy(*mid[1 + i]).start()

    def wait(self):
        for i in (0, 1):
            self._copy(self.got.at[i], self.got.at[i], 0, i, self.enc).wait_recv()

    def finish(self):
        end, mid = self._sends()

        @pl.when(jnp.logical_not(self.middle))
        def _():
            for args in end:
                self._copy(*args).wait_send()

        @pl.when(self.middle)
        def _():
            for args in mid:
                self._copy(*args).wait_send()


class ZScatter:
    def __init__(self, src_at, dst_at, where, sems, meet=None):
        self.src_at, self.dst_at, self.sems, self.meet = src_at, dst_at, sems, meet
        self.dp, self.enc = where[0], where[1]
        self.base = sems.take(3 if meet is None else 4)
        self.middle = (self.enc == 1) | (self.enc == 2)

    def _copy(self, place, merged=False):
        k = lax.rem(place - self.enc + 4, 4)
        s = self.sems
        return remote(
            self.meet if merged else self.src_at(place), self.dst_at(3 - k),
            s.send.at[self.base + k - 1], s.recv.at[self.base + 3 - k], (self.dp, place),
        )

    def _to_meet(self):
        s = self.sems
        far = 3 - self.enc
        return remote(
            self.src_at(far), self.meet, s.send.at[self.base + 3], s.recv.at[self.base + 3],
            (self.dp, 1 + lax.div(self.enc, 2)),
        )

    def start(self, place):
        self._copy(place).start()

    def start_all(self):
        enc = self.enc
        if self.meet is None:
            for k in (2, 1, 3):
                self.start(lax.rem(enc + k, 4))
            return

        @pl.when(jnp.logical_not(self.middle))
        def _():
            self._to_meet().start()
            self.start(lax.rem(enc + 2, 4))
            self.start(1 + lax.div(enc, 2))

        @pl.when(self.middle)
        def _():
            self.start(enc - 1)
            self.start(enc + 1)

    def merge(self):
        @pl.when(self.middle)
        def _():
            far = lax.rem(self.enc + 2, 4)
            self._to_meet().wait_recv()
            self.meet[...] = (self.meet[...].astype(F32) + self.src_at(far)[...].astype(F32)).astype(LOW)
            self._copy(far, merged=True).start()

    def _each(self, act):
        enc = self.enc
        if self.meet is None:
            for k in (1, 2, 3):
                act(lax.rem(enc + k, 4))
            return
        act(lax.rem(enc + 2, 4))

        @pl.when(enc > 0)
        def _():
            act(enc - 1)

        @pl.when(enc < 3)
        def _():
            act(enc + 1)

    def wait(self):
        def one(place):
            k = lax.rem(self.enc - place + 4, 4)
            s = self.sems
            remote(
                self.dst_at(3 - k), self.dst_at(3 - k), s.send.at[self.base], s.recv.at[self.base + 3 - k],
                (self.dp, self.enc),
            ).wait_recv()

        self._each(one)

    def clear(self):
        if self.meet is not None:

            @pl.when(self.enc == 0)
            def _():
                ref = self.dst_at(2)
                ref[...] = jnp.zeros(ref.shape, ref.dtype)

            @pl.when(self.enc == 3)
            def _():
                ref = self.dst_at(0)
                ref[...] = jnp.zeros(ref.shape, ref.dtype)

    def finish(self):
        self._each(lambda place: self._copy(place).wait_send())
        if self.meet is not None:

            @pl.when(jnp.logical_not(self.middle))
            def _():
                self._to_meet().wait_send()


class ChipReduce:
    def __init__(self, src, got, last, cuts, own, where, sems):
        self.src, self.got, self.last, self.cuts, self.own = src, got, last, cuts, own
        self.sems, self.where = sems, where
        self.x = lax.rem(lax.div(where[0], 2), 2)
        self.y = lax.div(where[0], 4)
        self.base = sems.take(2 * len(cuts))

    def _copy(self, i, second):
        dp, enc, sib, xn, yn = self.where
        m, lo, hi, by_x = self.cuts[i]
        s, at = self.sems, self.base + 2 * i + (1 if second else 0)
        if second:
            src = self.got.at[m, 1 - self.y if by_x else 1 - self.x, lo:hi]
            dst = self.last.at[m, lo:hi]
        else:
            src = self.src.at[m, :, 1 - self.x, lo:hi] if by_x else self.src.at[m, 1 - self.y, :, lo:hi]
            dst = self.got.at[m, :, lo:hi]
        target = xn if by_x != second else yn
        return remote(src, dst, s.send.at[at], s.recv.at[at], (target, enc))

    def start(self, only=None):
        for i in range(len(self.cuts)) if only is None else (only,):
            self._copy(i, False).start()

    def turn(self):
        for i, (m, lo, hi, by_x) in enumerate(self.cuts):
            self._copy(i, False).wait_recv()
            for k in range(2):
                self.got[m, k, lo:hi] = (
                    self.own(m, k, lo, hi, by_x).astype(F32) + self.got[m, k, lo:hi].astype(F32)
                ).astype(LOW)
            self._copy(i, True).start()

    def totals(self):
        out = []
        for i, (m, lo, hi, by_x) in enumerate(self.cuts):
            self._copy(i, True).wait_recv()
            mine = self.got[m, self.y if by_x else self.x, lo:hi]
            out.append(mine.astype(F32) + self.last[m, lo:hi].astype(F32))
        return out

    def finish(self):
        for i in range(len(self.cuts)):
            self._copy(i, False).wait_send()
            self._copy(i, True).wait_send()


def rms_back(values, gain, grad):
    inv = lax.rsqrt(jnp.mean(values * values, axis=-1, keepdims=True) + EPSILON)
    scaled = grad * gain
    mean = jnp.mean(values * scaled, axis=-1, keepdims=True)
    gain_grad = jnp.sum(grad * values * inv, axis=0, keepdims=True)
    return inv * scaled - values * (inv * inv * inv * mean), gain_grad


GELU_A = 0.7978845608028654
GELU_B = 0.044715


def ff_kernel(
    n3_ref, x2_hbm, dyall_ref, wff_ref, gain3,
    dx2_out, gain_out, down_out, part_out, sums_out,
    w, n3, dy, back, act, dgate, dup, part, got, meet, grads, core_got, own_sum, out_part, chip_got, chip_last, x2_ref, send, recv, local,
):
    where = places()
    dp, enc, sib, xn, yn = where
    core = lax.rem(dp, 2)
    sems = Sems(send, recv)
    own = n3_ref.shape[0]
    ff_rows = grads.shape[4]
    ff_half = (ff_rows // 2 + PAD - 1) // PAD * PAD
    chip_x = lax.rem(lax.div(dp, 2), 2)
    chip_y = lax.div(dp, 4)

    def rows_of(place):
        return pl.ds(pl.multiple_of(place * own, PAD), own)

    gather = ZGather(lambda e: n3.at[rows_of(e), :], n3_ref, where, sems)
    scatter = LineMeet(part, got, meet, where, sems)
    loads = [
        pltpu.make_async_copy(wff_ref, w, local.at[0]),
        pltpu.make_async_copy(dyall_ref, dy, local.at[1]),
    ]
    pull = pltpu.make_async_copy(x2_hbm, x2_ref, local.at[2])
    for c in loads + [pull]:
        c.start()
    enter(*where)
    gather.start()
    n3[rows_of(enc), :] = n3_ref[...]
    for c in loads:
        c.wait()

    back[...] = mm(dy[...], w[2], NT)

    def block(place):
        rows = rows_of(place)
        normed = n3[rows, :]
        gate = mm(normed, w[0], NT)
        up = mm(normed, w[1], NT)
        dh = back[rows, :]
        square = gate * gate
        t = jnp.tanh(GELU_A * gate * (1.0 + GELU_B * square))
        half = 0.5 * (1.0 + t)
        g = gate * half
        slope = half + 0.5 * gate * (1.0 - t * t) * (GELU_A * (1.0 + 3.0 * GELU_B * square))
        hidden = (g * up).astype(LOW)
        dg = (dh * up * slope).astype(LOW)
        du = (dh * g).astype(LOW)
        act[rows, :] = hidden
        dgate[rows, :] = dg
        dup[rows, :] = du
        return mm(dg, w[0]) + mm(du, w[1])

    own_sum[...] = block(enc)
    for step, place in enumerate(scatter.order()):
        gather.hop(step + 1)
        part[place] = block(place).astype(LOW)
        scatter.ready(step)

    base = sems.take(3)

    def swap(m):
        return remote(
            grads.at[m, :, :, 1 - core], core_got.at[m], send.at[base + m], recv.at[base + m], (sib, enc)
        )

    def put_grad(m, left, right):
        whole = mm(left[...], right[...], TN).astype(LOW)
        for y in range(2):
            for x in range(2):
                for c in range(2):
                    at = (4 * y + 2 * x + c) * ff_rows
                    grads[m, y, x, c] = whole[at : at + ff_rows]
        swap(m).start()

    def sum_cores(m):
        swap(m).wait_recv()
        for y in range(2):
            core_got[m, y] = (grads[m, y, :, core].astype(F32) + core_got[m, y].astype(F32)).astype(LOW)

    down = ChipReduce(
        core_got, chip_got, chip_last, ((2, 0, ff_half, True), (2, ff_half, ff_rows, False)),
        lambda m, k, lo, hi, by_x: core_got[m, k, chip_x, lo:hi] if by_x else core_got[m, chip_y, k, lo:hi],
        where, sems,
    )
    saves = [
        pltpu.make_async_copy(out_part, part_out, local.at[0]),
        pltpu.make_async_copy(core_got.at[0:2], sums_out, local.at[1]),
    ]
    put_grad(2, act, dy)
    out_part[...] = mm(act[...], w[2]).astype(LOW)
    saves[0].start()
    sum_cores(2)
    down.start()
    put_grad(0, dgate, n3)
    put_grad(1, dup, n3)
    scatter.merge()
    sum_cores(0)
    sum_cores(1)
    saves[1].start()
    down.turn()
    scatter.wait()
    dn3 = own_sum[...] + got[0].astype(F32) + got[1].astype(F32)
    pull.wait()
    dv, gain_grad = rms_back(x2_ref[...], gain3[...][None, :], dn3)
    dx2_out[...] = dy[rows_of(enc), :].astype(F32) + dv
    gain_out[...] = gain_grad
    for (m, lo, hi, by_x), total in zip(down.cuts, down.totals()):
        down_out[lo:hi] = total
    down.finish()
    gather.finish()
    scatter.finish()
    for m in range(3):
        swap(m).wait_send()
    for c in saves:
        c.wait()


def call_ff(n3, x2, dy_all, wff, gain3):
    own, wide = n3.shape
    ff_all = wff.shape[1]
    ff_rows = ff_all // 8
    group = 4 * own
    return pl.pallas_call(
        ff_kernel,
        out_shape=(
            sds((own, wide), F32),
            sds((1, wide), F32),
            sds((ff_rows, wide), F32),
            sds((group, wide), LOW),
            sds((2, 2, 2, ff_rows, wide), LOW),
        ),
        in_specs=[VM, ANY, ANY, ANY, VM],
        out_specs=(VM, VM, VM, ANY, ANY),
        scratch_shapes=[
            pltpu.VMEM((3, ff_all, wide), LOW),
            pltpu.VMEM((group, wide), LOW),
            pltpu.VMEM((group, wide), LOW),
            pltpu.VMEM((group, ff_all), F32),
            pltpu.VMEM((group, ff_all), LOW),
            pltpu.VMEM((group, ff_all), LOW),
            pltpu.VMEM((group, ff_all), LOW),
            pltpu.VMEM((4, own, wide), LOW),
            pltpu.VMEM((2, own, wide), LOW),
            pltpu.VMEM((2, own, wide), LOW),
            pltpu.VMEM((3, 2, 2, 2, ff_rows, wide), LOW),
            pltpu.VMEM((3, 2, 2, ff_rows, wide), LOW),
            pltpu.VMEM((own, wide), F32),
            pltpu.VMEM((group, wide), LOW),
            pltpu.VMEM((3, 2, ff_rows, wide), LOW),
            pltpu.VMEM((3, ff_rows, wide), LOW),
            pltpu.VMEM((own, wide), F32),
            pltpu.SemaphoreType.DMA((17,)),
            pltpu.SemaphoreType.DMA((17,)),
            pltpu.SemaphoreType.DMA((3,)),
        ],
        compiler_params=pltpu.CompilerParams(
            collective_id=2, has_side_effects=True, vmem_limit_bytes=60 * 2**20
        ),
        name="feed_forward",
    )(n3, x2, dy_all, wff, gain3)


class CoreReduce:
    def __init__(self, lo, grads, core_got, chip_got, chip_last, where, sems):
        self.lo, self.grads, self.core_got, self.where, self.sems = lo, grads, core_got, where, sems
        self.base = sems.take(2)
        rows = grads.shape[4]
        x = lax.rem(lax.div(where[0], 2), 2)
        y = lax.div(where[0], 4)

        def own(m, k, first, last, by_x):
            return core_got[m, k, x] if by_x else core_got[m, y, k]

        self.chips = ChipReduce(
            core_got, chip_got, chip_last, ((lo, 0, rows, True), (lo + 1, 0, rows, False)), own, where, sems
        )

    def _core(self, i):
        dp, enc, sib, xn, yn = self.where
        s, m = self.sems, self.lo + i
        return remote(
            self.grads.at[m, :, :, 1 - lax.rem(dp, 2)], self.core_got.at[m],
            s.send.at[self.base + i], s.recv.at[self.base + i], (sib, enc),
        )

    def start(self, i):
        self._core(i).start()

    def next(self):
        core = lax.rem(self.where[0], 2)
        for i in (0, 1):
            m = self.lo + i
            self._core(i).wait_recv()
            self.core_got[m] = (self.grads[m, :, :, core].astype(F32) + self.core_got[m].astype(F32)).astype(LOW)
            self.chips.start(i)

    def finish(self):
        for i in (0, 1):
            self._core(i).wait_send()
        self.chips.finish()


class LineReduce:
    def __init__(self, parts, width, line, got, meet, out, where, sems):
        self.parts, self.line, self.got, self.out, self.where = parts, line, got, out, where
        self.rows = line.shape[1]
        self.regroup = regroup_matrix(2 * len(parts), width, self.rows)
        self.z = ZScatter(lambda e: line.at[e], lambda slot: got.at[slot], where, sems, meet)

    def start(self):
        totals = [t.astype(LOW) for part in self.parts for t in part.chips.totals()]
        rows = mm(self.regroup, jnp.concatenate(totals, axis=0)).astype(LOW)
        for e in range(4):
            self.line[e] = rows[e * self.rows : (e + 1) * self.rows]
        self.z.start_all()

    def merge(self):
        self.z.merge()

    def done(self):
        self.z.wait()
        total = self.line[self.where[1]].astype(F32)
        for slot in range(3):
            total = total + self.got[slot].astype(F32)
        self.out[...] = total


def backward_pair(q_pair, k_pair, v_pair, probs_ref, pair, dnum, dtotals):
    rows = q_pair.shape[0]
    parts, scores = [], []
    for half in (0, 1):
        dw = mm(one_head(dnum, half), v_pair, NT)
        ds = (probs_ref[2 * pair + half].astype(F32) * (dw + dtotals[half])).astype(LOW)
        scores.append(ds)
        parts.append(mm(ds, k_pair))
    dq = jnp.where(low_lanes(rows), parts[0], parts[1])
    dk = mm(jnp.concatenate(scores, axis=0), jnp.concatenate([one_head(q_pair, h) for h in (0, 1)], axis=0), TN)
    probs = jnp.concatenate([probs_ref[2 * pair + h] for h in (0, 1)], axis=0)
    dv = mm(probs, jnp.concatenate([one_head(dnum, h) for h in (0, 1)], axis=0), TN)
    return dq, dk, dv, scores


def total_grads(product, total):
    low = low_lanes(product.shape[0])
    out = []
    for half in (0, 1):
        keep = low if half == 0 else jnp.logical_not(low)
        top = jnp.sum(jnp.where(keep, product, 0.0), axis=1, keepdims=True)
        tot = total[:, half * HEAD : half * HEAD + 1]
        out.append(-top / (tot * tot))
    return out


def backward_kernel(
    width,
    gain1, gain2, gain3_grad, buckets, q1, q2, num2, tot2,
    watt_ref, sums_ref, part_hbm, dx2_hbm, kv2_hbm, pr2_hbm, num1_hbm, tot1_hbm, x_hbm, e_hbm, x1_hbm, x2_hbm, kv1_hbm, pr1_hbm,
    att_out, small_out, hidden_out, hidden_grad, encoder_grad, gate_out, up_out,
    w, grads, core_got, chip_got, chip_last, line, line_got, line_meet,
    ff_own, ff_got, ff_last, part_got, part_meet,
    kvp1, kvp1_got, kvp1_meet, kvp2, kvp2_got, kvp2_meet, dq, vec, vec_got,
    part_ref, dx2_ref, kv2, pr2, num1, tot1, x_ref, e_ref, x1_ref, x2_ref, kv1, pr1, out_t, grad_t, enc_t, ff_sum, send, recv, local,
):
    where = places()
    dp, enc, sib, xn, yn = where
    sems = Sems(send, recv)
    own, wide = x_ref.shape
    own_enc = e_ref.shape[0]
    inner = HEADS * HEAD
    chip_x = lax.rem(lax.div(dp, 2), 2)
    chip_y = lax.div(dp, 4)
    ff_rows = ff_last.shape[1]
    part_rows = own * 3 // 8
    table_at = vec.shape[2] - 2 * HEAD

    out_z = [
        ZScatter(
            lambda e, a=a, b=b: part_ref.at[e, a:b], lambda slot, a=a, b=b: part_got.at[slot, a:b],
            where, sems, part_meet.at[a:b],
        )
        for a, b in ((0, part_rows), (part_rows, own))
    ]
    kv1_z = ZScatter(lambda e: kvp1.at[e], lambda slot: kvp1_got.at[slot], where, sems, kvp1_meet)
    kv2_z = [
        ZScatter(
            lambda e, p=p: kvp2.at[p, e], lambda slot, p=p: kvp2_got.at[p, slot], where, sems, kvp2_meet.at[p]
        )
        for p in range(HEADS // 2)
    ]
    batches = [CoreReduce(lo, grads, core_got, chip_got, chip_last, where, sems) for lo in (0, 2, 4, 6)]
    lines = [
        LineReduce(batches[2 * i : 2 * i + 2], width, line.at[i], line_got.at[i], line_meet.at[i], att_out.at[i], where, sems)
        for i in (0, 1)
    ]
    ff_cuts = ((0, 0, ff_rows, True), (1, 0, ff_rows, False))
    ff = ChipReduce(
        sums_ref, ff_got, ff_last, ff_cuts, lambda m, k, lo, hi, by_x: ff_own[m, k, lo:hi], where, sems
    )
    vec_base = sems.take(3)
    vec_z = ZScatter(lambda e: vec.at[3], lambda slot: vec_got.at[3 + slot], where, sems)

    def vec_copy(i):
        target = (sib, xn, yn)[i]
        return remote(
            vec.at[i], vec_got.at[i], send.at[vec_base + i], recv.at[vec_base + i], (target, enc)
        )

    def load(slot, m, i):
        return pltpu.make_async_copy(watt_ref.at[m], w.at[slot], local.at[i])

    pulls = [
        pltpu.make_async_copy(src, dst, local.at[12 + i])
        for i, (src, dst) in enumerate(
            (
                (part_hbm, part_ref), (x1_hbm, x1_ref), (kv1_hbm, kv1), (pr1_hbm, pr1), (x_hbm, x_ref),
                (e_hbm, e_ref), (x2_hbm, x2_ref), (dx2_hbm, dx2_ref), (kv2_hbm, kv2), (pr2_hbm, pr2),
                (num1_hbm, num1), (tot1_hbm, tot1),
            )
        )
    ]
    pushes = [
        pltpu.make_async_copy(src, dst, local.at[24 + i])
        for i, (src, dst) in enumerate(
            ((grad_t, hidden_grad), (enc_t, encoder_grad), (ff_sum.at[0], gate_out), (out_t, hidden_out), (ff_sum.at[1], up_out))
        )
    ]
    first_loads = [load(slot, m, slot) for slot, m in enumerate((7, 6, 5, 2, 3))]
    for c in [pulls[7], first_loads[0], pulls[0]] + pulls[8:10] + first_loads[1:3] + pulls[1:7] + pulls[10:] + first_loads[3:]:
        c.start()
    own_ff = [
        pltpu.make_async_copy(
            sums_ref.at[m, :, chip_x, lo:hi] if by_x else sums_ref.at[m, chip_y, :, lo:hi],
            ff_own.at[m, :, lo:hi], local.at[8 + i],
        )
        for i, (m, lo, hi, by_x) in enumerate(ff_cuts)
    ]
    for c in own_ff:
        c.start()
    enter(*where)
    pulls[0].wait()
    out_z[0].start_all()
    ff.start()
    for part in out_z + [kv1_z] + kv2_z + [line.z for line in lines]:
        part.clear()

    def put_grad(m, left, right):
        whole = mm(left, right, TN).astype(LOW)
        rows = 4 * width
        for y in range(2):
            for x in range(2):
                for c in range(2):
                    at = (4 * y + 2 * x + c) * rows
                    grads[m, y, x, c] = whole[at : at + rows]
        batches[m // 2].start(m % 2)

    pulls[7].wait()
    b2 = dx2_ref[...].astype(LOW)
    first_loads[0].wait()
    do2 = mm(b2, w[0], NT)
    dnum2 = (do2 / tot2[...]).astype(LOW)
    prod2 = do2 * num2[...]
    pulls[8].wait()
    pulls[9].wait()
    for pair in range(HEADS // 2):
        lanes = slice(pair * 2 * HEAD, (pair + 1) * 2 * HEAD)
        far = slice(inner + pair * 2 * HEAD, inner + (pair + 1) * 2 * HEAD)
        dtot = total_grads(prod2[:, lanes], tot2[:, lanes])
        dq_pair, dk, dv, _ = backward_pair(
            q2[:, lanes], kv2[:, lanes], kv2[:, far], pr2, pair, dnum2[:, lanes], dtot
        )
        dq[:, lanes] = dq_pair.astype(LOW)
        for e in range(4):
            kvp2[pair, e, :, : 2 * HEAD] = dk[e * own_enc : (e + 1) * own_enc].astype(LOW)
            kvp2[pair, e, :, 2 * HEAD :] = dv[e * own_enc : (e + 1) * own_enc].astype(LOW)
        kv2_z[pair].start_all()
    dq2 = dq[...]
    put_grad(0, (num2[...] / tot2[...]).astype(LOW), b2)
    pulls[1].wait()
    x1 = x1_ref[...]
    put_grad(1, dq2, rms_rows(x1, gain2[...][None, :]).astype(LOW))
    out_z[0].merge()
    first_loads[1].wait()
    dv2, gain2_grad = rms_back(x1, gain2[...][None, :], mm(dq2, w[1]))
    dx1 = dx2_ref[...] + dv2
    b1 = dx1.astype(LOW)
    first_loads[2].wait()
    do1 = mm(b1, w[2], NT)
    late = [load(2, 4, 5), load(0, 0, 6), load(1, 1, 7)]
    for c in late:
        c.start()
    pulls[10].wait()
    pulls[11].wait()
    dnum1 = (do1 / tot1[...]).astype(LOW)
    prod1 = do1 * num1[...]
    batches[0].next()
    pulls[2].wait()
    pulls[3].wait()
    all_scores = []
    for pair in range(HEADS // 2):
        lanes = slice(pair * 2 * HEAD, (pair + 1) * 2 * HEAD)
        far = slice(inner + pair * 2 * HEAD, inner + (pair + 1) * 2 * HEAD)
        dtot = total_grads(prod1[:, lanes], tot1[:, lanes])
        dq_pair, dk, dv, scores = backward_pair(
            q1[:, lanes], kv1[:, lanes], kv1[:, far], pr1, pair, dnum1[:, lanes], dtot
        )
        dq[:, lanes] = dq_pair.astype(LOW)
        for e in range(4):
            kvp1[e, :, lanes] = dk[e * own : (e + 1) * own].astype(LOW)
            kvp1[e, :, far] = dv[e * own : (e + 1) * own].astype(LOW)
        all_scores += scores
    kv1_z.start_all()
    out_z[1].start_all()
    dq1 = dq[...]
    pulls[4].wait()
    x = x_ref[...].astype(F32)
    n1 = rms_rows(x, gain1[...][None, :]).astype(LOW)
    put_grad(2, (num1[...] / tot1[...]).astype(LOW), b1)
    put_grad(3, dq1, n1)
    for z in kv2_z:
        z.merge()
    batches[1].next()
    for c in own_ff:
        c.wait()
    ff.turn()
    vec[0] = jnp.zeros(vec.shape[1:], F32)
    inside = bucket_rows(buckets, enc * own, own, 4 * own, own - 1)
    flip_row = lax.broadcasted_iota(jnp.int32, (own, own), 0)
    flip_col = lax.broadcasted_iota(jnp.int32, (own, own), 1)
    flip = jnp.where(flip_row + flip_col == own - 1, 1.0, 0.0).astype(LOW)
    for h, ds in enumerate(all_scores):
        long = jnp.concatenate([mm(flip, ds), jnp.zeros((own, own), F32)], axis=1)
        turned = pltpu.roll(long, 0, 1, stride=1, stride_axis=0)
        by_distance = jnp.sum(turned, axis=0, keepdims=True)
        vec[0, h : h + 1, table_at : table_at + BUCKETS] = lax.dot_general(
            by_distance, inside, NT, precision=lax.Precision.HIGHEST, preferred_element_type=F32
        )
    batches[0].chips.turn()
    for c in late:
        c.wait()
    dn1 = mm(dq1, w[2])
    batches[1].chips.turn()

    sums2 = []
    for p, z in enumerate(kv2_z):
        z.wait()
        sums2.append(
            (
                kvp2[p, enc].astype(F32) + kvp2_got[p, 0].astype(F32)
                + kvp2_got[p, 1].astype(F32) + kvp2_got[p, 2].astype(F32)
            ).astype(LOW)
        )
    dk2 = jnp.concatenate([t[:, : 2 * HEAD] for t in sums2], axis=1)
    dv2 = jnp.concatenate([t[:, 2 * HEAD :] for t in sums2], axis=1)
    pulls[5].wait()
    put_grad(4, dk2, e_ref[...])
    put_grad(5, dv2, e_ref[...])
    kv1_z.merge()
    lines[0].start()
    batches[2].next()
    enc_t[...] = jnp.transpose(mm(dk2, w[0]) + mm(dv2, w[1]))
    pushes[1].start()

    kv1_z.wait()
    low1 = (
        kvp1[enc].astype(F32) + kvp1_got[0].astype(F32) + kvp1_got[1].astype(F32) + kvp1_got[2].astype(F32)
    ).astype(LOW)
    dk1 = low1[:, :inner]
    dv1 = low1[:, inner:]
    put_grad(6, dk1, n1)
    put_grad(7, dv1, n1)
    batches[2].chips.turn()
    batches[3].next()
    first_loads[3].wait()
    first_loads[4].wait()
    dn1 = dn1 + mm(dk1, w[3]) + mm(dv1, w[4])
    dv_x, gain1_grad = rms_back(x, gain1[...][None, :], dn1)
    vec[0, 0:1, 0:wide] = gain1_grad
    vec[0, 1:2, 0:wide] = gain2_grad
    vec[0, 2:3, 0:wide] = gain3_grad[...]
    vec_copy(0).start()
    out_z[1].merge()
    vec_copy(0).wait_recv()
    vec[1] = vec[0] + vec_got[0]
    vec_copy(1).start()
    batches[3].chips.turn()
    vec_copy(1).wait_recv()
    vec[2] = vec[1] + vec_got[1]
    vec_copy(2).start()
    grad_t[...] = jnp.transpose(dx1 + dv_x)
    pushes[0].start()
    vec_copy(2).wait_recv()
    vec[3] = vec[2] + vec_got[2]
    vec_z.start_all()
    lines[1].start()
    lines[0].merge()
    for (m, lo, hi, by_x), total in zip(ff_cuts, ff.totals()):
        ff_sum[m, lo:hi] = total
    pushes[2].start()
    pushes[4].start()
    for z in out_z:
        z.wait()
    pulls[6].wait()
    out_t[...] = jnp.transpose(
        x2_ref[...] + (part_ref[enc].astype(F32) + part_got[0].astype(F32))
        + (part_got[1].astype(F32) + part_got[2].astype(F32))
    ).astype(LOW)
    pushes[3].start()
    lines[1].merge()
    lines[0].done()
    lines[1].done()
    vec_z.wait()
    small_out[...] = vec[3] + vec_got[3] + vec_got[4] + vec_got[5]
    for done in out_z + kv2_z + [kv1_z, vec_z, ff] + batches + [line.z for line in lines]:
        done.finish()
    for i in range(3):
        vec_copy(i).wait_send()
    for c in pushes:
        c.wait()


def call_backward(width, gain1, gain2, gain3_grad, buckets, small, watt, sums, part, dx2, kv2, pr2, num1, tot1, x, e, x1, x2, kv1, pr1):
    own, wide = x.shape
    own_enc = e.shape[0]
    inner = HEADS * HEAD
    rows = 4 * width
    ff_rows = sums.shape[3]
    small_wide = (wide + 127) // 128 * 128 + 2 * HEAD
    return pl.pallas_call(
        functools.partial(backward_kernel, width),
        out_shape=(
            sds((2, 4 * width, wide), F32),
            sds((8, small_wide), F32),
            sds((wide, own), LOW),
            sds((wide, own), F32),
            sds((wide, own_enc), F32),
            sds((ff_rows, wide), F32),
            sds((ff_rows, wide), F32),
        ),
        in_specs=[VM] * 8 + [ANY] * 14,
        out_specs=(VM,) * 2 + (ANY,) * 5,
        scratch_shapes=[
            pltpu.VMEM((5, inner, wide), LOW),
            pltpu.VMEM((8, 2, 2, 2, rows, wide), LOW),
            pltpu.VMEM((8, 2, 2, rows, wide), LOW),
            pltpu.VMEM((8, 2, rows, wide), LOW),
            pltpu.VMEM((8, rows, wide), LOW),
            pltpu.VMEM((2, 4, 4 * width, wide), LOW),
            pltpu.VMEM((2, 3, 4 * width, wide), LOW),
            pltpu.VMEM((2, 4 * width, wide), LOW),
            pltpu.VMEM((2, 2, ff_rows, wide), LOW),
            pltpu.VMEM((2, 2, ff_rows, wide), LOW),
            pltpu.VMEM((2, ff_rows, wide), LOW),
            pltpu.VMEM((3, own, wide), LOW),
            pltpu.VMEM((own, wide), LOW),
            pltpu.VMEM((4, own, 2 * inner), LOW),
            pltpu.VMEM((3, own, 2 * inner), LOW),
            pltpu.VMEM((own, 2 * inner), LOW),
            pltpu.VMEM((HEADS // 2, 4, own_enc, 4 * HEAD), LOW),
            pltpu.VMEM((HEADS // 2, 3, own_enc, 4 * HEAD), LOW),
            pltpu.VMEM((HEADS // 2, own_enc, 4 * HEAD), LOW),
            pltpu.VMEM((own, inner), LOW),
            pltpu.VMEM((4, 8, small_wide), F32),
            pltpu.VMEM((6, 8, small_wide), F32),
            pltpu.VMEM((4, own, wide), LOW),
            pltpu.VMEM((own, wide), F32),
            pltpu.VMEM(kv2.shape, LOW),
            pltpu.VMEM(pr2.shape, LOW),
            pltpu.VMEM((own, inner), F32),
            pltpu.VMEM((own, inner), F32),
            pltpu.VMEM((own, wide), LOW),
            pltpu.VMEM((own_enc, wide), LOW),
            pltpu.VMEM((own, wide), F32),
            pltpu.VMEM((own, wide), F32),
            pltpu.VMEM(kv1.shape, LOW),
            pltpu.VMEM(pr1.shape, LOW),
            pltpu.VMEM((wide, own), LOW),
            pltpu.VMEM((wide, own), F32),
            pltpu.VMEM((wide, own_enc), F32),
            pltpu.VMEM((2, ff_rows, wide), F32),
            pltpu.SemaphoreType.DMA((66,)),
            pltpu.SemaphoreType.DMA((66,)),
            pltpu.SemaphoreType.DMA((29,)),
        ],
        compiler_params=pltpu.CompilerParams(
            collective_id=3, has_side_effects=True, vmem_limit_bytes=62 * 2**20
        ),
        name="attention_backward",
    )(
        gain1, gain2, gain3_grad, buckets, *small, watt, sums,
        part.reshape(4, own, wide), dx2, kv2, pr2, num1, tot1, x, e, x1, x2, kv1, pr1,
    )


def outputs_kernel(width, *refs):
    big, (att, small) = refs[:6], refs[6:8]
    outs, rows, gains, table = refs[8:14], refs[14:22], refs[22:25], refs[25]
    held, (att_v, small_v), sem = refs[26:32], refs[32:34], refs[34]
    pulls = [pltpu.make_async_copy(a, b, sem.at[i]) for i, (a, b) in enumerate(zip((att, small) + big, (att_v, small_v) + held))]
    pushes = [pltpu.make_async_copy(a, b, sem.at[8 + i]) for i, (a, b) in enumerate(zip(held, outs))]
    for c in pulls:
        c.start()
    pulls[0].wait()
    pulls[1].wait()
    for i, ref in enumerate(rows):
        m = i % 4
        ref[...] = att_v[i // 4, m * width : (m + 1) * width]
    for i, ref in enumerate(gains):
        ref[...] = small_v[i, 0 : ref.shape[0]]
    table_at = small_v.shape[1] - 2 * HEAD
    table[...] = small_v[0:HEADS, table_at : table_at + BUCKETS]
    for pull, push in zip(pulls[2:], pushes):
        pull.wait()
        push.start()
    for push in pushes:
        push.wait()


def call_outputs(width, big, att, small):
    wide = att.shape[2]
    return pl.pallas_call(
        functools.partial(outputs_kernel, width),
        out_shape=tuple(sds(a.shape, a.dtype) for a in big)
        + (sds((width, wide), F32),) * 8
        + (sds((wide,), F32),) * 3
        + (sds((HEADS, BUCKETS), F32),),
        in_specs=[ANY] * 8,
        out_specs=(ANY,) * 6 + (VM,) * 12,
        scratch_shapes=[pltpu.VMEM(a.shape, a.dtype) for a in tuple(big) + (att, small)]
        + [pltpu.SemaphoreType.DMA((14,))],
        compiler_params=pltpu.CompilerParams(vmem_limit_bytes=62 * 2**20),
        name="results",
    )(*big, att, small)


def fast_body(
    hidden_in, encoder_out, grad_out, tgt_lengths, enc_lengths, rel_bucket, norm1_gain,
    self_q, self_k, self_v, self_o, rel_table, norm2_gain,
    cross_q, cross_k, cross_v, cross_o, norm3_gain, ff_gate, ff_up, ff_out,
):
    width = self_q.shape[1]
    mats = (cross_k.T, cross_v.T, self_k.T, self_v.T, self_q.T, self_o, cross_q.T, cross_o)
    (
        watt_all, wff_all, dy_all, x, e, x1, kv1, kv2, pr1, pr2,
        x2, n3, q1, q2, num1, num2, tot1, tot2,
    ) = call_forward(
        width, tgt_lengths, enc_lengths, hidden_in.T, encoder_out.T, grad_out.T, mats,
        (ff_gate.T, ff_up.T, ff_out), (norm1_gain, norm2_gain, norm3_gain), rel_bucket, rel_table.T,
    )
    dx2, gain3_grad, down, part, sums = call_ff(n3, x2, dy_all, wff_all, norm3_gain)
    att, small, hidden_out, hidden_grad, encoder_grad, gate, up = call_backward(
        width, norm1_gain, norm2_gain, gain3_grad, rel_bucket, (q1, q2, num2, tot2),
        watt_all, sums, part, dx2, kv2, pr2, num1, tot1, x, e, x1, x2, kv1, pr1,
    )
    (
        hidden_out, hidden_grad, encoder_grad, gate, up, down,
        o2, q2, o1, q1, k2, v2, k1, v1, g1, g2, g3, table,
    ) = call_outputs(width, (hidden_out, hidden_grad, encoder_grad, gate, up, down), att, small)
    return (
        hidden_out.T, hidden_grad.T, encoder_grad.T, g1, q1.T, k1.T, v1.T, o1, table.T,
        g2, q2.T, k2.T, v2.T, o2, g3, gate.T, up.T, down,
    )


def rms_scale(values, gain):
    return values * lax.rsqrt(jnp.mean(values * values, axis=-1, keepdims=True) + EPSILON) * gain


def gated_gelu(gate_pre, up_pre):
    return jax.nn.gelu(gate_pre, approximate=True) * up_pre


def item_ids(lengths, total_rows):
    ends = jnp.cumsum(lengths)
    places = jnp.arange(total_rows, dtype=jnp.int32)
    return jnp.sum((ends[None, :] <= places[:, None]).astype(jnp.int32), axis=1)


def product(left, right):
    return jnp.dot(left, right, preferred_element_type=jnp.float32)


def product_tn(left, right):
    return lax.dot_general(
        left, right, (((0,), (0,)), ((), ())), preferred_element_type=jnp.float32
    )


def product_nt(left, right):
    return lax.dot_general(
        left, right, (((1,), (1,)), ((), ())), preferred_element_type=jnp.float32
    )


def to_pieces(grad, shard_dim, shards):
    if shard_dim == 0:
        return grad.reshape(shards, -1)
    rows = grad.shape[0]
    return jnp.transpose(grad.reshape(rows, shards, -1), (1, 0, 2)).reshape(shards, -1)


def from_pieces(received, shard_dim, shape, shards):
    summed = jnp.sum(received, axis=0)
    if shard_dim == 0:
        return summed.reshape(shape[0] // shards, shape[1])
    return summed.reshape(shape[0], shape[1] // shards)


def head_pair(matrix, pair_index):
    return lax.dynamic_slice_in_dim(matrix, pair_index * 2 * HEAD, 2 * HEAD, 1).reshape(
        matrix.shape[0], 2, HEAD
    )


def pair_stats(stats, pair_index):
    return lax.dynamic_slice_in_dim(stats, pair_index * 2, 2, 0)


def relative_bias(distance, bias_info, pair_index):
    starts, table = bias_info
    table_pair = lax.dynamic_slice_in_dim(table, pair_index * 2, 2, 1)

    def add_step(bucket, total):
        rise = table_pair[bucket] - table_pair[bucket - 1]
        return total + jnp.where(distance[None] >= starts[bucket], rise[:, None, None], 0.0)

    start_bias = jnp.broadcast_to(table_pair[0][:, None, None], (2,) + distance.shape)
    return lax.fori_loop(1, BUCKETS, add_step, start_bias)


def relative_grads(distance, starts, score_grad):

    def one_step(bucket):
        return jnp.sum(jnp.where(distance[None] >= starts[bucket], score_grad, 0.0), axis=(1, 2))

    steps_sum = lax.map(one_step, jnp.arange(BUCKETS, dtype=jnp.int32))
    return steps_sum - jnp.concatenate([steps_sum[1:], jnp.zeros((1, 2), jnp.float32)], axis=0)


def pair_scores(query_block, key_rows, pair_index, layout):
    allowed, distance, bias_info = layout
    scores = jnp.einsum(
        "qhe,khe->hqk",
        head_pair(query_block, pair_index),
        head_pair(key_rows, pair_index),
        preferred_element_type=jnp.float32,
    )
    if bias_info is not None:
        scores = scores + relative_bias(distance, bias_info, pair_index)
    return jnp.where(allowed[None], scores, MASKED)


def forward_parts(query_block, key_rows, value_rows, layout):
    block_rows = query_block.shape[0]
    width = 2 * HEAD

    def forward_one_pair(pair_index, carry):
        numerator, largest, totals = carry
        scores = pair_scores(query_block, key_rows, pair_index, layout)
        pair_top = jnp.max(scores, axis=2)
        weights = jnp.exp(scores - pair_top[:, :, None])
        partial_sum = jnp.einsum(
            "hqk,khe->qhe",
            weights.astype(jnp.bfloat16),
            head_pair(value_rows, pair_index),
            preferred_element_type=jnp.float32,
        )
        numerator = lax.dynamic_update_slice_in_dim(
            numerator, partial_sum.reshape(block_rows, width), pair_index * width, 1
        )
        largest = lax.dynamic_update_slice_in_dim(largest, pair_top, pair_index * 2, 0)
        totals = lax.dynamic_update_slice_in_dim(
            totals, jnp.sum(weights, axis=2), pair_index * 2, 0
        )
        return (numerator, largest, totals)

    start_state = (
        jnp.zeros((block_rows, HEADS * HEAD), jnp.float32),
        jnp.zeros((HEADS, block_rows), jnp.float32),
        jnp.zeros((HEADS, block_rows), jnp.float32),
    )
    return lax.fori_loop(0, HEADS // 2, forward_one_pair, start_state)


def backward_parts(query_block, key_rows, value_rows, layout, top_rows, num_grad, total_grad):
    allowed, distance, bias_info = layout
    block_rows = query_block.shape[0]
    key_count = key_rows.shape[0]
    width = 2 * HEAD

    def backward_one_pair(pair_index, carry):
        query_grad, key_grad, value_grad, bias_grad = carry
        query_pair = head_pair(query_block, pair_index)
        key_pair = head_pair(key_rows, pair_index)
        value_pair = head_pair(value_rows, pair_index)
        grad_pair = head_pair(num_grad, pair_index)
        scores = pair_scores(query_block, key_rows, pair_index, layout)
        weights = jnp.exp(scores - pair_stats(top_rows, pair_index)[:, :, None])
        weight_grad = jnp.einsum(
            "qhe,khe->hqk", grad_pair, value_pair, preferred_element_type=jnp.float32
        )
        score_grad = (
            weights * (weight_grad + pair_stats(total_grad, pair_index)[:, :, None])
        ).astype(jnp.bfloat16)
        part_query = jnp.einsum(
            "hqk,khe->qhe", score_grad, key_pair, preferred_element_type=jnp.float32
        )
        part_key = jnp.einsum(
            "hqk,qhe->khe", score_grad, query_pair, preferred_element_type=jnp.float32
        )
        part_value = jnp.einsum(
            "hqk,qhe->khe",
            weights.astype(jnp.bfloat16),
            grad_pair,
            preferred_element_type=jnp.float32,
        )
        query_grad = lax.dynamic_update_slice_in_dim(
            query_grad, part_query.reshape(block_rows, width), pair_index * width, 1
        )
        key_grad = lax.dynamic_update_slice_in_dim(
            key_grad, part_key.reshape(key_count, width), pair_index * width, 1
        )
        value_grad = lax.dynamic_update_slice_in_dim(
            value_grad, part_value.reshape(key_count, width), pair_index * width, 1
        )
        if bias_info is not None:
            pair_bias_grad = relative_grads(distance, bias_info[0], score_grad.astype(jnp.float32))
            bias_grad = lax.dynamic_update_slice_in_dim(
                bias_grad, pair_bias_grad, pair_index * 2, 1
            )
        return (query_grad, key_grad, value_grad, bias_grad)

    bias_start = None if bias_info is None else jnp.zeros((BUCKETS, HEADS), jnp.float32)
    start_state = (
        jnp.zeros((block_rows, HEADS * HEAD), jnp.float32),
        jnp.zeros((key_count, HEADS * HEAD), jnp.float32),
        jnp.zeros((key_count, HEADS * HEAD), jnp.float32),
        bias_start,
    )
    return lax.fori_loop(0, HEADS // 2, backward_one_pair, start_state)


def normalize(numerator, totals):
    row_count = numerator.shape[0]
    shaped = numerator.reshape(row_count, HEADS, HEAD) / jnp.transpose(totals)[:, :, None]
    return shaped.reshape(row_count, HEADS * HEAD).astype(jnp.bfloat16)


def output_grads(out_grad, numerator, totals):
    row_count = out_grad.shape[0]
    per_total = jnp.transpose(totals)
    shaped_grad = out_grad.reshape(row_count, HEADS, HEAD)
    num_grad = (
        (shaped_grad / per_total[:, :, None]).reshape(row_count, HEADS * HEAD).astype(jnp.bfloat16)
    )
    total_grad = -jnp.sum(shaped_grad * numerator.reshape(row_count, HEADS, HEAD), axis=2) / (
        per_total * per_total
    )
    return (num_grad, jnp.transpose(total_grad))


def body(
    hidden_in,
    encoder_out,
    grad_out,
    tgt_lengths,
    enc_lengths,
    rel_bucket,
    norm1_gain,
    self_q,
    self_k,
    self_v,
    self_o,
    rel_table,
    norm2_gain,
    cross_q,
    cross_k,
    cross_v,
    cross_o,
    norm3_gain,
    ff_gate,
    ff_up,
    ff_out,
):
    w_query, w_key, w_value, w_out, c_query, c_key, c_value, c_out, w_gate, w_up, w_down = (
        lax.all_gather(self_q.astype(jnp.bfloat16), ("dp", "enc"), axis=1, tiled=True),
        lax.all_gather(self_k.astype(jnp.bfloat16), ("dp", "enc"), axis=1, tiled=True),
        lax.all_gather(self_v.astype(jnp.bfloat16), ("dp", "enc"), axis=1, tiled=True),
        lax.all_gather(self_o.astype(jnp.bfloat16), ("dp", "enc"), axis=0, tiled=True),
        lax.all_gather(cross_q.astype(jnp.bfloat16), ("dp", "enc"), axis=1, tiled=True),
        lax.all_gather(cross_k.astype(jnp.bfloat16), ("dp", "enc"), axis=1, tiled=True),
        lax.all_gather(cross_v.astype(jnp.bfloat16), ("dp", "enc"), axis=1, tiled=True),
        lax.all_gather(cross_o.astype(jnp.bfloat16), ("dp", "enc"), axis=0, tiled=True),
        lax.all_gather(ff_gate.astype(jnp.bfloat16), ("dp", "enc"), axis=1, tiled=True),
        lax.all_gather(ff_up.astype(jnp.bfloat16), ("dp", "enc"), axis=1, tiled=True),
        lax.all_gather(ff_out.astype(jnp.bfloat16), ("dp", "enc"), axis=0, tiled=True),
    )
    enc_count = lax.axis_size("enc")
    enc_place = lax.axis_index("enc")
    own_rows = hidden_in.shape[0]
    group_rows = own_rows * enc_count
    own_enc = encoder_out.shape[0]
    group_enc = own_enc * enc_count
    tgt_items = item_ids(tgt_lengths[0], group_rows)
    enc_items = item_ids(enc_lengths[0], group_enc)
    row_start = enc_place * own_rows
    own_items = lax.dynamic_slice_in_dim(tgt_items, row_start, own_rows)
    own_enc_items = lax.dynamic_slice_in_dim(enc_items, enc_place * own_enc, own_enc)
    bucket_starts = jnp.sum(
        (rel_bucket[None, :] < jnp.arange(BUCKETS, dtype=jnp.int32)[:, None]).astype(jnp.int32),
        axis=1,
    )
    query_place = row_start + jnp.arange(own_rows, dtype=jnp.int32)
    distance = query_place[:, None] - jnp.arange(group_rows, dtype=jnp.int32)[None, :]
    self_layout = (
        (distance >= 0) & (own_items[:, None] == tgt_items[None, :]),
        distance,
        (bucket_starts, rel_table),
    )
    hidden = hidden_in.astype(jnp.float32)
    normed_full, pull_one = jax.vjp(rms_scale, hidden, norm1_gain)
    normed = normed_full.astype(jnp.bfloat16)
    queries = product(normed, w_query).astype(jnp.bfloat16)
    key_own = product(normed, w_key).astype(jnp.bfloat16)
    value_own = product(normed, w_value).astype(jnp.bfloat16)
    key_group, value_group = (
        lax.all_gather(key_own, "enc", axis=0, tiled=True),
        lax.all_gather(value_own, "enc", axis=0, tiled=True),
    )
    self_num, self_top, self_total = forward_parts(queries, key_group, value_group, self_layout)
    attended = normalize(self_num, self_total)
    after_self = hidden + product(attended, w_out)
    normed_two_full, pull_two = jax.vjp(rms_scale, after_self, norm2_gain)
    normed_two = normed_two_full.astype(jnp.bfloat16)
    cross_queries = product(normed_two, c_query).astype(jnp.bfloat16)
    cross_keys = product(encoder_out, c_key).astype(jnp.bfloat16)
    cross_values = product(encoder_out, c_value).astype(jnp.bfloat16)
    query_group = lax.all_gather(cross_queries, "enc", axis=0, tiled=True)
    block_rows = min(512, group_rows)
    block_count = group_rows // block_rows

    def block_layout(first_row):
        query_items = lax.dynamic_slice_in_dim(tgt_items, first_row, block_rows)
        return (query_items[:, None] == own_enc_items[None, :], None, None)

    def block_forward(block_index, carry):
        numerator_all, top_all, total_all = carry
        first_row = block_index * block_rows
        block_num, block_top, block_total = forward_parts(
            lax.dynamic_slice_in_dim(query_group, first_row, block_rows, 0),
            cross_keys,
            cross_values,
            block_layout(first_row),
        )
        numerator_all = lax.dynamic_update_slice_in_dim(numerator_all, block_num, first_row, 0)
        top_all = lax.dynamic_update_slice_in_dim(top_all, block_top, first_row, 1)
        total_all = lax.dynamic_update_slice_in_dim(total_all, block_total, first_row, 1)
        return (numerator_all, top_all, total_all)

    numerator_all, local_tops, total_all = lax.fori_loop(
        0,
        block_count,
        block_forward,
        (
            jnp.zeros((group_rows, HEADS * HEAD), jnp.float32),
            jnp.zeros((HEADS, group_rows), jnp.float32),
            jnp.zeros((HEADS, group_rows), jnp.float32),
        ),
    )
    group_top = lax.pmax(local_tops, "enc")
    rescale = jnp.exp(local_tops - group_top)
    numerator_all = (
        numerator_all.reshape(group_rows, HEADS, HEAD) * jnp.transpose(rescale)[:, :, None]
    ).reshape(group_rows, HEADS * HEAD)
    total_all = total_all * rescale
    cross_num, cross_total = (
        lax.psum_scatter(
            numerator_all.astype(jnp.bfloat16), "enc", scatter_dimension=0, tiled=True
        ).astype(jnp.float32),
        lax.psum_scatter(
            total_all.astype(jnp.bfloat16), "enc", scatter_dimension=1, tiled=True
        ).astype(jnp.float32),
    )
    attended_two = normalize(cross_num, cross_total)
    after_cross = after_self + product(attended_two, c_out)
    normed_three_full, pull_three = jax.vjp(rms_scale, after_cross, norm3_gain)
    normed_three = normed_three_full.astype(jnp.bfloat16)
    gate_pre = product(normed_three, w_gate)
    up_pre = product(normed_three, w_up)
    activated, pull_act = jax.vjp(gated_gelu, gate_pre, up_pre)
    hidden_act = activated.astype(jnp.bfloat16)
    hidden_out = (after_cross + product(hidden_act, w_down)).astype(jnp.bfloat16)
    out_grad = grad_out.astype(jnp.float32)
    down_grad = product_tn(hidden_act, grad_out)
    act_grad = product_nt(grad_out, w_down)
    gate_grad_full, up_grad_full = pull_act(act_grad)
    gate_grad = gate_grad_full.astype(jnp.bfloat16)
    up_grad = up_grad_full.astype(jnp.bfloat16)
    gate_w_grad = product_tn(normed_three, gate_grad)
    up_w_grad = product_tn(normed_three, up_grad)
    normed_three_grad = product_nt(gate_grad, w_gate) + product_nt(up_grad, w_up)
    cross_res_grad, gain_three_grad = pull_three(normed_three_grad)
    after_cross_grad = out_grad + cross_res_grad
    branch_two = after_cross_grad.astype(jnp.bfloat16)
    c_out_grad = product_tn(attended_two, branch_two)
    cross_out_grad = product_nt(branch_two, c_out)
    cross_num_grad, cross_total_grad = output_grads(cross_out_grad, cross_num, cross_total)
    num_grad_group = lax.all_gather(cross_num_grad, "enc", axis=0, tiled=True)
    total_grad_group = lax.all_gather(cross_total_grad, "enc", axis=1, tiled=True)

    def block_backward(block_index, carry):
        query_grad_all, key_grad_sum, value_grad_sum = carry
        first_row = block_index * block_rows
        block_query_grad, block_key_grad, block_value_grad, unused_bias = backward_parts(
            lax.dynamic_slice_in_dim(query_group, first_row, block_rows, 0),
            cross_keys,
            cross_values,
            block_layout(first_row),
            lax.dynamic_slice_in_dim(group_top, first_row, block_rows, 1),
            lax.dynamic_slice_in_dim(num_grad_group, first_row, block_rows, 0),
            lax.dynamic_slice_in_dim(total_grad_group, first_row, block_rows, 1),
        )
        query_grad_all = lax.dynamic_update_slice_in_dim(
            query_grad_all, block_query_grad, first_row, 0
        )
        return (query_grad_all, key_grad_sum + block_key_grad, value_grad_sum + block_value_grad)

    query_grad_all, cross_key_grad, cross_value_grad = lax.fori_loop(
        0,
        block_count,
        block_backward,
        (
            jnp.zeros((group_rows, HEADS * HEAD), jnp.float32),
            jnp.zeros((own_enc, HEADS * HEAD), jnp.float32),
            jnp.zeros((own_enc, HEADS * HEAD), jnp.float32),
        ),
    )
    cross_query_grad = lax.psum_scatter(
        query_grad_all.astype(jnp.bfloat16), "enc", scatter_dimension=0, tiled=True
    )
    cross_key_low = cross_key_grad.astype(jnp.bfloat16)
    cross_value_low = cross_value_grad.astype(jnp.bfloat16)
    c_query_grad = product_tn(normed_two, cross_query_grad)
    c_key_grad = product_tn(encoder_out, cross_key_low)
    c_value_grad = product_tn(encoder_out, cross_value_low)
    encoder_grad = product_nt(cross_key_low, c_key) + product_nt(cross_value_low, c_value)
    self_res_grad, gain_two_grad = pull_two(product_nt(cross_query_grad, c_query))
    after_self_grad = after_cross_grad + self_res_grad
    branch_one = after_self_grad.astype(jnp.bfloat16)
    w_out_grad = product_tn(attended, branch_one)
    self_out_grad = product_nt(branch_one, w_out)
    self_num_grad, self_total_grad = output_grads(self_out_grad, self_num, self_total)
    self_query_grad, key_grad_rows, value_grad_rows, table_grad = backward_parts(
        queries, key_group, value_group, self_layout, self_top, self_num_grad, self_total_grad
    )
    self_key_grad, self_value_grad = (
        lax.psum_scatter(
            key_grad_rows.astype(jnp.bfloat16), "enc", scatter_dimension=0, tiled=True
        ).astype(jnp.float32),
        lax.psum_scatter(
            value_grad_rows.astype(jnp.bfloat16), "enc", scatter_dimension=0, tiled=True
        ).astype(jnp.float32),
    )
    query_low = self_query_grad.astype(jnp.bfloat16)
    key_low = self_key_grad.astype(jnp.bfloat16)
    value_low = self_value_grad.astype(jnp.bfloat16)
    w_query_grad = product_tn(normed, query_low)
    w_key_grad = product_tn(normed, key_low)
    w_value_grad = product_tn(normed, value_low)
    normed_grad = (
        product_nt(query_low, w_query) + product_nt(key_low, w_key) + product_nt(value_low, w_value)
    )
    input_res_grad, gain_one_grad = pull_one(normed_grad)
    hidden_grad = after_self_grad + input_res_grad
    shards = lax.axis_size(("dp", "enc"))
    full_grads = (
        w_query_grad,
        w_key_grad,
        w_value_grad,
        w_out_grad,
        c_query_grad,
        c_key_grad,
        c_value_grad,
        c_out_grad,
        gate_w_grad,
        up_w_grad,
        down_grad,
    )
    shard_dims = (1, 1, 1, 0, 1, 1, 1, 0, 1, 1, 0)
    piece_rows = tuple(
        (to_pieces(grad, place, shards) for grad, place in zip(full_grads, shard_dims))
    )
    received = (
        lax.all_to_all(
            piece_rows[0].astype(jnp.bfloat16),
            ("dp", "enc"),
            split_axis=0,
            concat_axis=0,
            tiled=True,
        ).astype(jnp.float32),
        lax.all_to_all(
            piece_rows[1].astype(jnp.bfloat16),
            ("dp", "enc"),
            split_axis=0,
            concat_axis=0,
            tiled=True,
        ).astype(jnp.float32),
        lax.all_to_all(
            piece_rows[2].astype(jnp.bfloat16),
            ("dp", "enc"),
            split_axis=0,
            concat_axis=0,
            tiled=True,
        ).astype(jnp.float32),
        lax.all_to_all(
            piece_rows[3].astype(jnp.bfloat16),
            ("dp", "enc"),
            split_axis=0,
            concat_axis=0,
            tiled=True,
        ).astype(jnp.float32),
        lax.all_to_all(
            piece_rows[4].astype(jnp.bfloat16),
            ("dp", "enc"),
            split_axis=0,
            concat_axis=0,
            tiled=True,
        ).astype(jnp.float32),
        lax.all_to_all(
            piece_rows[5].astype(jnp.bfloat16),
            ("dp", "enc"),
            split_axis=0,
            concat_axis=0,
            tiled=True,
        ).astype(jnp.float32),
        lax.all_to_all(
            piece_rows[6].astype(jnp.bfloat16),
            ("dp", "enc"),
            split_axis=0,
            concat_axis=0,
            tiled=True,
        ).astype(jnp.float32),
        lax.all_to_all(
            piece_rows[7].astype(jnp.bfloat16),
            ("dp", "enc"),
            split_axis=0,
            concat_axis=0,
            tiled=True,
        ).astype(jnp.float32),
        lax.all_to_all(
            piece_rows[8].astype(jnp.bfloat16),
            ("dp", "enc"),
            split_axis=0,
            concat_axis=0,
            tiled=True,
        ).astype(jnp.float32),
        lax.all_to_all(
            piece_rows[9].astype(jnp.bfloat16),
            ("dp", "enc"),
            split_axis=0,
            concat_axis=0,
            tiled=True,
        ).astype(jnp.float32),
        lax.all_to_all(
            piece_rows[10].astype(jnp.bfloat16),
            ("dp", "enc"),
            split_axis=0,
            concat_axis=0,
            tiled=True,
        ).astype(jnp.float32),
    )
    weight_grads = tuple(
        (
            from_pieces(piece, place, grad.shape, shards)
            for piece, place, grad in zip(received, shard_dims, full_grads)
        )
    )
    small_sums = lax.psum(
        (gain_one_grad, gain_two_grad, gain_three_grad, table_grad), ("dp", "enc")
    )
    return (
        hidden_out,
        hidden_grad,
        encoder_grad,
        small_sums[0],
        weight_grads[0],
        weight_grads[1],
        weight_grads[2],
        weight_grads[3],
        small_sums[3],
        small_sums[1],
        weight_grads[4],
        weight_grads[5],
        weight_grads[6],
        weight_grads[7],
        small_sums[2],
        weight_grads[8],
        weight_grads[9],
        weight_grads[10],
    )


def solution(mesh):
    return jax.shard_map(
        fast_body if dict(mesh.shape) == {"dp": 8, "enc": 4} else body,
        mesh=mesh,
        in_specs=(
            P(("dp", "enc"), None),
            P(("dp", "enc"), None),
            P(("dp", "enc"), None),
            P("dp", None),
            P("dp", None),
            P(),
            P(),
            P(None, ("dp", "enc")),
            P(None, ("dp", "enc")),
            P(None, ("dp", "enc")),
            P(("dp", "enc"), None),
            P(),
            P(),
            P(None, ("dp", "enc")),
            P(None, ("dp", "enc")),
            P(None, ("dp", "enc")),
            P(("dp", "enc"), None),
            P(),
            P(None, ("dp", "enc")),
            P(None, ("dp", "enc")),
            P(("dp", "enc"), None),
        ),
        out_specs=(
            P(("dp", "enc"), None),
            P(("dp", "enc"), None),
            P(("dp", "enc"), None),
            P(),
            P(None, ("dp", "enc")),
            P(None, ("dp", "enc")),
            P(None, ("dp", "enc")),
            P(("dp", "enc"), None),
            P(),
            P(),
            P(None, ("dp", "enc")),
            P(None, ("dp", "enc")),
            P(None, ("dp", "enc")),
            P(("dp", "enc"), None),
            P(),
            P(None, ("dp", "enc")),
            P(None, ("dp", "enc")),
            P(("dp", "enc"), None),
        ),
        check_vma=False,
    )
```

```python
import functools

import jax
import jax.numpy as jnp
from jax import lax
from jax.experimental import pallas as pl
from jax.experimental.pallas import tpu as pltpu
from jax.sharding import PartitionSpec as P

HEADS = 6
HEAD = 64
BUCKETS = 32
EPSILON = 1e-06
MASKED = -1e30
PAD = 16
MESH = pl.DeviceIdType.MESH
LOW = jnp.bfloat16
F32 = jnp.float32
NN = (((1,), (0,)), ((), ()))
NT = (((1,), (1,)), ((), ()))
TN = (((0,), (0,)), ((), ()))
ANY = pl.BlockSpec(memory_space=pl.ANY)
VM = pl.BlockSpec(memory_space=pltpu.VMEM)


def mm(left, right, dims=NN):
    return lax.dot_general(left, right, dims, preferred_element_type=F32)


def places():
    dp = lax.axis_index("dp")
    enc = lax.axis_index("enc")
    core = lax.rem(dp, 2)
    x = lax.rem(lax.div(dp, 2), 2)
    y = lax.div(dp, 4)
    sib = dp + 1 - 2 * core
    xn = dp + 2 - 4 * x
    yn = dp + 4 - 8 * y
    return dp, enc, sib, xn, yn


def enter(dp, enc, sib, xn, yn):
    barrier = pltpu.get_barrier_semaphore()
    targets = [(sib, enc), (xn, enc), (yn, enc), (xn + yn - dp, enc)]
    targets += [(dp, lax.rem(enc + k, 4)) for k in (1, 2, 3)]
    for target in targets:
        pl.semaphore_signal(barrier, inc=1, device_id=target, device_id_type=MESH)
    pl.semaphore_wait(barrier, len(targets))


class Sems:
    def __init__(self, send, recv):
        self.send, self.recv, self.used = send, recv, 0

    def take(self, count):
        first = self.used
        self.used += count
        return first


def remote(src, dst, send, recv, target):
    return pltpu.make_async_remote_copy(
        src_ref=src, dst_ref=dst, send_sem=send, recv_sem=recv, device_id=target, device_id_type=MESH
    )


class ZGather:
    def __init__(self, at, own, where, sems):
        self.at, self.own, self.sems = at, own, sems
        self.dp, self.enc = where[0], where[1]
        self.base = sems.take(6)

    def _copy(self, hop, side):
        s = self.sems
        place = self.enc - side * hop
        src = self.own if hop == 0 else self.at(place)
        return remote(
            src, self.at(place), s.send.at[self.base + hop + (3 if side == 1 else 0)],
            s.recv.at[self.base + place], (self.dp, self.enc + side),
        )

    def _has(self, hop, side):
        enc = self.enc
        return enc - hop >= 0 if side == 1 else enc + hop <= 3

    def _goes(self, side):
        return self.enc < 3 if side == 1 else self.enc > 0

    def start(self):
        for side in (1, -1):

            @pl.when(self._goes(side))
            def _(side=side):
                self._copy(0, side).start()

    def hop(self, hop):
        s = self.sems
        for side in (1, -1):

            @pl.when(self._has(hop, side))
            def _(side=side):
                place = self.enc - side * hop
                remote(
                    self.at(place), self.at(place), s.send.at[self.base], s.recv.at[self.base + place],
                    (self.dp, self.enc),
                ).wait_recv()

            if hop < 3:

                @pl.when(self._has(hop, side) & self._goes(side))
                def _(side=side):
                    self._copy(hop, side).start()

    def finish(self):
        for side in (1, -1):
            for hop in (0, 1, 2):

                @pl.when(self._has(hop, side) & self._goes(side))
                def _(side=side, hop=hop):
                    self._copy(hop, side).wait_send()


class ChipGather:
    def __init__(self, at, own, where, sems):
        self.at, self.own, self.sems, self.where = at, own, sems, where
        self.base = sems.take(9)

    def _copy(self, i):
        dp, enc, sib, xn, yn = self.where
        diag = xn + yn - dp
        block, part, target = (
            (dp, 0, xn),
            (dp, 0, yn),
            (dp, 0, sib),
            (xn, 0, sib),
            (yn, 0, sib),
            (xn, 1, yn),
            (yn, 2, xn),
            (diag, 1, sib),
            (diag, 2, sib),
        )[i]
        src = self.own if i < 3 else self.at(block, part)
        s = self.sems
        return remote(
            src, self.at(block, part), s.send.at[self.base + i], s.recv.at[self.base + i], (target, enc)
        )

    def step1(self):
        for i in (0, 1, 2):
            self._copy(i).start()

    def step2(self):
        self._copy(0).wait_recv()
        self._copy(5).start()
        self._copy(3).start()
        self._copy(1).wait_recv()
        self._copy(6).start()
        self._copy(4).start()

    def step3(self):
        self._copy(5).wait_recv()
        self._copy(7).start()
        self._copy(6).wait_recv()
        self._copy(8).start()

    def done(self):
        for i in (2, 3, 4, 7, 8):
            self._copy(i).wait_recv()

    def finish(self):
        for i in range(9):
            self._copy(i).wait_send()


def over(values, by):
    return lax.shift_right_logical(values * ((1 << 16) // by + 1), 16)


def regroup_matrix(count, width, block):
    shape = (4 * block, count * 4 * width)
    row = lax.broadcasted_iota(jnp.int32, shape, 0)
    col = lax.broadcasted_iota(jnp.int32, shape, 1)
    place = over(row, block)
    inside = row - place * block
    m = over(inside, width)
    take = (m * 4 + place) * width + inside - m * width
    return jnp.where((take == col) & (m < count), 1.0, 0.0).astype(LOW)


def rms_rows(values, gain):
    inv = lax.rsqrt(jnp.mean(values * values, axis=-1, keepdims=True) + EPSILON)
    return values * inv * gain


def low_lanes(rows):
    return lax.broadcasted_iota(jnp.int32, (rows, 2 * HEAD), 1) < HEAD


def one_head(pair, half):
    keep = low_lanes(pair.shape[0])
    if half:
        keep = jnp.logical_not(keep)
    return jnp.where(keep, pair.astype(F32), 0.0).astype(LOW)


def self_bias(rel_u, rows, cols):
    wide = jnp.broadcast_to(rel_u, (rows, rel_u.shape[1]))
    return pltpu.roll(wide, 0, 1, stride=1, stride_axis=0)[:, :cols]


def item_of(lengths_ref, place):
    end, item = jnp.int32(0), jnp.zeros_like(place)
    for b in range(4):
        end = end + lengths_ref[0, b]
        item = item + jnp.where(end <= place, 1, 0)
    return item


def attention_pair(q_pair, k_pair, v_pair, allowed, biases, keep_probs):
    rows = q_pair.shape[0]
    nums, totals = [], []
    for half in (0, 1):
        scores = mm(one_head(q_pair, half), k_pair, NT)
        if biases is not None:
            scores = scores + biases[half]
        scores = jnp.where(allowed, scores, MASKED)
        weights = jnp.exp(scores - jnp.max(scores, axis=1, keepdims=True))
        totals.append(jnp.sum(weights, axis=1, keepdims=True))
        probs = weights.astype(LOW)
        keep_probs(half, probs)
        nums.append(mm(probs, v_pair))
    low = low_lanes(rows)
    return jnp.where(low, nums[0], nums[1]), jnp.where(low, totals[0], totals[1])


def forward_kernel(
    width,
    tgt_len, enc_len, x_ref, e_ref, dy_ref, m0, m1, m2, m3, m4, m5, m6, m7, gate_ref, up_ref, down_ref, gain1, gain2, gain3, buckets, table,
    watt_out, wff_out, dy_out, x_out, e_out, x1_out, kv1_out, kv2_out, pr1_out, pr2_out,
    x2_out, n3_out, q1_out, q2_out, num1_out, num2_out, tot1_out, tot2_out,
    w, packed, own_att, ff_own, x_rows, e_rows, dy_rows, x1_rows, kv1, kv2, pr1, pr2, send, recv, local,
):
    where = places()
    dp, enc, sib, xn, yn = where
    sems = Sems(send, recv)
    own, wide = x_rows.shape
    own_enc = e_rows.shape[0]
    inner = HEADS * HEAD
    line = 4 * width
    ff_rows = ff_own.shape[1]
    ff_half = (ff_rows // 2 + PAD - 1) // PAD * PAD
    group = 4 * own

    def rows_at(ref, first, count):
        return ref.at[pl.ds(pl.multiple_of(first, PAD), count), :]

    def mats_at(ref, lo, hi, first, count):
        return ref.at[lo:hi, pl.ds(pl.multiple_of(first, PAD), count), :]

    zs = [
        ZGather(lambda e, g=g: packed.at[g, e], own_att.at[g], where, sems) for g in (0, 1)
    ]
    chips = []
    for lo in (0, 2, 4, 6):
        hi = lo + 2
        cuts = ((lo, hi), (lo, lo + 1), (lo + 1, hi))
        chips.append(
            ChipGather(
                lambda d, part, cuts=cuts: mats_at(w, *cuts[part], d * line, line),
                mats_at(w, lo, hi, dp * line, line), where, sems,
            )
        )
    ff_cuts = ((0, ff_rows), (0, ff_half), (ff_half, ff_rows - ff_half))
    ffs = [
        ChipGather(
            lambda d, part, m=m: mats_at(wff_out, m, m + 1, d * ff_rows + ff_cuts[part][0], ff_cuts[part][1]),
            ff_own.at[m : m + 1], where, sems,
        )
        for m in range(3)
    ]
    dyz = ZGather(lambda e: rows_at(dy_out, e * own, own), dy_rows, where, sems)
    kvz = ZGather(lambda e: rows_at(kv1, e * own, own), rows_at(kv1, enc * own, own), where, sems)
    kvz2 = ZGather(
        lambda e: rows_at(kv2, e * own_enc, own_enc), rows_at(kv2, enc * own_enc, own_enc), where, sems
    )

    def save(i, src, dst):
        return pltpu.make_async_copy(src, dst, local.at[i])

    saves = [
        save(0, dy_rows, rows_at(dy_out, enc * own, own)),
        save(1, ff_own, mats_at(wff_out, 0, 3, dp * ff_rows, ff_rows)),
        save(2, w, watt_out),
        save(3, x_rows, x_out),
        save(4, e_rows, e_out),
        save(5, x1_rows, x1_out),
        save(6, kv1, kv1_out),
        save(7, kv2, kv2_out),
        save(8, pr1, pr1_out),
        save(9, pr2, pr2_out),
    ]

    for g, refs in enumerate(((m0, m1, m2, m3), (m4, m5, m6, m7))):
        rows = jnp.concatenate([ref[...] for ref in refs], axis=0).astype(LOW)
        own_att[g] = rows
        packed[g, enc] = rows
    for m, ref in enumerate((gate_ref, up_ref, down_ref)):
        ff_own[m] = ref[...].astype(LOW)
    enter(*where)
    zs[0].start()
    zs[1].start()
    ffs[0].step1()
    regroup = regroup_matrix(4, width, 4 * width)

    def unpack(g):
        rows = mm(regroup, packed[g].reshape(4 * line, wide)).astype(LOW)
        for m in range(4):
            w[4 * g + m, pl.ds(pl.multiple_of(dp * line, PAD), line), :] = rows[m * line : (m + 1) * line]

    x = jnp.transpose(x_ref[...].astype(F32))
    x_rows[...] = x.astype(LOW)
    n1 = rms_rows(x, gain1[...][None, :]).astype(LOW)
    dy_rows[...] = jnp.transpose(dy_ref[...].astype(F32)).astype(LOW)
    e_rows[...] = jnp.transpose(e_ref[...].astype(F32)).astype(LOW)
    for i in (0, 1, 3, 4):
        saves[i].start()
    rel_u = rel_rows(buckets, table, enc * own, own, group)
    zs[0].hop(1)
    zs[0].hop(2)
    zs[1].hop(1)
    zs[0].hop(3)
    unpack(0)
    chips[0].step1()
    chips[1].step1()
    zs[1].hop(2)
    dyz.start()
    zs[1].hop(3)
    chips[0].step2()
    unpack(1)
    chips[1].step2()
    chips[2].step1()
    ffs[0].step2()
    chips[0].step3()
    dyz.hop(1)
    chips[0].done()
    own_enc_rows = pl.ds(pl.multiple_of(enc * own_enc, PAD), own_enc)
    kv2[own_enc_rows, 0:inner] = mm(e_rows[...], w[0], NT).astype(LOW)
    kv2[own_enc_rows, inner : 2 * inner] = mm(e_rows[...], w[1], NT).astype(LOW)
    kvz2.start()
    chips[3].step1()
    chips[1].step3()
    chips[1].done()
    own_rows = pl.ds(pl.multiple_of(enc * own, PAD), own)
    kv1[own_rows, 0:inner] = mm(n1, w[2], NT).astype(LOW)
    kv1[own_rows, inner : 2 * inner] = mm(n1, w[3], NT).astype(LOW)
    kvz.start()
    chips[2].step2()
    kvz2.hop(1)
    chips[3].step2()
    ffs[1].step1()
    ffs[2].step1()
    kvz.hop(1)
    chips[2].step3()
    ffs[0].step3()
    chips[2].done()
    q1 = mm(n1, w[4], NT).astype(LOW)
    q1_out[...] = q1
    kvz2.hop(2)
    kvz.hop(2)
    dyz.hop(2)
    chips[3].step3()
    ffs[1].step2()
    ffs[2].step2()
    ffs[1].step3()
    kvz.hop(3)

    row_place = enc * own + lax.broadcasted_iota(jnp.int32, (own, 1), 0)
    col_place = lax.broadcasted_iota(jnp.int32, (1, group), 1)
    own_items = item_of(tgt_len, row_place)
    allowed = (own_items == item_of(tgt_len, col_place)) & (col_place <= row_place)
    for pair in range(HEADS // 2):
        lanes = slice(pair * 2 * HEAD, (pair + 1) * 2 * HEAD)
        far = slice(inner + pair * 2 * HEAD, inner + (pair + 1) * 2 * HEAD)

        def keep(half, probs, pair=pair):
            pr1[2 * pair + half] = probs

        num, total = attention_pair(
            q1[:, lanes], kv1[:, lanes], kv1[:, far], allowed,
            [self_bias(rel_u[2 * pair + half : 2 * pair + half + 1, :], own, group) for half in (0, 1)],
            keep,
        )
        num1_out[:, lanes] = num
        tot1_out[:, lanes] = total
    chips[3].done()
    for i in (2, 6, 8):
        saves[i].start()
    o1 = (num1_out[...] / tot1_out[...]).astype(LOW)
    x1 = x + mm(o1, w[5])
    x1_rows[...] = x1
    saves[5].start()
    n2 = rms_rows(x1, gain2[...][None, :]).astype(LOW)
    q2 = mm(n2, w[6], NT).astype(LOW)
    q2_out[...] = q2
    ffs[2].step3()
    kvz2.hop(3)
    saves[7].start()
    enc_place = lax.broadcasted_iota(jnp.int32, (1, 4 * own_enc), 1)
    allowed2 = own_items == item_of(enc_len, enc_place)
    for pair in range(HEADS // 2):
        lanes = slice(pair * 2 * HEAD, (pair + 1) * 2 * HEAD)
        far = slice(inner + pair * 2 * HEAD, inner + (pair + 1) * 2 * HEAD)

        def keep2(half, probs, pair=pair):
            pr2[2 * pair + half] = probs

        num, total = attention_pair(
            q2[:, lanes], kv2[:, lanes], kv2[:, far], allowed2, None, keep2
        )
        num2_out[:, lanes] = num
        tot2_out[:, lanes] = total
    saves[9].start()
    o2 = (num2_out[...] / tot2_out[...]).astype(LOW)
    x2 = x1 + mm(o2, w[7])
    x2_out[...] = x2
    n3_out[...] = rms_rows(x2, gain3[...][None, :]).astype(LOW)
    dyz.hop(3)
    for part in ffs:
        part.done()
    for part in zs + chips + ffs + [dyz, kvz, kvz2]:
        part.finish()
    for c in saves:
        c.wait()


def sds(shape, dtype):
    return jax.ShapeDtypeStruct(shape, dtype)


def rel_rows(buckets, table, first, own, group):
    inside = bucket_rows(buckets, first, own, group, 0)
    return lax.dot_general(
        table[...], inside, NN, precision=lax.Precision.HIGHEST, preferred_element_type=F32
    )


def bucket_rows(buckets, first, own, group, turn):
    row = buckets[...][None, :]
    bucket = lax.broadcasted_iota(jnp.int32, (BUCKETS, row.shape[1]), 0)
    starts = jnp.sum(jnp.where(row < bucket, 1.0, 0.0), axis=1, keepdims=True)
    ends = jnp.sum(jnp.where(row <= bucket, 1.0, 0.0), axis=1, keepdims=True)
    k = lax.broadcasted_iota(jnp.int32, (1, group + own), 1)
    k = k - turn if turn else jnp.where(k < group, k, k - group - own)
    distance = (first - k).astype(F32)
    return jnp.where((distance >= starts) & (distance < ends), 1.0, 0.0)


def call_forward(width, tgt_len, enc_len, x, e, dy, mats, ffs, gains, buckets, table):
    wide, own = x.shape
    own_enc = e.shape[1]
    inner = HEADS * HEAD
    ff_rows = ffs[0].shape[0]
    SM = pl.BlockSpec(memory_space=pltpu.SMEM)
    saved = (
        sds((8, inner, wide), LOW),
        sds((3, 8 * ff_rows, wide), LOW),
        sds((4 * own, wide), LOW),
        sds((own, wide), LOW),
        sds((own_enc, wide), LOW),
        sds((own, wide), F32),
        sds((4 * own, 2 * inner), LOW),
        sds((4 * own_enc, 2 * inner), LOW),
        sds((HEADS, own, 4 * own), LOW),
        sds((HEADS, own, 4 * own_enc), LOW),
    )
    return pl.pallas_call(
        functools.partial(forward_kernel, width),
        out_shape=saved + (
            sds((own, wide), F32),
            sds((own, wide), LOW),
            sds((own, inner), LOW),
            sds((own, inner), LOW),
            sds((own, inner), F32),
            sds((own, inner), F32),
            sds((own, inner), F32),
            sds((own, inner), F32),
        ),
        in_specs=[SM, SM] + [VM] * 19,
        out_specs=(ANY,) * 10 + (VM,) * 8,
        scratch_shapes=[
            pltpu.VMEM((8, inner, wide), LOW),
            pltpu.VMEM((2, 4, 4 * width, wide), LOW),
            pltpu.VMEM((2, 4 * width, wide), LOW),
            pltpu.VMEM((3, ff_rows, wide), LOW),
            pltpu.VMEM((own, wide), LOW),
            pltpu.VMEM((own_enc, wide), LOW),
            pltpu.VMEM((own, wide), LOW),
            pltpu.VMEM((own, wide), F32),
            pltpu.VMEM((4 * own, 2 * inner), LOW),
            pltpu.VMEM((4 * own_enc, 2 * inner), LOW),
            pltpu.VMEM((HEADS, own, 4 * own), LOW),
            pltpu.VMEM((HEADS, own, 4 * own_enc), LOW),
            pltpu.SemaphoreType.DMA((96,)),
            pltpu.SemaphoreType.DMA((96,)),
            pltpu.SemaphoreType.DMA((10,)),
        ],
        compiler_params=pltpu.CompilerParams(
            collective_id=1, has_side_effects=True, vmem_limit_bytes=56 * 2**20
        ),
        name="attention_forward",
    )(tgt_len, enc_len, x, e, dy, *mats, *ffs, *gains, buckets, table)


class LineMeet:
    def __init__(self, src, got, meet, where, sems):
        self.src, self.got, self.meet, self.sems = src, got, meet, sems
        self.dp, self.enc = where[0], where[1]
        self.base = sems.take(4)
        self.middle = (self.enc == 1) | (self.enc == 2)
        self.far = jnp.where(self.middle, 3 * (2 - self.enc), 3 - self.enc)
        self.near = jnp.where(self.middle, 3 * (self.enc - 1), 1 + lax.div(self.enc, 2))
        self.other = jnp.where(self.middle, 3 - self.enc, 2 - lax.div(self.enc, 2))

    def _copy(self, src, dst, i, j, target):
        s = self.sems
        return remote(src, dst, s.send.at[self.base + i], s.recv.at[self.base + j], (self.dp, target))

    def _sends(self):
        src, got, meet = self.src, self.got, self.meet
        end = (
            (src.at[self.near], got.at[0], 0, 0, self.near),
            (src.at[self.other], meet.at[0], 1, 2, self.near),
            (src.at[self.far], got.at[0], 2, 0, self.far),
        )
        mid = (
            (src.at[self.far], meet.at[1], 0, 3, self.other),
            (meet.at[0], got.at[1], 1, 1, self.other),
            (meet.at[1], got.at[1], 2, 1, self.near),
        )
        return end, mid

    def ready(self, step):
        end, mid = self._sends()

        @pl.when(jnp.logical_not(self.middle))
        def _():
            self._copy(*end[step]).start()

        if step == 2:

            @pl.when(self.middle)
            def _():
                self._copy(*mid[0]).start()

    def order(self):
        return (
            jnp.where(self.middle, self.other, self.near), jnp.where(self.middle, self.near, self.other), self.far
        )

    def merge(self):
        end, mid = self._sends()

        @pl.when(self.middle)
        def _():
            for i, place in ((0, self.other), (1, self.near)):
                self._copy(self.meet.at[i], self.meet.at[i], 0, 2 + i, self.enc).wait_recv()
                self.meet[i] = (self.meet[i].astype(F32) + self.src[place].astype(F32)).astype(LOW)
                self._copy(*mid[1 + i]).start()

    def wait(self):
        for i in (0, 1):
            self._copy(self.got.at[i], self.got.at[i], 0, i, self.enc).wait_recv()

    def finish(self):
        end, mid = self._sends()

        @pl.when(jnp.logical_not(self.middle))
        def _():
            for args in end:
                self._copy(*args).wait_send()

        @pl.when(self.middle)
        def _():
            for args in mid:
                self._copy(*args).wait_send()


class ZScatter:
    def __init__(self, src_at, dst_at, where, sems, meet=None):
        self.src_at, self.dst_at, self.sems, self.meet = src_at, dst_at, sems, meet
        self.dp, self.enc = where[0], where[1]
        self.base = sems.take(3 if meet is None else 4)
        self.middle = (self.enc == 1) | (self.enc == 2)

    def _copy(self, place, merged=False):
        k = lax.rem(place - self.enc + 4, 4)
        s = self.sems
        return remote(
            self.meet if merged else self.src_at(place), self.dst_at(3 - k),
            s.send.at[self.base + k - 1], s.recv.at[self.base + 3 - k], (self.dp, place),
        )

    def _to_meet(self):
        s = self.sems
        far = 3 - self.enc
        return remote(
            self.src_at(far), self.meet, s.send.at[self.base + 3], s.recv.at[self.base + 3],
            (self.dp, 1 + lax.div(self.enc, 2)),
        )

    def start(self, place):
        self._copy(place).start()

    def start_all(self):
        enc = self.enc
        if self.meet is None:
            for k in (2, 1, 3):
                self.start(lax.rem(enc + k, 4))
            return

        @pl.when(jnp.logical_not(self.middle))
        def _():
            self._to_meet().start()
            self.start(lax.rem(enc + 2, 4))
            self.start(1 + lax.div(enc, 2))

        @pl.when(self.middle)
        def _():
            self.start(enc - 1)
            self.start(enc + 1)

    def merge(self):
        @pl.when(self.middle)
        def _():
            far = lax.rem(self.enc + 2, 4)
            self._to_meet().wait_recv()
            self.meet[...] = (self.meet[...].astype(F32) + self.src_at(far)[...].astype(F32)).astype(LOW)
            self._copy(far, merged=True).start()

    def _each(self, act):
        enc = self.enc
        if self.meet is None:
            for k in (1, 2, 3):
                act(lax.rem(enc + k, 4))
            return
        act(lax.rem(enc + 2, 4))

        @pl.when(enc > 0)
        def _():
            act(enc - 1)

        @pl.when(enc < 3)
        def _():
            act(enc + 1)

    def wait(self):
        def one(place):
            k = lax.rem(self.enc - place + 4, 4)
            s = self.sems
            remote(
                self.dst_at(3 - k), self.dst_at(3 - k), s.send.at[self.base], s.recv.at[self.base + 3 - k],
                (self.dp, self.enc),
            ).wait_recv()

        self._each(one)

    def clear(self):
        if self.meet is not None:

            @pl.when(self.enc == 0)
            def _():
                ref = self.dst_at(2)
                ref[...] = jnp.zeros(ref.shape, ref.dtype)

            @pl.when(self.enc == 3)
            def _():
                ref = self.dst_at(0)
                ref[...] = jnp.zeros(ref.shape, ref.dtype)

    def finish(self):
        self._each(lambda place: self._copy(place).wait_send())
        if self.meet is not None:

            @pl.when(jnp.logical_not(self.middle))
            def _():
                self._to_meet().wait_send()


class ChipReduce:
    def __init__(self, src, got, last, cuts, own, where, sems):
        self.src, self.got, self.last, self.cuts, self.own = src, got, last, cuts, own
        self.sems, self.where = sems, where
        self.x = lax.rem(lax.div(where[0], 2), 2)
        self.y = lax.div(where[0], 4)
        self.base = sems.take(2 * len(cuts))

    def _copy(self, i, second):
        dp, enc, sib, xn, yn = self.where
        m, lo, hi, by_x = self.cuts[i]
        s, at = self.sems, self.base + 2 * i + (1 if second else 0)
        if second:
            src = self.got.at[m, 1 - self.y if by_x else 1 - self.x, lo:hi]
            dst = self.last.at[m, lo:hi]
        else:
            src = self.src.at[m, :, 1 - self.x, lo:hi] if by_x else self.src.at[m, 1 - self.y, :, lo:hi]
            dst = self.got.at[m, :, lo:hi]
        target = xn if by_x != second else yn
        return remote(src, dst, s.send.at[at], s.recv.at[at], (target, enc))

    def start(self, only=None):
        for i in range(len(self.cuts)) if only is None else (only,):
            self._copy(i, False).start()

    def turn(self):
        for i, (m, lo, hi, by_x) in enumerate(self.cuts):
            self._copy(i, False).wait_recv()
            for k in range(2):
                self.got[m, k, lo:hi] = (
                    self.own(m, k, lo, hi, by_x).astype(F32) + self.got[m, k, lo:hi].astype(F32)
                ).astype(LOW)
            self._copy(i, True).start()

    def totals(self):
        out = []
        for i, (m, lo, hi, by_x) in enumerate(self.cuts):
            self._copy(i, True).wait_recv()
            mine = self.got[m, self.y if by_x else self.x, lo:hi]
            out.append(mine.astype(F32) + self.last[m, lo:hi].astype(F32))
        return out

    def finish(self):
        for i in range(len(self.cuts)):
            self._copy(i, False).wait_send()
            self._copy(i, True).wait_send()


def rms_back(values, gain, grad):
    inv = lax.rsqrt(jnp.mean(values * values, axis=-1, keepdims=True) + EPSILON)
    scaled = grad * gain
    mean = jnp.mean(values * scaled, axis=-1, keepdims=True)
    gain_grad = jnp.sum(grad * values * inv, axis=0, keepdims=True)
    return inv * scaled - values * (inv * inv * inv * mean), gain_grad


GELU_A = 0.7978845608028654
GELU_B = 0.044715


def ff_kernel(
    n3_ref, x2_hbm, dyall_ref, wff_ref, gain3,
    dx2_out, gain_out, down_out, part_out, sums_out,
    w, n3, dy, back, act, dgate, dup, part, got, meet, grads, core_got, own_sum, out_part, chip_got, chip_last, x2_ref, send, recv, local,
):
    where = places()
    dp, enc, sib, xn, yn = where
    core = lax.rem(dp, 2)
    sems = Sems(send, recv)
    own = n3_ref.shape[0]
    ff_rows = grads.shape[4]
    ff_half = (ff_rows // 2 + PAD - 1) // PAD * PAD
    chip_x = lax.rem(lax.div(dp, 2), 2)
    chip_y = lax.div(dp, 4)

    def rows_of(place):
        return pl.ds(pl.multiple_of(place * own, PAD), own)

    gather = ZGather(lambda e: n3.at[rows_of(e), :], n3_ref, where, sems)
    scatter = LineMeet(part, got, meet, where, sems)
    loads = [
        pltpu.make_async_copy(wff_ref, w, local.at[0]),
        pltpu.make_async_copy(dyall_ref, dy, local.at[1]),
    ]
    pull = pltpu.make_async_copy(x2_hbm, x2_ref, local.at[2])
    for c in loads + [pull]:
        c.start()
    enter(*where)
    gather.start()
    n3[rows_of(enc), :] = n3_ref[...]
    for c in loads:
        c.wait()

    back[...] = mm(dy[...], w[2], NT)

    def block(place):
        rows = rows_of(place)
        normed = n3[rows, :]
        gate = mm(normed, w[0], NT)
        up = mm(normed, w[1], NT)
        dh = back[rows, :]
        square = gate * gate
        t = jnp.tanh(GELU_A * gate * (1.0 + GELU_B * square))
        half = 0.5 * (1.0 + t)
        g = gate * half
        slope = half + 0.5 * gate * (1.0 - t * t) * (GELU_A * (1.0 + 3.0 * GELU_B * square))
        hidden = (g * up).astype(LOW)
        dg = (dh * up * slope).astype(LOW)
        du = (dh * g).astype(LOW)
        act[rows, :] = hidden
        dgate[rows, :] = dg
        dup[rows, :] = du
        return mm(dg, w[0]) + mm(du, w[1])

    own_sum[...] = block(enc)
    for step, place in enumerate(scatter.order()):
        gather.hop(step + 1)
        part[place] = block(place).astype(LOW)
        scatter.ready(step)

    base = sems.take(3)

    def swap(m):
        return remote(
            grads.at[m, :, :, 1 - core], core_got.at[m], send.at[base + m], recv.at[base + m], (sib, enc)
        )

    def put_grad(m, left, right):
        whole = mm(left[...], right[...], TN).astype(LOW)
        for y in range(2):
            for x in range(2):
                for c in range(2):
                    at = (4 * y + 2 * x + c) * ff_rows
                    grads[m, y, x, c] = whole[at : at + ff_rows]
        swap(m).start()

    def sum_cores(m):
        swap(m).wait_recv()
        for y in range(2):
            core_got[m, y] = (grads[m, y, :, core].astype(F32) + core_got[m, y].astype(F32)).astype(LOW)

    down = ChipReduce(
        core_got, chip_got, chip_last, ((2, 0, ff_half, True), (2, ff_half, ff_rows, False)),
        lambda m, k, lo, hi, by_x: core_got[m, k, chip_x, lo:hi] if by_x else core_got[m, chip_y, k, lo:hi],
        where, sems,
    )
    saves = [
        pltpu.make_async_copy(out_part, part_out, local.at[0]),
        pltpu.make_async_copy(core_got.at[0:2], sums_out, local.at[1]),
    ]
    put_grad(2, act, dy)
    out_part[...] = mm(act[...], w[2]).astype(LOW)
    saves[0].start()
    sum_cores(2)
    down.start()
    put_grad(0, dgate, n3)
    scatter.merge()
    put_grad(1, dup, n3)
    sum_cores(0)
    sum_cores(1)
    saves[1].start()
    down.turn()
    scatter.wait()
    dn3 = own_sum[...] + got[0].astype(F32) + got[1].astype(F32)
    pull.wait()
    dv, gain_grad = rms_back(x2_ref[...], gain3[...][None, :], dn3)
    dx2_out[...] = dy[rows_of(enc), :].astype(F32) + dv
    gain_out[...] = gain_grad
    for (m, lo, hi, by_x), total in zip(down.cuts, down.totals()):
        down_out[lo:hi] = total
    down.finish()
    gather.finish()
    scatter.finish()
    for m in range(3):
        swap(m).wait_send()
    for c in saves:
        c.wait()


def call_ff(n3, x2, dy_all, wff, gain3):
    own, wide = n3.shape
    ff_all = wff.shape[1]
    ff_rows = ff_all // 8
    group = 4 * own
    return pl.pallas_call(
        ff_kernel,
        out_shape=(
            sds((own, wide), F32),
            sds((1, wide), F32),
            sds((ff_rows, wide), F32),
            sds((group, wide), LOW),
            sds((2, 2, 2, ff_rows, wide), LOW),
        ),
        in_specs=[VM, ANY, ANY, ANY, VM],
        out_specs=(VM, VM, VM, ANY, ANY),
        scratch_shapes=[
            pltpu.VMEM((3, ff_all, wide), LOW),
            pltpu.VMEM((group, wide), LOW),
            pltpu.VMEM((group, wide), LOW),
            pltpu.VMEM((group, ff_all), F32),
            pltpu.VMEM((group, ff_all), LOW),
            pltpu.VMEM((group, ff_all), LOW),
            pltpu.VMEM((group, ff_all), LOW),
            pltpu.VMEM((4, own, wide), LOW),
            pltpu.VMEM((2, own, wide), LOW),
            pltpu.VMEM((2, own, wide), LOW),
            pltpu.VMEM((3, 2, 2, 2, ff_rows, wide), LOW),
            pltpu.VMEM((3, 2, 2, ff_rows, wide), LOW),
            pltpu.VMEM((own, wide), F32),
            pltpu.VMEM((group, wide), LOW),
            pltpu.VMEM((3, 2, ff_rows, wide), LOW),
            pltpu.VMEM((3, ff_rows, wide), LOW),
            pltpu.VMEM((own, wide), F32),
            pltpu.SemaphoreType.DMA((17,)),
            pltpu.SemaphoreType.DMA((17,)),
            pltpu.SemaphoreType.DMA((3,)),
        ],
        compiler_params=pltpu.CompilerParams(
            collective_id=2, has_side_effects=True, vmem_limit_bytes=60 * 2**20
        ),
        name="feed_forward",
    )(n3, x2, dy_all, wff, gain3)


class CoreReduce:
    def __init__(self, lo, grads, core_got, chip_got, chip_last, where, sems):
        self.lo, self.grads, self.core_got, self.where, self.sems = lo, grads, core_got, where, sems
        self.base = sems.take(2)
        rows = grads.shape[4]
        x = lax.rem(lax.div(where[0], 2), 2)
        y = lax.div(where[0], 4)

        def own(m, k, first, last, by_x):
            return core_got[m, k, x] if by_x else core_got[m, y, k]

        self.chips = ChipReduce(
            core_got, chip_got, chip_last, ((lo, 0, rows, True), (lo + 1, 0, rows, False)), own, where, sems
        )

    def _core(self, i):
        dp, enc, sib, xn, yn = self.where
        s, m = self.sems, self.lo + i
        return remote(
            self.grads.at[m, :, :, 1 - lax.rem(dp, 2)], self.core_got.at[m],
            s.send.at[self.base + i], s.recv.at[self.base + i], (sib, enc),
        )

    def start(self, i):
        self._core(i).start()

    def next(self):
        core = lax.rem(self.where[0], 2)
        for i in (0, 1):
            m = self.lo + i
            self._core(i).wait_recv()
            self.core_got[m] = (self.grads[m, :, :, core].astype(F32) + self.core_got[m].astype(F32)).astype(LOW)
            self.chips.start(i)

    def finish(self):
        for i in (0, 1):
            self._core(i).wait_send()
        self.chips.finish()


class LineReduce:
    def __init__(self, parts, width, line, got, meet, out, where, sems):
        self.parts, self.line, self.got, self.out, self.where = parts, line, got, out, where
        self.rows = line.shape[1]
        self.regroup = regroup_matrix(2 * len(parts), width, self.rows)
        self.z = ZScatter(lambda e: line.at[e], lambda slot: got.at[slot], where, sems, meet)

    def start(self):
        totals = [t.astype(LOW) for part in self.parts for t in part.chips.totals()]
        rows = mm(self.regroup, jnp.concatenate(totals, axis=0)).astype(LOW)
        for e in range(4):
            self.line[e] = rows[e * self.rows : (e + 1) * self.rows]
        self.z.start_all()

    def merge(self):
        self.z.merge()

    def done(self):
        self.z.wait()
        total = self.line[self.where[1]].astype(F32)
        for slot in range(3):
            total = total + self.got[slot].astype(F32)
        self.out[...] = total


def backward_pair(q_pair, k_pair, v_pair, probs_ref, pair, dnum, dtotals):
    rows = q_pair.shape[0]
    parts, scores = [], []
    for half in (0, 1):
        dw = mm(one_head(dnum, half), v_pair, NT)
        ds = (probs_ref[2 * pair + half].astype(F32) * (dw + dtotals[half])).astype(LOW)
        scores.append(ds)
        parts.append(mm(ds, k_pair))
    dq = jnp.where(low_lanes(rows), parts[0], parts[1])
    dk = mm(jnp.concatenate(scores, axis=0), jnp.concatenate([one_head(q_pair, h) for h in (0, 1)], axis=0), TN)
    probs = jnp.concatenate([probs_ref[2 * pair + h] for h in (0, 1)], axis=0)
    dv = mm(probs, jnp.concatenate([one_head(dnum, h) for h in (0, 1)], axis=0), TN)
    return dq, dk, dv, scores


def total_grads(product, total):
    low = low_lanes(product.shape[0])
    out = []
    for half in (0, 1):
        keep = low if half == 0 else jnp.logical_not(low)
        top = jnp.sum(jnp.where(keep, product, 0.0), axis=1, keepdims=True)
        tot = total[:, half * HEAD : half * HEAD + 1]
        out.append(-top / (tot * tot))
    return out


def backward_kernel(
    width,
    gain1, gain2, gain3_grad, buckets, q1, q2, num2, tot2,
    watt_ref, sums_ref, part_hbm, dx2_hbm, kv2_hbm, pr2_hbm, num1_hbm, tot1_hbm, x_hbm, e_hbm, x1_hbm, x2_hbm, kv1_hbm, pr1_hbm,
    att_out, small_out, hidden_out, hidden_grad, encoder_grad, gate_out, up_out,
    w, grads, core_got, chip_got, chip_last, line, line_got, line_meet,
    ff_own, ff_got, ff_last, part_got, part_meet,
    kvp1, kvp1_got, kvp1_meet, kvp2, kvp2_got, kvp2_meet, dq, vec, vec_got,
    part_ref, dx2_ref, kv2, pr2, num1, tot1, x_ref, e_ref, x1_ref, x2_ref, kv1, pr1, out_t, grad_t, enc_t, ff_sum, send, recv, local,
):
    where = places()
    dp, enc, sib, xn, yn = where
    sems = Sems(send, recv)
    own, wide = x_ref.shape
    own_enc = e_ref.shape[0]
    inner = HEADS * HEAD
    chip_x = lax.rem(lax.div(dp, 2), 2)
    chip_y = lax.div(dp, 4)
    ff_rows = ff_last.shape[1]
    part_rows = own // 4
    table_at = vec.shape[2] - 2 * HEAD

    out_z = [
        ZScatter(
            lambda e, a=a, b=b: part_ref.at[e, a:b], lambda slot, a=a, b=b: part_got.at[slot, a:b],
            where, sems, part_meet.at[a:b],
        )
        for a, b in ((0, part_rows), (part_rows, own))
    ]
    kv1_z = ZScatter(lambda e: kvp1.at[e], lambda slot: kvp1_got.at[slot], where, sems, kvp1_meet)
    kv2_z = [
        ZScatter(
            lambda e, p=p: kvp2.at[p, e], lambda slot, p=p: kvp2_got.at[p, slot], where, sems, kvp2_meet.at[p]
        )
        for p in range(HEADS // 2)
    ]
    batches = [CoreReduce(lo, grads, core_got, chip_got, chip_last, where, sems) for lo in (0, 2, 4, 6)]
    lines = [
        LineReduce(batches[2 * i : 2 * i + 2], width, line.at[i], line_got.at[i], line_meet.at[i], att_out.at[i], where, sems)
        for i in (0, 1)
    ]
    ff_cuts = ((0, 0, ff_rows, True), (1, 0, ff_rows, False))
    ff = ChipReduce(
        sums_ref, ff_got, ff_last, ff_cuts, lambda m, k, lo, hi, by_x: ff_own[m, k, lo:hi], where, sems
    )
    vec_base = sems.take(3)
    vec_z = ZScatter(lambda e: vec.at[3], lambda slot: vec_got.at[3 + slot], where, sems)

    def vec_copy(i):
        target = (sib, xn, yn)[i]
        return remote(
            vec.at[i], vec_got.at[i], send.at[vec_base + i], recv.at[vec_base + i], (target, enc)
        )

    def load(slot, m, i):
        return pltpu.make_async_copy(watt_ref.at[m], w.at[slot], local.at[i])

    pulls = [
        pltpu.make_async_copy(src, dst, local.at[12 + i])
        for i, (src, dst) in enumerate(
            (
                (part_hbm, part_ref), (x1_hbm, x1_ref), (kv1_hbm, kv1), (pr1_hbm, pr1), (x_hbm, x_ref),
                (e_hbm, e_ref), (x2_hbm, x2_ref), (dx2_hbm, dx2_ref), (kv2_hbm, kv2), (pr2_hbm, pr2),
                (num1_hbm, num1), (tot1_hbm, tot1),
            )
        )
    ]
    pushes = [
        pltpu.make_async_copy(src, dst, local.at[24 + i])
        for i, (src, dst) in enumerate(
            ((grad_t, hidden_grad), (enc_t, encoder_grad), (ff_sum.at[0], gate_out), (out_t, hidden_out), (ff_sum.at[1], up_out))
        )
    ]
    first_loads = [load(slot, m, slot) for slot, m in enumerate((7, 6, 5, 2, 3))]
    for c in [pulls[7], first_loads[0], pulls[0]] + pulls[8:10] + first_loads[1:3] + pulls[1:7] + pulls[10:] + first_loads[3:]:
        c.start()
    own_ff = [
        pltpu.make_async_copy(
            sums_ref.at[m, :, chip_x, lo:hi] if by_x else sums_ref.at[m, chip_y, :, lo:hi],
            ff_own.at[m, :, lo:hi], local.at[8 + i],
        )
        for i, (m, lo, hi, by_x) in enumerate(ff_cuts)
    ]
    for c in own_ff:
        c.start()
    enter(*where)
    pulls[0].wait()
    out_z[0].start_all()
    ff.start()
    for part in out_z + [kv1_z] + kv2_z + [line.z for line in lines]:
        part.clear()

    def put_grad(m, left, right):
        whole = mm(left, right, TN).astype(LOW)
        rows = 4 * width
        for y in range(2):
            for x in range(2):
                for c in range(2):
                    at = (4 * y + 2 * x + c) * rows
                    grads[m, y, x, c] = whole[at : at + rows]
        batches[m // 2].start(m % 2)

    pulls[7].wait()
    b2 = dx2_ref[...].astype(LOW)
    first_loads[0].wait()
    do2 = mm(b2, w[0], NT)
    dnum2 = (do2 / tot2[...]).astype(LOW)
    prod2 = do2 * num2[...]
    pulls[8].wait()
    pulls[9].wait()
    for pair in range(HEADS // 2):
        lanes = slice(pair * 2 * HEAD, (pair + 1) * 2 * HEAD)
        far = slice(inner + pair * 2 * HEAD, inner + (pair + 1) * 2 * HEAD)
        dtot = total_grads(prod2[:, lanes], tot2[:, lanes])
        dq_pair, dk, dv, _ = backward_pair(
            q2[:, lanes], kv2[:, lanes], kv2[:, far], pr2, pair, dnum2[:, lanes], dtot
        )
        dq[:, lanes] = dq_pair.astype(LOW)
        for e in range(4):
            kvp2[pair, e, :, : 2 * HEAD] = dk[e * own_enc : (e + 1) * own_enc].astype(LOW)
            kvp2[pair, e, :, 2 * HEAD :] = dv[e * own_enc : (e + 1) * own_enc].astype(LOW)
        kv2_z[pair].start_all()
    dq2 = dq[...]
    put_grad(0, (num2[...] / tot2[...]).astype(LOW), b2)
    pulls[1].wait()
    x1 = x1_ref[...]
    put_grad(1, dq2, rms_rows(x1, gain2[...][None, :]).astype(LOW))
    out_z[0].merge()
    first_loads[1].wait()
    dv2, gain2_grad = rms_back(x1, gain2[...][None, :], mm(dq2, w[1]))
    dx1 = dx2_ref[...] + dv2
    b1 = dx1.astype(LOW)
    first_loads[2].wait()
    do1 = mm(b1, w[2], NT)
    late = [load(2, 4, 5), load(0, 0, 6), load(1, 1, 7)]
    for c in late:
        c.start()
    pulls[10].wait()
    pulls[11].wait()
    dnum1 = (do1 / tot1[...]).astype(LOW)
    prod1 = do1 * num1[...]
    batches[0].next()
    pulls[2].wait()
    pulls[3].wait()
    all_scores = []
    for pair in range(HEADS // 2):
        lanes = slice(pair * 2 * HEAD, (pair + 1) * 2 * HEAD)
        far = slice(inner + pair * 2 * HEAD, inner + (pair + 1) * 2 * HEAD)
        dtot = total_grads(prod1[:, lanes], tot1[:, lanes])
        dq_pair, dk, dv, scores = backward_pair(
            q1[:, lanes], kv1[:, lanes], kv1[:, far], pr1, pair, dnum1[:, lanes], dtot
        )
        dq[:, lanes] = dq_pair.astype(LOW)
        for e in range(4):
            kvp1[e, :, lanes] = dk[e * own : (e + 1) * own].astype(LOW)
            kvp1[e, :, far] = dv[e * own : (e + 1) * own].astype(LOW)
        all_scores += scores
    kv1_z.start_all()
    out_z[1].start_all()
    dq1 = dq[...]
    pulls[4].wait()
    x = x_ref[...].astype(F32)
    n1 = rms_rows(x, gain1[...][None, :]).astype(LOW)
    put_grad(2, (num1[...] / tot1[...]).astype(LOW), b1)
    put_grad(3, dq1, n1)
    for z in kv2_z:
        z.merge()
    batches[1].next()
    for c in own_ff:
        c.wait()
    ff.turn()
    vec[0] = jnp.zeros(vec.shape[1:], F32)
    inside = bucket_rows(buckets, enc * own, own, 4 * own, own - 1)
    flip_row = lax.broadcasted_iota(jnp.int32, (own, own), 0)
    flip_col = lax.broadcasted_iota(jnp.int32, (own, own), 1)
    flip = jnp.where(flip_row + flip_col == own - 1, 1.0, 0.0).astype(LOW)
    for h, ds in enumerate(all_scores):
        long = jnp.concatenate([mm(flip, ds), jnp.zeros((own, own), F32)], axis=1)
        turned = pltpu.roll(long, 0, 1, stride=1, stride_axis=0)
        by_distance = jnp.sum(turned, axis=0, keepdims=True)
        vec[0, h : h + 1, table_at : table_at + BUCKETS] = lax.dot_general(
            by_distance, inside, NT, precision=lax.Precision.HIGHEST, preferred_element_type=F32
        )
    batches[0].chips.turn()
    for c in late:
        c.wait()
    dn1 = mm(dq1, w[2])
    batches[1].chips.turn()

    sums2 = []
    for p, z in enumerate(kv2_z):
        z.wait()
        sums2.append(
            (
                kvp2[p, enc].astype(F32) + kvp2_got[p, 0].astype(F32)
                + kvp2_got[p, 1].astype(F32) + kvp2_got[p, 2].astype(F32)
            ).astype(LOW)
        )
    dk2 = jnp.concatenate([t[:, : 2 * HEAD] for t in sums2], axis=1)
    dv2 = jnp.concatenate([t[:, 2 * HEAD :] for t in sums2], axis=1)
    pulls[5].wait()
    put_grad(4, dk2, e_ref[...])
    put_grad(5, dv2, e_ref[...])
    kv1_z.merge()
    lines[0].start()
    batches[2].next()
    enc_t[...] = jnp.transpose(mm(dk2, w[0]) + mm(dv2, w[1]))
    pushes[1].start()

    kv1_z.wait()
    low1 = (
        kvp1[enc].astype(F32) + kvp1_got[0].astype(F32) + kvp1_got[1].astype(F32) + kvp1_got[2].astype(F32)
    ).astype(LOW)
    dk1 = low1[:, :inner]
    dv1 = low1[:, inner:]
    put_grad(6, dk1, n1)
    put_grad(7, dv1, n1)
    batches[2].chips.turn()
    batches[3].next()
    first_loads[3].wait()
    first_loads[4].wait()
    dn1 = dn1 + mm(dk1, w[3]) + mm(dv1, w[4])
    dv_x, gain1_grad = rms_back(x, gain1[...][None, :], dn1)
    vec[0, 0:1, 0:wide] = gain1_grad
    vec[0, 1:2, 0:wide] = gain2_grad
    vec[0, 2:3, 0:wide] = gain3_grad[...]
    vec_copy(0).start()
    out_z[1].merge()
    vec_copy(0).wait_recv()
    vec[1] = vec[0] + vec_got[0]
    vec_copy(1).start()
    batches[3].chips.turn()
    vec_copy(1).wait_recv()
    vec[2] = vec[1] + vec_got[1]
    vec_copy(2).start()
    grad_t[...] = jnp.transpose(dx1 + dv_x)
    pushes[0].start()
    vec_copy(2).wait_recv()
    vec[3] = vec[2] + vec_got[2]
    vec_z.start_all()
    lines[1].start()
    lines[0].merge()
    for (m, lo, hi, by_x), total in zip(ff_cuts, ff.totals()):
        ff_sum[m, lo:hi] = total
    pushes[2].start()
    pushes[4].start()
    for z in out_z:
        z.wait()
    pulls[6].wait()
    out_t[...] = jnp.transpose(
        x2_ref[...] + (part_ref[enc].astype(F32) + part_got[0].astype(F32))
        + (part_got[1].astype(F32) + part_got[2].astype(F32))
    ).astype(LOW)
    pushes[3].start()
    lines[1].merge()
    lines[0].done()
    lines[1].done()
    vec_z.wait()
    small_out[...] = vec[3] + vec_got[3] + vec_got[4] + vec_got[5]
    for done in out_z + kv2_z + [kv1_z, vec_z, ff] + batches + [line.z for line in lines]:
        done.finish()
    for i in range(3):
        vec_copy(i).wait_send()
    for c in pushes:
        c.wait()


def call_backward(width, gain1, gain2, gain3_grad, buckets, small, watt, sums, part, dx2, kv2, pr2, num1, tot1, x, e, x1, x2, kv1, pr1):
    own, wide = x.shape
    own_enc = e.shape[0]
    inner = HEADS * HEAD
    rows = 4 * width
    ff_rows = sums.shape[3]
    small_wide = (wide + 127) // 128 * 128 + 2 * HEAD
    return pl.pallas_call(
        functools.partial(backward_kernel, width),
        out_shape=(
            sds((2, 4 * width, wide), F32),
            sds((8, small_wide), F32),
            sds((wide, own), LOW),
            sds((wide, own), F32),
            sds((wide, own_enc), F32),
            sds((ff_rows, wide), F32),
            sds((ff_rows, wide), F32),
        ),
        in_specs=[VM] * 8 + [ANY] * 14,
        out_specs=(VM,) * 2 + (ANY,) * 5,
        scratch_shapes=[
            pltpu.VMEM((5, inner, wide), LOW),
            pltpu.VMEM((8, 2, 2, 2, rows, wide), LOW),
            pltpu.VMEM((8, 2, 2, rows, wide), LOW),
            pltpu.VMEM((8, 2, rows, wide), LOW),
            pltpu.VMEM((8, rows, wide), LOW),
            pltpu.VMEM((2, 4, 4 * width, wide), LOW),
            pltpu.VMEM((2, 3, 4 * width, wide), LOW),
            pltpu.VMEM((2, 4 * width, wide), LOW),
            pltpu.VMEM((2, 2, ff_rows, wide), LOW),
            pltpu.VMEM((2, 2, ff_rows, wide), LOW),
            pltpu.VMEM((2, ff_rows, wide), LOW),
            pltpu.VMEM((3, own, wide), LOW),
            pltpu.VMEM((own, wide), LOW),
            pltpu.VMEM((4, own, 2 * inner), LOW),
            pltpu.VMEM((3, own, 2 * inner), LOW),
            pltpu.VMEM((own, 2 * inner), LOW),
            pltpu.VMEM((HEADS // 2, 4, own_enc, 4 * HEAD), LOW),
            pltpu.VMEM((HEADS // 2, 3, own_enc, 4 * HEAD), LOW),
            pltpu.VMEM((HEADS // 2, own_enc, 4 * HEAD), LOW),
            pltpu.VMEM((own, inner), LOW),
            pltpu.VMEM((4, 8, small_wide), F32),
            pltpu.VMEM((6, 8, small_wide), F32),
            pltpu.VMEM((4, own, wide), LOW),
            pltpu.VMEM((own, wide), F32),
            pltpu.VMEM(kv2.shape, LOW),
            pltpu.VMEM(pr2.shape, LOW),
            pltpu.VMEM((own, inner), F32),
            pltpu.VMEM((own, inner), F32),
            pltpu.VMEM((own, wide), LOW),
            pltpu.VMEM((own_enc, wide), LOW),
            pltpu.VMEM((own, wide), F32),
            pltpu.VMEM((own, wide), F32),
            pltpu.VMEM(kv1.shape, LOW),
            pltpu.VMEM(pr1.shape, LOW),
            pltpu.VMEM((wide, own), LOW),
            pltpu.VMEM((wide, own), F32),
            pltpu.VMEM((wide, own_enc), F32),
            pltpu.VMEM((2, ff_rows, wide), F32),
            pltpu.SemaphoreType.DMA((66,)),
            pltpu.SemaphoreType.DMA((66,)),
            pltpu.SemaphoreType.DMA((29,)),
        ],
        compiler_params=pltpu.CompilerParams(
            collective_id=3, has_side_effects=True, vmem_limit_bytes=62 * 2**20
        ),
        name="attention_backward",
    )(
        gain1, gain2, gain3_grad, buckets, *small, watt, sums,
        part.reshape(4, own, wide), dx2, kv2, pr2, num1, tot1, x, e, x1, x2, kv1, pr1,
    )


def outputs_kernel(width, *refs):
    big, (att, small) = refs[:6], refs[6:8]
    outs, rows, gains, table = refs[8:14], refs[14:22], refs[22:25], refs[25]
    held, (att_v, small_v), sem = refs[26:32], refs[32:34], refs[34]
    pulls = [pltpu.make_async_copy(a, b, sem.at[i]) for i, (a, b) in enumerate(zip((att, small) + big, (att_v, small_v) + held))]
    pushes = [pltpu.make_async_copy(a, b, sem.at[8 + i]) for i, (a, b) in enumerate(zip(held, outs))]
    for c in pulls:
        c.start()
    pulls[0].wait()
    pulls[1].wait()
    for i, ref in enumerate(rows):
        m = i % 4
        ref[...] = att_v[i // 4, m * width : (m + 1) * width]
    for i, ref in enumerate(gains):
        ref[...] = small_v[i, 0 : ref.shape[0]]
    table_at = small_v.shape[1] - 2 * HEAD
    table[...] = small_v[0:HEADS, table_at : table_at + BUCKETS]
    for pull, push in zip(pulls[2:], pushes):
        pull.wait()
        push.start()
    for push in pushes:
        push.wait()


def call_outputs(width, big, att, small):
    wide = att.shape[2]
    return pl.pallas_call(
        functools.partial(outputs_kernel, width),
        out_shape=tuple(sds(a.shape, a.dtype) for a in big)
        + (sds((width, wide), F32),) * 8
        + (sds((wide,), F32),) * 3
        + (sds((HEADS, BUCKETS), F32),),
        in_specs=[ANY] * 8,
        out_specs=(ANY,) * 6 + (VM,) * 12,
        scratch_shapes=[pltpu.VMEM(a.shape, a.dtype) for a in tuple(big) + (att, small)]
        + [pltpu.SemaphoreType.DMA((14,))],
        compiler_params=pltpu.CompilerParams(vmem_limit_bytes=62 * 2**20),
        name="results",
    )(*big, att, small)


def fast_body(
    hidden_in, encoder_out, grad_out, tgt_lengths, enc_lengths, rel_bucket, norm1_gain,
    self_q, self_k, self_v, self_o, rel_table, norm2_gain,
    cross_q, cross_k, cross_v, cross_o, norm3_gain, ff_gate, ff_up, ff_out,
):
    width = self_q.shape[1]
    mats = (cross_k.T, cross_v.T, self_k.T, self_v.T, self_q.T, self_o, cross_q.T, cross_o)
    (
        watt_all, wff_all, dy_all, x, e, x1, kv1, kv2, pr1, pr2,
        x2, n3, q1, q2, num1, num2, tot1, tot2,
    ) = call_forward(
        width, tgt_lengths, enc_lengths, hidden_in.T, encoder_out.T, grad_out.T, mats,
        (ff_gate.T, ff_up.T, ff_out), (norm1_gain, norm2_gain, norm3_gain), rel_bucket, rel_table.T,
    )
    dx2, gain3_grad, down, part, sums = call_ff(n3, x2, dy_all, wff_all, norm3_gain)
    att, small, hidden_out, hidden_grad, encoder_grad, gate, up = call_backward(
        width, norm1_gain, norm2_gain, gain3_grad, rel_bucket, (q1, q2, num2, tot2),
        watt_all, sums, part, dx2, kv2, pr2, num1, tot1, x, e, x1, x2, kv1, pr1,
    )
    (
        hidden_out, hidden_grad, encoder_grad, gate, up, down,
        o2, q2, o1, q1, k2, v2, k1, v1, g1, g2, g3, table,
    ) = call_outputs(width, (hidden_out, hidden_grad, encoder_grad, gate, up, down), att, small)
    return (
        hidden_out.T, hidden_grad.T, encoder_grad.T, g1, q1.T, k1.T, v1.T, o1, table.T,
        g2, q2.T, k2.T, v2.T, o2, g3, gate.T, up.T, down,
    )


def rms_scale(values, gain):
    return values * lax.rsqrt(jnp.mean(values * values, axis=-1, keepdims=True) + EPSILON) * gain


def gated_gelu(gate_pre, up_pre):
    return jax.nn.gelu(gate_pre, approximate=True) * up_pre


def item_ids(lengths, total_rows):
    ends = jnp.cumsum(lengths)
    places = jnp.arange(total_rows, dtype=jnp.int32)
    return jnp.sum((ends[None, :] <= places[:, None]).astype(jnp.int32), axis=1)


def product(left, right):
    return jnp.dot(left, right, preferred_element_type=jnp.float32)


def product_tn(left, right):
    return lax.dot_general(
        left, right, (((0,), (0,)), ((), ())), preferred_element_type=jnp.float32
    )


def product_nt(left, right):
    return lax.dot_general(
        left, right, (((1,), (1,)), ((), ())), preferred_element_type=jnp.float32
    )


def to_pieces(grad, shard_dim, shards):
    if shard_dim == 0:
        return grad.reshape(shards, -1)
    rows = grad.shape[0]
    return jnp.transpose(grad.reshape(rows, shards, -1), (1, 0, 2)).reshape(shards, -1)


def from_pieces(received, shard_dim, shape, shards):
    summed = jnp.sum(received, axis=0)
    if shard_dim == 0:
        return summed.reshape(shape[0] // shards, shape[1])
    return summed.reshape(shape[0], shape[1] // shards)


def head_pair(matrix, pair_index):
    return lax.dynamic_slice_in_dim(matrix, pair_index * 2 * HEAD, 2 * HEAD, 1).reshape(
        matrix.shape[0], 2, HEAD
    )


def pair_stats(stats, pair_index):
    return lax.dynamic_slice_in_dim(stats, pair_index * 2, 2, 0)


def relative_bias(distance, bias_info, pair_index):
    starts, table = bias_info
    table_pair = lax.dynamic_slice_in_dim(table, pair_index * 2, 2, 1)

    def add_step(bucket, total):
        rise = table_pair[bucket] - table_pair[bucket - 1]
        return total + jnp.where(distance[None] >= starts[bucket], rise[:, None, None], 0.0)

    start_bias = jnp.broadcast_to(table_pair[0][:, None, None], (2,) + distance.shape)
    return lax.fori_loop(1, BUCKETS, add_step, start_bias)


def relative_grads(distance, starts, score_grad):

    def one_step(bucket):
        return jnp.sum(jnp.where(distance[None] >= starts[bucket], score_grad, 0.0), axis=(1, 2))

    steps_sum = lax.map(one_step, jnp.arange(BUCKETS, dtype=jnp.int32))
    return steps_sum - jnp.concatenate([steps_sum[1:], jnp.zeros((1, 2), jnp.float32)], axis=0)


def pair_scores(query_block, key_rows, pair_index, layout):
    allowed, distance, bias_info = layout
    scores = jnp.einsum(
        "qhe,khe->hqk",
        head_pair(query_block, pair_index),
        head_pair(key_rows, pair_index),
        preferred_element_type=jnp.float32,
    )
    if bias_info is not None:
        scores = scores + relative_bias(distance, bias_info, pair_index)
    return jnp.where(allowed[None], scores, MASKED)


def forward_parts(query_block, key_rows, value_rows, layout):
    block_rows = query_block.shape[0]
    width = 2 * HEAD

    def forward_one_pair(pair_index, carry):
        numerator, largest, totals = carry
        scores = pair_scores(query_block, key_rows, pair_index, layout)
        pair_top = jnp.max(scores, axis=2)
        weights = jnp.exp(scores - pair_top[:, :, None])
        partial_sum = jnp.einsum(
            "hqk,khe->qhe",
            weights.astype(jnp.bfloat16),
            head_pair(value_rows, pair_index),
            preferred_element_type=jnp.float32,
        )
        numerator = lax.dynamic_update_slice_in_dim(
            numerator, partial_sum.reshape(block_rows, width), pair_index * width, 1
        )
        largest = lax.dynamic_update_slice_in_dim(largest, pair_top, pair_index * 2, 0)
        totals = lax.dynamic_update_slice_in_dim(
            totals, jnp.sum(weights, axis=2), pair_index * 2, 0
        )
        return (numerator, largest, totals)

    start_state = (
        jnp.zeros((block_rows, HEADS * HEAD), jnp.float32),
        jnp.zeros((HEADS, block_rows), jnp.float32),
        jnp.zeros((HEADS, block_rows), jnp.float32),
    )
    return lax.fori_loop(0, HEADS // 2, forward_one_pair, start_state)


def backward_parts(query_block, key_rows, value_rows, layout, top_rows, num_grad, total_grad):
    allowed, distance, bias_info = layout
    block_rows = query_block.shape[0]
    key_count = key_rows.shape[0]
    width = 2 * HEAD

    def backward_one_pair(pair_index, carry):
        query_grad, key_grad, value_grad, bias_grad = carry
        query_pair = head_pair(query_block, pair_index)
        key_pair = head_pair(key_rows, pair_index)
        value_pair = head_pair(value_rows, pair_index)
        grad_pair = head_pair(num_grad, pair_index)
        scores = pair_scores(query_block, key_rows, pair_index, layout)
        weights = jnp.exp(scores - pair_stats(top_rows, pair_index)[:, :, None])
        weight_grad = jnp.einsum(
            "qhe,khe->hqk", grad_pair, value_pair, preferred_element_type=jnp.float32
        )
        score_grad = (
            weights * (weight_grad + pair_stats(total_grad, pair_index)[:, :, None])
        ).astype(jnp.bfloat16)
        part_query = jnp.einsum(
            "hqk,khe->qhe", score_grad, key_pair, preferred_element_type=jnp.float32
        )
        part_key = jnp.einsum(
            "hqk,qhe->khe", score_grad, query_pair, preferred_element_type=jnp.float32
        )
        part_value = jnp.einsum(
            "hqk,qhe->khe",
            weights.astype(jnp.bfloat16),
            grad_pair,
            preferred_element_type=jnp.float32,
        )
        query_grad = lax.dynamic_update_slice_in_dim(
            query_grad, part_query.reshape(block_rows, width), pair_index * width, 1
        )
        key_grad = lax.dynamic_update_slice_in_dim(
            key_grad, part_key.reshape(key_count, width), pair_index * width, 1
        )
        value_grad = lax.dynamic_update_slice_in_dim(
            value_grad, part_value.reshape(key_count, width), pair_index * width, 1
        )
        if bias_info is not None:
            pair_bias_grad = relative_grads(distance, bias_info[0], score_grad.astype(jnp.float32))
            bias_grad = lax.dynamic_update_slice_in_dim(
                bias_grad, pair_bias_grad, pair_index * 2, 1
            )
        return (query_grad, key_grad, value_grad, bias_grad)

    bias_start = None if bias_info is None else jnp.zeros((BUCKETS, HEADS), jnp.float32)
    start_state = (
        jnp.zeros((block_rows, HEADS * HEAD), jnp.float32),
        jnp.zeros((key_count, HEADS * HEAD), jnp.float32),
        jnp.zeros((key_count, HEADS * HEAD), jnp.float32),
        bias_start,
    )
    return lax.fori_loop(0, HEADS // 2, backward_one_pair, start_state)


def normalize(numerator, totals):
    row_count = numerator.shape[0]
    shaped = numerator.reshape(row_count, HEADS, HEAD) / jnp.transpose(totals)[:, :, None]
    return shaped.reshape(row_count, HEADS * HEAD).astype(jnp.bfloat16)


def output_grads(out_grad, numerator, totals):
    row_count = out_grad.shape[0]
    per_total = jnp.transpose(totals)
    shaped_grad = out_grad.reshape(row_count, HEADS, HEAD)
    num_grad = (
        (shaped_grad / per_total[:, :, None]).reshape(row_count, HEADS * HEAD).astype(jnp.bfloat16)
    )
    total_grad = -jnp.sum(shaped_grad * numerator.reshape(row_count, HEADS, HEAD), axis=2) / (
        per_total * per_total
    )
    return (num_grad, jnp.transpose(total_grad))


def body(
    hidden_in,
    encoder_out,
    grad_out,
    tgt_lengths,
    enc_lengths,
    rel_bucket,
    norm1_gain,
    self_q,
    self_k,
    self_v,
    self_o,
    rel_table,
    norm2_gain,
    cross_q,
    cross_k,
    cross_v,
    cross_o,
    norm3_gain,
    ff_gate,
    ff_up,
    ff_out,
):
    w_query, w_key, w_value, w_out, c_query, c_key, c_value, c_out, w_gate, w_up, w_down = (
        lax.all_gather(self_q.astype(jnp.bfloat16), ("dp", "enc"), axis=1, tiled=True),
        lax.all_gather(self_k.astype(jnp.bfloat16), ("dp", "enc"), axis=1, tiled=True),
        lax.all_gather(self_v.astype(jnp.bfloat16), ("dp", "enc"), axis=1, tiled=True),
        lax.all_gather(self_o.astype(jnp.bfloat16), ("dp", "enc"), axis=0, tiled=True),
        lax.all_gather(cross_q.astype(jnp.bfloat16), ("dp", "enc"), axis=1, tiled=True),
        lax.all_gather(cross_k.astype(jnp.bfloat16), ("dp", "enc"), axis=1, tiled=True),
        lax.all_gather(cross_v.astype(jnp.bfloat16), ("dp", "enc"), axis=1, tiled=True),
        lax.all_gather(cross_o.astype(jnp.bfloat16), ("dp", "enc"), axis=0, tiled=True),
        lax.all_gather(ff_gate.astype(jnp.bfloat16), ("dp", "enc"), axis=1, tiled=True),
        lax.all_gather(ff_up.astype(jnp.bfloat16), ("dp", "enc"), axis=1, tiled=True),
        lax.all_gather(ff_out.astype(jnp.bfloat16), ("dp", "enc"), axis=0, tiled=True),
    )
    enc_count = lax.axis_size("enc")
    enc_place = lax.axis_index("enc")
    own_rows = hidden_in.shape[0]
    group_rows = own_rows * enc_count
    own_enc = encoder_out.shape[0]
    group_enc = own_enc * enc_count
    tgt_items = item_ids(tgt_lengths[0], group_rows)
    enc_items = item_ids(enc_lengths[0], group_enc)
    row_start = enc_place * own_rows
    own_items = lax.dynamic_slice_in_dim(tgt_items, row_start, own_rows)
    own_enc_items = lax.dynamic_slice_in_dim(enc_items, enc_place * own_enc, own_enc)
    bucket_starts = jnp.sum(
        (rel_bucket[None, :] < jnp.arange(BUCKETS, dtype=jnp.int32)[:, None]).astype(jnp.int32),
        axis=1,
    )
    query_place = row_start + jnp.arange(own_rows, dtype=jnp.int32)
    distance = query_place[:, None] - jnp.arange(group_rows, dtype=jnp.int32)[None, :]
    self_layout = (
        (distance >= 0) & (own_items[:, None] == tgt_items[None, :]),
        distance,
        (bucket_starts, rel_table),
    )
    hidden = hidden_in.astype(jnp.float32)
    normed_full, pull_one = jax.vjp(rms_scale, hidden, norm1_gain)
    normed = normed_full.astype(jnp.bfloat16)
    queries = product(normed, w_query).astype(jnp.bfloat16)
    key_own = product(normed, w_key).astype(jnp.bfloat16)
    value_own = product(normed, w_value).astype(jnp.bfloat16)
    key_group, value_group = (
        lax.all_gather(key_own, "enc", axis=0, tiled=True),
        lax.all_gather(value_own, "enc", axis=0, tiled=True),
    )
    self_num, self_top, self_total = forward_parts(queries, key_group, value_group, self_layout)
    attended = normalize(self_num, self_total)
    after_self = hidden + product(attended, w_out)
    normed_two_full, pull_two = jax.vjp(rms_scale, after_self, norm2_gain)
    normed_two = normed_two_full.astype(jnp.bfloat16)
    cross_queries = product(normed_two, c_query).astype(jnp.bfloat16)
    cross_keys = product(encoder_out, c_key).astype(jnp.bfloat16)
    cross_values = product(encoder_out, c_value).astype(jnp.bfloat16)
    query_group = lax.all_gather(cross_queries, "enc", axis=0, tiled=True)
    block_rows = min(512, group_rows)
    block_count = group_rows // block_rows

    def block_layout(first_row):
        query_items = lax.dynamic_slice_in_dim(tgt_items, first_row, block_rows)
        return (query_items[:, None] == own_enc_items[None, :], None, None)

    def block_forward(block_index, carry):
        numerator_all, top_all, total_all = carry
        first_row = block_index * block_rows
        block_num, block_top, block_total = forward_parts(
            lax.dynamic_slice_in_dim(query_group, first_row, block_rows, 0),
            cross_keys,
            cross_values,
            block_layout(first_row),
        )
        numerator_all = lax.dynamic_update_slice_in_dim(numerator_all, block_num, first_row, 0)
        top_all = lax.dynamic_update_slice_in_dim(top_all, block_top, first_row, 1)
        total_all = lax.dynamic_update_slice_in_dim(total_all, block_total, first_row, 1)
        return (numerator_all, top_all, total_all)

    numerator_all, local_tops, total_all = lax.fori_loop(
        0,
        block_count,
        block_forward,
        (
            jnp.zeros((group_rows, HEADS * HEAD), jnp.float32),
            jnp.zeros((HEADS, group_rows), jnp.float32),
            jnp.zeros((HEADS, group_rows), jnp.float32),
        ),
    )
    group_top = lax.pmax(local_tops, "enc")
    rescale = jnp.exp(local_tops - group_top)
    numerator_all = (
        numerator_all.reshape(group_rows, HEADS, HEAD) * jnp.transpose(rescale)[:, :, None]
    ).reshape(group_rows, HEADS * HEAD)
    total_all = total_all * rescale
    cross_num, cross_total = (
        lax.psum_scatter(
            numerator_all.astype(jnp.bfloat16), "enc", scatter_dimension=0, tiled=True
        ).astype(jnp.float32),
        lax.psum_scatter(
            total_all.astype(jnp.bfloat16), "enc", scatter_dimension=1, tiled=True
        ).astype(jnp.float32),
    )
    attended_two = normalize(cross_num, cross_total)
    after_cross = after_self + product(attended_two, c_out)
    normed_three_full, pull_three = jax.vjp(rms_scale, after_cross, norm3_gain)
    normed_three = normed_three_full.astype(jnp.bfloat16)
    gate_pre = product(normed_three, w_gate)
    up_pre = product(normed_three, w_up)
    activated, pull_act = jax.vjp(gated_gelu, gate_pre, up_pre)
    hidden_act = activated.astype(jnp.bfloat16)
    hidden_out = (after_cross + product(hidden_act, w_down)).astype(jnp.bfloat16)
    out_grad = grad_out.astype(jnp.float32)
    down_grad = product_tn(hidden_act, grad_out)
    act_grad = product_nt(grad_out, w_down)
    gate_grad_full, up_grad_full = pull_act(act_grad)
    gate_grad = gate_grad_full.astype(jnp.bfloat16)
    up_grad = up_grad_full.astype(jnp.bfloat16)
    gate_w_grad = product_tn(normed_three, gate_grad)
    up_w_grad = product_tn(normed_three, up_grad)
    normed_three_grad = product_nt(gate_grad, w_gate) + product_nt(up_grad, w_up)
    cross_res_grad, gain_three_grad = pull_three(normed_three_grad)
    after_cross_grad = out_grad + cross_res_grad
    branch_two = after_cross_grad.astype(jnp.bfloat16)
    c_out_grad = product_tn(attended_two, branch_two)
    cross_out_grad = product_nt(branch_two, c_out)
    cross_num_grad, cross_total_grad = output_grads(cross_out_grad, cross_num, cross_total)
    num_grad_group = lax.all_gather(cross_num_grad, "enc", axis=0, tiled=True)
    total_grad_group = lax.all_gather(cross_total_grad, "enc", axis=1, tiled=True)

    def block_backward(block_index, carry):
        query_grad_all, key_grad_sum, value_grad_sum = carry
        first_row = block_index * block_rows
        block_query_grad, block_key_grad, block_value_grad, unused_bias = backward_parts(
            lax.dynamic_slice_in_dim(query_group, first_row, block_rows, 0),
            cross_keys,
            cross_values,
            block_layout(first_row),
            lax.dynamic_slice_in_dim(group_top, first_row, block_rows, 1),
            lax.dynamic_slice_in_dim(num_grad_group, first_row, block_rows, 0),
            lax.dynamic_slice_in_dim(total_grad_group, first_row, block_rows, 1),
        )
        query_grad_all = lax.dynamic_update_slice_in_dim(
            query_grad_all, block_query_grad, first_row, 0
        )
        return (query_grad_all, key_grad_sum + block_key_grad, value_grad_sum + block_value_grad)

    query_grad_all, cross_key_grad, cross_value_grad = lax.fori_loop(
        0,
        block_count,
        block_backward,
        (
            jnp.zeros((group_rows, HEADS * HEAD), jnp.float32),
            jnp.zeros((own_enc, HEADS * HEAD), jnp.float32),
            jnp.zeros((own_enc, HEADS * HEAD), jnp.float32),
        ),
    )
    cross_query_grad = lax.psum_scatter(
        query_grad_all.astype(jnp.bfloat16), "enc", scatter_dimension=0, tiled=True
    )
    cross_key_low = cross_key_grad.astype(jnp.bfloat16)
    cross_value_low = cross_value_grad.astype(jnp.bfloat16)
    c_query_grad = product_tn(normed_two, cross_query_grad)
    c_key_grad = product_tn(encoder_out, cross_key_low)
    c_value_grad = product_tn(encoder_out, cross_value_low)
    encoder_grad = product_nt(cross_key_low, c_key) + product_nt(cross_value_low, c_value)
    self_res_grad, gain_two_grad = pull_two(product_nt(cross_query_grad, c_query))
    after_self_grad = after_cross_grad + self_res_grad
    branch_one = after_self_grad.astype(jnp.bfloat16)
    w_out_grad = product_tn(attended, branch_one)
    self_out_grad = product_nt(branch_one, w_out)
    self_num_grad, self_total_grad = output_grads(self_out_grad, self_num, self_total)
    self_query_grad, key_grad_rows, value_grad_rows, table_grad = backward_parts(
        queries, key_group, value_group, self_layout, self_top, self_num_grad, self_total_grad
    )
    self_key_grad, self_value_grad = (
        lax.psum_scatter(
            key_grad_rows.astype(jnp.bfloat16), "enc", scatter_dimension=0, tiled=True
        ).astype(jnp.float32),
        lax.psum_scatter(
            value_grad_rows.astype(jnp.bfloat16), "enc", scatter_dimension=0, tiled=True
        ).astype(jnp.float32),
    )
    query_low = self_query_grad.astype(jnp.bfloat16)
    key_low = self_key_grad.astype(jnp.bfloat16)
    value_low = self_value_grad.astype(jnp.bfloat16)
    w_query_grad = product_tn(normed, query_low)
    w_key_grad = product_tn(normed, key_low)
    w_value_grad = product_tn(normed, value_low)
    normed_grad = (
        product_nt(query_low, w_query) + product_nt(key_low, w_key) + product_nt(value_low, w_value)
    )
    input_res_grad, gain_one_grad = pull_one(normed_grad)
    hidden_grad = after_self_grad + input_res_grad
    shards = lax.axis_size(("dp", "enc"))
    full_grads = (
        w_query_grad,
        w_key_grad,
        w_value_grad,
        w_out_grad,
        c_query_grad,
        c_key_grad,
        c_value_grad,
        c_out_grad,
        gate_w_grad,
        up_w_grad,
        down_grad,
    )
    shard_dims = (1, 1, 1, 0, 1, 1, 1, 0, 1, 1, 0)
    piece_rows = tuple(
        (to_pieces(grad, place, shards) for grad, place in zip(full_grads, shard_dims))
    )
    received = (
        lax.all_to_all(
            piece_rows[0].astype(jnp.bfloat16),
            ("dp", "enc"),
            split_axis=0,
            concat_axis=0,
            tiled=True,
        ).astype(jnp.float32),
        lax.all_to_all(
            piece_rows[1].astype(jnp.bfloat16),
            ("dp", "enc"),
            split_axis=0,
            concat_axis=0,
            tiled=True,
        ).astype(jnp.float32),
        lax.all_to_all(
            piece_rows[2].astype(jnp.bfloat16),
            ("dp", "enc"),
            split_axis=0,
            concat_axis=0,
            tiled=True,
        ).astype(jnp.float32),
        lax.all_to_all(
            piece_rows[3].astype(jnp.bfloat16),
            ("dp", "enc"),
            split_axis=0,
            concat_axis=0,
            tiled=True,
        ).astype(jnp.float32),
        lax.all_to_all(
            piece_rows[4].astype(jnp.bfloat16),
            ("dp", "enc"),
            split_axis=0,
            concat_axis=0,
            tiled=True,
        ).astype(jnp.float32),
        lax.all_to_all(
            piece_rows[5].astype(jnp.bfloat16),
            ("dp", "enc"),
            split_axis=0,
            concat_axis=0,
            tiled=True,
        ).astype(jnp.float32),
        lax.all_to_all(
            piece_rows[6].astype(jnp.bfloat16),
            ("dp", "enc"),
            split_axis=0,
            concat_axis=0,
            tiled=True,
        ).astype(jnp.float32),
        lax.all_to_all(
            piece_rows[7].astype(jnp.bfloat16),
            ("dp", "enc"),
            split_axis=0,
            concat_axis=0,
            tiled=True,
        ).astype(jnp.float32),
        lax.all_to_all(
            piece_rows[8].astype(jnp.bfloat16),
            ("dp", "enc"),
            split_axis=0,
            concat_axis=0,
            tiled=True,
        ).astype(jnp.float32),
        lax.all_to_all(
            piece_rows[9].astype(jnp.bfloat16),
            ("dp", "enc"),
            split_axis=0,
            concat_axis=0,
            tiled=True,
        ).astype(jnp.float32),
        lax.all_to_all(
            piece_rows[10].astype(jnp.bfloat16),
            ("dp", "enc"),
            split_axis=0,
            concat_axis=0,
            tiled=True,
        ).astype(jnp.float32),
    )
    weight_grads = tuple(
        (
            from_pieces(piece, place, grad.shape, shards)
            for piece, place, grad in zip(received, shard_dims, full_grads)
        )
    )
    small_sums = lax.psum(
        (gain_one_grad, gain_two_grad, gain_three_grad, table_grad), ("dp", "enc")
    )
    return (
        hidden_out,
        hidden_grad,
        encoder_grad,
        small_sums[0],
        weight_grads[0],
        weight_grads[1],
        weight_grads[2],
        weight_grads[3],
        small_sums[3],
        small_sums[1],
        weight_grads[4],
        weight_grads[5],
        weight_grads[6],
        weight_grads[7],
        small_sums[2],
        weight_grads[8],
        weight_grads[9],
        weight_grads[10],
    )


def solution(mesh):
    return jax.shard_map(
        fast_body if dict(mesh.shape) == {"dp": 8, "enc": 4} else body,
        mesh=mesh,
        in_specs=(
            P(("dp", "enc"), None),
            P(("dp", "enc"), None),
            P(("dp", "enc"), None),
            P("dp", None),
            P("dp", None),
            P(),
            P(),
            P(None, ("dp", "enc")),
            P(None, ("dp", "enc")),
            P(None, ("dp", "enc")),
            P(("dp", "enc"), None),
            P(),
            P(),
            P(None, ("dp", "enc")),
            P(None, ("dp", "enc")),
            P(None, ("dp", "enc")),
            P(("dp", "enc"), None),
            P(),
            P(None, ("dp", "enc")),
            P(None, ("dp", "enc")),
            P(("dp", "enc"), None),
        ),
        out_specs=(
            P(("dp", "enc"), None),
            P(("dp", "enc"), None),
            P(("dp", "enc"), None),
            P(),
            P(None, ("dp", "enc")),
            P(None, ("dp", "enc")),
            P(None, ("dp", "enc")),
            P(("dp", "enc"), None),
            P(),
            P(),
            P(None, ("dp", "enc")),
            P(None, ("dp", "enc")),
            P(None, ("dp", "enc")),
            P(("dp", "enc"), None),
            P(),
            P(None, ("dp", "enc")),
            P(None, ("dp", "enc")),
            P(("dp", "enc"), None),
        ),
        check_vma=False,
    )
```

```python
import functools

import jax
import jax.numpy as jnp
from jax import lax
from jax.experimental import pallas as pl
from jax.experimental.pallas import tpu as pltpu
from jax.sharding import PartitionSpec as P

HEADS = 6
HEAD = 64
BUCKETS = 32
EPSILON = 1e-06
MASKED = -1e30
PAD = 16
MESH = pl.DeviceIdType.MESH
LOW = jnp.bfloat16
F32 = jnp.float32
NN = (((1,), (0,)), ((), ()))
NT = (((1,), (1,)), ((), ()))
TN = (((0,), (0,)), ((), ()))
ANY = pl.BlockSpec(memory_space=pl.ANY)
VM = pl.BlockSpec(memory_space=pltpu.VMEM)


def mm(left, right, dims=NN):
    return lax.dot_general(left, right, dims, preferred_element_type=F32)


def places():
    dp = lax.axis_index("dp")
    enc = lax.axis_index("enc")
    core = lax.rem(dp, 2)
    x = lax.rem(lax.div(dp, 2), 2)
    y = lax.div(dp, 4)
    sib = dp + 1 - 2 * core
    xn = dp + 2 - 4 * x
    yn = dp + 4 - 8 * y
    return dp, enc, sib, xn, yn


def enter(dp, enc, sib, xn, yn):
    barrier = pltpu.get_barrier_semaphore()
    targets = [(sib, enc), (xn, enc), (yn, enc), (xn + yn - dp, enc)]
    targets += [(dp, lax.rem(enc + k, 4)) for k in (1, 2, 3)]
    for target in targets:
        pl.semaphore_signal(barrier, inc=1, device_id=target, device_id_type=MESH)
    pl.semaphore_wait(barrier, len(targets))


class Sems:
    def __init__(self, send, recv):
        self.send, self.recv, self.used = send, recv, 0

    def take(self, count):
        first = self.used
        self.used += count
        return first


def remote(src, dst, send, recv, target):
    return pltpu.make_async_remote_copy(
        src_ref=src, dst_ref=dst, send_sem=send, recv_sem=recv, device_id=target, device_id_type=MESH
    )


class ZGather:
    def __init__(self, at, own, where, sems):
        self.at, self.own, self.sems = at, own, sems
        self.dp, self.enc = where[0], where[1]
        self.base = sems.take(6)

    def _copy(self, hop, side):
        s = self.sems
        place = self.enc - side * hop
        src = self.own if hop == 0 else self.at(place)
        return remote(
            src, self.at(place), s.send.at[self.base + hop + (3 if side == 1 else 0)],
            s.recv.at[self.base + place], (self.dp, self.enc + side),
        )

    def _has(self, hop, side):
        enc = self.enc
        return enc - hop >= 0 if side == 1 else enc + hop <= 3

    def _goes(self, side):
        return self.enc < 3 if side == 1 else self.enc > 0

    def start(self):
        for side in (1, -1):

            @pl.when(self._goes(side))
            def _(side=side):
                self._copy(0, side).start()

    def hop(self, hop):
        s = self.sems
        for side in (1, -1):

            @pl.when(self._has(hop, side))
            def _(side=side):
                place = self.enc - side * hop
                remote(
                    self.at(place), self.at(place), s.send.at[self.base], s.recv.at[self.base + place],
                    (self.dp, self.enc),
                ).wait_recv()

            if hop < 3:

                @pl.when(self._has(hop, side) & self._goes(side))
                def _(side=side):
                    self._copy(hop, side).start()

    def finish(self):
        for side in (1, -1):
            for hop in (0, 1, 2):

                @pl.when(self._has(hop, side) & self._goes(side))
                def _(side=side, hop=hop):
                    self._copy(hop, side).wait_send()


class ChipGather:
    def __init__(self, at, own, where, sems):
        self.at, self.own, self.sems, self.where = at, own, sems, where
        self.base = sems.take(9)

    def _copy(self, i):
        dp, enc, sib, xn, yn = self.where
        diag = xn + yn - dp
        block, part, target = (
            (dp, 0, xn),
            (dp, 0, yn),
            (dp, 0, sib),
            (xn, 0, sib),
            (yn, 0, sib),
            (xn, 1, yn),
            (yn, 2, xn),
            (diag, 1, sib),
            (diag, 2, sib),
        )[i]
        src = self.own if i < 3 else self.at(block, part)
        s = self.sems
        return remote(
            src, self.at(block, part), s.send.at[self.base + i], s.recv.at[self.base + i], (target, enc)
        )

    def step1(self):
        for i in (0, 1, 2):
            self._copy(i).start()

    def step2(self):
        self._copy(0).wait_recv()
        self._copy(5).start()
        self._copy(3).start()
        self._copy(1).wait_recv()
        self._copy(6).start()
        self._copy(4).start()

    def step3(self):
        self._copy(5).wait_recv()
        self._copy(7).start()
        self._copy(6).wait_recv()
        self._copy(8).start()

    def done(self):
        for i in (2, 3, 4, 7, 8):
            self._copy(i).wait_recv()

    def finish(self):
        for i in range(9):
            self._copy(i).wait_send()


def over(values, by):
    return lax.shift_right_logical(values * ((1 << 16) // by + 1), 16)


def regroup_matrix(count, width, block):
    shape = (4 * block, count * 4 * width)
    row = lax.broadcasted_iota(jnp.int32, shape, 0)
    col = lax.broadcasted_iota(jnp.int32, shape, 1)
    place = over(row, block)
    inside = row - place * block
    m = over(inside, width)
    take = (m * 4 + place) * width + inside - m * width
    return jnp.where((take == col) & (m < count), 1.0, 0.0).astype(LOW)


def rms_rows(values, gain):
    inv = lax.rsqrt(jnp.mean(values * values, axis=-1, keepdims=True) + EPSILON)
    return values * inv * gain


def low_lanes(rows):
    return lax.broadcasted_iota(jnp.int32, (rows, 2 * HEAD), 1) < HEAD


def one_head(pair, half):
    keep = low_lanes(pair.shape[0])
    if half:
        keep = jnp.logical_not(keep)
    return jnp.where(keep, pair.astype(F32), 0.0).astype(LOW)


def self_bias(rel_u, rows, cols):
    wide = jnp.broadcast_to(rel_u, (rows, rel_u.shape[1]))
    return pltpu.roll(wide, 0, 1, stride=1, stride_axis=0)[:, :cols]


def item_of(lengths_ref, place):
    end, item = jnp.int32(0), jnp.zeros_like(place)
    for b in range(4):
        end = end + lengths_ref[0, b]
        item = item + jnp.where(end <= place, 1, 0)
    return item


def attention_pair(q_pair, k_pair, v_pair, allowed, biases, keep_probs):
    rows = q_pair.shape[0]
    nums, totals = [], []
    for half in (0, 1):
        scores = mm(one_head(q_pair, half), k_pair, NT)
        if biases is not None:
            scores = scores + biases[half]
        scores = jnp.where(allowed, scores, MASKED)
        weights = jnp.exp(scores - jnp.max(scores, axis=1, keepdims=True))
        totals.append(jnp.sum(weights, axis=1, keepdims=True))
        probs = weights.astype(LOW)
        keep_probs(half, probs)
        nums.append(mm(probs, v_pair))
    low = low_lanes(rows)
    return jnp.where(low, nums[0], nums[1]), jnp.where(low, totals[0], totals[1])


def forward_kernel(
    width,
    tgt_len, enc_len, x_ref, e_ref, dy_ref, m0, m1, m2, m3, m4, m5, m6, m7, gate_ref, up_ref, down_ref, gain1, gain2, gain3, buckets, table,
    watt_out, wff_out, dy_out, x_out, e_out, x1_out, kv1_out, kv2_out, pr1_out, pr2_out,
    x2_out, n3_out, q1_out, q2_out, num1_out, num2_out, tot1_out, tot2_out,
    w, packed, own_att, ff_own, x_rows, e_rows, dy_rows, x1_rows, kv1, kv2, pr1, pr2, send, recv, local,
):
    where = places()
    dp, enc, sib, xn, yn = where
    sems = Sems(send, recv)
    own, wide = x_rows.shape
    own_enc = e_rows.shape[0]
    inner = HEADS * HEAD
    line = 4 * width
    ff_rows = ff_own.shape[1]
    ff_half = (ff_rows // 2 + PAD - 1) // PAD * PAD
    group = 4 * own

    def rows_at(ref, first, count):
        return ref.at[pl.ds(pl.multiple_of(first, PAD), count), :]

    def mats_at(ref, lo, hi, first, count):
        return ref.at[lo:hi, pl.ds(pl.multiple_of(first, PAD), count), :]

    zs = [
        ZGather(lambda e, g=g: packed.at[g, e], own_att.at[g], where, sems) for g in (0, 1)
    ]
    chips = []
    for lo in (0, 2, 4, 6):
        hi = lo + 2
        cuts = ((lo, hi), (lo, lo + 1), (lo + 1, hi))
        chips.append(
            ChipGather(
                lambda d, part, cuts=cuts: mats_at(w, *cuts[part], d * line, line),
                mats_at(w, lo, hi, dp * line, line), where, sems,
            )
        )
    ff_cuts = ((0, ff_rows), (0, ff_half), (ff_half, ff_rows - ff_half))
    ffs = [
        ChipGather(
            lambda d, part, m=m: mats_at(wff_out, m, m + 1, d * ff_rows + ff_cuts[part][0], ff_cuts[part][1]),
            ff_own.at[m : m + 1], where, sems,
        )
        for m in range(3)
    ]
    dyz = ZGather(lambda e: rows_at(dy_out, e * own, own), dy_rows, where, sems)
    kvz = ZGather(lambda e: rows_at(kv1, e * own, own), rows_at(kv1, enc * own, own), where, sems)
    kvz2 = ZGather(
        lambda e: rows_at(kv2, e * own_enc, own_enc), rows_at(kv2, enc * own_enc, own_enc), where, sems
    )

    def save(i, src, dst):
        return pltpu.make_async_copy(src, dst, local.at[i])

    saves = [
        save(0, dy_rows, rows_at(dy_out, enc * own, own)),
        save(1, ff_own, mats_at(wff_out, 0, 3, dp * ff_rows, ff_rows)),
        save(2, w, watt_out),
        save(3, x_rows, x_out),
        save(4, e_rows, e_out),
        save(5, x1_rows, x1_out),
        save(6, kv1, kv1_out),
        save(7, kv2, kv2_out),
        save(8, pr1, pr1_out),
        save(9, pr2, pr2_out),
    ]

    for g, refs in enumerate(((m0, m1, m2, m3), (m4, m5, m6, m7))):
        rows = jnp.concatenate([ref[...] for ref in refs], axis=0).astype(LOW)
        own_att[g] = rows
        packed[g, enc] = rows
    for m, ref in enumerate((gate_ref, up_ref, down_ref)):
        ff_own[m] = ref[...].astype(LOW)
    enter(*where)
    zs[0].start()
    zs[1].start()
    ffs[0].step1()
    regroup = regroup_matrix(4, width, 4 * width)

    def unpack(g):
        rows = mm(regroup, packed[g].reshape(4 * line, wide)).astype(LOW)
        for m in range(4):
            w[4 * g + m, pl.ds(pl.multiple_of(dp * line, PAD), line), :] = rows[m * line : (m + 1) * line]

    x = jnp.transpose(x_ref[...].astype(F32))
    x_rows[...] = x.astype(LOW)
    n1 = rms_rows(x, gain1[...][None, :]).astype(LOW)
    dy_rows[...] = jnp.transpose(dy_ref[...].astype(F32)).astype(LOW)
    e_rows[...] = jnp.transpose(e_ref[...].astype(F32)).astype(LOW)
    for i in (0, 1, 3, 4):
        saves[i].start()
    rel_u = rel_rows(buckets, table, enc * own, own, group)
    zs[0].hop(1)
    zs[0].hop(2)
    zs[1].hop(1)
    zs[0].hop(3)
    unpack(0)
    chips[0].step1()
    chips[1].step1()
    zs[1].hop(2)
    dyz.start()
    zs[1].hop(3)
    chips[0].step2()
    unpack(1)
    chips[1].step2()
    chips[2].step1()
    ffs[0].step2()
    chips[0].step3()
    dyz.hop(1)
    chips[0].done()
    own_enc_rows = pl.ds(pl.multiple_of(enc * own_enc, PAD), own_enc)
    kv2[own_enc_rows, 0:inner] = mm(e_rows[...], w[0], NT).astype(LOW)
    kv2[own_enc_rows, inner : 2 * inner] = mm(e_rows[...], w[1], NT).astype(LOW)
    kvz2.start()
    chips[3].step1()
    chips[1].step3()
    chips[1].done()
    own_rows = pl.ds(pl.multiple_of(enc * own, PAD), own)
    kv1[own_rows, 0:inner] = mm(n1, w[2], NT).astype(LOW)
    kv1[own_rows, inner : 2 * inner] = mm(n1, w[3], NT).astype(LOW)
    kvz.start()
    chips[2].step2()
    kvz2.hop(1)
    chips[3].step2()
    ffs[1].step1()
    ffs[2].step1()
    kvz.hop(1)
    chips[2].step3()
    ffs[0].step3()
    chips[2].done()
    q1 = mm(n1, w[4], NT).astype(LOW)
    q1_out[...] = q1
    kvz2.hop(2)
    kvz.hop(2)
    dyz.hop(2)
    chips[3].step3()
    ffs[1].step2()
    ffs[2].step2()
    ffs[1].step3()
    kvz.hop(3)

    row_place = enc * own + lax.broadcasted_iota(jnp.int32, (own, 1), 0)
    col_place = lax.broadcasted_iota(jnp.int32, (1, group), 1)
    own_items = item_of(tgt_len, row_place)
    allowed = (own_items == item_of(tgt_len, col_place)) & (col_place <= row_place)
    for pair in range(HEADS // 2):
        lanes = slice(pair * 2 * HEAD, (pair + 1) * 2 * HEAD)
        far = slice(inner + pair * 2 * HEAD, inner + (pair + 1) * 2 * HEAD)

        def keep(half, probs, pair=pair):
            pr1[2 * pair + half] = probs

        num, total = attention_pair(
            q1[:, lanes], kv1[:, lanes], kv1[:, far], allowed,
            [self_bias(rel_u[2 * pair + half : 2 * pair + half + 1, :], own, group) for half in (0, 1)],
            keep,
        )
        num1_out[:, lanes] = num
        tot1_out[:, lanes] = total
    chips[3].done()
    for i in (2, 6, 8):
        saves[i].start()
    o1 = (num1_out[...] / tot1_out[...]).astype(LOW)
    x1 = x + mm(o1, w[5])
    x1_rows[...] = x1
    saves[5].start()
    n2 = rms_rows(x1, gain2[...][None, :]).astype(LOW)
    q2 = mm(n2, w[6], NT).astype(LOW)
    q2_out[...] = q2
    ffs[2].step3()
    kvz2.hop(3)
    saves[7].start()
    enc_place = lax.broadcasted_iota(jnp.int32, (1, 4 * own_enc), 1)
    allowed2 = own_items == item_of(enc_len, enc_place)
    for pair in range(HEADS // 2):
        lanes = slice(pair * 2 * HEAD, (pair + 1) * 2 * HEAD)
        far = slice(inner + pair * 2 * HEAD, inner + (pair + 1) * 2 * HEAD)

        def keep2(half, probs, pair=pair):
            pr2[2 * pair + half] = probs

        num, total = attention_pair(
            q2[:, lanes], kv2[:, lanes], kv2[:, far], allowed2, None, keep2
        )
        num2_out[:, lanes] = num
        tot2_out[:, lanes] = total
    saves[9].start()
    o2 = (num2_out[...] / tot2_out[...]).astype(LOW)
    x2 = x1 + mm(o2, w[7])
    x2_out[...] = x2
    n3_out[...] = rms_rows(x2, gain3[...][None, :]).astype(LOW)
    dyz.hop(3)
    for part in ffs:
        part.done()
    for part in zs + chips + ffs + [dyz, kvz, kvz2]:
        part.finish()
    for c in saves:
        c.wait()


def sds(shape, dtype):
    return jax.ShapeDtypeStruct(shape, dtype)


def rel_rows(buckets, table, first, own, group):
    inside = bucket_rows(buckets, first, own, group, 0)
    return lax.dot_general(
        table[...], inside, NN, precision=lax.Precision.HIGHEST, preferred_element_type=F32
    )


def bucket_rows(buckets, first, own, group, turn):
    row = buckets[...][None, :]
    bucket = lax.broadcasted_iota(jnp.int32, (BUCKETS, row.shape[1]), 0)
    starts = jnp.sum(jnp.where(row < bucket, 1.0, 0.0), axis=1, keepdims=True)
    ends = jnp.sum(jnp.where(row <= bucket, 1.0, 0.0), axis=1, keepdims=True)
    k = lax.broadcasted_iota(jnp.int32, (1, group + own), 1)
    k = k - turn if turn else jnp.where(k < group, k, k - group - own)
    distance = (first - k).astype(F32)
    return jnp.where((distance >= starts) & (distance < ends), 1.0, 0.0)


def call_forward(width, tgt_len, enc_len, x, e, dy, mats, ffs, gains, buckets, table):
    wide, own = x.shape
    own_enc = e.shape[1]
    inner = HEADS * HEAD
    ff_rows = ffs[0].shape[0]
    SM = pl.BlockSpec(memory_space=pltpu.SMEM)
    saved = (
        sds((8, inner, wide), LOW),
        sds((3, 8 * ff_rows, wide), LOW),
        sds((4 * own, wide), LOW),
        sds((own, wide), LOW),
        sds((own_enc, wide), LOW),
        sds((own, wide), F32),
        sds((4 * own, 2 * inner), LOW),
        sds((4 * own_enc, 2 * inner), LOW),
        sds((HEADS, own, 4 * own), LOW),
        sds((HEADS, own, 4 * own_enc), LOW),
    )
    return pl.pallas_call(
        functools.partial(forward_kernel, width),
        out_shape=saved + (
            sds((own, wide), F32),
            sds((own, wide), LOW),
            sds((own, inner), LOW),
            sds((own, inner), LOW),
            sds((own, inner), F32),
            sds((own, inner), F32),
            sds((own, inner), F32),
            sds((own, inner), F32),
        ),
        in_specs=[SM, SM] + [VM] * 19,
        out_specs=(ANY,) * 10 + (VM,) * 8,
        scratch_shapes=[
            pltpu.VMEM((8, inner, wide), LOW),
            pltpu.VMEM((2, 4, 4 * width, wide), LOW),
            pltpu.VMEM((2, 4 * width, wide), LOW),
            pltpu.VMEM((3, ff_rows, wide), LOW),
            pltpu.VMEM((own, wide), LOW),
            pltpu.VMEM((own_enc, wide), LOW),
            pltpu.VMEM((own, wide), LOW),
            pltpu.VMEM((own, wide), F32),
            pltpu.VMEM((4 * own, 2 * inner), LOW),
            pltpu.VMEM((4 * own_enc, 2 * inner), LOW),
            pltpu.VMEM((HEADS, own, 4 * own), LOW),
            pltpu.VMEM((HEADS, own, 4 * own_enc), LOW),
            pltpu.SemaphoreType.DMA((96,)),
            pltpu.SemaphoreType.DMA((96,)),
            pltpu.SemaphoreType.DMA((10,)),
        ],
        compiler_params=pltpu.CompilerParams(
            collective_id=1, has_side_effects=True, vmem_limit_bytes=56 * 2**20
        ),
        name="attention_forward",
    )(tgt_len, enc_len, x, e, dy, *mats, *ffs, *gains, buckets, table)


class LineMeet:
    def __init__(self, src, got, meet, where, sems):
        self.src, self.got, self.meet, self.sems = src, got, meet, sems
        self.dp, self.enc = where[0], where[1]
        self.base = sems.take(4)
        self.middle = (self.enc == 1) | (self.enc == 2)
        self.far = jnp.where(self.middle, 3 * (2 - self.enc), 3 - self.enc)
        self.near = jnp.where(self.middle, 3 * (self.enc - 1), 1 + lax.div(self.enc, 2))
        self.other = jnp.where(self.middle, 3 - self.enc, 2 - lax.div(self.enc, 2))

    def _copy(self, src, dst, i, j, target):
        s = self.sems
        return remote(src, dst, s.send.at[self.base + i], s.recv.at[self.base + j], (self.dp, target))

    def _sends(self):
        src, got, meet = self.src, self.got, self.meet
        end = (
            (src.at[self.near], got.at[0], 0, 0, self.near),
            (src.at[self.other], meet.at[0], 1, 2, self.near),
            (src.at[self.far], got.at[0], 2, 0, self.far),
        )
        mid = (
            (src.at[self.far], meet.at[1], 0, 3, self.other),
            (meet.at[0], got.at[1], 1, 1, self.other),
            (meet.at[1], got.at[1], 2, 1, self.near),
        )
        return end, mid

    def ready(self, step):
        end, mid = self._sends()

        @pl.when(jnp.logical_not(self.middle))
        def _():
            self._copy(*end[step]).start()

        if step == 2:

            @pl.when(self.middle)
            def _():
                self._copy(*mid[0]).start()

    def order(self):
        return (
            jnp.where(self.middle, self.other, self.near), jnp.where(self.middle, self.near, self.other), self.far
        )

    def merge(self):
        end, mid = self._sends()

        @pl.when(self.middle)
        def _():
            for i, place in ((0, self.other), (1, self.near)):
                self._copy(self.meet.at[i], self.meet.at[i], 0, 2 + i, self.enc).wait_recv()
                self.meet[i] = (self.meet[i].astype(F32) + self.src[place].astype(F32)).astype(LOW)
                self._copy(*mid[1 + i]).start()

    def wait(self):
        for i in (0, 1):
            self._copy(self.got.at[i], self.got.at[i], 0, i, self.enc).wait_recv()

    def finish(self):
        end, mid = self._sends()

        @pl.when(jnp.logical_not(self.middle))
        def _():
            for args in end:
                self._copy(*args).wait_send()

        @pl.when(self.middle)
        def _():
            for args in mid:
                self._copy(*args).wait_send()


class ZScatter:
    def __init__(self, src_at, dst_at, where, sems, meet=None):
        self.src_at, self.dst_at, self.sems, self.meet = src_at, dst_at, sems, meet
        self.dp, self.enc = where[0], where[1]
        self.base = sems.take(3 if meet is None else 4)
        self.middle = (self.enc == 1) | (self.enc == 2)

    def _copy(self, place, merged=False):
        k = lax.rem(place - self.enc + 4, 4)
        s = self.sems
        return remote(
            self.meet if merged else self.src_at(place), self.dst_at(3 - k),
            s.send.at[self.base + k - 1], s.recv.at[self.base + 3 - k], (self.dp, place),
        )

    def _to_meet(self):
        s = self.sems
        far = 3 - self.enc
        return remote(
            self.src_at(far), self.meet, s.send.at[self.base + 3], s.recv.at[self.base + 3],
            (self.dp, 1 + lax.div(self.enc, 2)),
        )

    def start(self, place):
        self._copy(place).start()

    def start_all(self):
        enc = self.enc
        if self.meet is None:
            for k in (2, 1, 3):
                self.start(lax.rem(enc + k, 4))
            return

        @pl.when(jnp.logical_not(self.middle))
        def _():
            self._to_meet().start()
            self.start(lax.rem(enc + 2, 4))
            self.start(1 + lax.div(enc, 2))

        @pl.when(self.middle)
        def _():
            self.start(enc - 1)
            self.start(enc + 1)

    def merge(self):
        @pl.when(self.middle)
        def _():
            far = lax.rem(self.enc + 2, 4)
            self._to_meet().wait_recv()
            self.meet[...] = (self.meet[...].astype(F32) + self.src_at(far)[...].astype(F32)).astype(LOW)
            self._copy(far, merged=True).start()

    def _each(self, act):
        enc = self.enc
        if self.meet is None:
            for k in (1, 2, 3):
                act(lax.rem(enc + k, 4))
            return
        act(lax.rem(enc + 2, 4))

        @pl.when(enc > 0)
        def _():
            act(enc - 1)

        @pl.when(enc < 3)
        def _():
            act(enc + 1)

    def wait(self):
        def one(place):
            k = lax.rem(self.enc - place + 4, 4)
            s = self.sems
            remote(
                self.dst_at(3 - k), self.dst_at(3 - k), s.send.at[self.base], s.recv.at[self.base + 3 - k],
                (self.dp, self.enc),
            ).wait_recv()

        self._each(one)

    def clear(self):
        if self.meet is not None:

            @pl.when(self.enc == 0)
            def _():
                ref = self.dst_at(2)
                ref[...] = jnp.zeros(ref.shape, ref.dtype)

            @pl.when(self.enc == 3)
            def _():
                ref = self.dst_at(0)
                ref[...] = jnp.zeros(ref.shape, ref.dtype)

    def finish(self):
        self._each(lambda place: self._copy(place).wait_send())
        if self.meet is not None:

            @pl.when(jnp.logical_not(self.middle))
            def _():
                self._to_meet().wait_send()


class ChipReduce:
    def __init__(self, src, got, last, cuts, own, where, sems):
        self.src, self.got, self.last, self.cuts, self.own = src, got, last, cuts, own
        self.sems, self.where = sems, where
        self.x = lax.rem(lax.div(where[0], 2), 2)
        self.y = lax.div(where[0], 4)
        self.base = sems.take(2 * len(cuts))

    def _copy(self, i, second):
        dp, enc, sib, xn, yn = self.where
        m, lo, hi, by_x = self.cuts[i]
        s, at = self.sems, self.base + 2 * i + (1 if second else 0)
        if second:
            src = self.got.at[m, 1 - self.y if by_x else 1 - self.x, lo:hi]
            dst = self.last.at[m, lo:hi]
        else:
            src = self.src.at[m, :, 1 - self.x, lo:hi] if by_x else self.src.at[m, 1 - self.y, :, lo:hi]
            dst = self.got.at[m, :, lo:hi]
        target = xn if by_x != second else yn
        return remote(src, dst, s.send.at[at], s.recv.at[at], (target, enc))

    def start(self, only=None):
        for i in range(len(self.cuts)) if only is None else (only,):
            self._copy(i, False).start()

    def turn(self):
        for i, (m, lo, hi, by_x) in enumerate(self.cuts):
            self._copy(i, False).wait_recv()
            for k in range(2):
                self.got[m, k, lo:hi] = (
                    self.own(m, k, lo, hi, by_x).astype(F32) + self.got[m, k, lo:hi].astype(F32)
                ).astype(LOW)
            self._copy(i, True).start()

    def totals(self):
        out = []
        for i, (m, lo, hi, by_x) in enumerate(self.cuts):
            self._copy(i, True).wait_recv()
            mine = self.got[m, self.y if by_x else self.x, lo:hi]
            out.append(mine.astype(F32) + self.last[m, lo:hi].astype(F32))
        return out

    def finish(self):
        for i in range(len(self.cuts)):
            self._copy(i, False).wait_send()
            self._copy(i, True).wait_send()


def rms_back(values, gain, grad):
    inv = lax.rsqrt(jnp.mean(values * values, axis=-1, keepdims=True) + EPSILON)
    scaled = grad * gain
    mean = jnp.mean(values * scaled, axis=-1, keepdims=True)
    gain_grad = jnp.sum(grad * values * inv, axis=0, keepdims=True)
    return inv * scaled - values * (inv * inv * inv * mean), gain_grad


GELU_A = 0.7978845608028654
GELU_B = 0.044715


def ff_kernel(
    n3_ref, x2_hbm, dyall_ref, wff_ref, gain3,
    dx2_out, gain_out, down_out, part_out, sums_out,
    w, n3, dy, back, act, dgate, dup, part, got, meet, grads, core_got, own_sum, out_part, chip_got, chip_last, x2_ref, send, recv, local,
):
    where = places()
    dp, enc, sib, xn, yn = where
    core = lax.rem(dp, 2)
    sems = Sems(send, recv)
    own = n3_ref.shape[0]
    ff_rows = grads.shape[4]
    ff_half = (ff_rows // 2 + PAD - 1) // PAD * PAD
    chip_x = lax.rem(lax.div(dp, 2), 2)
    chip_y = lax.div(dp, 4)

    def rows_of(place):
        return pl.ds(pl.multiple_of(place * own, PAD), own)

    gather = ZGather(lambda e: n3.at[rows_of(e), :], n3_ref, where, sems)
    scatter = LineMeet(part, got, meet, where, sems)
    loads = [
        pltpu.make_async_copy(wff_ref, w, local.at[0]),
        pltpu.make_async_copy(dyall_ref, dy, local.at[1]),
    ]
    pull = pltpu.make_async_copy(x2_hbm, x2_ref, local.at[2])
    for c in loads + [pull]:
        c.start()
    enter(*where)
    gather.start()
    n3[rows_of(enc), :] = n3_ref[...]
    for c in loads:
        c.wait()

    back[...] = mm(dy[...], w[2], NT)

    def block(place):
        rows = rows_of(place)
        normed = n3[rows, :]
        gate = mm(normed, w[0], NT)
        up = mm(normed, w[1], NT)
        dh = back[rows, :]
        square = gate * gate
        t = jnp.tanh(GELU_A * gate * (1.0 + GELU_B * square))
        half = 0.5 * (1.0 + t)
        g = gate * half
        slope = half + 0.5 * gate * (1.0 - t * t) * (GELU_A * (1.0 + 3.0 * GELU_B * square))
        hidden = (g * up).astype(LOW)
        dg = (dh * up * slope).astype(LOW)
        du = (dh * g).astype(LOW)
        act[rows, :] = hidden
        dgate[rows, :] = dg
        dup[rows, :] = du
        return mm(dg, w[0]) + mm(du, w[1])

    own_sum[...] = block(enc)
    for step, place in enumerate(scatter.order()):
        gather.hop(step + 1)
        part[place] = block(place).astype(LOW)
        scatter.ready(step)

    base = sems.take(3)

    def swap(m):
        return remote(
            grads.at[m, :, :, 1 - core], core_got.at[m], send.at[base + m], recv.at[base + m], (sib, enc)
        )

    def put_grad(m, left, right):
        whole = mm(left[...], right[...], TN).astype(LOW)
        for y in range(2):
            for x in range(2):
                for c in range(2):
                    at = (4 * y + 2 * x + c) * ff_rows
                    grads[m, y, x, c] = whole[at : at + ff_rows]
        swap(m).start()

    def sum_cores(m):
        swap(m).wait_recv()
        for y in range(2):
            core_got[m, y] = (grads[m, y, :, core].astype(F32) + core_got[m, y].astype(F32)).astype(LOW)

    down = ChipReduce(
        core_got, chip_got, chip_last, ((2, 0, ff_half, True), (2, ff_half, ff_rows, False)),
        lambda m, k, lo, hi, by_x: core_got[m, k, chip_x, lo:hi] if by_x else core_got[m, chip_y, k, lo:hi],
        where, sems,
    )
    saves = [
        pltpu.make_async_copy(out_part, part_out, local.at[0]),
        pltpu.make_async_copy(core_got.at[0:2], sums_out, local.at[1]),
    ]
    put_grad(2, act, dy)
    put_grad(0, dgate, n3)
    sum_cores(2)
    down.start()
    scatter.merge()
    put_grad(1, dup, n3)
    out_part[...] = mm(act[...], w[2]).astype(LOW)
    saves[0].start()
    sum_cores(0)
    sum_cores(1)
    saves[1].start()
    down.turn()
    scatter.wait()
    dn3 = own_sum[...] + got[0].astype(F32) + got[1].astype(F32)
    pull.wait()
    dv, gain_grad = rms_back(x2_ref[...], gain3[...][None, :], dn3)
    dx2_out[...] = dy[rows_of(enc), :].astype(F32) + dv
    gain_out[...] = gain_grad
    for (m, lo, hi, by_x), total in zip(down.cuts, down.totals()):
        down_out[lo:hi] = total
    down.finish()
    gather.finish()
    scatter.finish()
    for m in range(3):
        swap(m).wait_send()
    for c in saves:
        c.wait()


def call_ff(n3, x2, dy_all, wff, gain3):
    own, wide = n3.shape
    ff_all = wff.shape[1]
    ff_rows = ff_all // 8
    group = 4 * own
    return pl.pallas_call(
        ff_kernel,
        out_shape=(
            sds((own, wide), F32),
            sds((1, wide), F32),
            sds((ff_rows, wide), F32),
            sds((group, wide), LOW),
            sds((2, 2, 2, ff_rows, wide), LOW),
        ),
        in_specs=[VM, ANY, ANY, ANY, VM],
        out_specs=(VM, VM, VM, ANY, ANY),
        scratch_shapes=[
            pltpu.VMEM((3, ff_all, wide), LOW),
            pltpu.VMEM((group, wide), LOW),
            pltpu.VMEM((group, wide), LOW),
            pltpu.VMEM((group, ff_all), F32),
            pltpu.VMEM((group, ff_all), LOW),
            pltpu.VMEM((group, ff_all), LOW),
            pltpu.VMEM((group, ff_all), LOW),
            pltpu.VMEM((4, own, wide), LOW),
            pltpu.VMEM((2, own, wide), LOW),
            pltpu.VMEM((2, own, wide), LOW),
            pltpu.VMEM((3, 2, 2, 2, ff_rows, wide), LOW),
            pltpu.VMEM((3, 2, 2, ff_rows, wide), LOW),
            pltpu.VMEM((own, wide), F32),
            pltpu.VMEM((group, wide), LOW),
            pltpu.VMEM((3, 2, ff_rows, wide), LOW),
            pltpu.VMEM((3, ff_rows, wide), LOW),
            pltpu.VMEM((own, wide), F32),
            pltpu.SemaphoreType.DMA((17,)),
            pltpu.SemaphoreType.DMA((17,)),
            pltpu.SemaphoreType.DMA((3,)),
        ],
        compiler_params=pltpu.CompilerParams(
            collective_id=2, has_side_effects=True, vmem_limit_bytes=60 * 2**20
        ),
        name="feed_forward",
    )(n3, x2, dy_all, wff, gain3)


class CoreReduce:
    def __init__(self, lo, grads, core_got, chip_got, chip_last, where, sems):
        self.lo, self.grads, self.core_got, self.where, self.sems = lo, grads, core_got, where, sems
        self.base = sems.take(2)
        rows = grads.shape[4]
        x = lax.rem(lax.div(where[0], 2), 2)
        y = lax.div(where[0], 4)

        def own(m, k, first, last, by_x):
            return core_got[m, k, x] if by_x else core_got[m, y, k]

        self.chips = ChipReduce(
            core_got, chip_got, chip_last, ((lo, 0, rows, True), (lo + 1, 0, rows, False)), own, where, sems
        )

    def _core(self, i):
        dp, enc, sib, xn, yn = self.where
        s, m = self.sems, self.lo + i
        return remote(
            self.grads.at[m, :, :, 1 - lax.rem(dp, 2)], self.core_got.at[m],
            s.send.at[self.base + i], s.recv.at[self.base + i], (sib, enc),
        )

    def start(self, i):
        self._core(i).start()

    def next(self):
        core = lax.rem(self.where[0], 2)
        for i in (0, 1):
            m = self.lo + i
            self._core(i).wait_recv()
            self.core_got[m] = (self.grads[m, :, :, core].astype(F32) + self.core_got[m].astype(F32)).astype(LOW)
            self.chips.start(i)

    def finish(self):
        for i in (0, 1):
            self._core(i).wait_send()
        self.chips.finish()


class LineReduce:
    def __init__(self, parts, width, line, got, meet, out, where, sems):
        self.parts, self.line, self.got, self.out, self.where = parts, line, got, out, where
        self.rows = line.shape[1]
        self.regroup = regroup_matrix(2 * len(parts), width, self.rows)
        self.z = ZScatter(lambda e: line.at[e], lambda slot: got.at[slot], where, sems, meet)

    def start(self):
        totals = [t.astype(LOW) for part in self.parts for t in part.chips.totals()]
        rows = mm(self.regroup, jnp.concatenate(totals, axis=0)).astype(LOW)
        for e in range(4):
            self.line[e] = rows[e * self.rows : (e + 1) * self.rows]
        self.z.start_all()

    def merge(self):
        self.z.merge()

    def done(self):
        self.z.wait()
        total = self.line[self.where[1]].astype(F32)
        for slot in range(3):
            total = total + self.got[slot].astype(F32)
        self.out[...] = total


def backward_pair(q_pair, k_pair, v_pair, probs_ref, pair, dnum, dtotals):
    rows = q_pair.shape[0]
    parts, scores = [], []
    for half in (0, 1):
        dw = mm(one_head(dnum, half), v_pair, NT)
        ds = (probs_ref[2 * pair + half].astype(F32) * (dw + dtotals[half])).astype(LOW)
        scores.append(ds)
        parts.append(mm(ds, k_pair))
    dq = jnp.where(low_lanes(rows), parts[0], parts[1])
    dk = mm(jnp.concatenate(scores, axis=0), jnp.concatenate([one_head(q_pair, h) for h in (0, 1)], axis=0), TN)
    probs = jnp.concatenate([probs_ref[2 * pair + h] for h in (0, 1)], axis=0)
    dv = mm(probs, jnp.concatenate([one_head(dnum, h) for h in (0, 1)], axis=0), TN)
    return dq, dk, dv, scores


def total_grads(product, total):
    low = low_lanes(product.shape[0])
    out = []
    for half in (0, 1):
        keep = low if half == 0 else jnp.logical_not(low)
        top = jnp.sum(jnp.where(keep, product, 0.0), axis=1, keepdims=True)
        tot = total[:, half * HEAD : half * HEAD + 1]
        out.append(-top / (tot * tot))
    return out


def backward_kernel(
    width,
    gain1, gain2, gain3_grad, buckets, q1, q2, num2, tot2,
    watt_ref, sums_ref, part_hbm, dx2_hbm, kv2_hbm, pr2_hbm, num1_hbm, tot1_hbm, x_hbm, e_hbm, x1_hbm, x2_hbm, kv1_hbm, pr1_hbm,
    att_out, small_out, hidden_out, hidden_grad, encoder_grad, gate_out, up_out,
    w, grads, core_got, chip_got, chip_last, line, line_got, line_meet,
    ff_own, ff_got, ff_last, part_got, part_meet,
    kvp1, kvp1_got, kvp1_meet, kvp2, kvp2_got, kvp2_meet, dq, vec, vec_got,
    part_ref, dx2_ref, kv2, pr2, num1, tot1, x_ref, e_ref, x1_ref, x2_ref, kv1, pr1, out_t, grad_t, enc_t, ff_sum, send, recv, local,
):
    where = places()
    dp, enc, sib, xn, yn = where
    sems = Sems(send, recv)
    own, wide = x_ref.shape
    own_enc = e_ref.shape[0]
    inner = HEADS * HEAD
    chip_x = lax.rem(lax.div(dp, 2), 2)
    chip_y = lax.div(dp, 4)
    ff_rows = ff_last.shape[1]
    part_rows = own // 4
    table_at = vec.shape[2] - 2 * HEAD

    out_z = [
        ZScatter(
            lambda e, a=a, b=b: part_ref.at[e, a:b], lambda slot, a=a, b=b: part_got.at[slot, a:b],
            where, sems, part_meet.at[a:b],
        )
        for a, b in ((0, part_rows), (part_rows, own))
    ]
    kv1_z = ZScatter(lambda e: kvp1.at[e], lambda slot: kvp1_got.at[slot], where, sems, kvp1_meet)
    kv2_z = [
        ZScatter(
            lambda e, p=p: kvp2.at[p, e], lambda slot, p=p: kvp2_got.at[p, slot], where, sems, kvp2_meet.at[p]
        )
        for p in range(HEADS // 2)
    ]
    batches = [CoreReduce(lo, grads, core_got, chip_got, chip_last, where, sems) for lo in (0, 2, 4, 6)]
    lines = [
        LineReduce(batches[2 * i : 2 * i + 2], width, line.at[i], line_got.at[i], line_meet.at[i], att_out.at[i], where, sems)
        for i in (0, 1)
    ]
    ff_cuts = ((0, 0, ff_rows, True), (1, 0, ff_rows, False))
    ff = ChipReduce(
        sums_ref, ff_got, ff_last, ff_cuts, lambda m, k, lo, hi, by_x: ff_own[m, k, lo:hi], where, sems
    )
    vec_base = sems.take(3)
    vec_z = ZScatter(lambda e: vec.at[3], lambda slot: vec_got.at[3 + slot], where, sems)

    def vec_copy(i):
        target = (sib, xn, yn)[i]
        return remote(
            vec.at[i], vec_got.at[i], send.at[vec_base + i], recv.at[vec_base + i], (target, enc)
        )

    def load(slot, m, i):
        return pltpu.make_async_copy(watt_ref.at[m], w.at[slot], local.at[i])

    pulls = [
        pltpu.make_async_copy(src, dst, local.at[12 + i])
        for i, (src, dst) in enumerate(
            (
                (part_hbm, part_ref), (x1_hbm, x1_ref), (kv1_hbm, kv1), (pr1_hbm, pr1), (x_hbm, x_ref),
                (e_hbm, e_ref), (x2_hbm, x2_ref), (dx2_hbm, dx2_ref), (kv2_hbm, kv2), (pr2_hbm, pr2),
                (num1_hbm, num1), (tot1_hbm, tot1),
            )
        )
    ]
    pushes = [
        pltpu.make_async_copy(src, dst, local.at[24 + i])
        for i, (src, dst) in enumerate(
            ((grad_t, hidden_grad), (enc_t, encoder_grad), (ff_sum.at[0], gate_out), (out_t, hidden_out), (ff_sum.at[1], up_out))
        )
    ]
    first_loads = [load(slot, m, slot) for slot, m in enumerate((7, 6, 5, 2, 3))]
    for c in [pulls[7], first_loads[0], pulls[0]] + pulls[8:10] + first_loads[1:3] + pulls[1:7] + pulls[10:] + first_loads[3:]:
        c.start()
    own_ff = [
        pltpu.make_async_copy(
            sums_ref.at[m, :, chip_x, lo:hi] if by_x else sums_ref.at[m, chip_y, :, lo:hi],
            ff_own.at[m, :, lo:hi], local.at[8 + i],
        )
        for i, (m, lo, hi, by_x) in enumerate(ff_cuts)
    ]
    for c in own_ff:
        c.start()
    enter(*where)
    pulls[0].wait()
    out_z[0].start_all()
    ff.start()
    for part in out_z + [kv1_z] + kv2_z + [line.z for line in lines]:
        part.clear()

    def put_grad(m, left, right):
        whole = mm(left, right, TN).astype(LOW)
        rows = 4 * width
        for y in range(2):
            for x in range(2):
                for c in range(2):
                    at = (4 * y + 2 * x + c) * rows
                    grads[m, y, x, c] = whole[at : at + rows]
        batches[m // 2].start(m % 2)

    pulls[7].wait()
    b2 = dx2_ref[...].astype(LOW)
    first_loads[0].wait()
    do2 = mm(b2, w[0], NT)
    dnum2 = (do2 / tot2[...]).astype(LOW)
    prod2 = do2 * num2[...]
    pulls[8].wait()
    pulls[9].wait()
    for pair in range(HEADS // 2):
        lanes = slice(pair * 2 * HEAD, (pair + 1) * 2 * HEAD)
        far = slice(inner + pair * 2 * HEAD, inner + (pair + 1) * 2 * HEAD)
        dtot = total_grads(prod2[:, lanes], tot2[:, lanes])
        dq_pair, dk, dv, _ = backward_pair(
            q2[:, lanes], kv2[:, lanes], kv2[:, far], pr2, pair, dnum2[:, lanes], dtot
        )
        dq[:, lanes] = dq_pair.astype(LOW)
        for e in range(4):
            kvp2[pair, e, :, : 2 * HEAD] = dk[e * own_enc : (e + 1) * own_enc].astype(LOW)
            kvp2[pair, e, :, 2 * HEAD :] = dv[e * own_enc : (e + 1) * own_enc].astype(LOW)
        kv2_z[pair].start_all()
    dq2 = dq[...]
    put_grad(0, (num2[...] / tot2[...]).astype(LOW), b2)
    pulls[1].wait()
    x1 = x1_ref[...]
    put_grad(1, dq2, rms_rows(x1, gain2[...][None, :]).astype(LOW))
    out_z[0].merge()
    first_loads[1].wait()
    dv2, gain2_grad = rms_back(x1, gain2[...][None, :], mm(dq2, w[1]))
    dx1 = dx2_ref[...] + dv2
    b1 = dx1.astype(LOW)
    first_loads[2].wait()
    do1 = mm(b1, w[2], NT)
    late = [load(2, 4, 5), load(0, 0, 6), load(1, 1, 7)]
    for c in late:
        c.start()
    pulls[10].wait()
    pulls[11].wait()
    dnum1 = (do1 / tot1[...]).astype(LOW)
    prod1 = do1 * num1[...]
    batches[0].next()
    pulls[2].wait()
    pulls[3].wait()
    all_scores = []
    for pair in range(HEADS // 2):
        lanes = slice(pair * 2 * HEAD, (pair + 1) * 2 * HEAD)
        far = slice(inner + pair * 2 * HEAD, inner + (pair + 1) * 2 * HEAD)
        dtot = total_grads(prod1[:, lanes], tot1[:, lanes])
        dq_pair, dk, dv, scores = backward_pair(
            q1[:, lanes], kv1[:, lanes], kv1[:, far], pr1, pair, dnum1[:, lanes], dtot
        )
        dq[:, lanes] = dq_pair.astype(LOW)
        for e in range(4):
            kvp1[e, :, lanes] = dk[e * own : (e + 1) * own].astype(LOW)
            kvp1[e, :, far] = dv[e * own : (e + 1) * own].astype(LOW)
        all_scores += scores
    kv1_z.start_all()
    out_z[1].start_all()
    dq1 = dq[...]
    pulls[4].wait()
    x = x_ref[...].astype(F32)
    n1 = rms_rows(x, gain1[...][None, :]).astype(LOW)
    put_grad(2, (num1[...] / tot1[...]).astype(LOW), b1)
    put_grad(3, dq1, n1)
    for z in kv2_z:
        z.merge()
    batches[1].next()
    for c in own_ff:
        c.wait()
    ff.turn()
    vec[0] = jnp.zeros(vec.shape[1:], F32)
    inside = bucket_rows(buckets, enc * own, own, 4 * own, own - 1)
    flip_row = lax.broadcasted_iota(jnp.int32, (own, own), 0)
    flip_col = lax.broadcasted_iota(jnp.int32, (own, own), 1)
    flip = jnp.where(flip_row + flip_col == own - 1, 1.0, 0.0).astype(LOW)
    for h, ds in enumerate(all_scores):
        long = jnp.concatenate([mm(flip, ds), jnp.zeros((own, own), F32)], axis=1)
        turned = pltpu.roll(long, 0, 1, stride=1, stride_axis=0)
        by_distance = jnp.sum(turned, axis=0, keepdims=True)
        vec[0, h : h + 1, table_at : table_at + BUCKETS] = lax.dot_general(
            by_distance, inside, NT, precision=lax.Precision.HIGHEST, preferred_element_type=F32
        )
    batches[0].chips.turn()
    for c in late:
        c.wait()
    dn1 = mm(dq1, w[2])
    batches[1].chips.turn()

    sums2 = []
    for p, z in enumerate(kv2_z):
        z.wait()
        sums2.append(
            (
                kvp2[p, enc].astype(F32) + kvp2_got[p, 0].astype(F32)
                + kvp2_got[p, 1].astype(F32) + kvp2_got[p, 2].astype(F32)
            ).astype(LOW)
        )
    dk2 = jnp.concatenate([t[:, : 2 * HEAD] for t in sums2], axis=1)
    dv2 = jnp.concatenate([t[:, 2 * HEAD :] for t in sums2], axis=1)
    pulls[5].wait()
    put_grad(4, dk2, e_ref[...])
    put_grad(5, dv2, e_ref[...])
    kv1_z.merge()
    lines[0].start()
    batches[2].next()
    enc_t[...] = jnp.transpose(mm(dk2, w[0]) + mm(dv2, w[1]))
    pushes[1].start()

    kv1_z.wait()
    low1 = (
        kvp1[enc].astype(F32) + kvp1_got[0].astype(F32) + kvp1_got[1].astype(F32) + kvp1_got[2].astype(F32)
    ).astype(LOW)
    dk1 = low1[:, :inner]
    dv1 = low1[:, inner:]
    put_grad(6, dk1, n1)
    put_grad(7, dv1, n1)
    batches[2].chips.turn()
    batches[3].next()
    first_loads[3].wait()
    first_loads[4].wait()
    dn1 = dn1 + mm(dk1, w[3]) + mm(dv1, w[4])
    dv_x, gain1_grad = rms_back(x, gain1[...][None, :], dn1)
    vec[0, 0:1, 0:wide] = gain1_grad
    vec[0, 1:2, 0:wide] = gain2_grad
    vec[0, 2:3, 0:wide] = gain3_grad[...]
    vec_copy(0).start()
    out_z[1].merge()
    vec_copy(0).wait_recv()
    vec[1] = vec[0] + vec_got[0]
    vec_copy(1).start()
    batches[3].chips.turn()
    vec_copy(1).wait_recv()
    vec[2] = vec[1] + vec_got[1]
    vec_copy(2).start()
    grad_t[...] = jnp.transpose(dx1 + dv_x)
    pushes[0].start()
    vec_copy(2).wait_recv()
    vec[3] = vec[2] + vec_got[2]
    vec_z.start_all()
    lines[1].start()
    lines[0].merge()
    for (m, lo, hi, by_x), total in zip(ff_cuts, ff.totals()):
        ff_sum[m, lo:hi] = total
    pushes[2].start()
    pushes[4].start()
    for z in out_z:
        z.wait()
    pulls[6].wait()
    out_t[...] = jnp.transpose(
        x2_ref[...] + (part_ref[enc].astype(F32) + part_got[0].astype(F32))
        + (part_got[1].astype(F32) + part_got[2].astype(F32))
    ).astype(LOW)
    pushes[3].start()
    lines[1].merge()
    lines[0].done()
    lines[1].done()
    vec_z.wait()
    small_out[...] = vec[3] + vec_got[3] + vec_got[4] + vec_got[5]
    for done in out_z + kv2_z + [kv1_z, vec_z, ff] + batches + [line.z for line in lines]:
        done.finish()
    for i in range(3):
        vec_copy(i).wait_send()
    for c in pushes:
        c.wait()


def call_backward(width, gain1, gain2, gain3_grad, buckets, small, watt, sums, part, dx2, kv2, pr2, num1, tot1, x, e, x1, x2, kv1, pr1):
    own, wide = x.shape
    own_enc = e.shape[0]
    inner = HEADS * HEAD
    rows = 4 * width
    ff_rows = sums.shape[3]
    small_wide = (wide + 127) // 128 * 128 + 2 * HEAD
    return pl.pallas_call(
        functools.partial(backward_kernel, width),
        out_shape=(
            sds((2, 4 * width, wide), F32),
            sds((8, small_wide), F32),
            sds((wide, own), LOW),
            sds((wide, own), F32),
            sds((wide, own_enc), F32),
            sds((ff_rows, wide), F32),
            sds((ff_rows, wide), F32),
        ),
        in_specs=[VM] * 8 + [ANY] * 14,
        out_specs=(VM,) * 2 + (ANY,) * 5,
        scratch_shapes=[
            pltpu.VMEM((5, inner, wide), LOW),
            pltpu.VMEM((8, 2, 2, 2, rows, wide), LOW),
            pltpu.VMEM((8, 2, 2, rows, wide), LOW),
            pltpu.VMEM((8, 2, rows, wide), LOW),
            pltpu.VMEM((8, rows, wide), LOW),
            pltpu.VMEM((2, 4, 4 * width, wide), LOW),
            pltpu.VMEM((2, 3, 4 * width, wide), LOW),
            pltpu.VMEM((2, 4 * width, wide), LOW),
            pltpu.VMEM((2, 2, ff_rows, wide), LOW),
            pltpu.VMEM((2, 2, ff_rows, wide), LOW),
            pltpu.VMEM((2, ff_rows, wide), LOW),
            pltpu.VMEM((3, own, wide), LOW),
            pltpu.VMEM((own, wide), LOW),
            pltpu.VMEM((4, own, 2 * inner), LOW),
            pltpu.VMEM((3, own, 2 * inner), LOW),
            pltpu.VMEM((own, 2 * inner), LOW),
            pltpu.VMEM((HEADS // 2, 4, own_enc, 4 * HEAD), LOW),
            pltpu.VMEM((HEADS // 2, 3, own_enc, 4 * HEAD), LOW),
            pltpu.VMEM((HEADS // 2, own_enc, 4 * HEAD), LOW),
            pltpu.VMEM((own, inner), LOW),
            pltpu.VMEM((4, 8, small_wide), F32),
            pltpu.VMEM((6, 8, small_wide), F32),
            pltpu.VMEM((4, own, wide), LOW),
            pltpu.VMEM((own, wide), F32),
            pltpu.VMEM(kv2.shape, LOW),
            pltpu.VMEM(pr2.shape, LOW),
            pltpu.VMEM((own, inner), F32),
            pltpu.VMEM((own, inner), F32),
            pltpu.VMEM((own, wide), LOW),
            pltpu.VMEM((own_enc, wide), LOW),
            pltpu.VMEM((own, wide), F32),
            pltpu.VMEM((own, wide), F32),
            pltpu.VMEM(kv1.shape, LOW),
            pltpu.VMEM(pr1.shape, LOW),
            pltpu.VMEM((wide, own), LOW),
            pltpu.VMEM((wide, own), F32),
            pltpu.VMEM((wide, own_enc), F32),
            pltpu.VMEM((2, ff_rows, wide), F32),
            pltpu.SemaphoreType.DMA((66,)),
            pltpu.SemaphoreType.DMA((66,)),
            pltpu.SemaphoreType.DMA((29,)),
        ],
        compiler_params=pltpu.CompilerParams(
            collective_id=3, has_side_effects=True, vmem_limit_bytes=62 * 2**20
        ),
        name="attention_backward",
    )(
        gain1, gain2, gain3_grad, buckets, *small, watt, sums,
        part.reshape(4, own, wide), dx2, kv2, pr2, num1, tot1, x, e, x1, x2, kv1, pr1,
    )


def outputs_kernel(width, *refs):
    big, (att, small) = refs[:6], refs[6:8]
    outs, rows, gains, table = refs[8:14], refs[14:22], refs[22:25], refs[25]
    held, (att_v, small_v), sem = refs[26:32], refs[32:34], refs[34]
    pulls = [pltpu.make_async_copy(a, b, sem.at[i]) for i, (a, b) in enumerate(zip((att, small) + big, (att_v, small_v) + held))]
    pushes = [pltpu.make_async_copy(a, b, sem.at[8 + i]) for i, (a, b) in enumerate(zip(held, outs))]
    for c in pulls:
        c.start()
    pulls[0].wait()
    pulls[1].wait()
    for i, ref in enumerate(rows):
        m = i % 4
        ref[...] = att_v[i // 4, m * width : (m + 1) * width]
    for i, ref in enumerate(gains):
        ref[...] = small_v[i, 0 : ref.shape[0]]
    table_at = small_v.shape[1] - 2 * HEAD
    table[...] = small_v[0:HEADS, table_at : table_at + BUCKETS]
    for pull, push in zip(pulls[2:], pushes):
        pull.wait()
        push.start()
    for push in pushes:
        push.wait()


def call_outputs(width, big, att, small):
    wide = att.shape[2]
    return pl.pallas_call(
        functools.partial(outputs_kernel, width),
        out_shape=tuple(sds(a.shape, a.dtype) for a in big)
        + (sds((width, wide), F32),) * 8
        + (sds((wide,), F32),) * 3
        + (sds((HEADS, BUCKETS), F32),),
        in_specs=[ANY] * 8,
        out_specs=(ANY,) * 6 + (VM,) * 12,
        scratch_shapes=[pltpu.VMEM(a.shape, a.dtype) for a in tuple(big) + (att, small)]
        + [pltpu.SemaphoreType.DMA((14,))],
        compiler_params=pltpu.CompilerParams(vmem_limit_bytes=62 * 2**20),
        name="results",
    )(*big, att, small)


def fast_body(
    hidden_in, encoder_out, grad_out, tgt_lengths, enc_lengths, rel_bucket, norm1_gain,
    self_q, self_k, self_v, self_o, rel_table, norm2_gain,
    cross_q, cross_k, cross_v, cross_o, norm3_gain, ff_gate, ff_up, ff_out,
):
    width = self_q.shape[1]
    mats = (cross_k.T, cross_v.T, self_k.T, self_v.T, self_q.T, self_o, cross_q.T, cross_o)
    (
        watt_all, wff_all, dy_all, x, e, x1, kv1, kv2, pr1, pr2,
        x2, n3, q1, q2, num1, num2, tot1, tot2,
    ) = call_forward(
        width, tgt_lengths, enc_lengths, hidden_in.T, encoder_out.T, grad_out.T, mats,
        (ff_gate.T, ff_up.T, ff_out), (norm1_gain, norm2_gain, norm3_gain), rel_bucket, rel_table.T,
    )
    dx2, gain3_grad, down, part, sums = call_ff(n3, x2, dy_all, wff_all, norm3_gain)
    att, small, hidden_out, hidden_grad, encoder_grad, gate, up = call_backward(
        width, norm1_gain, norm2_gain, gain3_grad, rel_bucket, (q1, q2, num2, tot2),
        watt_all, sums, part, dx2, kv2, pr2, num1, tot1, x, e, x1, x2, kv1, pr1,
    )
    (
        hidden_out, hidden_grad, encoder_grad, gate, up, down,
        o2, q2, o1, q1, k2, v2, k1, v1, g1, g2, g3, table,
    ) = call_outputs(width, (hidden_out, hidden_grad, encoder_grad, gate, up, down), att, small)
    return (
        hidden_out.T, hidden_grad.T, encoder_grad.T, g1, q1.T, k1.T, v1.T, o1, table.T,
        g2, q2.T, k2.T, v2.T, o2, g3, gate.T, up.T, down,
    )


def rms_scale(values, gain):
    return values * lax.rsqrt(jnp.mean(values * values, axis=-1, keepdims=True) + EPSILON) * gain


def gated_gelu(gate_pre, up_pre):
    return jax.nn.gelu(gate_pre, approximate=True) * up_pre


def item_ids(lengths, total_rows):
    ends = jnp.cumsum(lengths)
    places = jnp.arange(total_rows, dtype=jnp.int32)
    return jnp.sum((ends[None, :] <= places[:, None]).astype(jnp.int32), axis=1)


def product(left, right):
    return jnp.dot(left, right, preferred_element_type=jnp.float32)


def product_tn(left, right):
    return lax.dot_general(
        left, right, (((0,), (0,)), ((), ())), preferred_element_type=jnp.float32
    )


def product_nt(left, right):
    return lax.dot_general(
        left, right, (((1,), (1,)), ((), ())), preferred_element_type=jnp.float32
    )


def to_pieces(grad, shard_dim, shards):
    if shard_dim == 0:
        return grad.reshape(shards, -1)
    rows = grad.shape[0]
    return jnp.transpose(grad.reshape(rows, shards, -1), (1, 0, 2)).reshape(shards, -1)


def from_pieces(received, shard_dim, shape, shards):
    summed = jnp.sum(received, axis=0)
    if shard_dim == 0:
        return summed.reshape(shape[0] // shards, shape[1])
    return summed.reshape(shape[0], shape[1] // shards)


def head_pair(matrix, pair_index):
    return lax.dynamic_slice_in_dim(matrix, pair_index * 2 * HEAD, 2 * HEAD, 1).reshape(
        matrix.shape[0], 2, HEAD
    )


def pair_stats(stats, pair_index):
    return lax.dynamic_slice_in_dim(stats, pair_index * 2, 2, 0)


def relative_bias(distance, bias_info, pair_index):
    starts, table = bias_info
    table_pair = lax.dynamic_slice_in_dim(table, pair_index * 2, 2, 1)

    def add_step(bucket, total):
        rise = table_pair[bucket] - table_pair[bucket - 1]
        return total + jnp.where(distance[None] >= starts[bucket], rise[:, None, None], 0.0)

    start_bias = jnp.broadcast_to(table_pair[0][:, None, None], (2,) + distance.shape)
    return lax.fori_loop(1, BUCKETS, add_step, start_bias)


def relative_grads(distance, starts, score_grad):

    def one_step(bucket):
        return jnp.sum(jnp.where(distance[None] >= starts[bucket], score_grad, 0.0), axis=(1, 2))

    steps_sum = lax.map(one_step, jnp.arange(BUCKETS, dtype=jnp.int32))
    return steps_sum - jnp.concatenate([steps_sum[1:], jnp.zeros((1, 2), jnp.float32)], axis=0)


def pair_scores(query_block, key_rows, pair_index, layout):
    allowed, distance, bias_info = layout
    scores = jnp.einsum(
        "qhe,khe->hqk",
        head_pair(query_block, pair_index),
        head_pair(key_rows, pair_index),
        preferred_element_type=jnp.float32,
    )
    if bias_info is not None:
        scores = scores + relative_bias(distance, bias_info, pair_index)
    return jnp.where(allowed[None], scores, MASKED)


def forward_parts(query_block, key_rows, value_rows, layout):
    block_rows = query_block.shape[0]
    width = 2 * HEAD

    def forward_one_pair(pair_index, carry):
        numerator, largest, totals = carry
        scores = pair_scores(query_block, key_rows, pair_index, layout)
        pair_top = jnp.max(scores, axis=2)
        weights = jnp.exp(scores - pair_top[:, :, None])
        partial_sum = jnp.einsum(
            "hqk,khe->qhe",
            weights.astype(jnp.bfloat16),
            head_pair(value_rows, pair_index),
            preferred_element_type=jnp.float32,
        )
        numerator = lax.dynamic_update_slice_in_dim(
            numerator, partial_sum.reshape(block_rows, width), pair_index * width, 1
        )
        largest = lax.dynamic_update_slice_in_dim(largest, pair_top, pair_index * 2, 0)
        totals = lax.dynamic_update_slice_in_dim(
            totals, jnp.sum(weights, axis=2), pair_index * 2, 0
        )
        return (numerator, largest, totals)

    start_state = (
        jnp.zeros((block_rows, HEADS * HEAD), jnp.float32),
        jnp.zeros((HEADS, block_rows), jnp.float32),
        jnp.zeros((HEADS, block_rows), jnp.float32),
    )
    return lax.fori_loop(0, HEADS // 2, forward_one_pair, start_state)


def backward_parts(query_block, key_rows, value_rows, layout, top_rows, num_grad, total_grad):
    allowed, distance, bias_info = layout
    block_rows = query_block.shape[0]
    key_count = key_rows.shape[0]
    width = 2 * HEAD

    def backward_one_pair(pair_index, carry):
        query_grad, key_grad, value_grad, bias_grad = carry
        query_pair = head_pair(query_block, pair_index)
        key_pair = head_pair(key_rows, pair_index)
        value_pair = head_pair(value_rows, pair_index)
        grad_pair = head_pair(num_grad, pair_index)
        scores = pair_scores(query_block, key_rows, pair_index, layout)
        weights = jnp.exp(scores - pair_stats(top_rows, pair_index)[:, :, None])
        weight_grad = jnp.einsum(
            "qhe,khe->hqk", grad_pair, value_pair, preferred_element_type=jnp.float32
        )
        score_grad = (
            weights * (weight_grad + pair_stats(total_grad, pair_index)[:, :, None])
        ).astype(jnp.bfloat16)
        part_query = jnp.einsum(
            "hqk,khe->qhe", score_grad, key_pair, preferred_element_type=jnp.float32
        )
        part_key = jnp.einsum(
            "hqk,qhe->khe", score_grad, query_pair, preferred_element_type=jnp.float32
        )
        part_value = jnp.einsum(
            "hqk,qhe->khe",
            weights.astype(jnp.bfloat16),
            grad_pair,
            preferred_element_type=jnp.float32,
        )
        query_grad = lax.dynamic_update_slice_in_dim(
            query_grad, part_query.reshape(block_rows, width), pair_index * width, 1
        )
        key_grad = lax.dynamic_update_slice_in_dim(
            key_grad, part_key.reshape(key_count, width), pair_index * width, 1
        )
        value_grad = lax.dynamic_update_slice_in_dim(
            value_grad, part_value.reshape(key_count, width), pair_index * width, 1
        )
        if bias_info is not None:
            pair_bias_grad = relative_grads(distance, bias_info[0], score_grad.astype(jnp.float32))
            bias_grad = lax.dynamic_update_slice_in_dim(
                bias_grad, pair_bias_grad, pair_index * 2, 1
            )
        return (query_grad, key_grad, value_grad, bias_grad)

    bias_start = None if bias_info is None else jnp.zeros((BUCKETS, HEADS), jnp.float32)
    start_state = (
        jnp.zeros((block_rows, HEADS * HEAD), jnp.float32),
        jnp.zeros((key_count, HEADS * HEAD), jnp.float32),
        jnp.zeros((key_count, HEADS * HEAD), jnp.float32),
        bias_start,
    )
    return lax.fori_loop(0, HEADS // 2, backward_one_pair, start_state)


def normalize(numerator, totals):
    row_count = numerator.shape[0]
    shaped = numerator.reshape(row_count, HEADS, HEAD) / jnp.transpose(totals)[:, :, None]
    return shaped.reshape(row_count, HEADS * HEAD).astype(jnp.bfloat16)


def output_grads(out_grad, numerator, totals):
    row_count = out_grad.shape[0]
    per_total = jnp.transpose(totals)
    shaped_grad = out_grad.reshape(row_count, HEADS, HEAD)
    num_grad = (
        (shaped_grad / per_total[:, :, None]).reshape(row_count, HEADS * HEAD).astype(jnp.bfloat16)
    )
    total_grad = -jnp.sum(shaped_grad * numerator.reshape(row_count, HEADS, HEAD), axis=2) / (
        per_total * per_total
    )
    return (num_grad, jnp.transpose(total_grad))


def body(
    hidden_in,
    encoder_out,
    grad_out,
    tgt_lengths,
    enc_lengths,
    rel_bucket,
    norm1_gain,
    self_q,
    self_k,
    self_v,
    self_o,
    rel_table,
    norm2_gain,
    cross_q,
    cross_k,
    cross_v,
    cross_o,
    norm3_gain,
    ff_gate,
    ff_up,
    ff_out,
):
    w_query, w_key, w_value, w_out, c_query, c_key, c_value, c_out, w_gate, w_up, w_down = (
        lax.all_gather(self_q.astype(jnp.bfloat16), ("dp", "enc"), axis=1, tiled=True),
        lax.all_gather(self_k.astype(jnp.bfloat16), ("dp", "enc"), axis=1, tiled=True),
        lax.all_gather(self_v.astype(jnp.bfloat16), ("dp", "enc"), axis=1, tiled=True),
        lax.all_gather(self_o.astype(jnp.bfloat16), ("dp", "enc"), axis=0, tiled=True),
        lax.all_gather(cross_q.astype(jnp.bfloat16), ("dp", "enc"), axis=1, tiled=True),
        lax.all_gather(cross_k.astype(jnp.bfloat16), ("dp", "enc"), axis=1, tiled=True),
        lax.all_gather(cross_v.astype(jnp.bfloat16), ("dp", "enc"), axis=1, tiled=True),
        lax.all_gather(cross_o.astype(jnp.bfloat16), ("dp", "enc"), axis=0, tiled=True),
        lax.all_gather(ff_gate.astype(jnp.bfloat16), ("dp", "enc"), axis=1, tiled=True),
        lax.all_gather(ff_up.astype(jnp.bfloat16), ("dp", "enc"), axis=1, tiled=True),
        lax.all_gather(ff_out.astype(jnp.bfloat16), ("dp", "enc"), axis=0, tiled=True),
    )
    enc_count = lax.axis_size("enc")
    enc_place = lax.axis_index("enc")
    own_rows = hidden_in.shape[0]
    group_rows = own_rows * enc_count
    own_enc = encoder_out.shape[0]
    group_enc = own_enc * enc_count
    tgt_items = item_ids(tgt_lengths[0], group_rows)
    enc_items = item_ids(enc_lengths[0], group_enc)
    row_start = enc_place * own_rows
    own_items = lax.dynamic_slice_in_dim(tgt_items, row_start, own_rows)
    own_enc_items = lax.dynamic_slice_in_dim(enc_items, enc_place * own_enc, own_enc)
    bucket_starts = jnp.sum(
        (rel_bucket[None, :] < jnp.arange(BUCKETS, dtype=jnp.int32)[:, None]).astype(jnp.int32),
        axis=1,
    )
    query_place = row_start + jnp.arange(own_rows, dtype=jnp.int32)
    distance = query_place[:, None] - jnp.arange(group_rows, dtype=jnp.int32)[None, :]
    self_layout = (
        (distance >= 0) & (own_items[:, None] == tgt_items[None, :]),
        distance,
        (bucket_starts, rel_table),
    )
    hidden = hidden_in.astype(jnp.float32)
    normed_full, pull_one = jax.vjp(rms_scale, hidden, norm1_gain)
    normed = normed_full.astype(jnp.bfloat16)
    queries = product(normed, w_query).astype(jnp.bfloat16)
    key_own = product(normed, w_key).astype(jnp.bfloat16)
    value_own = product(normed, w_value).astype(jnp.bfloat16)
    key_group, value_group = (
        lax.all_gather(key_own, "enc", axis=0, tiled=True),
        lax.all_gather(value_own, "enc", axis=0, tiled=True),
    )
    self_num, self_top, self_total = forward_parts(queries, key_group, value_group, self_layout)
    attended = normalize(self_num, self_total)
    after_self = hidden + product(attended, w_out)
    normed_two_full, pull_two = jax.vjp(rms_scale, after_self, norm2_gain)
    normed_two = normed_two_full.astype(jnp.bfloat16)
    cross_queries = product(normed_two, c_query).astype(jnp.bfloat16)
    cross_keys = product(encoder_out, c_key).astype(jnp.bfloat16)
    cross_values = product(encoder_out, c_value).astype(jnp.bfloat16)
    query_group = lax.all_gather(cross_queries, "enc", axis=0, tiled=True)
    block_rows = min(512, group_rows)
    block_count = group_rows // block_rows

    def block_layout(first_row):
        query_items = lax.dynamic_slice_in_dim(tgt_items, first_row, block_rows)
        return (query_items[:, None] == own_enc_items[None, :], None, None)

    def block_forward(block_index, carry):
        numerator_all, top_all, total_all = carry
        first_row = block_index * block_rows
        block_num, block_top, block_total = forward_parts(
            lax.dynamic_slice_in_dim(query_group, first_row, block_rows, 0),
            cross_keys,
            cross_values,
            block_layout(first_row),
        )
        numerator_all = lax.dynamic_update_slice_in_dim(numerator_all, block_num, first_row, 0)
        top_all = lax.dynamic_update_slice_in_dim(top_all, block_top, first_row, 1)
        total_all = lax.dynamic_update_slice_in_dim(total_all, block_total, first_row, 1)
        return (numerator_all, top_all, total_all)

    numerator_all, local_tops, total_all = lax.fori_loop(
        0,
        block_count,
        block_forward,
        (
            jnp.zeros((group_rows, HEADS * HEAD), jnp.float32),
            jnp.zeros((HEADS, group_rows), jnp.float32),
            jnp.zeros((HEADS, group_rows), jnp.float32),
        ),
    )
    group_top = lax.pmax(local_tops, "enc")
    rescale = jnp.exp(local_tops - group_top)
    numerator_all = (
        numerator_all.reshape(group_rows, HEADS, HEAD) * jnp.transpose(rescale)[:, :, None]
    ).reshape(group_rows, HEADS * HEAD)
    total_all = total_all * rescale
    cross_num, cross_total = (
        lax.psum_scatter(
            numerator_all.astype(jnp.bfloat16), "enc", scatter_dimension=0, tiled=True
        ).astype(jnp.float32),
        lax.psum_scatter(
            total_all.astype(jnp.bfloat16), "enc", scatter_dimension=1, tiled=True
        ).astype(jnp.float32),
    )
    attended_two = normalize(cross_num, cross_total)
    after_cross = after_self + product(attended_two, c_out)
    normed_three_full, pull_three = jax.vjp(rms_scale, after_cross, norm3_gain)
    normed_three = normed_three_full.astype(jnp.bfloat16)
    gate_pre = product(normed_three, w_gate)
    up_pre = product(normed_three, w_up)
    activated, pull_act = jax.vjp(gated_gelu, gate_pre, up_pre)
    hidden_act = activated.astype(jnp.bfloat16)
    hidden_out = (after_cross + product(hidden_act, w_down)).astype(jnp.bfloat16)
    out_grad = grad_out.astype(jnp.float32)
    down_grad = product_tn(hidden_act, grad_out)
    act_grad = product_nt(grad_out, w_down)
    gate_grad_full, up_grad_full = pull_act(act_grad)
    gate_grad = gate_grad_full.astype(jnp.bfloat16)
    up_grad = up_grad_full.astype(jnp.bfloat16)
    gate_w_grad = product_tn(normed_three, gate_grad)
    up_w_grad = product_tn(normed_three, up_grad)
    normed_three_grad = product_nt(gate_grad, w_gate) + product_nt(up_grad, w_up)
    cross_res_grad, gain_three_grad = pull_three(normed_three_grad)
    after_cross_grad = out_grad + cross_res_grad
    branch_two = after_cross_grad.astype(jnp.bfloat16)
    c_out_grad = product_tn(attended_two, branch_two)
    cross_out_grad = product_nt(branch_two, c_out)
    cross_num_grad, cross_total_grad = output_grads(cross_out_grad, cross_num, cross_total)
    num_grad_group = lax.all_gather(cross_num_grad, "enc", axis=0, tiled=True)
    total_grad_group = lax.all_gather(cross_total_grad, "enc", axis=1, tiled=True)

    def block_backward(block_index, carry):
        query_grad_all, key_grad_sum, value_grad_sum = carry
        first_row = block_index * block_rows
        block_query_grad, block_key_grad, block_value_grad, unused_bias = backward_parts(
            lax.dynamic_slice_in_dim(query_group, first_row, block_rows, 0),
            cross_keys,
            cross_values,
            block_layout(first_row),
            lax.dynamic_slice_in_dim(group_top, first_row, block_rows, 1),
            lax.dynamic_slice_in_dim(num_grad_group, first_row, block_rows, 0),
            lax.dynamic_slice_in_dim(total_grad_group, first_row, block_rows, 1),
        )
        query_grad_all = lax.dynamic_update_slice_in_dim(
            query_grad_all, block_query_grad, first_row, 0
        )
        return (query_grad_all, key_grad_sum + block_key_grad, value_grad_sum + block_value_grad)

    query_grad_all, cross_key_grad, cross_value_grad = lax.fori_loop(
        0,
        block_count,
        block_backward,
        (
            jnp.zeros((group_rows, HEADS * HEAD), jnp.float32),
            jnp.zeros((own_enc, HEADS * HEAD), jnp.float32),
            jnp.zeros((own_enc, HEADS * HEAD), jnp.float32),
        ),
    )
    cross_query_grad = lax.psum_scatter(
        query_grad_all.astype(jnp.bfloat16), "enc", scatter_dimension=0, tiled=True
    )
    cross_key_low = cross_key_grad.astype(jnp.bfloat16)
    cross_value_low = cross_value_grad.astype(jnp.bfloat16)
    c_query_grad = product_tn(normed_two, cross_query_grad)
    c_key_grad = product_tn(encoder_out, cross_key_low)
    c_value_grad = product_tn(encoder_out, cross_value_low)
    encoder_grad = product_nt(cross_key_low, c_key) + product_nt(cross_value_low, c_value)
    self_res_grad, gain_two_grad = pull_two(product_nt(cross_query_grad, c_query))
    after_self_grad = after_cross_grad + self_res_grad
    branch_one = after_self_grad.astype(jnp.bfloat16)
    w_out_grad = product_tn(attended, branch_one)
    self_out_grad = product_nt(branch_one, w_out)
    self_num_grad, self_total_grad = output_grads(self_out_grad, self_num, self_total)
    self_query_grad, key_grad_rows, value_grad_rows, table_grad = backward_parts(
        queries, key_group, value_group, self_layout, self_top, self_num_grad, self_total_grad
    )
    self_key_grad, self_value_grad = (
        lax.psum_scatter(
            key_grad_rows.astype(jnp.bfloat16), "enc", scatter_dimension=0, tiled=True
        ).astype(jnp.float32),
        lax.psum_scatter(
            value_grad_rows.astype(jnp.bfloat16), "enc", scatter_dimension=0, tiled=True
        ).astype(jnp.float32),
    )
    query_low = self_query_grad.astype(jnp.bfloat16)
    key_low = self_key_grad.astype(jnp.bfloat16)
    value_low = self_value_grad.astype(jnp.bfloat16)
    w_query_grad = product_tn(normed, query_low)
    w_key_grad = product_tn(normed, key_low)
    w_value_grad = product_tn(normed, value_low)
    normed_grad = (
        product_nt(query_low, w_query) + product_nt(key_low, w_key) + product_nt(value_low, w_value)
    )
    input_res_grad, gain_one_grad = pull_one(normed_grad)
    hidden_grad = after_self_grad + input_res_grad
    shards = lax.axis_size(("dp", "enc"))
    full_grads = (
        w_query_grad,
        w_key_grad,
        w_value_grad,
        w_out_grad,
        c_query_grad,
        c_key_grad,
        c_value_grad,
        c_out_grad,
        gate_w_grad,
        up_w_grad,
        down_grad,
    )
    shard_dims = (1, 1, 1, 0, 1, 1, 1, 0, 1, 1, 0)
    piece_rows = tuple(
        (to_pieces(grad, place, shards) for grad, place in zip(full_grads, shard_dims))
    )
    received = (
        lax.all_to_all(
            piece_rows[0].astype(jnp.bfloat16),
            ("dp", "enc"),
            split_axis=0,
            concat_axis=0,
            tiled=True,
        ).astype(jnp.float32),
        lax.all_to_all(
            piece_rows[1].astype(jnp.bfloat16),
            ("dp", "enc"),
            split_axis=0,
            concat_axis=0,
            tiled=True,
        ).astype(jnp.float32),
        lax.all_to_all(
            piece_rows[2].astype(jnp.bfloat16),
            ("dp", "enc"),
            split_axis=0,
            concat_axis=0,
            tiled=True,
        ).astype(jnp.float32),
        lax.all_to_all(
            piece_rows[3].astype(jnp.bfloat16),
            ("dp", "enc"),
            split_axis=0,
            concat_axis=0,
            tiled=True,
        ).astype(jnp.float32),
        lax.all_to_all(
            piece_rows[4].astype(jnp.bfloat16),
            ("dp", "enc"),
            split_axis=0,
            concat_axis=0,
            tiled=True,
        ).astype(jnp.float32),
        lax.all_to_all(
            piece_rows[5].astype(jnp.bfloat16),
            ("dp", "enc"),
            split_axis=0,
            concat_axis=0,
            tiled=True,
        ).astype(jnp.float32),
        lax.all_to_all(
            piece_rows[6].astype(jnp.bfloat16),
            ("dp", "enc"),
            split_axis=0,
            concat_axis=0,
            tiled=True,
        ).astype(jnp.float32),
        lax.all_to_all(
            piece_rows[7].astype(jnp.bfloat16),
            ("dp", "enc"),
            split_axis=0,
            concat_axis=0,
            tiled=True,
        ).astype(jnp.float32),
        lax.all_to_all(
            piece_rows[8].astype(jnp.bfloat16),
            ("dp", "enc"),
            split_axis=0,
            concat_axis=0,
            tiled=True,
        ).astype(jnp.float32),
        lax.all_to_all(
            piece_rows[9].astype(jnp.bfloat16),
            ("dp", "enc"),
            split_axis=0,
            concat_axis=0,
            tiled=True,
        ).astype(jnp.float32),
        lax.all_to_all(
            piece_rows[10].astype(jnp.bfloat16),
            ("dp", "enc"),
            split_axis=0,
            concat_axis=0,
            tiled=True,
        ).astype(jnp.float32),
    )
    weight_grads = tuple(
        (
            from_pieces(piece, place, grad.shape, shards)
            for piece, place, grad in zip(received, shard_dims, full_grads)
        )
    )
    small_sums = lax.psum(
        (gain_one_grad, gain_two_grad, gain_three_grad, table_grad), ("dp", "enc")
    )
    return (
        hidden_out,
        hidden_grad,
        encoder_grad,
        small_sums[0],
        weight_grads[0],
        weight_grads[1],
        weight_grads[2],
        weight_grads[3],
        small_sums[3],
        small_sums[1],
        weight_grads[4],
        weight_grads[5],
        weight_grads[6],
        weight_grads[7],
        small_sums[2],
        weight_grads[8],
        weight_grads[9],
        weight_grads[10],
    )


def solution(mesh):
    return jax.shard_map(
        fast_body if dict(mesh.shape) == {"dp": 8, "enc": 4} else body,
        mesh=mesh,
        in_specs=(
            P(("dp", "enc"), None),
            P(("dp", "enc"), None),
            P(("dp", "enc"), None),
            P("dp", None),
            P("dp", None),
            P(),
            P(),
            P(None, ("dp", "enc")),
            P(None, ("dp", "enc")),
            P(None, ("dp", "enc")),
            P(("dp", "enc"), None),
            P(),
            P(),
            P(None, ("dp", "enc")),
            P(None, ("dp", "enc")),
            P(None, ("dp", "enc")),
            P(("dp", "enc"), None),
            P(),
            P(None, ("dp", "enc")),
            P(None, ("dp", "enc")),
            P(("dp", "enc"), None),
        ),
        out_specs=(
            P(("dp", "enc"), None),
            P(("dp", "enc"), None),
            P(("dp", "enc"), None),
            P(),
            P(None, ("dp", "enc")),
            P(None, ("dp", "enc")),
            P(None, ("dp", "enc")),
            P(("dp", "enc"), None),
            P(),
            P(),
            P(None, ("dp", "enc")),
            P(None, ("dp", "enc")),
            P(None, ("dp", "enc")),
            P(("dp", "enc"), None),
            P(),
            P(None, ("dp", "enc")),
            P(None, ("dp", "enc")),
            P(("dp", "enc"), None),
        ),
        check_vma=False,
    )
```
